32 devices in a mesh: parts: 2 (over y), wide: 8 (over z, core), tp: 2 (over x), sub: 1.
Axes of the slice: x: 2, y: 2, z: 4, core: 2. Of those that a mesh axis runs over, the one named last changes fastest.
Arguments:
- queries: bfloat16 [4096, 8192], P(('parts', 'wide'), ('tp', 'sub')), parts along dimension 0, may hold values from -130 to 130
- resp_kv: bfloat16 [4096, 2048], P(('parts', 'wide'), ('tp', 'sub')), parts along dimension 0, may hold values from -6 to 6
- prefix_pool: bfloat16 [16384, 2048], P(('parts', 'wide'), ('tp', 'sub')), parts along dimension 0, may hold values from -6 to 6
- out_weight: bfloat16 [8192, 5120], P(('tp', 'sub')), may hold values from -0.375 to 0.375
- pre_len: int32 [8], P('parts'), parts along dimension 0, may hold values from 1 to 16, 40 in all
- prompt_blocks: int32 [8], P('parts'), parts along dimension 0, may hold values from 1 to 5, 12 in all
- prompt_owner: int32 [8], P('parts'), parts along dimension 0, may hold values from 0 to 7
- resp_seg: int32 [32], P(('parts', 'wide')), parts along dimension 0, may hold values from 0 to 15, as said below
Outputs:
- scored: bfloat16 [4096, 5120], P(('parts', 'wide'), ('tp', 'sub')), parts along dimension 0
The draws below stay inside these ranges and needn't reach their ends.
There are 2 independent parts, one for each index of `parts`. The reference program is written for one: setup_inputs(seed, part) draws one part's arguments, and reference() takes and returns one part's arrays. A program takes and returns all parts, laid end to end along the dimension named above; an argument that names none is the same for every part. Nothing has to cross between parts.
Inputs may be any that keep to these rules, and one draw needn't show every extreme that they name: prompt_blocks sums to 2 * (8 - 4) + 4. resp_seg never falls along the blocks, and blocks with equal resp_seg lie in one aligned group of 2 blocks.
All inputs are finite; a program needn't handle non-finite values.
Results may differ from the reference program's by a relative error of at most 0.02.
Values may be sent and summed in bfloat16 or wider, within the bound.
No kernel may reach another device: no remote copies, remote signals or barrier semaphores. Data moves between devices by JAX's collectives and lax.ppermute only.
A program may use at most 192 MiB of HBM per device.

```python
import math
import jax
import jax.numpy as jnp
import numpy as np
from jax import lax

D = 5120
QH = 64
KVH = 8
HD = 128
BLOCK = 128
RB_DEV = 2
PROMPTS = 4
PMAX = 16
GROUP = 8
TOK_DEV = 256
TOKENS = 2048
RBLOCKS = 16
PSTRIDE = 2
POOL = 8192
N_WIDE = 8
N_TP = 2
N_SUB = 1


def shared_keys(key):
    return jax.random.truncated_normal(key, -6.0, 6.0, (TOKENS, KVH, 2, HD), jnp.float32)


def draw_queries(key, part):
    key = jax.random.fold_in(key, 11)
    drawn = 2.0 * jax.random.truncated_normal(key, -6.0, 6.0, (TOKENS, KVH, GROUP, HD), jnp.float32)
    return drawn.reshape(TOKENS, QH * HD).astype(jnp.bfloat16)


def draw_resp_kv(key, part):
    keys_values = shared_keys(key)
    return keys_values.reshape(TOKENS, KVH * 2 * HD).astype(jnp.bfloat16)


def draw_resp_seg(key, part):
    key = jax.random.fold_in(key, 21)
    group_count = RBLOCKS // RB_DEV
    group_ids = jnp.arange(group_count, dtype=jnp.int32)
    cuts = jax.random.randint(key, (group_count,), 0, RB_DEV + 1).astype(jnp.int32)
    cuts = jnp.where(group_ids == 0, 1, cuts)
    cuts = jnp.where(group_ids == group_count - 1, 0, cuts).astype(jnp.int32)
    block_ids = jnp.arange(RBLOCKS, dtype=jnp.int32)
    owner_group = block_ids // RB_DEV
    within = block_ids % RB_DEV
    return (2 * owner_group + (within >= cuts[owner_group]).astype(jnp.int32)).astype(jnp.int32)


def place_ends(values, rng, least, top_value):
    longest = values.shape.index(max(values.shape))
    spots = []
    for shift in (0, 1):
        where = [jax.random.randint(jax.random.fold_in(rng, axis), (), 0, length) for axis, length in enumerate(values.shape)]
        where[longest] = (where[longest] + shift) % values.shape[longest]
        spots.append(tuple(where))
    return values.at[spots[0]].set(least).at[spots[1]].set(top_value)


def spiked(values, key, source, target, shards_of, factor):
    owner, partner = [(jnp.arange(values.shape[axis_at]) // (values.shape[axis_at] // shards_of)).reshape([-1 if axis == axis_at else 1 for axis in range(values.ndim)]) for axis_at in (source, target)]
    chosen = jax.random.permutation(key, shards_of)[partner]
    strong = (owner == chosen) | (owner == (partner + shards_of // 2) % shards_of)
    return jnp.where(strong, factor * values, values)


def shard_levels(rng, extent, split, smallest, top_value):
    factor_of, own = 1.0, jax.random.fold_in(rng, 6)
    for dim, shards_of in split:
        draws = jnp.exp(jax.random.uniform(jax.random.fold_in(own, dim), (shards_of,), jnp.float32, smallest / len(split), top_value / len(split)))
        factor_of = factor_of * jnp.repeat(draws, extent[dim] // shards_of).reshape([-1 if axis == dim else 1 for axis in range(len(extent))])
    return factor_of


def split_up(amount, total, reach, skew):
    portions = [(1 << 20) // math.isqrt(standing ** skew) + 1 for standing in range(2, amount + 1)]
    surplus, counts = total - reach - (amount - 1), [1] * (amount - 1)
    while surplus > 0:
        movable = [i for i in range(amount - 1) if counts[i] < reach]
        mass, remaining = sum([portions[i] for i in movable]), surplus
        for i in movable:
            extra = min(reach - counts[i], max(1, remaining * portions[i] // mass), surplus)
            counts[i] = counts[i] + extra
            surplus = surplus - extra
    return np.array([reach] + counts)


def uneven_parts(stream_key, count, total, most, skew):
    if count == 2:
        one = jax.random.randint(stream_key, (), max(1, total - most), min(most, total - 1) + 1)
        return jnp.stack([one, total - one])
    lengths = jnp.asarray(split_up(count, total, most, skew), jnp.int32)
    twos = (count - 1) // 2
    source_of, taker = lengths[1:1 + 2 * twos:2], lengths[2:2 + 2 * twos:2]
    slack = jnp.minimum(source_of - 1, most - taker)
    passed = jax.random.randint(jax.random.fold_in(stream_key, 1), (twos,), 0, 1 << 20) % (slack + 1)
    lengths = lengths.at[1:1 + 2 * twos:2].set(source_of - passed).at[2:2 + 2 * twos:2].set(taker + passed)
    return lengths[jax.random.permutation(jax.random.fold_in(stream_key, 2), count)]


def scatter_about(rng, extent, width, most, shards=(), kind=jnp.bfloat16):
    level = shard_levels(rng, extent, shards, -0.22, 0.18) if shards else 1.0
    values = jax.random.normal(rng, extent, jnp.float32) * width * level
    return jnp.minimum(jnp.maximum(values, -most), most).astype(kind)


def heavy_noise(stream_key, extent, spread, most, shards, heavy, held_as=jnp.bfloat16):
    values = spread * jax.random.normal(stream_key, extent, jnp.float32)
    if shards:
        values = values * shard_levels(stream_key, extent, shards, -0.22, 0.18)
    return jnp.clip(spiked(values, jax.random.fold_in(stream_key, 3), *heavy), -most, most).astype(held_as)


def setup_inputs(seed: int = 0, part: int = 0) -> dict:
    keys = jax.random.split(jax.random.key(seed), 9)
    part_keys = jax.random.split(jax.random.fold_in(keys[8], part), 9)
    queries = draw_queries(jax.random.fold_in(jax.random.fold_in(keys[8], part), 71), part)
    resp_kv = draw_resp_kv(jax.random.fold_in(jax.random.fold_in(keys[8], part), 71), part)
    prefix_pool = scatter_about(part_keys[2], (POOL, KVH * 2 * HD), 1.0, 6.0, ((0, 8), (1, 2)))
    out_weight = heavy_noise(keys[3], (QH * HD, D), (4 * HD) ** -0.5, 0.375, ((0, 2),), (0, 1, 2, 2.0))
    pre_len = uneven_parts(part_keys[4], PROMPTS, PROMPTS * PMAX * 5 // 8, PMAX, 2).astype(jnp.int32)
    prompt_blocks = uneven_parts(part_keys[5], PROMPTS, RB_DEV * (N_WIDE - PROMPTS) + PROMPTS, RB_DEV * (N_WIDE - PROMPTS) // 2 + 1, 2).astype(jnp.int32)
    prompt_owner = place_ends(jax.random.randint(part_keys[6], (PROMPTS,), 0, N_WIDE), jax.random.fold_in(part_keys[6], 1), 0, N_WIDE - 1).astype(jnp.int32)
    resp_seg = draw_resp_seg(jax.random.fold_in(jax.random.fold_in(keys[8], part), 71), part)
    return {"queries": queries, "resp_kv": resp_kv, "prefix_pool": prefix_pool, "out_weight": out_weight, "pre_len": pre_len, "prompt_blocks": prompt_blocks, "prompt_owner": prompt_owner, "resp_seg": resp_seg}


def head_attention(operands, visible):
    head_queries, head_keys = operands
    scores = jnp.einsum('teh,kh->tek', head_queries, head_keys[:, 0], precision=lax.Precision.HIGHEST) / math.sqrt(HD)
    scores = jnp.where(visible[:, None, :], scores, -jnp.inf)
    row_max = lax.optimization_barrier(jnp.max(scores, axis=-1, keepdims=True))
    weights = jnp.where(visible[:, None, :], jnp.exp(scores - row_max), 0.0)
    denominator = lax.optimization_barrier(jnp.sum(weights, axis=-1, keepdims=True))
    rounded = lax.optimization_barrier(weights.astype(jnp.bfloat16)).astype(jnp.float32)
    blended = jnp.einsum('tek,kh->teh', rounded, head_keys[:, 1], precision=lax.Precision.HIGHEST)
    return (blended / denominator).astype(jnp.bfloat16)

def reference(queries, resp_kv, prefix_pool, out_weight, pre_len, prompt_blocks, prompt_owner, resp_seg):
    block_ends = jnp.cumsum(prompt_blocks + (RB_DEV - 1))
    all_blocks = jnp.arange(RBLOCKS, dtype=jnp.int32)
    block_prompt = lax.optimization_barrier(jnp.sum((all_blocks[:, None] >= block_ends[None, :]).astype(jnp.int32), axis=1)).astype(jnp.int32)
    per_owner = PROMPTS * PSTRIDE
    stored = prefix_pool.reshape(N_WIDE * per_owner, BLOCK, KVH, 2, HD)

    def one_group(group_id):
        prompts_here = lax.dynamic_slice_in_dim(block_prompt, (group_id * RB_DEV).astype(jnp.int32), RB_DEV)
        seg_here = lax.dynamic_slice_in_dim(resp_seg, (group_id * RB_DEV).astype(jnp.int32), RB_DEV)
        tok_prompt = jnp.repeat(prompts_here, BLOCK)
        tok_seg = jnp.repeat(seg_here, BLOCK)
        slot_prompts = jnp.stack([prompts_here[0], prompts_here[RB_DEV - 1]])
        second = slot_prompts[1] != slot_prompts[0]
        page_no = jnp.arange(PMAX, dtype=jnp.int32)
        owner_dev = (prompt_owner[slot_prompts][:, None] + page_no[None, :]) % N_WIDE
        page_rows = (owner_dev * per_owner + slot_prompts[:, None] * PSTRIDE + page_no[None, :] // N_WIDE).astype(jnp.int32)
        usable = (page_no[None, :] < pre_len[slot_prompts][:, None]) & jnp.stack([jnp.array(True), second])[:, None]
        fetched = stored[page_rows.reshape(-1)]
        prefix_keys = fetched.reshape(2 * PMAX * BLOCK, KVH, 2, HD)
        key_prompt = jnp.repeat(slot_prompts, PMAX * BLOCK)
        key_usable = jnp.repeat(usable.reshape(-1), BLOCK)
        own_keys = lax.dynamic_slice_in_dim(resp_kv, (group_id * TOK_DEV).astype(jnp.int32), TOK_DEV).reshape(TOK_DEV, KVH, 2, HD)
        keys_all = jnp.concatenate([prefix_keys, own_keys], axis=0).astype(jnp.float32)
        positions = jnp.arange(TOK_DEV, dtype=jnp.int32)
        own_mask = (tok_seg[:, None] == tok_seg[None, :]) & (tok_prompt[:, None] == tok_prompt[None, :]) & (positions[None, :] <= positions[:, None])
        prefix_mask = (key_prompt[None, :] == tok_prompt[:, None]) & key_usable[None, :]
        visible = jnp.concatenate([prefix_mask, own_mask], axis=1)
        query_rows = lax.dynamic_slice_in_dim(queries, (group_id * TOK_DEV).astype(jnp.int32), TOK_DEV)
        query_rows = query_rows.reshape(TOK_DEV, KVH, GROUP, HD).astype(jnp.float32)
        per_head = lax.map(partial_head(visible), (jnp.moveaxis(query_rows, 1, 0), jnp.moveaxis(keys_all, 1, 0)))
        return jnp.moveaxis(per_head, 0, 1).reshape(TOK_DEV, QH * HD)
    attended = lax.map(one_group, jnp.arange(N_WIDE, dtype=jnp.int32)).reshape(TOKENS, QH * HD)
    groups = N_TP * N_SUB
    rows_each = QH * HD // groups
    result = jnp.zeros((TOKENS, D), jnp.float32)
    for part_id in range(groups):
        term = jnp.dot(attended[:, part_id * rows_each:(part_id + 1) * rows_each], out_weight[part_id * rows_each:(part_id + 1) * rows_each], preferred_element_type=jnp.float32)
        rounded = lax.optimization_barrier(term.astype(jnp.bfloat16))
        result = result + rounded.astype(jnp.float32)
    return result.astype(jnp.bfloat16)

def partial_head(visible):

    def apply_head(operands):
        return head_attention(operands, visible)
    return apply_head
```

```python
import math

import jax
import jax.numpy as jnp
from jax import lax
from jax.experimental import pallas as pl
from jax.experimental.pallas import tpu as pltpu
from jax.sharding import PartitionSpec as P

HD = 128
BLOCK = 128
RB_DEV = 2
PROMPTS = 4
PMAX = 16
GROUP = 8
PAIR = 2 * HD
WIDTH = GROUP * HD
ROWS = 256
SPAN = 4
NEAR = 6
FAR = 4
NEG_LARGE = -1e30
SCALE = math.log2(math.e) / math.sqrt(HD)
VMEM_BYTES = 48 * 1024 * 1024

LEN_AT, BLOCKS_AT, OWNER_AT, SEG_AT, ME_AT = 0, 4, 8, 12, 14


def params():
    return pltpu.CompilerParams(vmem_limit_bytes=VMEM_BYTES)


def as_int(flag):
    return jnp.where(flag, 1, 0)


class Layout:
    def __init__(self, ctrl, wide, cores):
        self.ctrl, self.wide, self.cores = ctrl, wide, cores
        self.stride = (PMAX + wide - 1) // wide
        self.me = ctrl[ME_AT]
        self.z, self.core = self.me // cores, self.me % cores
        ends, total = [], 0
        for p in range(PROMPTS):
            total = total + ctrl[BLOCKS_AT + p] + (RB_DEV - 1)
            ends.append(total)
        self.ends = ends

    def prompt_of(self, block):
        return sum(as_int(block >= end) for end in self.ends[:-1])

    def first_of(self, chip):
        return self.prompt_of(chip * self.cores * RB_DEV)

    def last_of(self, chip):
        return self.prompt_of((chip + 1) * self.cores * RB_DEV - 1)

    def length(self, p):
        return self.ctrl[LEN_AT + p]

    def held_by(self, p, j):
        return lax.rem(self.ctrl[OWNER_AT + p] + j, self.wide)

    def held(self, p, who):
        first = lax.rem(who - self.ctrl[OWNER_AT + p] + self.wide, self.wide)
        return sum(as_int(first + k * self.wide < self.length(p)) for k in range(self.stride))

    def above(self, who, p, top):
        return sum(
            jnp.where((o > p) & (o <= top), self.held(o, who), 0) for o in range(PROMPTS)
        )

    def below(self, who, p, low):
        return sum(
            jnp.where((o < p) & (o >= low), self.held(o, who), 0) for o in range(PROMPTS)
        )

    def near_top(self, chip):
        return jnp.where(chip == 0, self.last_of(1), PROMPTS - 1)

    def near_low(self, chip):
        return jnp.where(chip == 3, self.first_of(2), 0)

    def in_plane(self, p, j):
        who = self.held_by(p, j)
        chip = who // self.cores
        gap = chip - self.z
        k = j // self.wide
        down = self.above(who, p, self.near_top(chip)) + k
        far_down = self.above(who, p, PROMPTS - 1) + k
        up = self.below(who, p, self.near_low(chip)) + k
        far_up = self.below(who, p, 0) + k
        inner = (self.z == 1) | (self.z == 2)
        far = jnp.where(gap < 0, far_down, far_up)
        two = (gap == 2) | (gap == -2)
        three = (gap == 3) | (gap == -3)
        return [
            (gap == 0, 0, p * self.stride + k),
            (gap == -1, 1, down),
            (gap == 1, 2, up),
            (two & inner, 3, far),
            ((two & jnp.logical_not(inner)) | three, 4, far + jnp.where(two, FAR, 0)),
        ]


def page_at(buffers, which, page, column):
    rows = pl.ds(pl.multiple_of(page * BLOCK, BLOCK), BLOCK)
    wide = buffers[which].shape[1] > PAIR
    return buffers[which].at[rows, pl.ds(column if wide else 0, PAIR)]


def start_page(buffers, places, column, target, sem):
    for cond, which, page in places:

        @pl.when(cond)
        def _(which=which, page=page):
            pltpu.make_async_copy(page_at(buffers, which, page, column), target, sem).start()


def wait_page(source, target, sem):
    pltpu.make_async_copy(source.at[pl.ds(0, BLOCK), pl.ds(0, PAIR)], target, sem).wait()


def spot(ref, page):
    return ref.at[pl.ds(pl.multiple_of(page * BLOCK, BLOCK), BLOCK), :]


def send_kernel(wide, cores, column, ctrl, pool, right, left, far, sems):
    lay = Layout(ctrl, wide, cores)
    z, last = lay.z, wide // cores - 1
    plans = []
    for p in range(PROMPTS):
        count = lay.held(p, lay.me)
        for k in range(lay.stride):
            here = k < count
            low, top = lay.first_of(z + 1), lay.near_top(z)
            plans.append(
                (here & (z < last) & (p >= low) & (p <= top), p, k, right, 0, lay.above(lay.me, p, top) + k)
            )
            low, top = lay.near_low(z), lay.last_of(z - 1)
            plans.append(
                (here & (z > 0) & (p >= low) & (p <= top), p, k, left, 1, lay.below(lay.me, p, low) + k)
            )
            low = lay.first_of(2)
            plans.append(
                (here & (z == 0) & (p >= low), p, k, far, 2, lay.above(lay.me, p, PROMPTS - 1) + k)
            )
            top = lay.last_of(1)
            plans.append(
                (here & (z == last) & (p <= top), p, k, far, 2, lay.below(lay.me, p, 0) + k)
            )

    def copy(plan):
        _, p, k, target, lane, rank = plan
        page = p * lay.stride + k
        return pltpu.make_async_copy(
            page_at([pool], 0, page, column), spot(target, rank), sems.at[lane, page]
        )

    for plan in plans:
        pl.when(plan[0])(lambda plan=plan: copy(plan).start())
    for plan in plans:
        pl.when(plan[0])(lambda plan=plan: copy(plan).wait())


def share_kernel(wide, cores, column, ctrl, *refs):
    buffers, out, sems = refs[:5], refs[5], refs[6]
    lay = Layout(ctrl, wide, cores)
    other = lay.z * cores + (cores - 1 - lay.core)
    half = PMAX // cores
    firsts = [lay.prompt_of(other * RB_DEV), lay.prompt_of(other * RB_DEV + 1)]
    moves = []
    for slot in range(RB_DEV):
        p = firsts[slot]
        shift = lax.rem(lay.core - lay.ctrl[OWNER_AT + p] + wide, cores)
        count = (lay.length(p) - shift + cores - 1) // cores
        if slot == 1:
            count = jnp.where(firsts[1] == firsts[0], 0, count)

        def begin(i, carry, slot=slot, p=p, shift=shift):
            start_page(
                buffers,
                lay.in_plane(p, i * cores + shift),
                column,
                spot(out, slot * half + i),
                sems.at[slot * half + i],
            )
            return carry

        lax.fori_loop(0, count, begin, 0)
        moves.append((slot, count))
    for slot, count in moves:

        def finish(i, carry, slot=slot):
            wait_page(buffers[0], spot(out, slot * half + i), sems.at[slot * half + i])
            return carry

        lax.fori_loop(0, count, finish, 0)


def attend_kernel(wide, cores, column, ctrl, queries, own, *refs):
    buffers, out = refs[:-6], refs[-6]
    store, stacked, peak, total, sems = refs[-5:]
    lay = Layout(ctrl, wide, cores)
    prompts = [lay.prompt_of(lay.me * RB_DEV + b) for b in range(RB_DEV)]
    same = prompts[0] == prompts[1]
    half = PMAX // cores

    def places(slot, p, j):
        if len(buffers) == 1:
            page = (lay.held_by(p, j) * PROMPTS + p) * lay.stride + j // wide
            return [(j >= 0, 0, page)]
        mine = lax.rem(lay.held_by(p, j), cores) == lay.core
        spots = [(cond & mine, which, page) for cond, which, page in lay.in_plane(p, j)]
        return spots + [(jnp.logical_not(mine), 5, slot * half + j // cores)]

    counts = []
    for slot in range(RB_DEV):
        count = lay.length(prompts[slot])
        if slot == 1:
            count = jnp.where(same, 0, count)

        def begin(j, carry, slot=slot):
            start_page(
                buffers,
                places(slot, prompts[slot], j),
                column,
                spot(store, slot * PMAX + j),
                sems.at[slot * PMAX + j],
            )
            return carry

        lax.fori_loop(0, count, begin, 0)
        counts.append(count)

    def absorb(keys_values, first, mask=None):
        span = keys_values.shape[0]
        keys = keys_values[:, :HD]
        values = jnp.concatenate(
            [keys_values[:, HD:], jnp.ones((span, HD), jnp.bfloat16)], axis=1
        )
        for r in range(0, GROUP * BLOCK, ROWS):
            rows = pl.ds(r, ROWS)
            scores = lax.dot_general(
                stacked[rows, :], keys, (((1,), (1,)), ((), ())), preferred_element_type=jnp.float32
            )
            if mask is not None:
                scores = jnp.where(mask, scores, NEG_LARGE)
            top = jnp.broadcast_to(jnp.max(scores, axis=1, keepdims=True), (ROWS, HD))
            if not first:
                before = peak[rows, :]
                top = jnp.maximum(before, top)
            spread = jnp.concatenate([top] * (span // HD), axis=1)
            weights = jnp.exp2((scores - spread) * SCALE).astype(jnp.bfloat16)
            blended = jnp.dot(weights, values, preferred_element_type=jnp.float32)
            if not first:
                fade = jnp.exp2((before - top) * SCALE)
                blended = total[rows, :] * jnp.concatenate([fade, fade], axis=1) + blended
            peak[rows, :] = top
            total[rows, :] = blended

    for b in range(RB_DEV):
        for e in range(GROUP):
            stacked[e * BLOCK : (e + 1) * BLOCK, :] = queries[
                b * BLOCK : (b + 1) * BLOCK, e * HD : (e + 1) * HD
            ]
        span = (b + 1) * BLOCK
        row = lax.broadcasted_iota(jnp.int32, (ROWS, span), 0) % BLOCK
        key = lax.broadcasted_iota(jnp.int32, (ROWS, span), 1)
        mask = key <= row + b * BLOCK
        if b == 1:
            joined = same & (lay.ctrl[SEG_AT] == lay.ctrl[SEG_AT + 1])
            mask = mask & (key >= jnp.where(joined, 0, BLOCK))
        absorb(own[0:span, :], True, mask)

        def finish(j, carry, b=b):
            wait_page(buffers[0], spot(store, b * PMAX + j), sems.at[b * PMAX + j])
            return carry

        lax.fori_loop(0, counts[b], finish, 0)
        length = lay.length(prompts[b])
        base = 0 if b == 0 else jnp.where(same, 0, PMAX)

        def tile(page, pages):
            at = pl.multiple_of(page * BLOCK, BLOCK)
            absorb(store[pl.ds(at, pages * BLOCK), :], False)

        def full(i, carry, base=base):
            tile(base + i * SPAN, SPAN)
            return carry

        lax.fori_loop(0, length // SPAN, full, 0)
        left = SPAN // 2
        while left:
            done = length // (2 * left) * (2 * left)
            pl.when(length // left % 2 == 1)(
                lambda left=left, done=done, base=base: tile(base + done, left)
            )
            left //= 2
        for e in range(GROUP):
            rows = slice(e * BLOCK, (e + 1) * BLOCK)
            out[b * BLOCK : (b + 1) * BLOCK, e * HD : (e + 1) * HD] = (
                total[rows, :HD] / total[rows, HD:]
            ).astype(jnp.bfloat16)


def attend(wide, cores, head, ctrl, queries, resp_kv, buffers):
    tokens = queries.shape[0]
    return pl.pallas_call(
        lambda *refs: attend_kernel(wide, cores, head * PAIR, *refs),
        out_shape=jax.ShapeDtypeStruct((tokens, WIDTH), jnp.bfloat16),
        grid_spec=pltpu.PrefetchScalarGridSpec(
            num_scalar_prefetch=1,
            grid=(1,),
            in_specs=[
                pl.BlockSpec((tokens, WIDTH), lambda i, c: (0, head)),
                pl.BlockSpec((tokens, PAIR), lambda i, c: (0, head)),
            ]
            + [pl.BlockSpec(memory_space=pl.ANY)] * len(buffers),
            out_specs=pl.BlockSpec((tokens, WIDTH), lambda i, c: (0, 0)),
            scratch_shapes=[
                pltpu.VMEM((RB_DEV * PMAX * BLOCK, PAIR), jnp.bfloat16),
                pltpu.VMEM((GROUP * BLOCK, HD), jnp.bfloat16),
                pltpu.VMEM((GROUP * BLOCK, HD), jnp.float32),
                pltpu.VMEM((GROUP * BLOCK, 2 * HD), jnp.float32),
                pltpu.SemaphoreType.DMA((RB_DEV * PMAX,)),
            ],
        ),
        compiler_params=params(),
        cost_estimate=pl.CostEstimate(
            flops=2 * 2 * tokens * WIDTH * 18 * BLOCK,
            bytes_accessed=2 * tokens * WIDTH * 2 + PMAX * BLOCK * PAIR * 2,
            transcendentals=tokens * GROUP * 18 * BLOCK,
        ),
        name=f"attend_head_{head}",
    )(ctrl, queries, resp_kv, *buffers)


def pages_shape(count):
    return jax.ShapeDtypeStruct((count * BLOCK, PAIR), jnp.bfloat16)


def pack_send(wide, cores, head, ctrl, pool):
    any_spec = pl.BlockSpec(memory_space=pl.ANY)
    return pl.pallas_call(
        lambda *refs: send_kernel(wide, cores, head * PAIR, *refs),
        out_shape=[pages_shape(NEAR)] * 3,
        grid_spec=pltpu.PrefetchScalarGridSpec(
            num_scalar_prefetch=1,
            grid=(1,),
            in_specs=[any_spec],
            out_specs=[any_spec] * 3,
            scratch_shapes=[pltpu.SemaphoreType.DMA((3, PROMPTS * ((PMAX + wide - 1) // wide)))],
        ),
        compiler_params=params(),
        cost_estimate=pl.CostEstimate(
            flops=0, bytes_accessed=2 * 12 * BLOCK * PAIR * 2, transcendentals=0
        ),
        name=f"pack_send_{head}",
    )(ctrl, pool)


def pack_share(wide, cores, head, ctrl, buffers):
    any_spec = pl.BlockSpec(memory_space=pl.ANY)
    return pl.pallas_call(
        lambda *refs: share_kernel(wide, cores, head * PAIR, *refs),
        out_shape=pages_shape(PMAX),
        grid_spec=pltpu.PrefetchScalarGridSpec(
            num_scalar_prefetch=1,
            grid=(1,),
            in_specs=[any_spec] * len(buffers),
            out_specs=any_spec,
            scratch_shapes=[pltpu.SemaphoreType.DMA((PMAX,))],
        ),
        compiler_params=params(),
        cost_estimate=pl.CostEstimate(
            flops=0, bytes_accessed=2 * 8 * BLOCK * PAIR * 2, transcendentals=0
        ),
        name=f"pack_share_{head}",
    )(ctrl, *buffers)


def fetch_pages(wide, cores, head, ctrl, pool):
    def hop(x, moves):
        pairs = [(a * cores + c, b * cores + c) for a, b in moves for c in range(cores)]
        return lax.ppermute(x, "wide", pairs)

    right, left, far = pack_send(wide, cores, head, ctrl, pool)
    from_left = hop(right, [(0, 1), (1, 2), (2, 3)])
    from_right = hop(left, [(3, 2), (2, 1), (1, 0)])
    from_far = hop(far, [(0, 2), (3, 1)])
    rows = FAR * BLOCK
    ahead = jnp.where(ctrl[ME_AT] // cores == 2, from_left[:rows], from_right[:rows])
    relayed = hop(jnp.concatenate([from_far[:rows], ahead], axis=0), [(2, 3), (1, 0)])
    buffers = [pool, from_left, from_right, from_far, relayed]
    shared = pack_share(wide, cores, head, ctrl, buffers)
    swap = [(d, d // cores * cores + (cores - 1 - d % cores)) for d in range(wide)]
    return buffers + [lax.ppermute(shared, "wide", swap)]


def project_kernel(at, *refs):
    parts, weight, out = refs[:-2], refs[-2], refs[-1]
    total = None
    for i, part in enumerate(parts):
        term = jnp.dot(
            part[...], weight[i * WIDTH : (i + 1) * WIDTH, :], preferred_element_type=jnp.float32
        )
        total = term if total is None else total + term
    out[...] = total.astype(jnp.bfloat16)


def project(parts, weight, first_column, columns):
    tokens = parts[0].shape[0]
    tile = math.gcd(columns, 512)
    at = jnp.reshape(first_column // tile, (1,)).astype(jnp.int32)
    return pl.pallas_call(
        project_kernel,
        out_shape=jax.ShapeDtypeStruct((tokens, columns), jnp.bfloat16),
        grid_spec=pltpu.PrefetchScalarGridSpec(
            num_scalar_prefetch=1,
            grid=(columns // tile,),
            in_specs=[pl.BlockSpec((tokens, WIDTH), lambda i, at: (0, 0))] * len(parts)
            + [pl.BlockSpec((weight.shape[0], tile), lambda i, at: (0, at[0] + i))],
            out_specs=pl.BlockSpec((tokens, tile), lambda i, at: (0, i)),
        ),
        compiler_params=params(),
        cost_estimate=pl.CostEstimate(
            flops=2 * tokens * columns * weight.shape[0],
            bytes_accessed=2 * columns * weight.shape[0],
            transcendentals=0,
        ),
        name="project",
    )(at, *parts, weight)


def local(
    queries, resp_kv, prefix_pool, out_weight, pre_len, prompt_blocks, prompt_owner, resp_seg
):
    wide, groups = lax.axis_size("wide"), lax.axis_size("tp") * lax.axis_size("sub")
    cores = 2 // lax.axis_size("sub")
    heads = resp_kv.shape[1] // PAIR
    me = lax.axis_index("wide").astype(jnp.int32)
    ctrl = jnp.concatenate([pre_len, prompt_blocks, prompt_owner, resp_seg, me[None]])
    if wide == 8 and cores == 2:
        buffers = [fetch_pages(wide, cores, g, ctrl, prefix_pool) for g in range(heads)]
    else:
        buffers = [[lax.all_gather(prefix_pool, "wide", axis=0, tiled=True)]] * heads
    parts = [
        attend(wide, cores, g, ctrl, queries, resp_kv, buffers[g]) for g in range(heads)
    ]
    columns = out_weight.shape[1]
    if groups != 2:
        terms = project(parts, out_weight, jnp.int32(0), columns)
        return lax.psum_scatter(terms, ("tp", "sub"), scatter_dimension=1, tiled=True)
    share = columns // groups
    group = lax.axis_index("tp") * lax.axis_size("sub") + lax.axis_index("sub")
    theirs = project(parts, out_weight, (1 - group) * share, share)
    axis = "tp" if lax.axis_size("tp") == 2 else "sub"
    arrived = lax.ppermute(theirs, axis, [(0, 1), (1, 0)])
    mine = project(parts, out_weight, group * share, share)
    return (mine.astype(jnp.float32) + arrived.astype(jnp.float32)).astype(jnp.bfloat16)


def solution(mesh):
    return jax.shard_map(
        local,
        mesh=mesh,
        in_specs=(
            P(("parts", "wide"), ("tp", "sub")),
            P(("parts", "wide"), ("tp", "sub")),
            P(("parts", "wide"), ("tp", "sub")),
            P(("tp", "sub"), None),
            P("parts"),
            P("parts"),
            P("parts"),
            P(("parts", "wide")),
        ),
        out_specs=P(("parts", "wide"), ("tp", "sub")),
        check_vma=False,
    )
```

```python
import math

import jax
import jax.numpy as jnp
from jax import lax
from jax.experimental import pallas as pl
from jax.experimental.pallas import tpu as pltpu
from jax.sharding import PartitionSpec as P

HD = 128
BLOCK = 128
RB_DEV = 2
PROMPTS = 4
PMAX = 16
GROUP = 8
PAIR = 2 * HD
WIDTH = GROUP * HD
ROWS = 256
SPAN = 4
NEG_LARGE = -1e30
SCALE = math.log2(math.e) / math.sqrt(HD)
VMEM_BYTES = 48 * 1024 * 1024

LEN_AT, BLOCKS_AT, OWNER_AT, SEG_AT, ME_AT, OTHER_AT = 0, 4, 8, 12, 14, 15


def params():
    return pltpu.CompilerParams(vmem_limit_bytes=VMEM_BYTES)


def as_int(flag):
    return jnp.where(flag, 1, 0)


class Layout:
    def __init__(self, ctrl, wide, cores):
        self.ctrl, self.wide, self.cores = ctrl, wide, cores
        self.stride = (PMAX + wide - 1) // wide
        self.me = ctrl[ME_AT]
        self.z, self.core = self.div(self.me, cores), self.mod(self.me, cores)
        ends, total = [], 0
        for p in range(PROMPTS):
            total = total + ctrl[BLOCKS_AT + p] + (RB_DEV - 1)
            ends.append(total)
        self.ends = ends

    def mod(self, value, size):
        return value & (size - 1) if size & (size - 1) == 0 else lax.rem(value, size)

    def div(self, value, size):
        if size & (size - 1) == 0:
            return lax.shift_right_logical(value, size.bit_length() - 1)
        return lax.div(value, size)

    def prompt_of(self, block):
        return sum(as_int(block >= end) for end in self.ends[:-1])

    def first_of(self, chip):
        return self.prompt_of(chip * self.cores * RB_DEV)

    def last_of(self, chip):
        return self.prompt_of((chip + 1) * self.cores * RB_DEV - 1)

    def length(self, p):
        return self.ctrl[LEN_AT + p]

    def held_by(self, p, j):
        return self.mod(self.ctrl[OWNER_AT + p] + j, self.wide)

    def held(self, p, who):
        first = self.mod(who - self.ctrl[OWNER_AT + p] + self.wide, self.wide)
        return sum(as_int(first + k * self.wide < self.length(p)) for k in range(self.stride))

    def in_plane(self, p, j, caps, above, below):
        who = self.held_by(p, j)
        chip = self.div(who, self.cores)
        gap = chip - self.z
        k = self.div(j, self.wide)
        at = who * PROMPTS
        down = above[at + p] + k
        up = below[at + p] + k
        near_down = down - jnp.where(chip == 0, above[at + self.last_of(1)], 0)
        near_up = up - jnp.where(chip == 3, below[at + self.first_of(2)], 0)
        far = jnp.where(gap < 0, down, up)
        two = (gap == 2) | (gap == -2)
        direct = two & ((self.z == 1) | (self.z == 2))
        which = jnp.where(
            gap == 0, 0, jnp.where(gap == -1, 1, jnp.where(gap == 1, 2, jnp.where(direct, 3, 4)))
        )
        page = jnp.where(
            gap == 0,
            p * self.stride + k,
            jnp.where(
                gap == -1,
                near_down,
                jnp.where(gap == 1, near_up, far + jnp.where(two & ~direct, caps.relay, 0)),
            ),
        )
        return which * CODE + page


CODE = 256
SHARED = 5
SLOT_AT, SHARE_AT, COUNT_AT, SHARES_AT, LENGTH_AT, BASE_AT, LOW_AT, THEIRS_AT, TABLE = (
    0, 32, 48, 50, 52, 54, 56, 58, 64
)


class Caps:
    def __init__(self, near, relay):
        self.near, self.relay = near, relay


FULL = Caps(6, 4)


def plan_kernel(wide, cores, caps, ctrl, table, above, below):
    lay = Layout(ctrl, wide, cores)
    half = PMAX // cores
    for at in range(TABLE):
        table[at] = 0
    table[THEIRS_AT] = ctrl[OTHER_AT]
    if caps is not None:

        def tally(who, carry):
            held = [lay.held(p, who) for p in range(PROMPTS)]
            for p in range(PROMPTS):
                above[who * PROMPTS + p] = sum(held[p + 1 :], jnp.int32(0))
                below[who * PROMPTS + p] = sum(held[:p], jnp.int32(0))
            return carry

        lax.fori_loop(0, wide, tally, 0)

    def prompts_of(device):
        return [lay.prompt_of(device * RB_DEV + b) for b in range(RB_DEV)]

    mine = prompts_of(lay.me)
    same = mine[0] == mine[1]
    joined = same & (ctrl[SEG_AT] == ctrl[SEG_AT + 1])
    for slot in range(RB_DEV):
        p = mine[slot]
        count = lay.length(p)
        table[LENGTH_AT + slot] = count
        if slot == 1:
            count = jnp.where(same, 0, count)
        table[COUNT_AT + slot] = count
        table[BASE_AT + slot] = jnp.where(same, 0, PMAX) if slot else 0
        table[LOW_AT + slot] = jnp.where(joined, 0, BLOCK) if slot else 0

        def place(j, carry, slot=slot, p=p):
            who = lay.held_by(p, j)
            if caps is None:
                code = (who * PROMPTS + p) * lay.stride + lay.div(j, wide)
            else:
                code = jnp.where(
                    lay.mod(who, cores) == lay.core,
                    lay.in_plane(p, j, caps, above, below),
                    SHARED * CODE + slot * half + lay.div(j, cores),
                )
            table[SLOT_AT + slot * PMAX + j] = code
            return carry

        lax.fori_loop(0, count, place, 0)
    if caps is None:
        return
    theirs = prompts_of(lay.z * cores + (cores - 1 - lay.core))
    for slot in range(RB_DEV):
        p = theirs[slot]
        shift = lay.mod(lay.core - ctrl[OWNER_AT + p] + wide, cores)
        count = lay.div(lay.length(p) - shift + cores - 1, cores)
        if slot == 1:
            count = jnp.where(theirs[1] == theirs[0], 0, count)
        table[SHARES_AT + slot] = count

        def share(i, carry, slot=slot, p=p, shift=shift):
            table[SHARE_AT + slot * half + i] = lay.in_plane(
                p, i * cores + shift, caps, above, below
            )
            return carry

        lax.fori_loop(0, count, share, 0)


def make_plan(wide, cores, caps, ctrl):
    return pl.pallas_call(
        lambda *refs: plan_kernel(wide, cores, caps, *refs),
        out_shape=jax.ShapeDtypeStruct((TABLE,), jnp.int32),
        in_specs=[pl.BlockSpec(memory_space=pltpu.SMEM)],
        out_specs=pl.BlockSpec(memory_space=pltpu.SMEM),
        scratch_shapes=[pltpu.SMEM((wide * PROMPTS,), jnp.int32)] * 2,
        compiler_params=params(),
        name="plan",
    )(ctrl)


def spot(ref, page):
    return ref.at[pl.ds(pl.multiple_of(page * BLOCK, BLOCK), BLOCK), :]


def page_at(buffer, page, column):
    rows = pl.ds(pl.multiple_of(page * BLOCK, BLOCK), BLOCK)
    return buffer.at[rows, pl.ds(column if buffer.shape[1] > PAIR else 0, PAIR)]


def start_page(buffers, code, column, target, sem):
    which = lax.shift_right_logical(code, CODE.bit_length() - 1)
    page = code & (CODE - 1)
    for i, buffer in enumerate(buffers):

        @pl.when(which == i)
        def _(buffer=buffer):
            pltpu.make_async_copy(page_at(buffer, page, column), target, sem).start()


def wait_page(target, sem):
    pltpu.make_async_copy(target, target, sem).wait()


def send_kernel(wide, cores, heads, ctrl, pool, *refs):
    outs, sems = refs[:-1], refs[-1]
    lay = Layout(ctrl, wide, cores)
    z, last = lay.z, wide // cores - 1
    held = [lay.held(p, lay.me) for p in range(PROMPTS)]

    def above(p, top):
        return sum([jnp.where(o <= top, held[o], 0) for o in range(p + 1, PROMPTS)], jnp.int32(0))

    def below(p, low):
        return sum([jnp.where(o >= low, held[o], 0) for o in range(p)], jnp.int32(0))

    near_top = jnp.where(z == 0, lay.last_of(1), PROMPTS - 1)
    near_low = jnp.where(z == last, lay.first_of(2), 0)
    first_up, last_down = lay.first_of(z + 1), lay.last_of(z - 1)
    first_two, last_one = lay.first_of(2), lay.last_of(1)
    plans = []
    for p in range(PROMPTS):
        right = (z < last) & (p >= first_up) & (p <= near_top)
        left = (z > 0) & (p >= near_low) & (p <= last_down)
        far_up = (z == 0) & (p >= first_two)
        far_down = (z == last) & (p <= last_one)
        ranks = (above(p, near_top), below(p, near_low), above(p, PROMPTS - 1), below(p, 0))
        for k in range(lay.stride):
            for lane, wanted, rank in zip((0, 1, 2, 2), (right, left, far_up, far_down), ranks):
                plans.append((wanted & (k < held[p]), p * lay.stride + k, lane, rank + k))

    def copies(plan):
        _, page, lane, rank = plan
        return [
            pltpu.make_async_copy(
                page_at(pool, page, g * PAIR), spot(outs[g * 3 + lane], rank), sems.at[lane, page, g]
            )
            for g in range(heads)
        ]

    for plan in plans:

        @pl.when(plan[0])
        def _(plan=plan):
            for copy in copies(plan):
                copy.start()

    for plan in plans:

        @pl.when(plan[0])
        def _(plan=plan):
            for copy in copies(plan):
                copy.wait()


def share_kernel(cores, column, table, *refs):
    buffers, out, sems = refs[:-2], refs[-2], refs[-1]
    half = PMAX // cores
    for slot in range(RB_DEV):

        def begin(i, carry, slot=slot):
            at = slot * half + i
            start_page(buffers, table[SHARE_AT + at], column, spot(out, at), sems.at[at])
            return carry

        lax.fori_loop(0, table[SHARES_AT + slot], begin, 0)
    for slot in range(RB_DEV):

        def finish(i, carry, slot=slot):
            at = slot * half + i
            wait_page(spot(out, at), sems.at[at])
            return carry

        lax.fori_loop(0, table[SHARES_AT + slot], finish, 0)


def attend_kernel(column, carried, project, table, queries, own, *refs):
    refs = list(refs)
    weight = refs.pop(0) if project else None
    summed = refs.pop(0) if carried else None
    sems, total, peak, stacked = [refs.pop() for _ in range(4)]
    slab = refs.pop() if project else None
    store = refs.pop()
    terms = refs.pop() if project else None
    out = refs.pop()
    buffers = refs
    for slot in range(RB_DEV):

        def begin(j, carry, slot=slot):
            at = slot * PMAX + j
            start_page(buffers, table[SLOT_AT + at], column, spot(store, at), sems.at[at])
            return carry

        lax.fori_loop(0, table[COUNT_AT + slot], begin, 0)
    if project:
        share = slab.shape[1]
        theirs = pl.multiple_of(table[THEIRS_AT] * share, share)
        rows = column // PAIR * WIDTH
        fetch = pltpu.make_async_copy(
            weight.at[pl.ds(rows, WIDTH), pl.ds(theirs, share)], slab, sems.at[RB_DEV * PMAX]
        )
        fetch.start()

    def absorb(keys_values, first, mask=None):
        span = keys_values.shape[0]
        keys = keys_values[:, :HD]
        values = jnp.concatenate(
            [keys_values[:, HD:], jnp.ones((span, HD), jnp.bfloat16)], axis=1
        )

        def score(r):
            return lax.dot_general(
                stacked[pl.ds(r, ROWS), :],
                keys,
                (((1,), (1,)), ((), ())),
                preferred_element_type=jnp.float32,
            )

        following = score(0)
        for r in range(0, GROUP * BLOCK, ROWS):
            rows = pl.ds(r, ROWS)
            scores = following
            if r + ROWS < GROUP * BLOCK:
                following = score(r + ROWS)
            if mask is not None:
                scores = jnp.where(mask, scores, NEG_LARGE)
            top = jnp.broadcast_to(jnp.max(scores, axis=1, keepdims=True), (ROWS, HD))
            if not first:
                before = peak[rows, :]
                top = jnp.maximum(before, top)
            spread = jnp.concatenate([top] * (span // HD), axis=1)
            weights = jnp.exp2((scores - spread) * SCALE).astype(jnp.bfloat16)
            blended = jnp.dot(weights, values, preferred_element_type=jnp.float32)
            if not first:
                fade = jnp.exp2((before - top) * SCALE)
                blended = total[rows, :] * jnp.concatenate([fade, fade], axis=1) + blended
            peak[rows, :] = top
            total[rows, :] = blended

    def one_block(b, carry):
        tokens = pl.ds(pl.multiple_of(b * BLOCK, BLOCK), BLOCK)
        for e in range(GROUP):
            stacked[e * BLOCK : (e + 1) * BLOCK, :] = queries[tokens, e * HD : (e + 1) * HD]
        span = RB_DEV * BLOCK
        row = lax.broadcasted_iota(jnp.int32, (ROWS, span), 0) & (BLOCK - 1)
        key = lax.broadcasted_iota(jnp.int32, (ROWS, span), 1)
        mask = (key <= row + b * BLOCK) & (key >= table[LOW_AT + b])
        absorb(own[...], True, mask)

        def finish(j, carry):
            at = b * PMAX + j
            wait_page(spot(store, at), sems.at[at])
            return carry

        lax.fori_loop(0, table[COUNT_AT + b], finish, 0)
        length, base = table[LENGTH_AT + b], table[BASE_AT + b]

        def tile(page, pages):
            at = pl.multiple_of(page * BLOCK, BLOCK)
            absorb(store[pl.ds(at, pages * BLOCK), :], False)

        def full(i, carry):
            tile(base + i * SPAN, SPAN)
            return carry

        lax.fori_loop(0, lax.shift_right_logical(length, SPAN.bit_length() - 1), full, 0)
        left = SPAN // 2
        while left:
            done = length & -(2 * left)
            pl.when((length & left) != 0)(lambda left=left, done=done: tile(base + done, left))
            left //= 2
        for e in range(GROUP):
            rows = slice(e * BLOCK, (e + 1) * BLOCK)
            out[tokens, e * HD : (e + 1) * HD] = (total[rows, :HD] / total[rows, HD:]).astype(
                jnp.bfloat16
            )
        return carry

    lax.fori_loop(0, RB_DEV, one_block, 0)
    if project:
        fetch.wait()
        attended = out[...]
        step = math.gcd(share, 512)
        for n in range(0, share, step):
            term = jnp.dot(attended, slab[:, n : n + step], preferred_element_type=jnp.float32)
            if carried:
                term = term + summed[:, n : n + step]
            terms[:, n : n + step] = term.astype(terms.dtype)


def attend(head, heads, table, queries, resp_kv, buffers, weight=None, share=0, summed=None):
    tokens = queries.shape[0]
    project, carried, final = weight is not None, summed is not None, head == heads - 1
    any_spec = pl.BlockSpec(memory_space=pl.ANY)
    whole = pl.BlockSpec((tokens, share), lambda i, c: (0, 0))
    out_shape = [jax.ShapeDtypeStruct((tokens, WIDTH), jnp.bfloat16)]
    out_specs = [pl.BlockSpec((tokens, WIDTH), lambda i, c: (0, 0))]
    operands, in_specs = [], []
    scratch = [pltpu.VMEM((RB_DEV * PMAX * BLOCK, PAIR), jnp.bfloat16)]
    if project:
        operands, in_specs = [weight], [any_spec]
        out_shape.append(
            jax.ShapeDtypeStruct((tokens, share), jnp.bfloat16 if final else jnp.float32)
        )
        out_specs.append(whole)
        scratch.append(pltpu.VMEM((WIDTH, share), jnp.bfloat16))
    if carried:
        operands, in_specs = operands + [summed], in_specs + [whole]
    return pl.pallas_call(
        lambda *refs: attend_kernel(head * PAIR, carried, project, *refs),
        out_shape=out_shape,
        grid_spec=pltpu.PrefetchScalarGridSpec(
            num_scalar_prefetch=1,
            grid=(1,),
            in_specs=[
                pl.BlockSpec((tokens, WIDTH), lambda i, c: (0, head)),
                pl.BlockSpec((tokens, PAIR), lambda i, c: (0, head)),
            ]
            + in_specs
            + [any_spec] * len(buffers),
            out_specs=out_specs,
            scratch_shapes=scratch
            + [
                pltpu.VMEM((GROUP * BLOCK, HD), jnp.bfloat16),
                pltpu.VMEM((GROUP * BLOCK, HD), jnp.float32),
                pltpu.VMEM((GROUP * BLOCK, 2 * HD), jnp.float32),
                pltpu.SemaphoreType.DMA((RB_DEV * PMAX + 1,)),
            ],
        ),
        compiler_params=params(),
        cost_estimate=pl.CostEstimate(
            flops=2 * 2 * tokens * WIDTH * 18 * BLOCK * 2,
            bytes_accessed=2 * tokens * WIDTH * 2 + PMAX * BLOCK * PAIR * 2 + share * WIDTH * 2,
            transcendentals=tokens * GROUP * 18 * BLOCK,
        ),
        name=f"attend_head_{head}",
    )(table, queries, resp_kv, *operands, *buffers)


def pages_shape(count):
    return jax.ShapeDtypeStruct((count * BLOCK, PAIR), jnp.bfloat16)


def pack_send(wide, cores, heads, caps, ctrl, pool):
    any_spec = pl.BlockSpec(memory_space=pl.ANY)
    pages = PROMPTS * ((PMAX + wide - 1) // wide)
    out = pl.pallas_call(
        lambda *refs: send_kernel(wide, cores, heads, *refs),
        out_shape=[pages_shape(caps.near)] * 3 * heads,
        grid_spec=pltpu.PrefetchScalarGridSpec(
            num_scalar_prefetch=1,
            grid=(1,),
            in_specs=[any_spec],
            out_specs=[any_spec] * 3 * heads,
            scratch_shapes=[pltpu.SemaphoreType.DMA((3, pages, heads))],
        ),
        compiler_params=params(),
        cost_estimate=pl.CostEstimate(
            flops=0, bytes_accessed=2 * 12 * BLOCK * PAIR * 2 * heads, transcendentals=0
        ),
        name="pack_send",
    )(ctrl, pool)
    return [out[3 * g : 3 * g + 3] for g in range(heads)]


def pack_share(cores, head, table, buffers):
    any_spec = pl.BlockSpec(memory_space=pl.ANY)
    return pl.pallas_call(
        lambda *refs: share_kernel(cores, head * PAIR, *refs),
        out_shape=pages_shape(PMAX),
        grid_spec=pltpu.PrefetchScalarGridSpec(
            num_scalar_prefetch=1,
            grid=(1,),
            in_specs=[any_spec] * len(buffers),
            out_specs=any_spec,
            scratch_shapes=[pltpu.SemaphoreType.DMA((PMAX,))],
        ),
        compiler_params=params(),
        cost_estimate=pl.CostEstimate(
            flops=0, bytes_accessed=2 * 8 * BLOCK * PAIR * 2, transcendentals=0
        ),
        name=f"pack_share_{head}",
    )(table, *buffers)


def after(value, *earlier):
    return lax.optimization_barrier((value, *earlier))[0]


def line_attend(wide, cores, caps, ctrl, queries, resp_kv, pool, weight, share):
    heads = resp_kv.shape[1] // PAIR

    def hop(x, moves):
        pairs = [(a * cores + c, b * cores + c) for a, b in moves for c in range(cores)]
        return lax.ppermute(x, "wide", pairs)

    swap = [(d, d // cores * cores + (cores - 1 - d % cores)) for d in range(wide)]
    sends = pack_send(wide, cores, heads, caps, ctrl, pool)
    table = make_plan(wide, cores, caps, ctrl)
    inner = ctrl[ME_AT] // cores == 2
    rows = caps.relay * BLOCK
    buffers, parts, summed = [], [], None
    arrived = []
    for g in range(heads):
        right, left, far = sends[g]
        arrived.append(
            (
                hop(far, [(0, 2), (3, 1)]),
                hop(right, [(0, 1), (1, 2), (2, 3)]),
                hop(left, [(3, 2), (2, 1), (1, 0)]),
            )
        )

    def relay(g):
        from_far, from_left, from_right = arrived[g]
        ahead = jnp.where(inner, from_left[:rows], from_right[:rows])
        onward = jnp.concatenate([from_far[:rows], ahead], axis=0)
        if g >= 3:
            onward = after(onward, parts[g - 3])
        relayed = hop(onward, [(2, 3), (1, 0)])
        return [pool, from_left, from_right, from_far, relayed]

    def exchange(g, held):
        plan = after(table, parts[g - 2]) if g >= 2 else table
        return held + [lax.ppermute(pack_share(cores, g, plan, held), "wide", swap)]

    held = [None] * heads
    for step in range(heads + 2):
        if step < heads:
            held[step] = relay(step)
        if 1 <= step <= heads:
            held[step - 1] = exchange(step - 1, held[step - 1])
        if step >= 2:
            g = step - 2
            attended, summed = attend(
                g, heads, table, queries, resp_kv, held[g], weight, share, summed
            )
            parts.append(attended)
    return parts, summed


def project_kernel(at, *refs):
    parts, weight, out = refs[:-2], refs[-2], refs[-1]
    total = None
    for i, part in enumerate(parts):
        term = jnp.dot(
            part[...], weight[i * WIDTH : (i + 1) * WIDTH, :], preferred_element_type=jnp.float32
        )
        total = term if total is None else total + term
    out[...] = total.astype(jnp.bfloat16)


def project(parts, weight, first_column, columns):
    tokens = parts[0].shape[0]
    tile = math.gcd(columns, 512)
    at = jnp.reshape(first_column // tile, (1,)).astype(jnp.int32)
    return pl.pallas_call(
        project_kernel,
        out_shape=jax.ShapeDtypeStruct((tokens, columns), jnp.bfloat16),
        grid_spec=pltpu.PrefetchScalarGridSpec(
            num_scalar_prefetch=1,
            grid=(columns // tile,),
            in_specs=[pl.BlockSpec((tokens, WIDTH), lambda i, at: (0, 0))] * len(parts)
            + [pl.BlockSpec((weight.shape[0], tile), lambda i, at: (0, at[0] + i))],
            out_specs=pl.BlockSpec((tokens, tile), lambda i, at: (0, i)),
        ),
        compiler_params=params(),
        cost_estimate=pl.CostEstimate(
            flops=2 * tokens * columns * weight.shape[0],
            bytes_accessed=2 * columns * weight.shape[0],
            transcendentals=0,
        ),
        name="project",
    )(at, *parts, weight)


def local(
    queries, resp_kv, prefix_pool, out_weight, pre_len, prompt_blocks, prompt_owner, resp_seg
):
    wide, groups = lax.axis_size("wide"), lax.axis_size("tp") * lax.axis_size("sub")
    cores = 2 // lax.axis_size("sub")
    heads = resp_kv.shape[1] // PAIR
    me = lax.axis_index("wide").astype(jnp.int32)
    group = lax.axis_index("tp") * lax.axis_size("sub") + lax.axis_index("sub")
    where = jnp.stack([me, (1 - group).astype(jnp.int32)])
    ctrl = jnp.concatenate([pre_len, prompt_blocks, prompt_owner, resp_seg, where])
    columns = out_weight.shape[1]
    share = columns // groups
    if wide == 8 and cores == 2 and groups == 2:
        parts, theirs = line_attend(
            wide, cores, FULL, ctrl, queries, resp_kv, prefix_pool, out_weight, share
        )
        axis = "tp" if lax.axis_size("tp") == 2 else "sub"
        arrived = lax.ppermute(theirs, axis, [(0, 1), (1, 0)])
        mine = project(parts, out_weight, group * share, share)
        return (mine.astype(jnp.float32) + arrived.astype(jnp.float32)).astype(jnp.bfloat16)
    table = make_plan(wide, cores, None, ctrl)
    buffers = [lax.all_gather(prefix_pool, "wide", axis=0, tiled=True)]
    parts = [attend(g, heads, table, queries, resp_kv, buffers)[0] for g in range(heads)]
    terms = project(parts, out_weight, jnp.int32(0), columns)
    return lax.psum_scatter(terms, ("tp", "sub"), scatter_dimension=1, tiled=True)


def solution(mesh):
    return jax.shard_map(
        local,
        mesh=mesh,
        in_specs=(
            P(("parts", "wide"), ("tp", "sub")),
            P(("parts", "wide"), ("tp", "sub")),
            P(("parts", "wide"), ("tp", "sub")),
            P(("tp", "sub"), None),
            P("parts"),
            P("parts"),
            P("parts"),
            P(("parts", "wide")),
        ),
        out_specs=P(("parts", "wide"), ("tp", "sub")),
        check_vma=False,
    )
```

```python
import math

import jax
import jax.numpy as jnp
from jax import lax
from jax.experimental import pallas as pl
from jax.experimental.pallas import tpu as pltpu
from jax.sharding import PartitionSpec as P

HD = 128
BLOCK = 128
RB_DEV = 2
PROMPTS = 4
PMAX = 16
GROUP = 8
PAIR = 2 * HD
WIDTH = GROUP * HD
ROWS = 256
NEG_LARGE = -1e30
SCALE = math.log2(math.e) / math.sqrt(HD)
VMEM_BYTES = 48 * 1024 * 1024

LEN_AT, BLOCKS_AT, OWNER_AT, SEG_AT, ME_AT, OTHER_AT = 0, 4, 8, 12, 14, 15


def params():
    return pltpu.CompilerParams(vmem_limit_bytes=VMEM_BYTES)


def as_int(flag):
    return jnp.where(flag, 1, 0)


class Layout:
    def __init__(self, ctrl, wide, cores):
        self.ctrl, self.wide, self.cores = ctrl, wide, cores
        self.stride = (PMAX + wide - 1) // wide
        self.me = ctrl[ME_AT]
        self.z, self.core = self.div(self.me, cores), self.mod(self.me, cores)
        ends, total = [], 0
        for p in range(PROMPTS):
            total = total + ctrl[BLOCKS_AT + p] + (RB_DEV - 1)
            ends.append(total)
        self.ends = ends

    def mod(self, value, size):
        return value & (size - 1) if size & (size - 1) == 0 else lax.rem(value, size)

    def div(self, value, size):
        if size & (size - 1) == 0:
            return lax.shift_right_logical(value, size.bit_length() - 1)
        return lax.div(value, size)

    def prompt_of(self, block):
        return sum(as_int(block >= end) for end in self.ends[:-1])

    def first_of(self, chip):
        return self.prompt_of(chip * self.cores * RB_DEV)

    def last_of(self, chip):
        return self.prompt_of((chip + 1) * self.cores * RB_DEV - 1)

    def length(self, p):
        return self.ctrl[LEN_AT + p]

    def held_by(self, p, j):
        return self.mod(self.ctrl[OWNER_AT + p] + j, self.wide)

    def held(self, p, who):
        first = self.mod(who - self.ctrl[OWNER_AT + p] + self.wide, self.wide)
        return sum(as_int(first + k * self.wide < self.length(p)) for k in range(self.stride))

    def in_plane(self, p, j, sums):
        who = self.held_by(p, j)
        chip = self.div(who, self.cores)
        gap = chip - self.z
        k = self.div(j, self.wide)
        at = who * SUMS
        down = sums[at + PROMPTS] - sums[at + p + 1] + k
        up = sums[at + p] + k
        near_down = down - jnp.where(
            chip == 0, sums[at + PROMPTS] - sums[at + self.last_of(1) + 1], 0
        )
        near_up = up - jnp.where(chip == 3, sums[at + self.first_of(2)], 0)
        far = jnp.where(gap < 0, down, up)
        two = (gap == 2) | (gap == -2)
        direct = two & ((self.z == 1) | (self.z == 2))
        code = jnp.where(two, 5 * CODE, 4 * CODE) + far
        code = jnp.where(direct, 3 * CODE + far, code)
        code = jnp.where(gap == 1, 2 * CODE + near_up, code)
        code = jnp.where(gap == -1, CODE + near_down, code)
        return jnp.where(gap == 0, p * self.stride + k, code)


CODE = 256
SHARED = 6
SUMS = 8
SLOT_AT, SHARE_AT, COUNT_AT, SHARES_AT, LENGTH_AT, BASE_AT, LOW_AT, THEIRS_AT, LEVEL_AT, TABLE = (
    0, 32, 48, 50, 52, 54, 56, 58, 59, 64
)


class Caps:
    def __init__(self, near, far, relay):
        self.near, self.far, self.relay = near, far, relay


LEVELS = [Caps(4, 4, 3), Caps(5, 5, 3), Caps(5, 5, 4), Caps(6, 6, 4)]


def needs(lay, sums, cores):
    first, last = [lay.first_of(c) for c in range(4)], [lay.last_of(c) for c in range(4)]
    near, far, relay = jnp.int32(0), jnp.int32(0), jnp.int32(0)
    for core in range(cores):

        def held(chip, low, high, core=core):
            at = (chip * cores + core) * SUMS
            return sums[at + high + 1] - sums[at + low]

        top = PROMPTS - 1
        edge = [held(1, 0, last[0]), held(2, first[3], top)]
        for amount in edge + [
            held(0, first[1], last[1]),
            held(1, first[2], top),
            held(2, 0, last[1]),
            held(3, first[2], last[2]),
        ]:
            near = jnp.maximum(near, amount)
        for amount in (held(0, first[2], top), held(3, 0, last[1])):
            far = jnp.maximum(far, amount)
        for amount in edge + [held(0, first[3], top), held(3, 0, last[0])] + [
            held(1, first[3], top),
            held(2, 0, last[0]),
        ]:
            relay = jnp.maximum(relay, amount)
    return near, far, relay


def plan_kernel(wide, cores, line, ctrl, table, sums):
    lay = Layout(ctrl, wide, cores)
    half = PMAX // cores
    table[THEIRS_AT] = ctrl[OTHER_AT]
    table[LEVEL_AT] = 0
    if line:

        def tally(who, carry):
            total = jnp.int32(0)
            for p in range(PROMPTS):
                sums[who * SUMS + p] = total
                total = total + lay.held(p, who)
            sums[who * SUMS + PROMPTS] = total
            return carry

        lax.fori_loop(0, wide, tally, 0)
        near, far, relay = needs(lay, sums, cores)
        level = jnp.int32(0)
        for caps in LEVELS[:-1]:
            level = level + as_int((near > caps.near) | (far > caps.far) | (relay > caps.relay))
        table[LEVEL_AT] = level

    def prompts_of(device):
        return [lay.prompt_of(device * RB_DEV + b) for b in range(RB_DEV)]

    mine = prompts_of(lay.me)
    same = mine[0] == mine[1]
    joined = same & (ctrl[SEG_AT] == ctrl[SEG_AT + 1])
    for slot in range(RB_DEV):
        p = mine[slot]
        count = lay.length(p)
        table[LENGTH_AT + slot] = count
        if slot == 1:
            count = jnp.where(same, 0, count)
        table[COUNT_AT + slot] = count
        table[BASE_AT + slot] = jnp.where(same, 0, PMAX) if slot else 0
        table[LOW_AT + slot] = jnp.where(joined, 0, BLOCK) if slot else 0

        def place(j, carry, slot=slot, p=p):
            who = lay.held_by(p, j)
            if line:
                code = jnp.where(
                    lay.mod(who, cores) == lay.core,
                    lay.in_plane(p, j, sums),
                    SHARED * CODE + slot * half + lay.div(j, cores),
                )
            else:
                code = (who * PROMPTS + p) * lay.stride + lay.div(j, wide)
            table[SLOT_AT + slot * PMAX + j] = code
            return carry

        lax.fori_loop(0, count, place, 0)
    if not line:
        return
    theirs = prompts_of(lay.z * cores + (cores - 1 - lay.core))
    for slot in range(RB_DEV):
        p = theirs[slot]
        shift = lay.mod(lay.core - ctrl[OWNER_AT + p] + wide, cores)
        count = lay.div(lay.length(p) - shift + cores - 1, cores)
        if slot == 1:
            count = jnp.where(theirs[1] == theirs[0], 0, count)
        table[SHARES_AT + slot] = count

        def share(i, carry, slot=slot, p=p, shift=shift):
            table[SHARE_AT + slot * half + i] = lay.in_plane(p, i * cores + shift, sums)
            return carry

        lax.fori_loop(0, count, share, 0)


def make_plan(wide, cores, line, ctrl):
    return pl.pallas_call(
        lambda *refs: plan_kernel(wide, cores, line, *refs),
        out_shape=jax.ShapeDtypeStruct((TABLE,), jnp.int32),
        in_specs=[pl.BlockSpec(memory_space=pltpu.SMEM)],
        out_specs=pl.BlockSpec(memory_space=pltpu.SMEM),
        scratch_shapes=[pltpu.SMEM((wide * SUMS,), jnp.int32)],
        compiler_params=params(),
        name="plan",
    )(ctrl)


def spot(ref, page):
    return ref.at[pl.ds(pl.multiple_of(page * BLOCK, BLOCK), BLOCK), :]


def page_at(buffer, page, column):
    rows = pl.ds(pl.multiple_of(page * BLOCK, BLOCK), BLOCK)
    return buffer.at[rows, pl.ds(column if buffer.shape[1] > PAIR else 0, PAIR)]


def start_page(buffers, code, column, target, sem):
    which = lax.shift_right_logical(code, CODE.bit_length() - 1)
    page = code & (CODE - 1)
    for i, (buffer, offset) in enumerate(buffers):

        @pl.when(which == i)
        def _(buffer=buffer, offset=offset):
            source = page_at(buffer, page + offset, column)
            pltpu.make_async_copy(source, target, sem).start()


def wait_page(target, sem):
    pltpu.make_async_copy(target, target, sem).wait()


def send_kernel(wide, cores, heads, ctrl, pool, *refs):
    outs, sems = refs[:-1], refs[-1]
    lay = Layout(ctrl, wide, cores)
    z, last = lay.z, wide // cores - 1
    held = [lay.held(p, lay.me) for p in range(PROMPTS)]

    def above(p, top):
        return sum([jnp.where(o <= top, held[o], 0) for o in range(p + 1, PROMPTS)], jnp.int32(0))

    def below(p, low):
        return sum([jnp.where(o >= low, held[o], 0) for o in range(p)], jnp.int32(0))

    near_top = jnp.where(z == 0, lay.last_of(1), PROMPTS - 1)
    near_low = jnp.where(z == last, lay.first_of(2), 0)
    first_up, last_down = lay.first_of(z + 1), lay.last_of(z - 1)
    first_two, last_one = lay.first_of(2), lay.last_of(1)
    plans = []
    for p in range(PROMPTS):
        right = (z < last) & (p >= first_up) & (p <= near_top)
        left = (z > 0) & (p >= near_low) & (p <= last_down)
        far_up = (z == 0) & (p >= first_two)
        far_down = (z == last) & (p <= last_one)
        ranks = (above(p, near_top), below(p, near_low), above(p, PROMPTS - 1), below(p, 0))
        for k in range(lay.stride):
            for lane, wanted, rank in zip((0, 1, 2, 2), (right, left, far_up, far_down), ranks):
                plans.append((wanted & (k < held[p]), p * lay.stride + k, lane, rank + k))

    def copies(plan):
        _, page, lane, rank = plan
        return [
            pltpu.make_async_copy(
                page_at(pool, page, g * PAIR), spot(outs[g * 3 + lane], rank), sems.at[lane, page, g]
            )
            for g in range(heads)
        ]

    for plan in plans:

        @pl.when(plan[0])
        def _(plan=plan):
            for copy in copies(plan):
                copy.start()

    for plan in plans:

        @pl.when(plan[0])
        def _(plan=plan):
            for copy in copies(plan):
                copy.wait()


def relay_kernel(cores, rows, ctrl, far, left, right, out, sems):
    def copy(source, section):
        target = out.at[pl.ds(section * rows, rows), :]
        return pltpu.make_async_copy(source.at[pl.ds(0, rows), :], target, sems.at[section])

    inner = ctrl[ME_AT] == 2 * cores
    for core in range(1, cores):
        inner = inner | (ctrl[ME_AT] == 2 * cores + core)
    copy(far, 0).start()
    pl.when(inner)(lambda: copy(left, 1).start())
    pl.when(jnp.logical_not(inner))(lambda: copy(right, 1).start())
    copy(far, 0).wait()
    copy(far, 1).wait()


def with_offsets(refs, relay):
    if len(refs) == 1:
        return [(refs[0], 0)]
    pairs = [(ref, 0) for ref in refs]
    return pairs[:5] + [(refs[4], relay)] + pairs[5:]


def share_kernel(cores, column, relay, table, *refs):
    buffers, out, sems = with_offsets(refs[:-2], relay), refs[-2], refs[-1]
    half = PMAX // cores
    for slot in range(RB_DEV):

        def begin(i, carry, slot=slot):
            at = slot * half + i
            start_page(buffers, table[SHARE_AT + at], column, spot(out, at), sems.at[at])
            return carry

        lax.fori_loop(0, table[SHARES_AT + slot], begin, 0)
    for slot in range(RB_DEV):

        def finish(i, carry, slot=slot):
            at = slot * half + i
            wait_page(spot(out, at), sems.at[at])
            return carry

        lax.fori_loop(0, table[SHARES_AT + slot], finish, 0)


def attend_kernel(column, relay, carried, project, table, queries, own, *refs):
    refs = list(refs)
    weight = refs.pop(0) if project else None
    summed = refs.pop(0) if carried else None
    sems, total, peak, stacked = [refs.pop() for _ in range(4)]
    slab = refs.pop() if project else None
    store = refs.pop()
    terms = refs.pop() if project else None
    out = refs.pop()
    buffers = with_offsets(refs, relay)
    for slot in range(RB_DEV):

        def begin(j, carry, slot=slot):
            at = slot * PMAX + j
            start_page(buffers, table[SLOT_AT + at], column, spot(store, at), sems.at[at])
            return carry

        lax.fori_loop(0, table[COUNT_AT + slot], begin, 0)
    if project:
        share = slab.shape[1]
        theirs = pl.multiple_of(table[THEIRS_AT] * share, share)
        rows = column // PAIR * WIDTH
        fetch = pltpu.make_async_copy(
            weight.at[pl.ds(rows, WIDTH), pl.ds(theirs, share)], slab, sems.at[RB_DEV * PMAX]
        )
        fetch.start()

    def absorb(keys_values, first, mask=None):
        span = keys_values.shape[0]
        keys = keys_values[:, :HD]
        values = jnp.concatenate(
            [keys_values[:, HD:], jnp.ones((span, HD), jnp.bfloat16)], axis=1
        )

        def score(r):
            return lax.dot_general(
                stacked[pl.ds(r, ROWS), :],
                keys,
                (((1,), (1,)), ((), ())),
                preferred_element_type=jnp.float32,
            )

        following = score(0)
        for r in range(0, GROUP * BLOCK, ROWS):
            rows = pl.ds(r, ROWS)
            scores = following
            if r + ROWS < GROUP * BLOCK:
                following = score(r + ROWS)
            if mask is not None:
                scores = jnp.where(mask, scores, NEG_LARGE)
            top = jnp.broadcast_to(jnp.max(scores, axis=1, keepdims=True), (ROWS, HD))
            if not first:
                before = peak[rows, :]
                top = jnp.maximum(before, top)
            spread = jnp.concatenate([top] * (span // HD), axis=1)
            weights = jnp.exp2((scores - spread) * SCALE).astype(jnp.bfloat16)
            blended = jnp.dot(weights, values, preferred_element_type=jnp.float32)
            if not first:
                fade = jnp.exp2((before - top) * SCALE)
                blended = total[rows, :] * jnp.concatenate([fade, fade], axis=1) + blended
            peak[rows, :] = top
            total[rows, :] = blended

    def one_block(b, carry):
        tokens = pl.ds(pl.multiple_of(b * BLOCK, BLOCK), BLOCK)
        for e in range(GROUP):
            stacked[e * BLOCK : (e + 1) * BLOCK, :] = queries[tokens, e * HD : (e + 1) * HD]
        span = RB_DEV * BLOCK
        row = lax.broadcasted_iota(jnp.int32, (ROWS, span), 0) & (BLOCK - 1)
        key = lax.broadcasted_iota(jnp.int32, (ROWS, span), 1)
        mask = (key <= row + b * BLOCK) & (key >= table[LOW_AT + b])
        absorb(own[...], True, mask)

        def finish(j, carry):
            at = b * PMAX + j
            wait_page(spot(store, at), sems.at[at])
            return carry

        lax.fori_loop(0, table[COUNT_AT + b], finish, 0)
        length, base = table[LENGTH_AT + b], table[BASE_AT + b]

        def tile(page, pages):
            at = pl.multiple_of(page * BLOCK, BLOCK)
            absorb(store[pl.ds(at, pages * BLOCK), :], False)

        pages = PMAX
        while pages:
            done = length & -(2 * pages)
            pl.when((length & pages) != 0)(lambda pages=pages, done=done: tile(base + done, pages))
            pages //= 2
        for e in range(GROUP):
            rows = slice(e * BLOCK, (e + 1) * BLOCK)
            out[tokens, e * HD : (e + 1) * HD] = (total[rows, :HD] / total[rows, HD:]).astype(
                jnp.bfloat16
            )
        return carry

    lax.fori_loop(0, RB_DEV, one_block, 0)
    if project:
        fetch.wait()
        attended = out[...]
        step = math.gcd(share, 512)
        for n in range(0, share, step):
            term = jnp.dot(attended, slab[:, n : n + step], preferred_element_type=jnp.float32)
            if carried:
                term = term + summed[:, n : n + step]
            terms[:, n : n + step] = term.astype(terms.dtype)


def attend(
    head, heads, relay, table, queries, resp_kv, buffers, weight=None, share=0, summed=None
):
    tokens = queries.shape[0]
    project, carried, final = weight is not None, summed is not None, head == heads - 1
    any_spec = pl.BlockSpec(memory_space=pl.ANY)
    whole = pl.BlockSpec((tokens, share), lambda i, c: (0, 0))
    out_shape = [jax.ShapeDtypeStruct((tokens, WIDTH), jnp.bfloat16)]
    out_specs = [pl.BlockSpec((tokens, WIDTH), lambda i, c: (0, 0))]
    operands, in_specs = [], []
    scratch = [pltpu.VMEM((RB_DEV * PMAX * BLOCK, PAIR), jnp.bfloat16)]
    if project:
        operands, in_specs = [weight], [any_spec]
        out_shape.append(
            jax.ShapeDtypeStruct((tokens, share), jnp.bfloat16 if final else jnp.float32)
        )
        out_specs.append(whole)
        scratch.append(pltpu.VMEM((WIDTH, share), jnp.bfloat16))
    if carried:
        operands, in_specs = operands + [summed], in_specs + [whole]
    return pl.pallas_call(
        lambda *refs: attend_kernel(head * PAIR, relay, carried, project, *refs),
        out_shape=out_shape,
        grid_spec=pltpu.PrefetchScalarGridSpec(
            num_scalar_prefetch=1,
            grid=(1,),
            in_specs=[
                pl.BlockSpec((tokens, WIDTH), lambda i, c: (0, head)),
                pl.BlockSpec((tokens, PAIR), lambda i, c: (0, head)),
            ]
            + in_specs
            + [any_spec] * len(buffers),
            out_specs=out_specs,
            scratch_shapes=scratch
            + [
                pltpu.VMEM((GROUP * BLOCK, HD), jnp.bfloat16),
                pltpu.VMEM((GROUP * BLOCK, HD), jnp.float32),
                pltpu.VMEM((GROUP * BLOCK, 2 * HD), jnp.float32),
                pltpu.SemaphoreType.DMA((RB_DEV * PMAX + 1,)),
            ],
        ),
        compiler_params=params(),
        cost_estimate=pl.CostEstimate(
            flops=2 * 2 * tokens * WIDTH * 18 * BLOCK * 2,
            bytes_accessed=2 * tokens * WIDTH * 2 + PMAX * BLOCK * PAIR * 2 + share * WIDTH * 2,
            transcendentals=tokens * GROUP * 18 * BLOCK,
        ),
        name=f"attend_head_{head}",
    )(table, queries, resp_kv, *operands, *buffers)


def pages_shape(count):
    return jax.ShapeDtypeStruct((count * BLOCK, PAIR), jnp.bfloat16)


def pack_send(wide, cores, heads, caps, ctrl, pool):
    any_spec = pl.BlockSpec(memory_space=pl.ANY)
    pages = PROMPTS * ((PMAX + wide - 1) // wide)
    out = pl.pallas_call(
        lambda *refs: send_kernel(wide, cores, heads, *refs),
        out_shape=[pages_shape(n) for n in (caps.near, caps.near, caps.far)] * heads,
        grid_spec=pltpu.PrefetchScalarGridSpec(
            num_scalar_prefetch=1,
            grid=(1,),
            in_specs=[pl.BlockSpec(pool.shape, lambda i, c: (0, 0))],
            out_specs=[any_spec] * 3 * heads,
            scratch_shapes=[pltpu.SemaphoreType.DMA((3, pages, heads))],
        ),
        compiler_params=params(),
        cost_estimate=pl.CostEstimate(
            flops=0, bytes_accessed=2 * 12 * BLOCK * PAIR * 2 * heads, transcendentals=0
        ),
        name="pack_send",
    )(ctrl, pool)
    return [out[3 * g : 3 * g + 3] for g in range(heads)]


def pack_share(cores, head, relay, table, buffers):
    any_spec = pl.BlockSpec(memory_space=pl.ANY)
    return pl.pallas_call(
        lambda *refs: share_kernel(cores, head * PAIR, relay, *refs),
        out_shape=pages_shape(PMAX),
        grid_spec=pltpu.PrefetchScalarGridSpec(
            num_scalar_prefetch=1,
            grid=(1,),
            in_specs=[any_spec] * len(buffers),
            out_specs=any_spec,
            scratch_shapes=[pltpu.SemaphoreType.DMA((PMAX,))],
        ),
        compiler_params=params(),
        cost_estimate=pl.CostEstimate(
            flops=0, bytes_accessed=2 * 8 * BLOCK * PAIR * 2, transcendentals=0
        ),
        name=f"pack_share_{head}",
    )(table, *buffers)


def pack_relay(cores, head, caps, ctrl, far, left, right):
    any_spec = pl.BlockSpec(memory_space=pl.ANY)
    return pl.pallas_call(
        lambda *refs: relay_kernel(cores, caps.relay * BLOCK, *refs),
        out_shape=pages_shape(2 * caps.relay),
        grid_spec=pltpu.PrefetchScalarGridSpec(
            num_scalar_prefetch=1,
            grid=(1,),
            in_specs=[any_spec] * 3,
            out_specs=any_spec,
            scratch_shapes=[pltpu.SemaphoreType.DMA((2,))],
        ),
        compiler_params=params(),
        cost_estimate=pl.CostEstimate(
            flops=0, bytes_accessed=4 * caps.relay * BLOCK * PAIR * 2, transcendentals=0
        ),
        name=f"pack_relay_{head}",
    )(ctrl, far, left, right)


def after(value, *earlier):
    return lax.optimization_barrier((value, *earlier))[0]


def line_attend(wide, cores, caps, ctrl, table, queries, resp_kv, pool, weight):
    heads = resp_kv.shape[1] // PAIR
    share = weight.shape[1] // 2

    def hop(x, moves):
        pairs = [(a * cores + c, b * cores + c) for a, b in moves for c in range(cores)]
        return lax.ppermute(x, "wide", pairs)

    swap = [(d, d // cores * cores + (cores - 1 - d % cores)) for d in range(wide)]
    sends = pack_send(wide, cores, heads, caps, ctrl, pool)
    parts, summed, arrived = [], None, []
    for g in range(heads):
        right, left, far = sends[g]
        arrived.append(
            (
                hop(far, [(0, 2), (3, 1)]),
                hop(right, [(0, 1), (1, 2), (2, 3)]),
                hop(left, [(3, 2), (2, 1), (1, 0)]),
            )
        )

    def relay(g):
        far, left, right = arrived[g]
        plan = after(ctrl, parts[g - 3]) if g >= 3 else ctrl
        onward = pack_relay(cores, g, caps, plan, far, left, right)
        return [pool, left, right, far, hop(onward, [(2, 3), (1, 0)])]

    def exchange(g, held):
        plan = after(table, parts[g - 2]) if g >= 2 else table
        shared = pack_share(cores, g, caps.relay, plan, held)
        return held + [lax.ppermute(shared, "wide", swap)]

    held = [None] * heads
    for step in range(heads + 2):
        if step < heads:
            held[step] = relay(step)
        if 1 <= step <= heads:
            held[step - 1] = exchange(step - 1, held[step - 1])
        if step >= 2:
            g = step - 2
            attended, summed = attend(
                g, heads, caps.relay, table, queries, resp_kv, held[g], weight, share, summed
            )
            parts.append(attended)
    return (*parts, summed)


def project_kernel(at, *refs):
    parts, weight, out = refs[:-2], refs[-2], refs[-1]
    total = None
    for i, part in enumerate(parts):
        term = jnp.dot(
            part[...], weight[i * WIDTH : (i + 1) * WIDTH, :], preferred_element_type=jnp.float32
        )
        total = term if total is None else total + term
    out[...] = total.astype(jnp.bfloat16)


def project(parts, weight, first_column, columns):
    tokens = parts[0].shape[0]
    tile = math.gcd(columns, 512)
    at = jnp.reshape(first_column // tile, (1,)).astype(jnp.int32)
    return pl.pallas_call(
        project_kernel,
        out_shape=jax.ShapeDtypeStruct((tokens, columns), jnp.bfloat16),
        grid_spec=pltpu.PrefetchScalarGridSpec(
            num_scalar_prefetch=1,
            grid=(columns // tile,),
            in_specs=[pl.BlockSpec((tokens, WIDTH), lambda i, at: (0, 0))] * len(parts)
            + [pl.BlockSpec((weight.shape[0], tile), lambda i, at: (0, at[0] + i))],
            out_specs=pl.BlockSpec((tokens, tile), lambda i, at: (0, i)),
        ),
        compiler_params=params(),
        cost_estimate=pl.CostEstimate(
            flops=2 * tokens * columns * weight.shape[0],
            bytes_accessed=2 * columns * weight.shape[0],
            transcendentals=0,
        ),
        name="project",
    )(at, *parts, weight)


def local(
    queries, resp_kv, prefix_pool, out_weight, pre_len, prompt_blocks, prompt_owner, resp_seg
):
    wide, groups = lax.axis_size("wide"), lax.axis_size("tp") * lax.axis_size("sub")
    cores = 2 // lax.axis_size("sub")
    heads = resp_kv.shape[1] // PAIR
    me = lax.axis_index("wide").astype(jnp.int32)
    group = lax.axis_index("tp") * lax.axis_size("sub") + lax.axis_index("sub")
    where = jnp.stack([me, (1 - group).astype(jnp.int32)])
    ctrl = jnp.concatenate([pre_len, prompt_blocks, prompt_owner, resp_seg, where])
    columns = out_weight.shape[1]
    share = columns // groups
    if wide == 8 and cores == 2 and groups == 2:
        table = make_plan(wide, cores, True, ctrl)

        def at_level(caps):
            return lambda *operands: line_attend(wide, cores, caps, *operands)

        *parts, theirs = lax.switch(
            table[LEVEL_AT],
            [at_level(caps) for caps in LEVELS],
            ctrl,
            table,
            queries,
            resp_kv,
            prefix_pool,
            out_weight,
        )
        axis = "tp" if lax.axis_size("tp") == 2 else "sub"
        arrived = lax.ppermute(theirs, axis, [(0, 1), (1, 0)])
        mine = project(parts, out_weight, group * share, share)
        return (mine.astype(jnp.float32) + arrived.astype(jnp.float32)).astype(jnp.bfloat16)
    table = make_plan(wide, cores, False, ctrl)
    buffers = [lax.all_gather(prefix_pool, "wide", axis=0, tiled=True)]
    parts = [attend(g, heads, 0, table, queries, resp_kv, buffers)[0] for g in range(heads)]
    terms = project(parts, out_weight, jnp.int32(0), columns)
    return lax.psum_scatter(terms, ("tp", "sub"), scatter_dimension=1, tiled=True)


def solution(mesh):
    return jax.shard_map(
        local,
        mesh=mesh,
        in_specs=(
            P(("parts", "wide"), ("tp", "sub")),
            P(("parts", "wide"), ("tp", "sub")),
            P(("parts", "wide"), ("tp", "sub")),
            P(("tp", "sub"), None),
            P("parts"),
            P("parts"),
            P("parts"),
            P(("parts", "wide")),
        ),
        out_specs=P(("parts", "wide"), ("tp", "sub")),
        check_vma=False,
    )
```

```python
import math

import jax
import jax.numpy as jnp
from jax import lax
from jax.experimental import pallas as pl
from jax.experimental.pallas import tpu as pltpu
from jax.sharding import PartitionSpec as P

HD = 128
BLOCK = 128
RB_DEV = 2
PROMPTS = 4
PMAX = 16
GROUP = 8
PAIR = 2 * HD
WIDTH = GROUP * HD
ROWS = 256
SPAN = 4
NEG_LARGE = -1e30
SCALE = math.log2(math.e) / math.sqrt(HD)
VMEM_BYTES = 48 * 1024 * 1024

LEN_AT, BLOCKS_AT, OWNER_AT, SEG_AT, ME_AT, OTHER_AT = 0, 4, 8, 12, 14, 15


def params():
    return pltpu.CompilerParams(vmem_limit_bytes=VMEM_BYTES)


def as_int(flag):
    return jnp.where(flag, 1, 0)


class Layout:
    def __init__(self, ctrl, wide, cores):
        self.ctrl, self.wide, self.cores = ctrl, wide, cores
        self.stride = (PMAX + wide - 1) // wide
        self.me = ctrl[ME_AT]
        self.z, self.core = self.div(self.me, cores), self.mod(self.me, cores)
        ends, total = [], 0
        for p in range(PROMPTS):
            total = total + ctrl[BLOCKS_AT + p] + (RB_DEV - 1)
            ends.append(total)
        self.ends = ends

    def mod(self, value, size):
        return value & (size - 1) if size & (size - 1) == 0 else lax.rem(value, size)

    def div(self, value, size):
        if size & (size - 1) == 0:
            return lax.shift_right_logical(value, size.bit_length() - 1)
        return lax.div(value, size)

    def prompt_of(self, block):
        return sum(as_int(block >= end) for end in self.ends[:-1])

    def first_of(self, chip):
        return self.prompt_of(chip * self.cores * RB_DEV)

    def last_of(self, chip):
        return self.prompt_of((chip + 1) * self.cores * RB_DEV - 1)

    def length(self, p):
        return self.ctrl[LEN_AT + p]

    def held_by(self, p, j):
        return self.mod(self.ctrl[OWNER_AT + p] + j, self.wide)

    def held(self, p, who):
        first = self.mod(who - self.ctrl[OWNER_AT + p] + self.wide, self.wide)
        return sum(as_int(first + k * self.wide < self.length(p)) for k in range(self.stride))

    def listed(self, which, rank, room):
        return jnp.where(
            rank < room, which * CODE + rank, (EXTRA + which - 1) * CODE + rank - room
        )

    def in_plane(self, p, j, sums):
        who = self.held_by(p, j)
        chip = self.div(who, self.cores)
        gap = chip - self.z
        k = self.div(j, self.wide)
        at = who * SUMS
        down = sums[at + PROMPTS] - sums[at + p + 1] + k
        up = sums[at + p] + k
        near_down = down - jnp.where(
            chip == 0, sums[at + PROMPTS] - sums[at + self.last_of(1) + 1], 0
        )
        near_up = up - jnp.where(chip == 3, sums[at + self.first_of(2)], 0)
        far = jnp.where(gap < 0, down, up)
        two = (gap == 2) | (gap == -2)
        direct = two & ((self.z == 1) | (self.z == 2))
        code = jnp.where(two, 5 * CODE, 4 * CODE) + far
        code = jnp.where(direct, self.listed(3, far, CAPS.far), code)
        code = jnp.where(gap == 1, self.listed(2, near_up, CAPS.near), code)
        code = jnp.where(gap == -1, self.listed(1, near_down, CAPS.near), code)
        return jnp.where(gap == 0, p * self.stride + k, code)


CODE = 256
SHARED = 6
EXTRA = 7
SUMS = 8
SLOT_AT, SHARE_AT, COUNT_AT, SHARES_AT, LENGTH_AT, BASE_AT, LOW_AT, THEIRS_AT, OVER_AT, TABLE = (
    0, 32, 48, 50, 52, 54, 56, 58, 59, 64
)


class Caps:
    def __init__(self, near, far, relay):
        self.near, self.far, self.relay = near, far, relay


CAPS = Caps(5, 5, 4)


def needs(lay, sums, cores):
    first, last = [lay.first_of(c) for c in range(4)], [lay.last_of(c) for c in range(4)]
    near, far = jnp.int32(0), jnp.int32(0)
    for core in range(cores):

        def held(chip, low, high, core=core):
            at = (chip * cores + core) * SUMS
            return sums[at + high + 1] - sums[at + low]

        top = PROMPTS - 1
        edge = [held(1, 0, last[0]), held(2, first[3], top)]
        for amount in edge + [
            held(0, first[1], last[1]),
            held(1, first[2], top),
            held(2, 0, last[1]),
            held(3, first[2], last[2]),
        ]:
            near = jnp.maximum(near, amount)
        for amount in (held(0, first[2], top), held(3, 0, last[1])):
            far = jnp.maximum(far, amount)
    return near, far


def plan_kernel(wide, cores, line, ctrl, table, sums):
    lay = Layout(ctrl, wide, cores)
    half = PMAX // cores
    table[THEIRS_AT] = ctrl[OTHER_AT]
    table[OVER_AT] = 0
    if line:

        def tally(who, carry):
            total = jnp.int32(0)
            for p in range(PROMPTS):
                sums[who * SUMS + p] = total
                total = total + lay.held(p, who)
            sums[who * SUMS + PROMPTS] = total
            return carry

        lax.fori_loop(0, wide, tally, 0)
        near, far = needs(lay, sums, cores)
        over = (near > CAPS.near) | (far > CAPS.far)
        table[OVER_AT] = as_int(over)

    def prompts_of(device):
        return [lay.prompt_of(device * RB_DEV + b) for b in range(RB_DEV)]

    mine = prompts_of(lay.me)
    same = mine[0] == mine[1]
    joined = same & (ctrl[SEG_AT] == ctrl[SEG_AT + 1])
    for slot in range(RB_DEV):
        p = mine[slot]
        count = lay.length(p)
        table[LENGTH_AT + slot] = count
        if slot == 1:
            count = jnp.where(same, 0, count)
        table[COUNT_AT + slot] = count
        table[BASE_AT + slot] = jnp.where(same, 0, PMAX) if slot else 0
        table[LOW_AT + slot] = jnp.where(joined, 0, BLOCK) if slot else 0

        def place(j, carry, slot=slot, p=p):
            who = lay.held_by(p, j)
            code = (who * PROMPTS + p) * lay.stride + lay.div(j, wide)
            if line:
                shared = (cores - 1 - lay.core) * PMAX + slot * half + lay.div(j, cores)
                passed = jnp.where(
                    lay.mod(who, cores) == lay.core,
                    lay.in_plane(p, j, sums),
                    SHARED * CODE + shared,
                )
                code = passed
            table[SLOT_AT + slot * PMAX + j] = code
            return carry

        lax.fori_loop(0, count, place, 0)
    if not line:
        return
    theirs = prompts_of(lay.z * cores + (cores - 1 - lay.core))
    for slot in range(RB_DEV):
        p = theirs[slot]
        shift = lay.mod(lay.core - ctrl[OWNER_AT + p] + wide, cores)
        count = lay.div(lay.length(p) - shift + cores - 1, cores)
        if slot == 1:
            count = jnp.where(theirs[1] == theirs[0], 0, count)
        table[SHARES_AT + slot] = count

        def share(i, carry, slot=slot, p=p, shift=shift):
            table[SHARE_AT + slot * half + i] = lay.in_plane(p, i * cores + shift, sums)
            return carry

        lax.fori_loop(0, count, share, 0)


def make_plan(wide, cores, line, ctrl):
    return pl.pallas_call(
        lambda *refs: plan_kernel(wide, cores, line, *refs),
        out_shape=jax.ShapeDtypeStruct((TABLE,), jnp.int32),
        in_specs=[pl.BlockSpec(memory_space=pltpu.SMEM)],
        out_specs=pl.BlockSpec(memory_space=pltpu.SMEM),
        scratch_shapes=[pltpu.SMEM((wide * SUMS,), jnp.int32)],
        compiler_params=params(),
        name="plan",
    )(ctrl)


def spot(ref, page):
    return ref.at[pl.ds(pl.multiple_of(page * BLOCK, BLOCK), BLOCK), :]


def page_at(buffer, page, column):
    rows = pl.ds(pl.multiple_of(page * BLOCK, BLOCK), BLOCK)
    return buffer.at[rows, pl.ds(column if buffer.shape[1] > PAIR else 0, PAIR)]


def start_page(buffers, code, column, target, sem):
    which = lax.shift_right_logical(code, CODE.bit_length() - 1)
    page = code & (CODE - 1)
    for i, buffer, offset in buffers:

        @pl.when(which == i)
        def _(buffer=buffer, offset=offset):
            source = page_at(buffer, page + offset, column)
            pltpu.make_async_copy(source, target, sem).start()


def wait_page(target, sem):
    pltpu.make_async_copy(target, target, sem).wait()


def send_kernel(wide, cores, heads, skip, ctrl, pool, *refs):
    outs, sems = refs[:-1], refs[-1]
    lay = Layout(ctrl, wide, cores)
    z, last = lay.z, wide // cores - 1
    held = [lay.held(p, lay.me) for p in range(PROMPTS)]

    def above(p, top):
        return sum([jnp.where(o <= top, held[o], 0) for o in range(p + 1, PROMPTS)], jnp.int32(0))

    def below(p, low):
        return sum([jnp.where(o >= low, held[o], 0) for o in range(p)], jnp.int32(0))

    near_top = jnp.where(z == 0, lay.last_of(1), PROMPTS - 1)
    near_low = jnp.where(z == last, lay.first_of(2), 0)
    first_up, last_down = lay.first_of(z + 1), lay.last_of(z - 1)
    first_two, last_one = lay.first_of(2), lay.last_of(1)
    plans = []
    for p in range(PROMPTS):
        right = (z < last) & (p >= first_up) & (p <= near_top)
        left = (z > 0) & (p >= near_low) & (p <= last_down)
        far_up = (z == 0) & (p >= first_two)
        far_down = (z == last) & (p <= last_one)
        ranks = (above(p, near_top), below(p, near_low), above(p, PROMPTS - 1), below(p, 0))
        for k in range(lay.stride):
            for lane, wanted, rank in zip((0, 1, 2, 2), (right, left, far_up, far_down), ranks):
                room = outs[lane].shape[0] // BLOCK
                at = rank + k - skip[lane]
                fits = (k < held[p]) & (at >= 0) & (at < room)
                plans.append((wanted & fits, p * lay.stride + k, lane, at))

    def copies(plan):
        _, page, lane, rank = plan
        return [
            pltpu.make_async_copy(
                page_at(pool, page, g * PAIR) if heads > 1 else spot(pool, page),
                spot(outs[g * 3 + lane], rank),
                sems.at[lane, page, g],
            )
            for g in range(heads)
        ]

    for plan in plans:

        @pl.when(plan[0])
        def _(plan=plan):
            for copy in copies(plan):
                copy.start()

    for plan in plans:

        @pl.when(plan[0])
        def _(plan=plan):
            for copy in copies(plan):
                copy.wait()


def relay_kernel(cores, rows, ctrl, far, left, right, out, sems):
    def copy(source, section):
        target = out.at[pl.ds(section * rows, rows), :]
        return pltpu.make_async_copy(source.at[pl.ds(0, rows), :], target, sems.at[section])

    inner = ctrl[ME_AT] == 2 * cores
    for core in range(1, cores):
        inner = inner | (ctrl[ME_AT] == 2 * cores + core)
    copy(far, 0).start()
    pl.when(inner)(lambda: copy(left, 1).start())
    pl.when(jnp.logical_not(inner))(lambda: copy(right, 1).start())
    copy(far, 0).wait()
    copy(far, 1).wait()


def numbered(refs, relay):
    if len(refs) == 1:
        return [(0, refs[0], 0)]
    found = [(i, ref, 0) for i, ref in enumerate(refs[:5])] + [(5, refs[4], relay)]
    if len(refs) == 9:
        found.append((SHARED, refs[5], 0))
    return found + [(EXTRA + i, ref, 0) for i, ref in enumerate(refs[-3:])]


def share_kernel(cores, column, relay, table, *refs):
    buffers, out, sems = numbered(refs[:-2], relay), refs[-2], refs[-1]
    half = PMAX // cores
    for slot in range(RB_DEV):

        def begin(i, carry, slot=slot):
            at = slot * half + i
            start_page(buffers, table[SHARE_AT + at], column, spot(out, at), sems.at[at])
            return carry

        lax.fori_loop(0, table[SHARES_AT + slot], begin, 0)
    for slot in range(RB_DEV):

        def finish(i, carry, slot=slot):
            at = slot * half + i
            wait_page(spot(out, at), sems.at[at])
            return carry

        lax.fori_loop(0, table[SHARES_AT + slot], finish, 0)


def attend_kernel(column, relay, carried, project, table, queries, own, *refs):
    refs = list(refs)
    weight = refs.pop(0) if project else None
    summed = refs.pop(0) if carried else None
    sems, stacked = refs.pop(), refs.pop()
    slab = refs.pop() if project else None
    store = refs.pop()
    terms = refs.pop() if project else None
    out = refs.pop()
    buffers = numbered(refs, relay)
    for slot in range(RB_DEV):

        def begin(j, carry, slot=slot):
            at = slot * PMAX + j
            start_page(buffers, table[SLOT_AT + at], column, spot(store, at), sems.at[at])
            return carry

        lax.fori_loop(0, table[COUNT_AT + slot], begin, 0)
    if project:
        share = slab.shape[1]
        theirs = pl.multiple_of(table[THEIRS_AT] * share, share)
        rows = column // PAIR * WIDTH
        fetch = pltpu.make_async_copy(
            weight.at[pl.ds(rows, WIDTH), pl.ds(theirs, share)], slab, sems.at[RB_DEV * PMAX]
        )
        fetch.start()

    for slot in range(RB_DEV):
        length = table[LENGTH_AT + slot]

        def clear(j, carry, slot=slot):
            rows = pl.ds(pl.multiple_of((slot * PMAX + j) * BLOCK, BLOCK), BLOCK)
            store[rows, :] = jnp.zeros((BLOCK, PAIR), jnp.bfloat16)
            return carry

        lax.fori_loop(length, (length + SPAN - 1) & -SPAN, clear, 0)

    def one_block(b, carry):
        tokens = pl.ds(pl.multiple_of(b * BLOCK, BLOCK), BLOCK)
        for e in range(GROUP):
            stacked[e * BLOCK : (e + 1) * BLOCK, :] = queries[tokens, e * HD : (e + 1) * HD]

        def finish(j, carry):
            at = b * PMAX + j
            wait_page(spot(store, at), sems.at[at])
            return carry

        lax.fori_loop(0, table[COUNT_AT + b], finish, 0)
        length, base = table[LENGTH_AT + b], table[BASE_AT + b]
        span = RB_DEV * BLOCK
        row = lax.broadcasted_iota(jnp.int32, (ROWS, span), 0) & (BLOCK - 1)
        key = lax.broadcasted_iota(jnp.int32, (ROWS, span), 1)
        own_mask = (key <= row + b * BLOCK) & (key >= table[LOW_AT + b])

        def run(spans):
            wide_key = lax.broadcasted_iota(jnp.int32, (ROWS, SPAN * BLOCK), 1)
            last_mask = wide_key < (length - (spans - 1) * SPAN) * BLOCK

            def piece(t):
                if t == 0:
                    return own[...]
                at = pl.multiple_of((base + (t - 1) * SPAN) * BLOCK, BLOCK)
                return store[pl.ds(at, SPAN * BLOCK), :]

            def score(r, t):
                scores = lax.dot_general(
                    stacked[r * ROWS : (r + 1) * ROWS, :],
                    pieces[t][:, :HD],
                    (((1,), (1,)), ((), ())),
                    preferred_element_type=jnp.float32,
                )
                if t == 0:
                    return jnp.where(own_mask, scores, NEG_LARGE)
                if t == spans:
                    return jnp.where(last_mask, scores, NEG_LARGE)
                return scores

            def highest(scores, sofar):
                for n in range(0, scores.shape[1], HD):
                    part = scores[:, n : n + HD]
                    sofar = part if sofar is None else jnp.maximum(sofar, part)
                return sofar

            def blend(scores, top, t):
                spread = jnp.concatenate([top] * (scores.shape[1] // HD), axis=1)
                weights = jnp.exp2((scores - spread) * SCALE).astype(jnp.bfloat16)
                values = pieces[t][:, HD:]
                values = jnp.concatenate([values, jnp.ones_like(values)], axis=1)
                return jnp.dot(weights, values, preferred_element_type=jnp.float32)

            pieces = [piece(t) for t in range(spans + 1)]
            chunks, ahead, peak = GROUP * BLOCK // ROWS, [], None
            for t in range(spans + 1):
                ahead.append(score(0, t))
                peak = highest(ahead[-1], peak)
            for r in range(chunks):
                now, ahead = ahead, []
                top = jnp.broadcast_to(jnp.max(peak, axis=1, keepdims=True), (ROWS, HD))
                total, peak = None, None
                for t in range(spans + 1):
                    if r + 1 < chunks:
                        ahead.append(score(r + 1, t))
                        peak = highest(ahead[-1], peak)
                    blended = blend(now[t], top, t)
                    total = blended if total is None else total + blended
                mean = (total[:, :HD] / total[:, HD:]).astype(jnp.bfloat16)
                for e in range(ROWS // BLOCK):
                    column = (r * (ROWS // BLOCK) + e) * HD
                    out[tokens, column : column + HD] = mean[e * BLOCK : (e + 1) * BLOCK, :]

        spans = lax.shift_right_logical(length + SPAN - 1, SPAN.bit_length() - 1)
        for n in range(1, PMAX // SPAN + 1):
            pl.when(spans == n)(lambda n=n: run(n))
        return carry

    lax.fori_loop(0, RB_DEV, one_block, 0)
    if project:
        fetch.wait()
        attended = out[...]
        step = math.gcd(share, 512)
        for n in range(0, share, step):
            term = jnp.dot(attended, slab[:, n : n + step], preferred_element_type=jnp.float32)
            if carried:
                term = term + summed[:, n : n + step]
            terms[:, n : n + step] = term.astype(terms.dtype)


def attend(
    head, heads, relay, table, queries, resp_kv, buffers, weight=None, share=0, summed=None
):
    tokens = queries.shape[0]
    project, carried, final = weight is not None, summed is not None, head == heads - 1
    any_spec = pl.BlockSpec(memory_space=pl.ANY)
    whole = pl.BlockSpec((tokens, share), lambda i, c: (0, 0))
    out_shape = [jax.ShapeDtypeStruct((tokens, WIDTH), jnp.bfloat16)]
    out_specs = [pl.BlockSpec((tokens, WIDTH), lambda i, c: (0, 0))]
    operands, in_specs = [], []
    scratch = [pltpu.VMEM((RB_DEV * PMAX * BLOCK, PAIR), jnp.bfloat16)]
    if project:
        operands, in_specs = [weight], [any_spec]
        out_shape.append(
            jax.ShapeDtypeStruct((tokens, share), jnp.bfloat16 if final else jnp.float32)
        )
        out_specs.append(whole)
        scratch.append(pltpu.VMEM((WIDTH, share), jnp.bfloat16))
    if carried:
        operands, in_specs = operands + [summed], in_specs + [whole]
    return pl.pallas_call(
        lambda *refs: attend_kernel(head * PAIR, relay, carried, project, *refs),
        out_shape=out_shape,
        grid_spec=pltpu.PrefetchScalarGridSpec(
            num_scalar_prefetch=1,
            grid=(1,),
            in_specs=[
                pl.BlockSpec((tokens, WIDTH), lambda i, c: (0, head)),
                pl.BlockSpec((tokens, PAIR), lambda i, c: (0, head)),
            ]
            + in_specs
            + [any_spec] * len(buffers),
            out_specs=out_specs,
            scratch_shapes=scratch
            + [
                pltpu.VMEM((GROUP * BLOCK, HD), jnp.bfloat16),
                pltpu.SemaphoreType.DMA((RB_DEV * PMAX + 1,)),
            ],
        ),
        compiler_params=params(),
        cost_estimate=pl.CostEstimate(
            flops=2 * 2 * tokens * WIDTH * 18 * BLOCK * 2,
            bytes_accessed=2 * tokens * WIDTH * 2 + PMAX * BLOCK * PAIR * 2 + share * WIDTH * 2,
            transcendentals=tokens * GROUP * 18 * BLOCK,
        ),
        name=f"attend_head_{head}",
    )(table, queries, resp_kv, *operands, *buffers)


def pages_shape(count):
    return jax.ShapeDtypeStruct((count * BLOCK, PAIR), jnp.bfloat16)


def pack_send(wide, cores, heads, shapes, skip, ctrl, pool):
    any_spec = pl.BlockSpec(memory_space=pl.ANY)
    pages = PROMPTS * ((PMAX + wide - 1) // wide)
    out = pl.pallas_call(
        lambda *refs: send_kernel(wide, cores, heads, skip, *refs),
        out_shape=shapes * heads,
        grid_spec=pltpu.PrefetchScalarGridSpec(
            num_scalar_prefetch=1,
            grid=(1,),
            in_specs=[pl.BlockSpec(pool.shape, lambda i, c: (0, 0))],
            out_specs=[any_spec] * 3 * heads,
            scratch_shapes=[pltpu.SemaphoreType.DMA((3, pages, heads))],
        ),
        compiler_params=params(),
        cost_estimate=pl.CostEstimate(
            flops=0, bytes_accessed=2 * 12 * BLOCK * PAIR * 2 * heads, transcendentals=0
        ),
        name="pack_send" if heads > 1 else "pack_extra",
    )(ctrl, pool)
    return [out[3 * g : 3 * g + 3] for g in range(heads)]


def pack_share(cores, head, relay, table, buffers):
    any_spec = pl.BlockSpec(memory_space=pl.ANY)
    return pl.pallas_call(
        lambda *refs: share_kernel(cores, head * PAIR, relay, *refs),
        out_shape=pages_shape(PMAX),
        grid_spec=pltpu.PrefetchScalarGridSpec(
            num_scalar_prefetch=1,
            grid=(1,),
            in_specs=[any_spec] * len(buffers),
            out_specs=any_spec,
            scratch_shapes=[pltpu.SemaphoreType.DMA((PMAX,))],
        ),
        compiler_params=params(),
        cost_estimate=pl.CostEstimate(
            flops=0, bytes_accessed=2 * 8 * BLOCK * PAIR * 2, transcendentals=0
        ),
        name=f"pack_share_{head}",
    )(table, *buffers)


def pack_relay(cores, head, caps, ctrl, far, left, right):
    any_spec = pl.BlockSpec(memory_space=pl.ANY)
    return pl.pallas_call(
        lambda *refs: relay_kernel(cores, caps.relay * BLOCK, *refs),
        out_shape=pages_shape(2 * caps.relay),
        grid_spec=pltpu.PrefetchScalarGridSpec(
            num_scalar_prefetch=1,
            grid=(1,),
            in_specs=[any_spec] * 3,
            out_specs=any_spec,
            scratch_shapes=[pltpu.SemaphoreType.DMA((2,))],
        ),
        compiler_params=params(),
        cost_estimate=pl.CostEstimate(
            flops=0, bytes_accessed=4 * caps.relay * BLOCK * PAIR * 2, transcendentals=0
        ),
        name=f"pack_relay_{head}",
    )(ctrl, far, left, right)


def after(value, *earlier):
    return lax.optimization_barrier((value, *earlier))[0]


def line_attend(wide, cores, caps, ctrl, table, queries, resp_kv, pool, weight):
    heads = resp_kv.shape[1] // PAIR
    share = weight.shape[1] // 2

    def hop(x, moves):
        pairs = [(a * cores + c, b * cores + c) for a, b in moves for c in range(cores)]
        return lax.ppermute(x, "wide", pairs)

    chips = [[z * cores + c for c in range(cores)] for z in range(wide // cores)]
    lists = [pages_shape(n) for n in (caps.near, caps.near, caps.far)]
    sends = pack_send(wide, cores, heads, lists, (0, 0, 0), ctrl, pool)
    one_page = jax.ShapeDtypeStruct((BLOCK, pool.shape[1]), jnp.bfloat16)

    def spread(right, left, far):
        return (
            hop(right, [(0, 1), (1, 2), (2, 3)]),
            hop(left, [(3, 2), (2, 1), (1, 0)]),
            hop(far, [(0, 2), (3, 1)]),
        )

    def past_the_end(ctrl, pool):
        skip = (caps.near, caps.near, caps.far)
        return spread(*pack_send(wide, cores, 1, [one_page] * 3, skip, ctrl, pool)[0])

    def nothing(ctrl, pool):
        return (jnp.zeros(one_page.shape, one_page.dtype),) * 3

    extra = list(lax.cond(table[OVER_AT] == 1, past_the_end, nothing, ctrl, pool))
    parts, summed, arrived = [], None, []
    for g in range(heads):
        left, right, far = spread(*sends[g])
        arrived.append((far, left, right))

    def relay(g):
        far, left, right = arrived[g]
        plan = after(ctrl, parts[g - 3]) if g >= 3 else ctrl
        onward = pack_relay(cores, g, caps, plan, far, left, right)
        return [pool, left, right, far, hop(onward, [(2, 3), (1, 0)])]

    def exchange(g, held):
        plan = after(table, parts[g - 2]) if g >= 2 else table
        shared = pack_share(cores, g, caps.relay, plan, held + extra)
        both = lax.all_gather(shared, "wide", axis=0, tiled=True, axis_index_groups=chips)
        return held + [both] + extra

    held = [None] * heads
    for step in range(heads + 2):
        if step < heads:
            held[step] = relay(step)
        if 1 <= step <= heads:
            held[step - 1] = exchange(step - 1, held[step - 1])
        if step >= 2:
            g = step - 2
            attended, summed = attend(
                g, heads, caps.relay, table, queries, resp_kv, held[g], weight, share, summed
            )
            parts.append(attended)
    return (*parts, summed)


def project_kernel(at, *refs):
    parts, weight, out = refs[:-2], refs[-2], refs[-1]
    total = None
    for i, part in enumerate(parts):
        term = jnp.dot(
            part[...], weight[i * WIDTH : (i + 1) * WIDTH, :], preferred_element_type=jnp.float32
        )
        total = term if total is None else total + term
    out[...] = total.astype(jnp.bfloat16)


def project(parts, weight, first_column, columns):
    tokens = parts[0].shape[0]
    tile = math.gcd(columns, 512)
    at = jnp.reshape(first_column // tile, (1,)).astype(jnp.int32)
    return pl.pallas_call(
        project_kernel,
        out_shape=jax.ShapeDtypeStruct((tokens, columns), jnp.bfloat16),
        grid_spec=pltpu.PrefetchScalarGridSpec(
            num_scalar_prefetch=1,
            grid=(columns // tile,),
            in_specs=[pl.BlockSpec((tokens, WIDTH), lambda i, at: (0, 0))] * len(parts)
            + [pl.BlockSpec((weight.shape[0], tile), lambda i, at: (0, at[0] + i))],
            out_specs=pl.BlockSpec((tokens, tile), lambda i, at: (0, i)),
        ),
        compiler_params=params(),
        cost_estimate=pl.CostEstimate(
            flops=2 * tokens * columns * weight.shape[0],
            bytes_accessed=2 * columns * weight.shape[0],
            transcendentals=0,
        ),
        name="project",
    )(at, *parts, weight)


def local(
    queries, resp_kv, prefix_pool, out_weight, pre_len, prompt_blocks, prompt_owner, resp_seg
):
    wide, groups = lax.axis_size("wide"), lax.axis_size("tp") * lax.axis_size("sub")
    cores = 2 // lax.axis_size("sub")
    heads = resp_kv.shape[1] // PAIR
    me = lax.axis_index("wide").astype(jnp.int32)
    group = lax.axis_index("tp") * lax.axis_size("sub") + lax.axis_index("sub")
    where = jnp.stack([me, (1 - group).astype(jnp.int32)])
    ctrl = jnp.concatenate([pre_len, prompt_blocks, prompt_owner, resp_seg, where])
    columns = out_weight.shape[1]
    share = columns // groups
    if wide == 8 and cores == 2 and groups == 2:
        table = make_plan(wide, cores, True, ctrl)

        *parts, theirs = line_attend(
            wide, cores, CAPS, ctrl, table, queries, resp_kv, prefix_pool, out_weight
        )
        axis = "tp" if lax.axis_size("tp") == 2 else "sub"
        arrived = lax.ppermute(theirs, axis, [(0, 1), (1, 0)])
        mine = project(parts, out_weight, group * share, share)
        return (mine.astype(jnp.float32) + arrived.astype(jnp.float32)).astype(jnp.bfloat16)
    table = make_plan(wide, cores, False, ctrl)
    buffers = [lax.all_gather(prefix_pool, "wide", axis=0, tiled=True)]
    parts = [attend(g, heads, 0, table, queries, resp_kv, buffers)[0] for g in range(heads)]
    terms = project(parts, out_weight, jnp.int32(0), columns)
    return lax.psum_scatter(terms, ("tp", "sub"), scatter_dimension=1, tiled=True)


def solution(mesh):
    return jax.shard_map(
        local,
        mesh=mesh,
        in_specs=(
            P(("parts", "wide"), ("tp", "sub")),
            P(("parts", "wide"), ("tp", "sub")),
            P(("parts", "wide"), ("tp", "sub")),
            P(("tp", "sub"), None),
            P("parts"),
            P("parts"),
            P("parts"),
            P(("parts", "wide")),
        ),
        out_specs=P(("parts", "wide"), ("tp", "sub")),
        check_vma=False,
    )
```

```python
import math

import jax
import jax.numpy as jnp
from jax import lax
from jax.experimental import pallas as pl
from jax.experimental.pallas import tpu as pltpu
from jax.sharding import PartitionSpec as P

HD = 128
BLOCK = 128
RB_DEV = 2
PROMPTS = 4
PMAX = 16
GROUP = 8
PAIR = 2 * HD
WIDTH = GROUP * HD
ROWS = 512
SPAN = 4
NEG_LARGE = -1e30
SCALE = math.log2(math.e) / math.sqrt(HD)
VMEM_BYTES = 48 * 1024 * 1024

LEN_AT, BLOCKS_AT, OWNER_AT, SEG_AT, ME_AT, OTHER_AT = 0, 4, 8, 12, 14, 15


def params():
    return pltpu.CompilerParams(vmem_limit_bytes=VMEM_BYTES)


def as_int(flag):
    return jnp.where(flag, 1, 0)


class Layout:
    def __init__(self, ctrl, wide, cores):
        self.ctrl, self.wide, self.cores = ctrl, wide, cores
        self.stride = (PMAX + wide - 1) // wide
        self.me = ctrl[ME_AT]
        self.z, self.core = self.div(self.me, cores), self.mod(self.me, cores)
        ends, total = [], 0
        for p in range(PROMPTS):
            total = total + ctrl[BLOCKS_AT + p] + (RB_DEV - 1)
            ends.append(total)
        self.ends = ends

    def mod(self, value, size):
        return value & (size - 1) if size & (size - 1) == 0 else lax.rem(value, size)

    def div(self, value, size):
        if size & (size - 1) == 0:
            return lax.shift_right_logical(value, size.bit_length() - 1)
        return lax.div(value, size)

    def prompt_of(self, block):
        return sum(as_int(block >= end) for end in self.ends[:-1])

    def first_of(self, chip):
        return self.prompt_of(chip * self.cores * RB_DEV)

    def last_of(self, chip):
        return self.prompt_of((chip + 1) * self.cores * RB_DEV - 1)

    def length(self, p):
        return self.ctrl[LEN_AT + p]

    def held_by(self, p, j):
        return self.mod(self.ctrl[OWNER_AT + p] + j, self.wide)

    def held(self, p, who):
        first = self.mod(who - self.ctrl[OWNER_AT + p] + self.wide, self.wide)
        return sum(as_int(first + k * self.wide < self.length(p)) for k in range(self.stride))

    def listed(self, which, rank, room):
        return jnp.where(
            rank < room, which * CODE + rank, (EXTRA + which - 1) * CODE + rank - room
        )

    def in_plane(self, p, j, sums):
        who = self.held_by(p, j)
        chip = self.div(who, self.cores)
        gap = chip - self.z
        k = self.div(j, self.wide)
        at = who * SUMS
        down = sums[at + PROMPTS] - sums[at + p + 1] + k
        up = sums[at + p] + k
        near_down = down - jnp.where(
            chip == 0, sums[at + PROMPTS] - sums[at + self.last_of(1) + 1], 0
        )
        near_up = up - jnp.where(chip == 3, sums[at + self.first_of(2)], 0)
        far = jnp.where(gap < 0, down, up)
        two = (gap == 2) | (gap == -2)
        direct = two & ((self.z == 1) | (self.z == 2))
        code = jnp.where(two, 5 * CODE, 4 * CODE) + far
        code = jnp.where(direct, self.listed(3, far, CAPS.far), code)
        code = jnp.where(gap == 1, self.listed(2, near_up, CAPS.near), code)
        code = jnp.where(gap == -1, self.listed(1, near_down, CAPS.near), code)
        return jnp.where(gap == 0, p * self.stride + k, code)


CODE = 256
SHARED = 6
EXTRA = 7
SUMS = 8
SLOT_AT, SHARE_AT, COUNT_AT, SHARES_AT, LENGTH_AT, BASE_AT, LOW_AT, THEIRS_AT, OVER_AT, TABLE = (
    0, 32, 48, 50, 52, 54, 56, 58, 59, 64
)


class Caps:
    def __init__(self, near, far, relay):
        self.near, self.far, self.relay = near, far, relay


CAPS = Caps(5, 5, 4)


def needs(lay, sums, cores):
    first, last = [lay.first_of(c) for c in range(4)], [lay.last_of(c) for c in range(4)]
    near, far = jnp.int32(0), jnp.int32(0)
    for core in range(cores):

        def held(chip, low, high, core=core):
            at = (chip * cores + core) * SUMS
            return sums[at + high + 1] - sums[at + low]

        top = PROMPTS - 1
        edge = [held(1, 0, last[0]), held(2, first[3], top)]
        for amount in edge + [
            held(0, first[1], last[1]),
            held(1, first[2], top),
            held(2, 0, last[1]),
            held(3, first[2], last[2]),
        ]:
            near = jnp.maximum(near, amount)
        for amount in (held(0, first[2], top), held(3, 0, last[1])):
            far = jnp.maximum(far, amount)
    return near, far


def plan_kernel(wide, cores, line, ctrl, table, sums):
    lay = Layout(ctrl, wide, cores)
    half = PMAX // cores
    table[THEIRS_AT] = ctrl[OTHER_AT]
    table[OVER_AT] = 0
    if line:

        def tally(who, carry):
            total = jnp.int32(0)
            for p in range(PROMPTS):
                sums[who * SUMS + p] = total
                total = total + lay.held(p, who)
            sums[who * SUMS + PROMPTS] = total
            return carry

        lax.fori_loop(0, wide, tally, 0)
        near, far = needs(lay, sums, cores)
        over = (near > CAPS.near) | (far > CAPS.far)
        table[OVER_AT] = as_int(over)

    def prompts_of(device):
        return [lay.prompt_of(device * RB_DEV + b) for b in range(RB_DEV)]

    mine = prompts_of(lay.me)
    same = mine[0] == mine[1]
    joined = same & (ctrl[SEG_AT] == ctrl[SEG_AT + 1])
    for slot in range(RB_DEV):
        p = mine[slot]
        count = lay.length(p)
        table[LENGTH_AT + slot] = count
        if slot == 1:
            count = jnp.where(same, 0, count)
        table[COUNT_AT + slot] = count
        table[BASE_AT + slot] = jnp.where(same, 0, PMAX) if slot else 0
        table[LOW_AT + slot] = jnp.where(joined, 0, BLOCK) if slot else 0

        def place(j, carry, slot=slot, p=p):
            who = lay.held_by(p, j)
            code = (who * PROMPTS + p) * lay.stride + lay.div(j, wide)
            if line:
                shared = slot * half + lay.div(j, cores)
                passed = jnp.where(
                    lay.mod(who, cores) == lay.core,
                    lay.in_plane(p, j, sums),
                    SHARED * CODE + shared,
                )
                code = passed
            table[SLOT_AT + slot * PMAX + j] = code
            return carry

        lax.fori_loop(0, count, place, 0)
    if not line:
        return
    theirs = prompts_of(lay.z * cores + (cores - 1 - lay.core))
    for slot in range(RB_DEV):
        p = theirs[slot]
        shift = lay.mod(lay.core - ctrl[OWNER_AT + p] + wide, cores)
        count = lay.div(lay.length(p) - shift + cores - 1, cores)
        if slot == 1:
            count = jnp.where(theirs[1] == theirs[0], 0, count)
        table[SHARES_AT + slot] = count

        def share(i, carry, slot=slot, p=p, shift=shift):
            table[SHARE_AT + slot * half + i] = lay.in_plane(p, i * cores + shift, sums)
            return carry

        lax.fori_loop(0, count, share, 0)


def make_plan(wide, cores, line, ctrl):
    return pl.pallas_call(
        lambda *refs: plan_kernel(wide, cores, line, *refs),
        out_shape=jax.ShapeDtypeStruct((TABLE,), jnp.int32),
        in_specs=[pl.BlockSpec(memory_space=pltpu.SMEM)],
        out_specs=pl.BlockSpec(memory_space=pltpu.SMEM),
        scratch_shapes=[pltpu.SMEM((wide * SUMS,), jnp.int32)],
        compiler_params=params(),
        name="plan",
    )(ctrl)


def spot(ref, page):
    return ref.at[pl.ds(pl.multiple_of(page * BLOCK, BLOCK), BLOCK), :]


def page_at(buffer, page, column):
    rows = pl.ds(pl.multiple_of(page * BLOCK, BLOCK), BLOCK)
    return buffer.at[rows, pl.ds(column if buffer.shape[1] > PAIR else 0, PAIR)]


def start_page(buffers, code, column, target, sem):
    which = lax.shift_right_logical(code, CODE.bit_length() - 1)
    page = code & (CODE - 1)
    for i, buffer, offset in buffers:

        @pl.when(which == i)
        def _(buffer=buffer, offset=offset):
            source = page_at(buffer, page + offset, column)
            pltpu.make_async_copy(source, target, sem).start()


def wait_page(target, sem):
    pltpu.make_async_copy(target, target, sem).wait()


def send_kernel(wide, cores, groups, caps, skip, ctrl, pool, *refs):
    outs, sems = refs[:-1], refs[-1]
    rooms = (caps.near, caps.near, caps.far)
    lay = Layout(ctrl, wide, cores)
    z, last = lay.z, wide // cores - 1
    held = [lay.held(p, lay.me) for p in range(PROMPTS)]

    def above(p, top):
        return sum([jnp.where(o <= top, held[o], 0) for o in range(p + 1, PROMPTS)], jnp.int32(0))

    def below(p, low):
        return sum([jnp.where(o >= low, held[o], 0) for o in range(p)], jnp.int32(0))

    near_top = jnp.where(z == 0, lay.last_of(1), PROMPTS - 1)
    near_low = jnp.where(z == last, lay.first_of(2), 0)
    first_up, last_down = lay.first_of(z + 1), lay.last_of(z - 1)
    first_two, last_one = lay.first_of(2), lay.last_of(1)
    plans = []
    for p in range(PROMPTS):
        right = (z < last) & (p >= first_up) & (p <= near_top)
        left = (z > 0) & (p >= near_low) & (p <= last_down)
        far_up = (z == 0) & (p >= first_two)
        far_down = (z == last) & (p <= last_one)
        ranks = (above(p, near_top), below(p, near_low), above(p, PROMPTS - 1), below(p, 0))
        for k in range(lay.stride):
            for lane, wanted, rank in zip((0, 1, 2, 2), (right, left, far_up, far_down), ranks):
                at = rank + k - skip[lane]
                fits = (k < held[p]) & (at >= 0) & (at < rooms[lane])
                plans.append((wanted & fits, p * lay.stride + k, lane, at))

    def copies(plan):
        _, page, lane, rank = plan
        if groups is None:
            return [
                pltpu.make_async_copy(
                    spot(pool, page), spot(outs[lane], rank), sems.at[lane, page, 0]
                )
            ]
        return [
            pltpu.make_async_copy(
                page_at(pool, page, g * PAIR),
                spot(outs[n * 3 + lane], h * rooms[lane] + rank),
                sems.at[lane, page, g],
            )
            for n, group in enumerate(groups)
            for h, g in enumerate(group)
        ]

    for plan in plans:

        @pl.when(plan[0])
        def _(plan=plan):
            for copy in copies(plan):
                copy.start()

    for plan in plans:

        @pl.when(plan[0])
        def _(plan=plan):
            for copy in copies(plan):
                copy.wait()


def relay_kernel(cores, caps, heads, ctrl, far, left, right, out, sems):
    rows = caps.relay * BLOCK

    def copy(source, room, h, section):
        target = out.at[pl.ds((2 * h + section) * rows, rows), :]
        return pltpu.make_async_copy(
            source.at[pl.ds(h * room * BLOCK, rows), :], target, sems.at[h, section]
        )

    inner = ctrl[ME_AT] == 2 * cores
    for core in range(1, cores):
        inner = inner | (ctrl[ME_AT] == 2 * cores + core)
    for h in range(heads):
        copy(far, caps.far, h, 0).start()
        pl.when(inner)(lambda h=h: copy(left, caps.near, h, 1).start())
        pl.when(jnp.logical_not(inner))(lambda h=h: copy(right, caps.near, h, 1).start())
    for h in range(heads):
        copy(far, caps.far, h, 0).wait()
        copy(left, caps.near, h, 1).wait()


def numbered(refs, caps, h):
    if len(refs) == 1:
        return [(0, refs[0], 0)]
    offsets = (0, h * caps.near, h * caps.near, h * caps.far, 2 * h * caps.relay)
    found = list(zip(range(5), refs[:5], offsets)) + [(5, refs[4], (2 * h + 1) * caps.relay)]
    if len(refs) == 9:
        found.append((SHARED, refs[5], h * PMAX))
    return found + [(EXTRA + i, ref, 0) for i, ref in enumerate(refs[-3:])]


def share_kernel(cores, caps, group, table, *refs):
    out, sems = refs[-2:]
    half = PMAX // cores
    for h, g in enumerate(group):
        buffers = numbered(refs[:-2], caps, h)
        for slot in range(RB_DEV):

            def begin(i, carry, slot=slot, h=h, g=g, buffers=buffers):
                at = slot * half + i
                target = spot(out, h * PMAX + at)
                start_page(buffers, table[SHARE_AT + at], g * PAIR, target, sems.at[h, at])
                return carry

            lax.fori_loop(0, table[SHARES_AT + slot], begin, 0)
    for h in range(len(group)):
        for slot in range(RB_DEV):

            def finish(i, carry, slot=slot, h=h):
                at = slot * half + i
                wait_page(spot(out, h * PMAX + at), sems.at[h, at])
                return carry

            lax.fori_loop(0, table[SHARES_AT + slot], finish, 0)


def attend_kernel(column, caps, h, carried, project, table, queries, own, *refs):
    refs = list(refs)
    weight = refs.pop(0) if project else None
    summed = refs.pop(0) if carried else None
    sems, stacked = refs.pop(), refs.pop()
    slab = refs.pop() if project else None
    store = refs.pop()
    terms = refs.pop() if project else None
    out = refs.pop()
    buffers = numbered(refs, caps, h)
    for slot in range(RB_DEV):

        def begin(j, carry, slot=slot):
            at = slot * PMAX + j
            start_page(buffers, table[SLOT_AT + at], column, spot(store, at), sems.at[at])
            return carry

        lax.fori_loop(0, table[COUNT_AT + slot], begin, 0)
    if project:
        share = slab.shape[1]
        theirs = pl.multiple_of(table[THEIRS_AT] * share, share)
        rows = column // PAIR * WIDTH
        fetch = pltpu.make_async_copy(
            weight.at[pl.ds(rows, WIDTH), pl.ds(theirs, share)], slab, sems.at[RB_DEV * PMAX]
        )
        fetch.start()

    for slot in range(RB_DEV):
        length = table[LENGTH_AT + slot]

        def clear(j, carry, slot=slot):
            rows = pl.ds(pl.multiple_of((slot * PMAX + j) * BLOCK, BLOCK), BLOCK)
            store[rows, :] = jnp.zeros((BLOCK, PAIR), jnp.bfloat16)
            return carry

        lax.fori_loop(length, (length + SPAN - 1) & -SPAN, clear, 0)

    def one_block(b, carry):
        tokens = pl.ds(pl.multiple_of(b * BLOCK, BLOCK), BLOCK)
        for e in range(GROUP):
            stacked[e * BLOCK : (e + 1) * BLOCK, :] = queries[tokens, e * HD : (e + 1) * HD]

        def finish(j, carry):
            at = b * PMAX + j
            wait_page(spot(store, at), sems.at[at])
            return carry

        lax.fori_loop(0, table[COUNT_AT + b], finish, 0)
        length, base = table[LENGTH_AT + b], table[BASE_AT + b]
        span = RB_DEV * BLOCK
        row = lax.broadcasted_iota(jnp.int32, (ROWS, span), 0) & (BLOCK - 1)
        key = lax.broadcasted_iota(jnp.int32, (ROWS, span), 1)
        own_mask = (key <= row + b * BLOCK) & (key >= table[LOW_AT + b])

        def run(spans):
            wide_key = lax.broadcasted_iota(jnp.int32, (ROWS, SPAN * BLOCK), 1)
            last_mask = wide_key < (length - (spans - 1) * SPAN) * BLOCK

            def piece(t):
                if t == 0:
                    return own[...]
                at = pl.multiple_of((base + (t - 1) * SPAN) * BLOCK, BLOCK)
                return store[pl.ds(at, SPAN * BLOCK), :]

            def score(r, t):
                scores = lax.dot_general(
                    stacked[r * ROWS : (r + 1) * ROWS, :],
                    pieces[t][:, :HD],
                    (((1,), (1,)), ((), ())),
                    preferred_element_type=jnp.float32,
                )
                if t == 0:
                    return jnp.where(own_mask, scores, NEG_LARGE)
                if t == spans:
                    return jnp.where(last_mask, scores, NEG_LARGE)
                return scores

            def highest(scores, sofar):
                for n in range(0, scores.shape[1], HD):
                    part = scores[:, n : n + HD]
                    sofar = part if sofar is None else jnp.maximum(sofar, part)
                return sofar

            def blend(scores, top, t):
                spread = jnp.concatenate([top] * (scores.shape[1] // HD), axis=1)
                weights = jnp.exp2((scores - spread) * SCALE).astype(jnp.bfloat16)
                values = pieces[t][:, HD:]
                values = jnp.concatenate([values, jnp.ones_like(values)], axis=1)
                return jnp.dot(weights, values, preferred_element_type=jnp.float32)

            pieces = [piece(t) for t in range(spans + 1)]
            chunks, ahead, peak = GROUP * BLOCK // ROWS, [], None
            for t in range(spans + 1):
                ahead.append(score(0, t))
                peak = highest(ahead[-1], peak)
            for r in range(chunks):
                now, ahead = ahead, []
                top = jnp.broadcast_to(jnp.max(peak, axis=1, keepdims=True), (ROWS, HD))
                total, peak = None, None
                for t in range(spans + 1):
                    if r + 1 < chunks:
                        ahead.append(score(r + 1, t))
                        peak = highest(ahead[-1], peak)
                    blended = blend(now[t], top, t)
                    total = blended if total is None else total + blended
                mean = (total[:, :HD] / total[:, HD:]).astype(jnp.bfloat16)
                for e in range(ROWS // BLOCK):
                    column = (r * (ROWS // BLOCK) + e) * HD
                    out[tokens, column : column + HD] = mean[e * BLOCK : (e + 1) * BLOCK, :]

        spans = lax.shift_right_logical(length + SPAN - 1, SPAN.bit_length() - 1)
        for n in range(1, PMAX // SPAN + 1):
            pl.when(spans == n)(lambda n=n: run(n))
        return carry

    lax.fori_loop(0, RB_DEV, one_block, 0)
    if project:
        fetch.wait()
        attended = out[...]
        step = math.gcd(share, 512)
        for n in range(0, share, step):
            term = jnp.dot(attended, slab[:, n : n + step], preferred_element_type=jnp.float32)
            if carried:
                term = term + summed[:, n : n + step]
            terms[:, n : n + step] = term.astype(terms.dtype)


def attend(
    head, heads, caps, h, table, queries, resp_kv, buffers, weight=None, share=0, summed=None
):
    tokens = queries.shape[0]
    project, carried, final = weight is not None, summed is not None, head == heads - 1
    any_spec = pl.BlockSpec(memory_space=pl.ANY)
    whole = pl.BlockSpec((tokens, share), lambda i, c: (0, 0))
    out_shape = [jax.ShapeDtypeStruct((tokens, WIDTH), jnp.bfloat16)]
    out_specs = [pl.BlockSpec((tokens, WIDTH), lambda i, c: (0, 0))]
    operands, in_specs = [], []
    scratch = [pltpu.VMEM((RB_DEV * PMAX * BLOCK, PAIR), jnp.bfloat16)]
    if project:
        operands, in_specs = [weight], [any_spec]
        out_shape.append(
            jax.ShapeDtypeStruct((tokens, share), jnp.bfloat16 if final else jnp.float32)
        )
        out_specs.append(whole)
        scratch.append(pltpu.VMEM((WIDTH, share), jnp.bfloat16))
    if carried:
        operands, in_specs = operands + [summed], in_specs + [whole]
    return pl.pallas_call(
        lambda *refs: attend_kernel(head * PAIR, caps, h, carried, project, *refs),
        out_shape=out_shape,
        grid_spec=pltpu.PrefetchScalarGridSpec(
            num_scalar_prefetch=1,
            grid=(1,),
            in_specs=[
                pl.BlockSpec((tokens, WIDTH), lambda i, c: (0, head)),
                pl.BlockSpec((tokens, PAIR), lambda i, c: (0, head)),
            ]
            + in_specs
            + [any_spec] * len(buffers),
            out_specs=out_specs,
            scratch_shapes=scratch
            + [
                pltpu.VMEM((GROUP * BLOCK, HD), jnp.bfloat16),
                pltpu.SemaphoreType.DMA((RB_DEV * PMAX + 1,)),
            ],
        ),
        compiler_params=params(),
        cost_estimate=pl.CostEstimate(
            flops=2 * 2 * tokens * WIDTH * 18 * BLOCK * 2,
            bytes_accessed=2 * tokens * WIDTH * 2 + PMAX * BLOCK * PAIR * 2 + share * WIDTH * 2,
            transcendentals=tokens * GROUP * 18 * BLOCK,
        ),
        name=f"attend_head_{head}",
    )(table, queries, resp_kv, *operands, *buffers)


def pages_shape(count):
    return jax.ShapeDtypeStruct((count * BLOCK, PAIR), jnp.bfloat16)


def pack_send(wide, cores, groups, caps, skip, ctrl, pool):
    any_spec = pl.BlockSpec(memory_space=pl.ANY)
    pages = PROMPTS * ((PMAX + wide - 1) // wide)
    rooms = (caps.near, caps.near, caps.far)
    if groups is None:
        shapes = [jax.ShapeDtypeStruct((n * BLOCK, pool.shape[1]), jnp.bfloat16) for n in rooms]
    else:
        shapes = [pages_shape(n * len(group)) for group in groups for n in rooms]
    heads = pool.shape[1] // PAIR
    out = pl.pallas_call(
        lambda *refs: send_kernel(wide, cores, groups, caps, skip, *refs),
        out_shape=shapes,
        grid_spec=pltpu.PrefetchScalarGridSpec(
            num_scalar_prefetch=1,
            grid=(1,),
            in_specs=[pl.BlockSpec(pool.shape, lambda i, c: (0, 0))],
            out_specs=[any_spec] * len(shapes),
            scratch_shapes=[pltpu.SemaphoreType.DMA((3, pages, heads))],
        ),
        compiler_params=params(),
        cost_estimate=pl.CostEstimate(
            flops=0, bytes_accessed=2 * 12 * BLOCK * PAIR * 2 * heads, transcendentals=0
        ),
        name="pack_extra" if groups is None else "pack_send",
    )(ctrl, pool)
    return [out[n : n + 3] for n in range(0, len(out), 3)]


def pack_share(cores, caps, group, table, buffers):
    any_spec = pl.BlockSpec(memory_space=pl.ANY)
    return pl.pallas_call(
        lambda *refs: share_kernel(cores, caps, group, *refs),
        out_shape=pages_shape(PMAX * len(group)),
        grid_spec=pltpu.PrefetchScalarGridSpec(
            num_scalar_prefetch=1,
            grid=(1,),
            in_specs=[any_spec] * len(buffers),
            out_specs=any_spec,
            scratch_shapes=[pltpu.SemaphoreType.DMA((len(group), PMAX))],
        ),
        compiler_params=params(),
        cost_estimate=pl.CostEstimate(
            flops=0, bytes_accessed=2 * 8 * BLOCK * PAIR * 2 * len(group), transcendentals=0
        ),
        name=f"pack_share_{group[0]}",
    )(table, *buffers)


def pack_relay(cores, caps, group, ctrl, far, left, right):
    any_spec = pl.BlockSpec(memory_space=pl.ANY)
    heads = len(group)
    return pl.pallas_call(
        lambda *refs: relay_kernel(cores, caps, heads, *refs),
        out_shape=pages_shape(2 * caps.relay * heads),
        grid_spec=pltpu.PrefetchScalarGridSpec(
            num_scalar_prefetch=1,
            grid=(1,),
            in_specs=[any_spec] * 3,
            out_specs=any_spec,
            scratch_shapes=[pltpu.SemaphoreType.DMA((heads, 2))],
        ),
        compiler_params=params(),
        cost_estimate=pl.CostEstimate(
            flops=0, bytes_accessed=4 * caps.relay * BLOCK * PAIR * 2 * heads, transcendentals=0
        ),
        name=f"pack_relay_{group[0]}",
    )(ctrl, far, left, right)


def after(value, *earlier):
    return lax.optimization_barrier((value, *earlier))[0]


def line_attend(wide, cores, caps, ctrl, table, queries, resp_kv, pool, weight):
    heads = resp_kv.shape[1] // PAIR
    share = weight.shape[1] // 2

    def hop(x, moves):
        pairs = [(a * cores + c, b * cores + c) for a, b in moves for c in range(cores)]
        return lax.ppermute(x, "wide", pairs)

    swap = [(d, d // cores * cores + (cores - 1 - d % cores)) for d in range(wide)]
    middle = heads // 2
    groups = [list(range(middle)), list(range(middle, heads))] if middle else [list(range(heads))]
    sends = pack_send(wide, cores, groups, caps, (0, 0, 0), ctrl, pool)

    def spread(right, left, far):
        return (
            hop(right, [(0, 1), (1, 2), (2, 3)]),
            hop(left, [(3, 2), (2, 1), (1, 0)]),
            hop(far, [(0, 2), (3, 1)]),
        )

    past = Caps(1, 1, 0)

    def past_the_end(ctrl, pool):
        skip = (caps.near, caps.near, caps.far)
        return spread(*pack_send(wide, cores, None, past, skip, ctrl, pool)[0])

    def nothing(ctrl, pool):
        return (jnp.zeros((past.near * BLOCK, pool.shape[1]), pool.dtype),) * 3

    extra = list(lax.cond(table[OVER_AT] == 1, past_the_end, nothing, ctrl, pool))

    def relay(n):
        left, right, far = spread(*sends[n])
        onward = pack_relay(cores, caps, groups[n], ctrl, far, left, right)
        return onward, [pool, left, right, far, hop(onward, [(2, 3), (1, 0)])]

    def exchange(n, held, plan):
        shared = pack_share(cores, caps, groups[n], plan, held + extra)
        return held + [lax.ppermute(shared, "wide", swap)] + extra

    relays = [relay(n) for n in range(len(groups))]
    parts, summed, plan = [], None, after(table, relays[-1][0])
    for n, group in enumerate(groups):
        buffers = exchange(n, relays[n][1], plan)
        for h, g in enumerate(group):
            attended, summed = attend(
                g, heads, caps, h, plan, queries, resp_kv, buffers, weight, share, summed
            )
            parts.append(attended)
        plan = after(table, attended)
    return (*parts, summed)


def project_kernel(at, *refs):
    parts, weight, out = refs[:-2], refs[-2], refs[-1]
    total = None
    for i, part in enumerate(parts):
        term = jnp.dot(
            part[...], weight[i * WIDTH : (i + 1) * WIDTH, :], preferred_element_type=jnp.float32
        )
        total = term if total is None else total + term
    out[...] = total.astype(jnp.bfloat16)


def project(parts, weight, first_column, columns):
    tokens = parts[0].shape[0]
    tile = math.gcd(columns, 512)
    at = jnp.reshape(first_column // tile, (1,)).astype(jnp.int32)
    return pl.pallas_call(
        project_kernel,
        out_shape=jax.ShapeDtypeStruct((tokens, columns), jnp.bfloat16),
        grid_spec=pltpu.PrefetchScalarGridSpec(
            num_scalar_prefetch=1,
            grid=(columns // tile,),
            in_specs=[pl.BlockSpec((tokens, WIDTH), lambda i, at: (0, 0))] * len(parts)
            + [pl.BlockSpec((weight.shape[0], tile), lambda i, at: (0, at[0] + i))],
            out_specs=pl.BlockSpec((tokens, tile), lambda i, at: (0, i)),
        ),
        compiler_params=params(),
        cost_estimate=pl.CostEstimate(
            flops=2 * tokens * columns * weight.shape[0],
            bytes_accessed=2 * columns * weight.shape[0],
            transcendentals=0,
        ),
        name="project",
    )(at, *parts, weight)


def local(
    queries, resp_kv, prefix_pool, out_weight, pre_len, prompt_blocks, prompt_owner, resp_seg
):
    wide, groups = lax.axis_size("wide"), lax.axis_size("tp") * lax.axis_size("sub")
    cores = 2 // lax.axis_size("sub")
    heads = resp_kv.shape[1] // PAIR
    me = lax.axis_index("wide").astype(jnp.int32)
    group = lax.axis_index("tp") * lax.axis_size("sub") + lax.axis_index("sub")
    where = jnp.stack([me, (1 - group).astype(jnp.int32)])
    ctrl = jnp.concatenate([pre_len, prompt_blocks, prompt_owner, resp_seg, where])
    columns = out_weight.shape[1]
    share = columns // groups
    if wide == 8 and cores == 2 and groups == 2:
        table = make_plan(wide, cores, True, ctrl)

        *parts, theirs = line_attend(
            wide, cores, CAPS, ctrl, table, queries, resp_kv, prefix_pool, out_weight
        )
        axis = "tp" if lax.axis_size("tp") == 2 else "sub"
        arrived = lax.ppermute(theirs, axis, [(0, 1), (1, 0)])
        mine = project(parts, out_weight, group * share, share)
        return (mine.astype(jnp.float32) + arrived.astype(jnp.float32)).astype(jnp.bfloat16)
    table = make_plan(wide, cores, False, ctrl)
    buffers = [lax.all_gather(prefix_pool, "wide", axis=0, tiled=True)]
    parts = [attend(g, heads, CAPS, 0, table, queries, resp_kv, buffers)[0] for g in range(heads)]
    terms = project(parts, out_weight, jnp.int32(0), columns)
    return lax.psum_scatter(terms, ("tp", "sub"), scatter_dimension=1, tiled=True)


def solution(mesh):
    return jax.shard_map(
        local,
        mesh=mesh,
        in_specs=(
            P(("parts", "wide"), ("tp", "sub")),
            P(("parts", "wide"), ("tp", "sub")),
            P(("parts", "wide"), ("tp", "sub")),
            P(("tp", "sub"), None),
            P("parts"),
            P("parts"),
            P("parts"),
            P(("parts", "wide")),
        ),
        out_specs=P(("parts", "wide"), ("tp", "sub")),
        check_vma=False,
    )
```

```python
import math

import jax
import jax.numpy as jnp
from jax import lax
from jax.experimental import pallas as pl
from jax.experimental.pallas import tpu as pltpu
from jax.sharding import PartitionSpec as P

HD = 128
BLOCK = 128
RB_DEV = 2
PROMPTS = 4
PMAX = 16
GROUP = 8
PAIR = 2 * HD
WIDTH = GROUP * HD
ROWS = 512
SPAN = 4
NEG_LARGE = -1e30
SCALE = math.log2(math.e) / math.sqrt(HD)
VMEM_BYTES = 48 * 1024 * 1024

LEN_AT, BLOCKS_AT, OWNER_AT, SEG_AT, ME_AT, OTHER_AT = 0, 4, 8, 12, 14, 15


def params():
    return pltpu.CompilerParams(vmem_limit_bytes=VMEM_BYTES)


def as_int(flag):
    return jnp.where(flag, 1, 0)


class Layout:
    def __init__(self, ctrl, wide, cores):
        self.ctrl, self.wide, self.cores = ctrl, wide, cores
        self.stride = (PMAX + wide - 1) // wide
        self.me = ctrl[ME_AT]
        self.z, self.core = self.div(self.me, cores), self.mod(self.me, cores)
        ends, total = [], 0
        for p in range(PROMPTS):
            total = total + ctrl[BLOCKS_AT + p] + (RB_DEV - 1)
            ends.append(total)
        self.ends = ends

    def mod(self, value, size):
        return value & (size - 1) if size & (size - 1) == 0 else lax.rem(value, size)

    def div(self, value, size):
        if size & (size - 1) == 0:
            return lax.shift_right_logical(value, size.bit_length() - 1)
        return lax.div(value, size)

    def prompt_of(self, block):
        return sum(as_int(block >= end) for end in self.ends[:-1])

    def first_of(self, chip):
        return self.prompt_of(chip * self.cores * RB_DEV)

    def last_of(self, chip):
        return self.prompt_of((chip + 1) * self.cores * RB_DEV - 1)

    def length(self, p):
        return self.ctrl[LEN_AT + p]

    def held_by(self, p, j):
        return self.mod(self.ctrl[OWNER_AT + p] + j, self.wide)

    def held(self, p, who):
        first = self.mod(who - self.ctrl[OWNER_AT + p] + self.wide, self.wide)
        return sum(as_int(first + k * self.wide < self.length(p)) for k in range(self.stride))

    def listed(self, which, rank, room):
        return jnp.where(
            rank < room, which * CODE + rank, (EXTRA + which - 1) * CODE + rank - room
        )

    def in_plane(self, p, j, sums):
        who = self.held_by(p, j)
        chip = self.div(who, self.cores)
        gap = chip - self.z
        k = self.div(j, self.wide)
        at = who * SUMS
        down = sums[at + PROMPTS] - sums[at + p + 1] + k
        up = sums[at + p] + k
        near_down = down - jnp.where(
            chip == 0, sums[at + PROMPTS] - sums[at + self.last_of(1) + 1], 0
        )
        near_up = up - jnp.where(chip == 3, sums[at + self.first_of(2)], 0)
        far = jnp.where(gap < 0, down, up)
        two = (gap == 2) | (gap == -2)
        direct = two & ((self.z == 1) | (self.z == 2))
        code = jnp.where(two, 5 * CODE, 4 * CODE) + far
        code = jnp.where(direct, self.listed(3, far, CAPS.far), code)
        code = jnp.where(gap == 1, self.listed(2, near_up, CAPS.near), code)
        code = jnp.where(gap == -1, self.listed(1, near_down, CAPS.near), code)
        return jnp.where(gap == 0, p * self.stride + k, code)


CODE = 256
SHARED = 6
EXTRA = 7
SUMS = 8
SLOT_AT, SHARE_AT, SHARES_AT, LENGTH_AT, BASE_AT, LOW_AT, THEIRS_AT, OVER_AT, TABLE = (
    0, 32, 50, 52, 54, 56, 58, 59, 64
)


class Caps:
    def __init__(self, near, far, relay):
        self.near, self.far, self.relay = near, far, relay


CAPS = Caps(5, 5, 4)


def needs(lay, sums, cores):
    first, last = [lay.first_of(c) for c in range(4)], [lay.last_of(c) for c in range(4)]
    near, far = jnp.int32(0), jnp.int32(0)
    for core in range(cores):

        def held(chip, low, high, core=core):
            at = (chip * cores + core) * SUMS
            return sums[at + high + 1] - sums[at + low]

        top = PROMPTS - 1
        edge = [held(1, 0, last[0]), held(2, first[3], top)]
        for amount in edge + [
            held(0, first[1], last[1]),
            held(1, first[2], top),
            held(2, 0, last[1]),
            held(3, first[2], last[2]),
        ]:
            near = jnp.maximum(near, amount)
        for amount in (held(0, first[2], top), held(3, 0, last[1])):
            far = jnp.maximum(far, amount)
    return near, far


def plan_kernel(wide, cores, line, ctrl, table, sums):
    lay = Layout(ctrl, wide, cores)
    half = PMAX // cores
    table[THEIRS_AT] = ctrl[OTHER_AT]
    table[OVER_AT] = 0
    if line:

        def tally(who, carry):
            total = jnp.int32(0)
            for p in range(PROMPTS):
                sums[who * SUMS + p] = total
                total = total + lay.held(p, who)
            sums[who * SUMS + PROMPTS] = total
            return carry

        lax.fori_loop(0, wide, tally, 0)
        near, far = needs(lay, sums, cores)
        over = (near > CAPS.near) | (far > CAPS.far)
        table[OVER_AT] = as_int(over)

    def prompts_of(device):
        return [lay.prompt_of(device * RB_DEV + b) for b in range(RB_DEV)]

    mine = prompts_of(lay.me)
    same = mine[0] == mine[1]
    joined = same & (ctrl[SEG_AT] == ctrl[SEG_AT + 1])
    for slot in range(RB_DEV):
        p = mine[slot]
        count = lay.length(p)
        table[LENGTH_AT + slot] = count
        if slot == 1:
            count = jnp.where(same, 0, count)
        table[BASE_AT + slot] = jnp.where(same, 0, PMAX) if slot else 0
        table[LOW_AT + slot] = jnp.where(joined, 0, BLOCK) if slot else 0

        def place(j, carry, slot=slot, p=p):
            who = lay.held_by(p, j)
            code = (who * PROMPTS + p) * lay.stride + lay.div(j, wide)
            if line:
                shared = slot * half + lay.div(j, cores)
                passed = jnp.where(
                    lay.mod(who, cores) == lay.core,
                    lay.in_plane(p, j, sums),
                    SHARED * CODE + shared,
                )
                code = passed
            table[SLOT_AT + slot * PMAX + j] = code
            return carry

        lax.fori_loop(0, count, place, 0)
    if not line:
        return
    theirs = prompts_of(lay.z * cores + (cores - 1 - lay.core))
    for slot in range(RB_DEV):
        p = theirs[slot]
        shift = lay.mod(lay.core - ctrl[OWNER_AT + p] + wide, cores)
        count = lay.div(lay.length(p) - shift + cores - 1, cores)
        if slot == 1:
            count = jnp.where(theirs[1] == theirs[0], 0, count)
        table[SHARES_AT + slot] = count

        def share(i, carry, slot=slot, p=p, shift=shift):
            table[SHARE_AT + slot * half + i] = lay.in_plane(p, i * cores + shift, sums)
            return carry

        lax.fori_loop(0, count, share, 0)


def make_plan(wide, cores, line, ctrl):
    return pl.pallas_call(
        lambda *refs: plan_kernel(wide, cores, line, *refs),
        out_shape=jax.ShapeDtypeStruct((TABLE,), jnp.int32),
        in_specs=[pl.BlockSpec(memory_space=pltpu.SMEM)],
        out_specs=pl.BlockSpec(memory_space=pltpu.SMEM),
        scratch_shapes=[pltpu.SMEM((wide * SUMS,), jnp.int32)],
        compiler_params=params(),
        name="plan",
    )(ctrl)


def spot(ref, page):
    return ref.at[pl.ds(pl.multiple_of(page * BLOCK, BLOCK), BLOCK), :]


def page_at(buffer, page, column):
    rows = pl.ds(pl.multiple_of(page * BLOCK, BLOCK), BLOCK)
    return buffer.at[rows, pl.ds(column if buffer.shape[1] > PAIR else 0, PAIR)]


def start_page(buffers, code, column, target, sem):
    which = lax.shift_right_logical(code, CODE.bit_length() - 1)
    page = code & (CODE - 1)
    for i, buffer, offset in buffers:

        @pl.when(which == i)
        def _(buffer=buffer, offset=offset):
            source = page_at(buffer, page + offset, column)
            pltpu.make_async_copy(source, target, sem).start()


def wait_page(target, sem):
    pltpu.make_async_copy(target, target, sem).wait()


def send_kernel(wide, cores, groups, caps, skip, ctrl, pool, *refs):
    outs, sems = refs[:-1], refs[-1]
    rooms = (caps.near, caps.near, caps.far)
    lay = Layout(ctrl, wide, cores)
    z, last = lay.z, wide // cores - 1
    held = [lay.held(p, lay.me) for p in range(PROMPTS)]

    def above(p, top):
        return sum([jnp.where(o <= top, held[o], 0) for o in range(p + 1, PROMPTS)], jnp.int32(0))

    def below(p, low):
        return sum([jnp.where(o >= low, held[o], 0) for o in range(p)], jnp.int32(0))

    near_top = jnp.where(z == 0, lay.last_of(1), PROMPTS - 1)
    near_low = jnp.where(z == last, lay.first_of(2), 0)
    first_up, last_down = lay.first_of(z + 1), lay.last_of(z - 1)
    first_two, last_one = lay.first_of(2), lay.last_of(1)
    plans = []
    for p in range(PROMPTS):
        right = (z < last) & (p >= first_up) & (p <= near_top)
        left = (z > 0) & (p >= near_low) & (p <= last_down)
        far_up = (z == 0) & (p >= first_two)
        far_down = (z == last) & (p <= last_one)
        ranks = (above(p, near_top), below(p, near_low), above(p, PROMPTS - 1), below(p, 0))
        for k in range(lay.stride):
            for lane, wanted, rank in zip((0, 1, 2, 2), (right, left, far_up, far_down), ranks):
                at = rank + k - skip[lane]
                fits = (k < held[p]) & (at >= 0) & (at < rooms[lane])
                plans.append((wanted & fits, p * lay.stride + k, lane, at))

    def copies(plan):
        _, page, lane, rank = plan
        if groups is None:
            return [
                pltpu.make_async_copy(
                    spot(pool, page), spot(outs[lane], rank), sems.at[lane, page, 0]
                )
            ]
        return [
            pltpu.make_async_copy(
                page_at(pool, page, g * PAIR),
                spot(outs[n * 3 + lane], h * rooms[lane] + rank),
                sems.at[lane, page, g],
            )
            for n, group in enumerate(groups)
            for h, g in enumerate(group)
        ]

    for plan in plans:

        @pl.when(plan[0])
        def _(plan=plan):
            for copy in copies(plan):
                copy.start()

    for plan in plans:

        @pl.when(plan[0])
        def _(plan=plan):
            for copy in copies(plan):
                copy.wait()


def relay_kernel(cores, caps, heads, ctrl, far, left, right, out, sems):
    rows = caps.relay * BLOCK

    def copy(source, room, h, section):
        target = out.at[pl.ds((2 * h + section) * rows, rows), :]
        return pltpu.make_async_copy(
            source.at[pl.ds(h * room * BLOCK, rows), :], target, sems.at[h, section]
        )

    inner = ctrl[ME_AT] == 2 * cores
    for core in range(1, cores):
        inner = inner | (ctrl[ME_AT] == 2 * cores + core)
    for h in range(heads):
        copy(far, caps.far, h, 0).start()
        pl.when(inner)(lambda h=h: copy(left, caps.near, h, 1).start())
        pl.when(jnp.logical_not(inner))(lambda h=h: copy(right, caps.near, h, 1).start())
    for h in range(heads):
        copy(far, caps.far, h, 0).wait()
        copy(left, caps.near, h, 1).wait()


def numbered(refs, caps, h):
    if len(refs) == 1:
        return [(0, refs[0], 0)]
    offsets = (0, h * caps.near, h * caps.near, h * caps.far, 2 * h * caps.relay)
    found = list(zip(range(5), refs[:5], offsets)) + [(5, refs[4], (2 * h + 1) * caps.relay)]
    if len(refs) == 9:
        found.append((SHARED, refs[5], h * PMAX))
    return found + [(EXTRA + i, ref, 0) for i, ref in enumerate(refs[-3:])]


def share_kernel(cores, caps, group, table, *refs):
    out, sems = refs[-2:]
    half = PMAX // cores
    for h, g in enumerate(group):
        buffers = numbered(refs[:-2], caps, h)
        for slot in range(RB_DEV):

            def begin(i, carry, slot=slot, h=h, g=g, buffers=buffers):
                at = slot * half + i
                target = spot(out, h * PMAX + at)
                start_page(buffers, table[SHARE_AT + at], g * PAIR, target, sems.at[h, at])
                return carry

            lax.fori_loop(0, table[SHARES_AT + slot], begin, 0)
    for h in range(len(group)):
        for slot in range(RB_DEV):

            def finish(i, carry, slot=slot, h=h):
                at = slot * half + i
                wait_page(spot(out, h * PMAX + at), sems.at[h, at])
                return carry

            lax.fori_loop(0, table[SHARES_AT + slot], finish, 0)


def attend_kernel(group, blocks, caps, carried, project, table, queries, own, *refs):
    refs = list(refs)
    weight = refs.pop(0) if project else None
    summed = refs.pop(0) if carried else None
    sems, stacked = refs.pop(), refs.pop()
    slab = refs.pop() if project else None
    store = refs.pop()
    terms = refs.pop() if project else None
    out = refs.pop()
    heads, room = len(group), len(blocks) * PMAX

    def region(i):
        if i == 0:
            return 0, table[LENGTH_AT + blocks[0]]
        base = table[BASE_AT + blocks[i]]
        return base, jnp.where(base == 0, 0, table[LENGTH_AT + blocks[i]])

    for h, g in enumerate(group):
        buffers = numbered(refs, caps, h)
        for i, b in enumerate(blocks):
            base, count = region(i)
            codes = SLOT_AT + table[BASE_AT + b]

            def begin(j, carry, h=h, g=g, buffers=buffers, base=base, codes=codes):
                at = h * room + base + j
                target, sem = spot(store, at), sems.at[at]
                start_page(buffers, table[codes + j], g * PAIR, target, sem)
                return carry

            lax.fori_loop(0, count, begin, 0)
            length = table[LENGTH_AT + b]

            def clear(j, carry, h=h, base=base):
                rows = pl.ds(pl.multiple_of((h * room + base + j) * BLOCK, BLOCK), BLOCK)
                store[rows, :] = jnp.zeros((BLOCK, PAIR), jnp.bfloat16)
                return carry

            lax.fori_loop(length, (length + SPAN - 1) & -SPAN, clear, 0)
    if project:
        share = slab.shape[1]
        theirs = pl.multiple_of(table[THEIRS_AT] * share, share)
        fetch = pltpu.make_async_copy(
            weight.at[pl.ds(group[0] * WIDTH, heads * WIDTH), pl.ds(theirs, share)],
            slab,
            sems.at[heads * room],
        )
        fetch.start()

    def one_block(h, i, b, base, count):
        tokens = pl.ds(pl.multiple_of(i * BLOCK, BLOCK), BLOCK)

        def columns(width, extra=0):
            return pl.ds(pl.multiple_of(h * width + extra, HD), min(width, HD))

        for e in range(GROUP):
            stacked[e * BLOCK : (e + 1) * BLOCK, :] = queries[tokens, columns(WIDTH, e * HD)]
        base = h * room + base

        def finish(j, carry):
            wait_page(spot(store, base + j), sems.at[base + j])
            return carry

        lax.fori_loop(0, count, finish, 0)
        length = table[LENGTH_AT + b]
        span = RB_DEV * BLOCK
        row = lax.broadcasted_iota(jnp.int32, (ROWS, span), 0) & (BLOCK - 1)
        key = lax.broadcasted_iota(jnp.int32, (ROWS, span), 1)
        own_mask = (key <= row + b * BLOCK) & (key >= table[LOW_AT + b])

        def run(spans):
            wide_key = lax.broadcasted_iota(jnp.int32, (ROWS, SPAN * BLOCK), 1)
            last_mask = wide_key < (length - (spans - 1) * SPAN) * BLOCK
            pieces = [(own[:, columns(PAIR)], own[:, columns(PAIR, HD)])]
            for t in range(spans):
                at = pl.multiple_of((base + t * SPAN) * BLOCK, BLOCK)
                piece = store[pl.ds(at, SPAN * BLOCK), :]
                pieces.append((piece[:, :HD], piece[:, HD:]))

            def score(r, t):
                scores = lax.dot_general(
                    stacked[r * ROWS : (r + 1) * ROWS, :],
                    pieces[t][0],
                    (((1,), (1,)), ((), ())),
                    preferred_element_type=jnp.float32,
                )
                if t == 0:
                    return jnp.where(own_mask, scores, NEG_LARGE)
                if t == spans:
                    return jnp.where(last_mask, scores, NEG_LARGE)
                return scores

            def highest(scores, sofar):
                for n in range(0, scores.shape[1], HD):
                    part = scores[:, n : n + HD]
                    sofar = part if sofar is None else jnp.maximum(sofar, part)
                return sofar

            def blend(scores, top, t):
                spread = jnp.concatenate([top] * (scores.shape[1] // HD), axis=1)
                weights = jnp.exp2(((scores - spread) * SCALE).astype(jnp.bfloat16))
                values = pieces[t][1]
                values = jnp.concatenate([values, jnp.ones_like(values)], axis=1)
                return jnp.dot(weights, values, preferred_element_type=jnp.float32)

            chunks, ahead, peak = GROUP * BLOCK // ROWS, [], None
            for t in range(spans + 1):
                ahead.append(score(0, t))
                peak = highest(ahead[-1], peak)
            for r in range(chunks):
                now, ahead = ahead, []
                top = jnp.broadcast_to(jnp.max(peak, axis=1, keepdims=True), (ROWS, HD))
                total, peak = None, None
                for t in range(spans + 1):
                    if r + 1 < chunks:
                        ahead.append(score(r + 1, t))
                        peak = highest(ahead[-1], peak)
                    blended = blend(now[t], top, t)
                    total = blended if total is None else total + blended
                mean = (total[:, :HD] / total[:, HD:]).astype(jnp.bfloat16)
                for e in range(ROWS // BLOCK):
                    at = columns(WIDTH, (r * (ROWS // BLOCK) + e) * HD)
                    out[tokens, at] = mean[e * BLOCK : (e + 1) * BLOCK, :]

        spans = lax.shift_right_logical(length + SPAN - 1, SPAN.bit_length() - 1)
        for n in range(1, PMAX // SPAN + 1):
            pl.when(spans == n)(lambda n=n: run(n))

    def step(n, carry):
        if len(blocks) == 1:
            one_block(n, 0, blocks[0], *region(0))
            return carry
        h, i = lax.shift_right_logical(n, 1), n & 1
        base = jnp.where(i == 0, 0, region(1)[0])
        one_block(h, i, i, base, jnp.where(i == 0, region(0)[1], region(1)[1]))
        return carry

    lax.fori_loop(0, heads * len(blocks), step, 0)
    if project:
        fetch.wait()
        attended = out[...]
        width = math.gcd(share, 512)
        for n in range(0, share, width):
            term = jnp.dot(attended, slab[:, n : n + width], preferred_element_type=jnp.float32)
            if carried:
                term = term + summed[:, n : n + width]
            terms[:, n : n + width] = term.astype(terms.dtype)


def attend(
    group, blocks, last, caps, table, queries, resp_kv, buffers, weight=None, share=0, summed=None
):
    tokens, heads = len(blocks) * BLOCK, len(group)
    at = blocks[0] // len(blocks)
    project, carried = weight is not None, summed is not None
    any_spec = pl.BlockSpec(memory_space=pl.ANY)
    whole = pl.BlockSpec((tokens, share), lambda i, c: (0, 0))
    out_shape = [jax.ShapeDtypeStruct((tokens, heads * WIDTH), jnp.bfloat16)]
    out_specs = [pl.BlockSpec((tokens, heads * WIDTH), lambda i, c: (0, 0))]
    operands, in_specs = [], []
    scratch = [pltpu.VMEM((heads * len(blocks) * PMAX * BLOCK, PAIR), jnp.bfloat16)]
    if project:
        operands, in_specs = [weight], [any_spec]
        kept = jnp.bfloat16 if last else jnp.float32
        out_shape.append(jax.ShapeDtypeStruct((tokens, share), kept))
        out_specs.append(whole)
        scratch.append(pltpu.VMEM((heads * WIDTH, share), jnp.bfloat16))
    if carried:
        operands = operands + [summed]
        in_specs = in_specs + [pl.BlockSpec((tokens, share), lambda i, c: (at, 0))]
    column = group[0] // heads
    return pl.pallas_call(
        lambda *refs: attend_kernel(group, blocks, caps, carried, project, *refs),
        out_shape=out_shape,
        grid_spec=pltpu.PrefetchScalarGridSpec(
            num_scalar_prefetch=1,
            grid=(1,),
            in_specs=[
                pl.BlockSpec((tokens, heads * WIDTH), lambda i, c: (at, column)),
                pl.BlockSpec((RB_DEV * BLOCK, heads * PAIR), lambda i, c: (0, column)),
            ]
            + in_specs
            + [any_spec] * len(buffers),
            out_specs=out_specs,
            scratch_shapes=scratch
            + [
                pltpu.VMEM((GROUP * BLOCK, HD), jnp.bfloat16),
                pltpu.SemaphoreType.DMA((heads * len(blocks) * PMAX + 1,)),
            ],
        ),
        compiler_params=params(),
        cost_estimate=pl.CostEstimate(
            flops=2 * 2 * tokens * heads * WIDTH * 18 * BLOCK * 2,
            bytes_accessed=heads * (4 * tokens * WIDTH + PMAX * BLOCK * PAIR * 2 + share * WIDTH * 2),
            transcendentals=tokens * heads * GROUP * 18 * BLOCK,
        ),
        name="attend_heads_" + "_".join(map(str, group)) + "_blocks_" + "_".join(map(str, blocks)),
    )(table, queries, resp_kv, *operands, *buffers)


def pages_shape(count):
    return jax.ShapeDtypeStruct((count * BLOCK, PAIR), jnp.bfloat16)


def pack_send(wide, cores, groups, caps, skip, ctrl, pool):
    any_spec = pl.BlockSpec(memory_space=pl.ANY)
    pages = PROMPTS * ((PMAX + wide - 1) // wide)
    rooms = (caps.near, caps.near, caps.far)
    if groups is None:
        shapes = [jax.ShapeDtypeStruct((n * BLOCK, pool.shape[1]), jnp.bfloat16) for n in rooms]
    else:
        shapes = [pages_shape(n * len(group)) for group in groups for n in rooms]
    heads = pool.shape[1] // PAIR
    out = pl.pallas_call(
        lambda *refs: send_kernel(wide, cores, groups, caps, skip, *refs),
        out_shape=shapes,
        grid_spec=pltpu.PrefetchScalarGridSpec(
            num_scalar_prefetch=1,
            grid=(1,),
            in_specs=[pl.BlockSpec(pool.shape, lambda i, c: (0, 0))],
            out_specs=[any_spec] * len(shapes),
            scratch_shapes=[pltpu.SemaphoreType.DMA((3, pages, heads))],
        ),
        compiler_params=params(),
        cost_estimate=pl.CostEstimate(
            flops=0, bytes_accessed=2 * 12 * BLOCK * PAIR * 2 * heads, transcendentals=0
        ),
        name="pack_extra" if groups is None else "pack_send",
    )(ctrl, pool)
    return [out[n : n + 3] for n in range(0, len(out), 3)]


def pack_share(cores, caps, group, table, buffers):
    any_spec = pl.BlockSpec(memory_space=pl.ANY)
    return pl.pallas_call(
        lambda *refs: share_kernel(cores, caps, group, *refs),
        out_shape=pages_shape(PMAX * len(group)),
        grid_spec=pltpu.PrefetchScalarGridSpec(
            num_scalar_prefetch=1,
            grid=(1,),
            in_specs=[any_spec] * len(buffers),
            out_specs=any_spec,
            scratch_shapes=[pltpu.SemaphoreType.DMA((len(group), PMAX))],
        ),
        compiler_params=params(),
        cost_estimate=pl.CostEstimate(
            flops=0, bytes_accessed=2 * 8 * BLOCK * PAIR * 2 * len(group), transcendentals=0
        ),
        name=f"pack_share_{group[0]}",
    )(table, *buffers)


def pack_relay(cores, caps, group, ctrl, far, left, right):
    any_spec = pl.BlockSpec(memory_space=pl.ANY)
    heads = len(group)
    return pl.pallas_call(
        lambda *refs: relay_kernel(cores, caps, heads, *refs),
        out_shape=pages_shape(2 * caps.relay * heads),
        grid_spec=pltpu.PrefetchScalarGridSpec(
            num_scalar_prefetch=1,
            grid=(1,),
            in_specs=[any_spec] * 3,
            out_specs=any_spec,
            scratch_shapes=[pltpu.SemaphoreType.DMA((heads, 2))],
        ),
        compiler_params=params(),
        cost_estimate=pl.CostEstimate(
            flops=0, bytes_accessed=4 * caps.relay * BLOCK * PAIR * 2 * heads, transcendentals=0
        ),
        name=f"pack_relay_{group[0]}",
    )(ctrl, far, left, right)


def after(value, *earlier):
    return lax.optimization_barrier((value, *earlier))[0]


def line_attend(wide, cores, caps, ctrl, table, queries, resp_kv, pool, weight):
    heads = resp_kv.shape[1] // PAIR
    share = weight.shape[1] // 2

    def hop(x, moves):
        pairs = [(a * cores + c, b * cores + c) for a, b in moves for c in range(cores)]
        return lax.ppermute(x, "wide", pairs)

    swap = [(d, d // cores * cores + (cores - 1 - d % cores)) for d in range(wide)]
    half = heads // 2
    groups = [[g] for g in range(half)] + [list(range(half, heads))]
    sends = pack_send(wide, cores, groups, caps, (0, 0, 0), ctrl, pool)

    def spread(right, left, far):
        return (
            hop(right, [(0, 1), (1, 2), (2, 3)]),
            hop(left, [(3, 2), (2, 1), (1, 0)]),
            hop(far, [(0, 2), (3, 1)]),
        )

    past = Caps(1, 1, 0)

    def past_the_end(ctrl, pool):
        skip = (caps.near, caps.near, caps.far)
        return spread(*pack_send(wide, cores, None, past, skip, ctrl, pool)[0])

    def nothing(ctrl, pool):
        return (jnp.zeros((past.near * BLOCK, pool.shape[1]), pool.dtype),) * 3

    extra = list(lax.cond(table[OVER_AT] == 1, past_the_end, nothing, ctrl, pool))

    def relay(n, plan):
        left, right, far = spread(*sends[n])
        onward = pack_relay(cores, caps, groups[n], plan, far, left, right)
        return onward, [pool, left, right, far, hop(onward, [(2, 3), (1, 0)])]

    def exchange(n, held, plan):
        shared = pack_share(cores, caps, groups[n], plan, held + extra)
        return held + [lax.ppermute(shared, "wide", swap)] + extra

    both, count = list(range(RB_DEV)), len(groups)
    parts, summed, plan = [], None, table
    relayed, onward = relay(0, ctrl)[::-1]
    for n, group in enumerate(groups[:-1]):
        later = after(ctrl, parts[-1]) if parts else ctrl
        onward, following = relay(n + 1, later)
        buffers = exchange(n, relayed, after(table, onward))
        attended, summed = attend(
            group, both, False, caps, table, queries, resp_kv, buffers, weight, share, summed
        )
        parts.append(attended)
        relayed = following
    buffers = exchange(count - 1, relayed, after(table, parts[-1]) if parts else table)
    ends, theirs, plan = [], [], table
    for b in both:
        attended, terms = attend(
            groups[-1], [b], True, caps, plan, queries, resp_kv, buffers, weight, share, summed
        )
        ends.append(attended)
        theirs.append(terms)
        plan = after(table, attended)
    return parts + [jnp.concatenate(ends, axis=0)], theirs


def project_kernel(at, *refs):
    parts, weight, out = refs[:-2], refs[-2], refs[-1]
    total, row = None, 0
    for part in parts:
        end = row + part.shape[1]
        term = jnp.dot(part[...], weight[row:end, :], preferred_element_type=jnp.float32)
        total, row = term if total is None else total + term, end
    out[...] = total.astype(jnp.bfloat16)


def project(parts, weight, first_column, columns):
    tokens = parts[0].shape[0]
    tile = math.gcd(columns, 512)
    at = jnp.reshape(first_column // tile, (1,)).astype(jnp.int32)
    return pl.pallas_call(
        project_kernel,
        out_shape=jax.ShapeDtypeStruct((tokens, columns), jnp.bfloat16),
        grid_spec=pltpu.PrefetchScalarGridSpec(
            num_scalar_prefetch=1,
            grid=(columns // tile,),
            in_specs=[pl.BlockSpec(part.shape, lambda i, at: (0, 0)) for part in parts]
            + [pl.BlockSpec((weight.shape[0], tile), lambda i, at: (0, at[0] + i))],
            out_specs=pl.BlockSpec((tokens, tile), lambda i, at: (0, i)),
        ),
        compiler_params=params(),
        cost_estimate=pl.CostEstimate(
            flops=2 * tokens * columns * weight.shape[0],
            bytes_accessed=2 * columns * weight.shape[0],
            transcendentals=0,
        ),
        name="project",
    )(at, *parts, weight)


def local(
    queries, resp_kv, prefix_pool, out_weight, pre_len, prompt_blocks, prompt_owner, resp_seg
):
    wide, groups = lax.axis_size("wide"), lax.axis_size("tp") * lax.axis_size("sub")
    cores = 2 // lax.axis_size("sub")
    heads = resp_kv.shape[1] // PAIR
    me = lax.axis_index("wide").astype(jnp.int32)
    group = lax.axis_index("tp") * lax.axis_size("sub") + lax.axis_index("sub")
    where = jnp.stack([me, (1 - group).astype(jnp.int32)])
    ctrl = jnp.concatenate([pre_len, prompt_blocks, prompt_owner, resp_seg, where])
    columns = out_weight.shape[1]
    share = columns // groups
    if wide == 8 and cores == 2 and groups == 2:
        table = make_plan(wide, cores, True, ctrl)

        parts, theirs = line_attend(
            wide, cores, CAPS, ctrl, table, queries, resp_kv, prefix_pool, out_weight
        )
        axis = "tp" if lax.axis_size("tp") == 2 else "sub"
        arrived = [lax.ppermute(terms, axis, [(0, 1), (1, 0)]) for terms in theirs]
        mine = project(parts, out_weight, after(group, arrived[0]) * share, share)
        arrived = jnp.concatenate(arrived, axis=0)
        return (mine.astype(jnp.float32) + arrived.astype(jnp.float32)).astype(jnp.bfloat16)
    table = make_plan(wide, cores, False, ctrl)
    buffers = [lax.all_gather(prefix_pool, "wide", axis=0, tiled=True)]
    blocks = list(range(RB_DEV))
    parts = [
        attend([g], blocks, False, CAPS, table, queries, resp_kv, buffers)[0] for g in range(heads)
    ]
    terms = project(parts, out_weight, jnp.int32(0), columns)
    return lax.psum_scatter(terms, ("tp", "sub"), scatter_dimension=1, tiled=True)


def solution(mesh):
    return jax.shard_map(
        local,
        mesh=mesh,
        in_specs=(
            P(("parts", "wide"), ("tp", "sub")),
            P(("parts", "wide"), ("tp", "sub")),
            P(("parts", "wide"), ("tp", "sub")),
            P(("tp", "sub"), None),
            P("parts"),
            P("parts"),
            P("parts"),
            P(("parts", "wide")),
        ),
        out_specs=P(("parts", "wide"), ("tp", "sub")),
        check_vma=False,
    )
```

```python
import math

import jax
import jax.numpy as jnp
from jax import lax
from jax.experimental import pallas as pl
from jax.experimental.pallas import tpu as pltpu
from jax.sharding import PartitionSpec as P

HD = 128
BLOCK = 128
RB_DEV = 2
PROMPTS = 4
PMAX = 16
GROUP = 8
PAIR = 2 * HD
WIDTH = GROUP * HD
ROWS = 512
SPAN = 4
NEG_LARGE = -1e30
SCALE = math.log2(math.e) / math.sqrt(HD)
VMEM_BYTES = 48 * 1024 * 1024

LEN_AT, BLOCKS_AT, OWNER_AT, SEG_AT, ME_AT, OTHER_AT = 0, 4, 8, 12, 14, 15


def params():
    return pltpu.CompilerParams(vmem_limit_bytes=VMEM_BYTES)


def as_int(flag):
    return jnp.where(flag, 1, 0)


class Layout:
    def __init__(self, ctrl, wide, cores):
        self.ctrl, self.wide, self.cores = ctrl, wide, cores
        self.stride = (PMAX + wide - 1) // wide
        self.me = ctrl[ME_AT]
        self.z, self.core = self.div(self.me, cores), self.mod(self.me, cores)
        ends, total = [], 0
        for p in range(PROMPTS):
            total = total + ctrl[BLOCKS_AT + p] + (RB_DEV - 1)
            ends.append(total)
        self.ends = ends

    def mod(self, value, size):
        return value & (size - 1) if size & (size - 1) == 0 else lax.rem(value, size)

    def div(self, value, size):
        if size & (size - 1) == 0:
            return lax.shift_right_logical(value, size.bit_length() - 1)
        return lax.div(value, size)

    def prompt_of(self, block):
        return sum(as_int(block >= end) for end in self.ends[:-1])

    def first_of(self, chip):
        return self.prompt_of(chip * self.cores * RB_DEV)

    def last_of(self, chip):
        return self.prompt_of((chip + 1) * self.cores * RB_DEV - 1)

    def length(self, p):
        return self.ctrl[LEN_AT + p]

    def held_by(self, p, j):
        return self.mod(self.ctrl[OWNER_AT + p] + j, self.wide)

    def held(self, p, who):
        first = self.mod(who - self.ctrl[OWNER_AT + p] + self.wide, self.wide)
        return sum(as_int(first + k * self.wide < self.length(p)) for k in range(self.stride))

    def listed(self, which, rank, room):
        return jnp.where(
            rank < room, which * CODE + rank, (EXTRA + which - 1) * CODE + rank - room
        )

    def in_plane(self, p, j, sums):
        who = self.held_by(p, j)
        chip = self.div(who, self.cores)
        gap = chip - self.z
        k = self.div(j, self.wide)
        at = who * SUMS
        down = sums[at + PROMPTS] - sums[at + p + 1] + k
        up = sums[at + p] + k
        near_down = down - jnp.where(
            chip == 0, sums[at + PROMPTS] - sums[at + self.last_of(1) + 1], 0
        )
        near_up = up - jnp.where(chip == 3, sums[at + self.first_of(2)], 0)
        far = jnp.where(gap < 0, down, up)
        two = (gap == 2) | (gap == -2)
        direct = two & ((self.z == 1) | (self.z == 2))
        code = jnp.where(two, 5 * CODE, 4 * CODE) + far
        code = jnp.where(direct, self.listed(3, far, CAPS.far), code)
        code = jnp.where(gap == 1, self.listed(2, near_up, CAPS.near), code)
        code = jnp.where(gap == -1, self.listed(1, near_down, CAPS.near), code)
        return jnp.where(gap == 0, p * self.stride + k, code)


CODE = 256
SHARED = 6
EXTRA = 7
SUMS = 8
SLOT_AT, SHARE_AT, SHARES_AT, LENGTH_AT, BASE_AT, LOW_AT, THEIRS_AT, OVER_AT, TABLE = (
    0, 32, 50, 52, 54, 56, 58, 59, 64
)


class Caps:
    def __init__(self, near, far, relay):
        self.near, self.far, self.relay = near, far, relay


CAPS = Caps(5, 5, 4)


def needs(lay, sums, cores):
    first, last = [lay.first_of(c) for c in range(4)], [lay.last_of(c) for c in range(4)]
    near, far = jnp.int32(0), jnp.int32(0)
    for core in range(cores):

        def held(chip, low, high, core=core):
            at = (chip * cores + core) * SUMS
            return sums[at + high + 1] - sums[at + low]

        top = PROMPTS - 1
        edge = [held(1, 0, last[0]), held(2, first[3], top)]
        for amount in edge + [
            held(0, first[1], last[1]),
            held(1, first[2], top),
            held(2, 0, last[1]),
            held(3, first[2], last[2]),
        ]:
            near = jnp.maximum(near, amount)
        for amount in (held(0, first[2], top), held(3, 0, last[1])):
            far = jnp.maximum(far, amount)
    return near, far


def plan_kernel(wide, cores, line, ctrl, table, sums):
    lay = Layout(ctrl, wide, cores)
    half = PMAX // cores
    table[THEIRS_AT] = ctrl[OTHER_AT]
    table[OVER_AT] = 0
    if line:

        def tally(who, carry):
            total = jnp.int32(0)
            for p in range(PROMPTS):
                sums[who * SUMS + p] = total
                total = total + lay.held(p, who)
            sums[who * SUMS + PROMPTS] = total
            return carry

        lax.fori_loop(0, wide, tally, 0)
        near, far = needs(lay, sums, cores)
        over = (near > CAPS.near) | (far > CAPS.far)
        table[OVER_AT] = as_int(over)

    def prompts_of(device):
        return [lay.prompt_of(device * RB_DEV + b) for b in range(RB_DEV)]

    mine = prompts_of(lay.me)
    same = mine[0] == mine[1]
    joined = same & (ctrl[SEG_AT] == ctrl[SEG_AT + 1])
    for slot in range(RB_DEV):
        p = mine[slot]
        count = lay.length(p)
        table[LENGTH_AT + slot] = count
        if slot == 1:
            count = jnp.where(same, 0, count)
        table[BASE_AT + slot] = jnp.where(same, 0, PMAX) if slot else 0
        table[LOW_AT + slot] = jnp.where(joined, 0, BLOCK) if slot else 0

        def place(j, carry, slot=slot, p=p):
            who = lay.held_by(p, j)
            code = (who * PROMPTS + p) * lay.stride + lay.div(j, wide)
            if line:
                shared = slot * half + lay.div(j, cores)
                passed = jnp.where(
                    lay.mod(who, cores) == lay.core,
                    lay.in_plane(p, j, sums),
                    SHARED * CODE + shared,
                )
                code = passed
            table[SLOT_AT + slot * PMAX + j] = code
            return carry

        lax.fori_loop(0, count, place, 0)
    if not line:
        return
    theirs = prompts_of(lay.z * cores + (cores - 1 - lay.core))
    for slot in range(RB_DEV):
        p = theirs[slot]
        shift = lay.mod(lay.core - ctrl[OWNER_AT + p] + wide, cores)
        count = lay.div(lay.length(p) - shift + cores - 1, cores)
        if slot == 1:
            count = jnp.where(theirs[1] == theirs[0], 0, count)
        table[SHARES_AT + slot] = count

        def share(i, carry, slot=slot, p=p, shift=shift):
            table[SHARE_AT + slot * half + i] = lay.in_plane(p, i * cores + shift, sums)
            return carry

        lax.fori_loop(0, count, share, 0)


def make_plan(wide, cores, line, ctrl):
    return pl.pallas_call(
        lambda *refs: plan_kernel(wide, cores, line, *refs),
        out_shape=jax.ShapeDtypeStruct((TABLE,), jnp.int32),
        in_specs=[pl.BlockSpec(memory_space=pltpu.SMEM)],
        out_specs=pl.BlockSpec(memory_space=pltpu.SMEM),
        scratch_shapes=[pltpu.SMEM((wide * SUMS,), jnp.int32)],
        compiler_params=params(),
        name="plan",
    )(ctrl)


def spot(ref, page):
    return ref.at[pl.ds(pl.multiple_of(page * BLOCK, BLOCK), BLOCK), :]


def page_at(buffer, page, column):
    rows = pl.ds(pl.multiple_of(page * BLOCK, BLOCK), BLOCK)
    return buffer.at[rows, pl.ds(column if buffer.shape[1] > PAIR else 0, PAIR)]


def start_page(buffers, code, column, target, sem):
    which = lax.shift_right_logical(code, CODE.bit_length() - 1)
    page = code & (CODE - 1)
    for i, buffer, offset in buffers:

        @pl.when(which == i)
        def _(buffer=buffer, offset=offset):
            source = page_at(buffer, page + offset, column)
            pltpu.make_async_copy(source, target, sem).start()


def wait_page(target, sem):
    pltpu.make_async_copy(target, target, sem).wait()


def send_kernel(wide, cores, groups, caps, skip, ctrl, pool, *refs):
    outs, sems = refs[:-1], refs[-1]
    rooms = (caps.near, caps.near, caps.far)
    lay = Layout(ctrl, wide, cores)
    z, last = lay.z, wide // cores - 1
    held = [lay.held(p, lay.me) for p in range(PROMPTS)]

    def above(p, top):
        return sum([jnp.where(o <= top, held[o], 0) for o in range(p + 1, PROMPTS)], jnp.int32(0))

    def below(p, low):
        return sum([jnp.where(o >= low, held[o], 0) for o in range(p)], jnp.int32(0))

    near_top = jnp.where(z == 0, lay.last_of(1), PROMPTS - 1)
    near_low = jnp.where(z == last, lay.first_of(2), 0)
    first_up, last_down = lay.first_of(z + 1), lay.last_of(z - 1)
    first_two, last_one = lay.first_of(2), lay.last_of(1)
    plans = []
    for p in range(PROMPTS):
        right = (z < last) & (p >= first_up) & (p <= near_top)
        left = (z > 0) & (p >= near_low) & (p <= last_down)
        far_up = (z == 0) & (p >= first_two)
        far_down = (z == last) & (p <= last_one)
        ranks = (above(p, near_top), below(p, near_low), above(p, PROMPTS - 1), below(p, 0))
        for k in range(lay.stride):
            for lane, wanted, rank in zip((0, 1, 2, 2), (right, left, far_up, far_down), ranks):
                at = rank + k - skip[lane]
                fits = (k < held[p]) & (at >= 0) & (at < rooms[lane])
                plans.append((wanted & fits, p * lay.stride + k, lane, at))

    def copies(plan):
        _, page, lane, rank = plan
        if groups is None:
            return [
                pltpu.make_async_copy(
                    spot(pool, page), spot(outs[lane], rank), sems.at[lane, page, 0]
                )
            ]
        return [
            pltpu.make_async_copy(
                page_at(pool, page, g * PAIR),
                spot(outs[n * 3 + lane], h * rooms[lane] + rank),
                sems.at[lane, page, g],
            )
            for n, group in enumerate(groups)
            for h, g in enumerate(group)
        ]

    for plan in plans:

        @pl.when(plan[0])
        def _(plan=plan):
            for copy in copies(plan):
                copy.start()

    for plan in plans:

        @pl.when(plan[0])
        def _(plan=plan):
            for copy in copies(plan):
                copy.wait()


def relay_kernel(cores, caps, h, ctrl, far, left, right, out, sems):
    rows = caps.relay * BLOCK

    def copy(source, room, section):
        target = out.at[pl.ds(section * rows, rows), :]
        return pltpu.make_async_copy(
            source.at[pl.ds(h * room * BLOCK, rows), :], target, sems.at[section]
        )

    inner = ctrl[ME_AT] == 2 * cores
    for core in range(1, cores):
        inner = inner | (ctrl[ME_AT] == 2 * cores + core)
    copy(far, caps.far, 0).start()
    pl.when(inner)(lambda: copy(left, caps.near, 1).start())
    pl.when(jnp.logical_not(inner))(lambda: copy(right, caps.near, 1).start())
    copy(far, caps.far, 0).wait()
    copy(left, caps.near, 1).wait()


def numbered(refs, caps, h):
    if len(refs) == 1:
        return [(0, refs[0], 0)]
    offsets = (0, h * caps.near, h * caps.near, h * caps.far, 0)
    found = list(zip(range(5), refs[:5], offsets)) + [(5, refs[4], caps.relay)]
    if len(refs) == 9:
        found.append((SHARED, refs[5], 0))
    return found + [(EXTRA + i, ref, 0) for i, ref in enumerate(refs[-3:])]


def share_kernel(cores, caps, h, g, table, *refs):
    out, sems = refs[-2:]
    half = PMAX // cores
    buffers = numbered(refs[:-2], caps, h)
    for slot in range(RB_DEV):

        def begin(i, carry, slot=slot):
            at = slot * half + i
            start_page(buffers, table[SHARE_AT + at], g * PAIR, spot(out, at), sems.at[at])
            return carry

        lax.fori_loop(0, table[SHARES_AT + slot], begin, 0)
    for slot in range(RB_DEV):

        def finish(i, carry, slot=slot):
            at = slot * half + i
            wait_page(spot(out, at), sems.at[at])
            return carry

        lax.fori_loop(0, table[SHARES_AT + slot], finish, 0)


def attend_kernel(group, first, blocks, caps, carried, project, table, queries, own, *refs):
    refs = list(refs)
    weight = refs.pop(0) if project else None
    summed = refs.pop(0) if carried else None
    sems, stacked = refs.pop(), refs.pop()
    slab = refs.pop() if project else None
    store = refs.pop()
    terms = refs.pop() if project else None
    out = refs.pop()
    heads, room = len(group), len(blocks) * PMAX

    def region(i):
        if i == 0:
            return 0, table[LENGTH_AT + blocks[0]]
        base = table[BASE_AT + blocks[i]]
        return base, jnp.where(base == 0, 0, table[LENGTH_AT + blocks[i]])

    for h, g in enumerate(group):
        buffers = numbered(refs, caps, first + h)
        for i, b in enumerate(blocks):
            base, count = region(i)
            codes = SLOT_AT + table[BASE_AT + b]

            def begin(j, carry, h=h, g=g, buffers=buffers, base=base, codes=codes):
                at = h * room + base + j
                target, sem = spot(store, at), sems.at[at]
                start_page(buffers, table[codes + j], g * PAIR, target, sem)
                return carry

            lax.fori_loop(0, count, begin, 0)
            length = table[LENGTH_AT + b]

            def clear(j, carry, h=h, base=base):
                rows = pl.ds(pl.multiple_of((h * room + base + j) * BLOCK, BLOCK), BLOCK)
                store[rows, :] = jnp.zeros((BLOCK, PAIR), jnp.bfloat16)
                return carry

            lax.fori_loop(length, (length + SPAN - 1) & -SPAN, clear, 0)
    if project:
        share = slab.shape[1]
        theirs = pl.multiple_of(table[THEIRS_AT] * share, share)
        fetch = pltpu.make_async_copy(
            weight.at[pl.ds(group[0] * WIDTH, heads * WIDTH), pl.ds(theirs, share)],
            slab,
            sems.at[heads * room],
        )
        fetch.start()

    def one_block(h, i, b, base, count):
        tokens = pl.ds(pl.multiple_of(i * BLOCK, BLOCK), BLOCK)

        def columns(width, extra=0):
            return pl.ds(pl.multiple_of(h * width + extra, HD), min(width, HD))

        for e in range(GROUP):
            stacked[e * BLOCK : (e + 1) * BLOCK, :] = queries[tokens, columns(WIDTH, e * HD)]
        base = h * room + base

        def finish(j, carry):
            wait_page(spot(store, base + j), sems.at[base + j])
            return carry

        lax.fori_loop(0, count, finish, 0)
        length = table[LENGTH_AT + b]
        span = RB_DEV * BLOCK
        row = lax.broadcasted_iota(jnp.int32, (ROWS, span), 0) & (BLOCK - 1)
        key = lax.broadcasted_iota(jnp.int32, (ROWS, span), 1)
        own_mask = (key <= row + b * BLOCK) & (key >= table[LOW_AT + b])

        def run(spans):
            wide_key = lax.broadcasted_iota(jnp.int32, (ROWS, SPAN * BLOCK), 1)
            last_mask = wide_key < (length - (spans - 1) * SPAN) * BLOCK
            pieces = [(own[:, columns(PAIR)], own[:, columns(PAIR, HD)])]
            for t in range(spans):
                at = pl.multiple_of((base + t * SPAN) * BLOCK, BLOCK)
                piece = store[pl.ds(at, SPAN * BLOCK), :]
                pieces.append((piece[:, :HD], piece[:, HD:]))

            def score(r, t):
                scores = lax.dot_general(
                    stacked[r * ROWS : (r + 1) * ROWS, :],
                    pieces[t][0],
                    (((1,), (1,)), ((), ())),
                    preferred_element_type=jnp.float32,
                )
                if t == 0:
                    return jnp.where(own_mask, scores, NEG_LARGE)
                if t == spans:
                    return jnp.where(last_mask, scores, NEG_LARGE)
                return scores

            def highest(scores, sofar):
                for n in range(0, scores.shape[1], HD):
                    part = scores[:, n : n + HD]
                    sofar = part if sofar is None else jnp.maximum(sofar, part)
                return sofar

            def blend(scores, top, t):
                spread = jnp.concatenate([top] * (scores.shape[1] // HD), axis=1)
                weights = jnp.exp2((scores - spread) * SCALE).astype(jnp.bfloat16)
                values = pieces[t][1]
                values = jnp.concatenate([values, jnp.ones_like(values)], axis=1)
                return jnp.dot(weights, values, preferred_element_type=jnp.float32)

            chunks, ahead, peak = GROUP * BLOCK // ROWS, [], None
            for t in range(spans + 1):
                ahead.append(score(0, t))
                peak = highest(ahead[-1], peak)
            for r in range(chunks):
                now, ahead = ahead, []
                top = jnp.broadcast_to(jnp.max(peak, axis=1, keepdims=True), (ROWS, HD))
                total, peak = None, None
                for t in range(spans + 1):
                    if r + 1 < chunks:
                        ahead.append(score(r + 1, t))
                        peak = highest(ahead[-1], peak)
                    blended = blend(now[t], top, t)
                    total = blended if total is None else total + blended
                mean = (total[:, :HD] / total[:, HD:]).astype(jnp.bfloat16)
                for e in range(ROWS // BLOCK):
                    at = columns(WIDTH, (r * (ROWS // BLOCK) + e) * HD)
                    out[tokens, at] = mean[e * BLOCK : (e + 1) * BLOCK, :]

        spans = lax.shift_right_logical(length + SPAN - 1, SPAN.bit_length() - 1)
        for n in range(1, PMAX // SPAN + 1):
            pl.when(spans == n)(lambda n=n: run(n))

    def step(n, carry):
        if len(blocks) == 1:
            one_block(n, 0, blocks[0], *region(0))
            return carry
        h, i = lax.shift_right_logical(n, 1), n & 1
        base = jnp.where(i == 0, 0, region(1)[0])
        one_block(h, i, i, base, jnp.where(i == 0, region(0)[1], region(1)[1]))
        return carry

    lax.fori_loop(0, heads * len(blocks), step, 0)
    if project:
        fetch.wait()
        attended = out[...]
        width = math.gcd(share, 512)
        for n in range(0, share, width):
            term = jnp.dot(attended, slab[:, n : n + width], preferred_element_type=jnp.float32)
            if carried:
                term = term + summed[:, n : n + width]
            terms[:, n : n + width] = term.astype(terms.dtype)


def attend(
    group, first, blocks, last, caps, table, queries, resp_kv, buffers, weight=None, share=0, summed=None
):
    tokens, heads = len(blocks) * BLOCK, len(group)
    at = blocks[0] // len(blocks)
    project, carried = weight is not None, summed is not None
    any_spec = pl.BlockSpec(memory_space=pl.ANY)
    whole = pl.BlockSpec((tokens, share), lambda i, c: (0, 0))
    out_shape = [jax.ShapeDtypeStruct((tokens, heads * WIDTH), jnp.bfloat16)]
    out_specs = [pl.BlockSpec((tokens, heads * WIDTH), lambda i, c: (0, 0))]
    operands, in_specs = [], []
    scratch = [pltpu.VMEM((heads * len(blocks) * PMAX * BLOCK, PAIR), jnp.bfloat16)]
    if project:
        operands, in_specs = [weight], [any_spec]
        kept = jnp.bfloat16 if last else jnp.float32
        out_shape.append(jax.ShapeDtypeStruct((tokens, share), kept))
        out_specs.append(whole)
        scratch.append(pltpu.VMEM((heads * WIDTH, share), jnp.bfloat16))
    if carried:
        operands = operands + [summed]
        in_specs = in_specs + [pl.BlockSpec((tokens, share), lambda i, c: (at, 0))]
    column = group[0] // heads
    return pl.pallas_call(
        lambda *refs: attend_kernel(group, first, blocks, caps, carried, project, *refs),
        out_shape=out_shape,
        grid_spec=pltpu.PrefetchScalarGridSpec(
            num_scalar_prefetch=1,
            grid=(1,),
            in_specs=[
                pl.BlockSpec((tokens, heads * WIDTH), lambda i, c: (at, column)),
                pl.BlockSpec((RB_DEV * BLOCK, heads * PAIR), lambda i, c: (0, column)),
            ]
            + in_specs
            + [any_spec] * len(buffers),
            out_specs=out_specs,
            scratch_shapes=scratch
            + [
                pltpu.VMEM((GROUP * BLOCK, HD), jnp.bfloat16),
                pltpu.SemaphoreType.DMA((heads * len(blocks) * PMAX + 1,)),
            ],
        ),
        compiler_params=params(),
        cost_estimate=pl.CostEstimate(
            flops=2 * 2 * tokens * heads * WIDTH * 18 * BLOCK * 2,
            bytes_accessed=heads * (4 * tokens * WIDTH + PMAX * BLOCK * PAIR * 2 + share * WIDTH * 2),
            transcendentals=tokens * heads * GROUP * 18 * BLOCK,
        ),
        name="attend_heads_" + "_".join(map(str, group)) + "_blocks_" + "_".join(map(str, blocks)),
    )(table, queries, resp_kv, *operands, *buffers)


def pages_shape(count):
    return jax.ShapeDtypeStruct((count * BLOCK, PAIR), jnp.bfloat16)


def pack_send(wide, cores, groups, caps, skip, ctrl, pool):
    any_spec = pl.BlockSpec(memory_space=pl.ANY)
    pages = PROMPTS * ((PMAX + wide - 1) // wide)
    rooms = (caps.near, caps.near, caps.far)
    if groups is None:
        shapes = [jax.ShapeDtypeStruct((n * BLOCK, pool.shape[1]), jnp.bfloat16) for n in rooms]
    else:
        shapes = [pages_shape(n * len(group)) for group in groups for n in rooms]
    heads = pool.shape[1] // PAIR
    out = pl.pallas_call(
        lambda *refs: send_kernel(wide, cores, groups, caps, skip, *refs),
        out_shape=shapes,
        grid_spec=pltpu.PrefetchScalarGridSpec(
            num_scalar_prefetch=1,
            grid=(1,),
            in_specs=[pl.BlockSpec(pool.shape, lambda i, c: (0, 0))],
            out_specs=[any_spec] * len(shapes),
            scratch_shapes=[pltpu.SemaphoreType.DMA((3, pages, heads))],
        ),
        compiler_params=params(),
        cost_estimate=pl.CostEstimate(
            flops=0, bytes_accessed=2 * 12 * BLOCK * PAIR * 2 * heads, transcendentals=0
        ),
        name="pack_extra" if groups is None else "pack_send",
    )(ctrl, pool)
    return [out[n : n + 3] for n in range(0, len(out), 3)]


def pack_share(cores, caps, h, g, table, buffers):
    any_spec = pl.BlockSpec(memory_space=pl.ANY)
    return pl.pallas_call(
        lambda *refs: share_kernel(cores, caps, h, g, *refs),
        out_shape=pages_shape(PMAX),
        grid_spec=pltpu.PrefetchScalarGridSpec(
            num_scalar_prefetch=1,
            grid=(1,),
            in_specs=[any_spec] * len(buffers),
            out_specs=any_spec,
            scratch_shapes=[pltpu.SemaphoreType.DMA((PMAX,))],
        ),
        compiler_params=params(),
        cost_estimate=pl.CostEstimate(
            flops=0, bytes_accessed=2 * 8 * BLOCK * PAIR * 2, transcendentals=0
        ),
        name=f"pack_share_{g}",
    )(table, *buffers)


def pack_relay(cores, caps, h, g, ctrl, far, left, right):
    any_spec = pl.BlockSpec(memory_space=pl.ANY)
    return pl.pallas_call(
        lambda *refs: relay_kernel(cores, caps, h, *refs),
        out_shape=pages_shape(2 * caps.relay),
        grid_spec=pltpu.PrefetchScalarGridSpec(
            num_scalar_prefetch=1,
            grid=(1,),
            in_specs=[any_spec] * 3,
            out_specs=any_spec,
            scratch_shapes=[pltpu.SemaphoreType.DMA((2,))],
        ),
        compiler_params=params(),
        cost_estimate=pl.CostEstimate(
            flops=0, bytes_accessed=4 * caps.relay * BLOCK * PAIR * 2, transcendentals=0
        ),
        name=f"pack_relay_{g}",
    )(ctrl, far, left, right)


def after(value, *earlier):
    return lax.optimization_barrier((value, *earlier))[0]


def line_attend(wide, cores, caps, ctrl, table, queries, resp_kv, pool, weight):
    heads = resp_kv.shape[1] // PAIR
    share = weight.shape[1] // 2

    def hop(x, moves):
        pairs = [(a * cores + c, b * cores + c) for a, b in moves for c in range(cores)]
        return lax.ppermute(x, "wide", pairs)

    swap = [(d, d // cores * cores + (cores - 1 - d % cores)) for d in range(wide)]
    half = heads // 2
    groups = [[g] for g in range(half)] + [list(range(half, heads))]
    sends = pack_send(wide, cores, groups, caps, (0, 0, 0), ctrl, pool)

    def spread(right, left, far):
        return (
            hop(right, [(0, 1), (1, 2), (2, 3)]),
            hop(left, [(3, 2), (2, 1), (1, 0)]),
            hop(far, [(0, 2), (3, 1)]),
        )

    past = Caps(1, 1, 0)

    def past_the_end(ctrl, pool):
        skip = (caps.near, caps.near, caps.far)
        return spread(*pack_send(wide, cores, None, past, skip, ctrl, pool)[0])

    def nothing(ctrl, pool):
        return (jnp.zeros((past.near * BLOCK, pool.shape[1]), pool.dtype),) * 3

    extra = list(lax.cond(table[OVER_AT] == 1, past_the_end, nothing, ctrl, pool))

    def exchange(h, g, held, plan):
        shared = pack_share(cores, caps, h, g, plan, held + extra)
        return held + [lax.ppermute(shared, "wide", swap)] + extra

    both = list(range(RB_DEV))
    units = [(n, h, g) for n, group in enumerate(groups) for h, g in enumerate(group)]
    spreads, parts, summed, held = {}, [], None, {}

    def relay(u, plan):
        n, h, g = units[u]
        if n not in spreads:
            spreads[n] = spread(*sends[n])
        left, right, far = spreads[n]
        onward = pack_relay(cores, caps, h, g, plan, far, left, right)
        held[u] = [pool, left, right, far, hop(onward, [(2, 3), (1, 0)])]
        return onward

    relay(0, after(ctrl, extra[0]))
    for u, (n, h, g) in enumerate(units[:-1]):
        onward = relay(u + 1, after(ctrl, parts[-1]) if parts else ctrl)
        buffers = exchange(h, g, held[u], after(table, onward))
        attended, summed = attend(
            [g], h, both, False, caps, table, queries, resp_kv, buffers, weight, share, summed
        )
        parts.append(attended)
    _, h, g = units[-1]
    plan = after(table, parts[-1]) if parts else table
    buffers = exchange(h, g, held[len(units) - 1], plan)
    ends, theirs, plan = [], [], table
    for b in both:
        attended, terms = attend(
            [g], h, [b], True, caps, plan, queries, resp_kv, buffers, weight, share, summed
        )
        ends.append(attended)
        theirs.append(terms)
        plan = after(table, attended)
    return parts + [jnp.concatenate(ends, axis=0)], theirs


def project_kernel(at, *refs):
    parts, weight, out = refs[:-2], refs[-2], refs[-1]
    total, row = None, 0
    for part in parts:
        end = row + part.shape[1]
        term = jnp.dot(part[...], weight[row:end, :], preferred_element_type=jnp.float32)
        total, row = term if total is None else total + term, end
    out[...] = total.astype(jnp.bfloat16)


def project(parts, weight, first_column, columns):
    tokens = parts[0].shape[0]
    tile = math.gcd(columns, 512)
    at = jnp.reshape(first_column // tile, (1,)).astype(jnp.int32)
    return pl.pallas_call(
        project_kernel,
        out_shape=jax.ShapeDtypeStruct((tokens, columns), jnp.bfloat16),
        grid_spec=pltpu.PrefetchScalarGridSpec(
            num_scalar_prefetch=1,
            grid=(columns // tile,),
            in_specs=[pl.BlockSpec(part.shape, lambda i, at: (0, 0)) for part in parts]
            + [pl.BlockSpec((weight.shape[0], tile), lambda i, at: (0, at[0] + i))],
            out_specs=pl.BlockSpec((tokens, tile), lambda i, at: (0, i)),
        ),
        compiler_params=params(),
        cost_estimate=pl.CostEstimate(
            flops=2 * tokens * columns * weight.shape[0],
            bytes_accessed=2 * columns * weight.shape[0],
            transcendentals=0,
        ),
        name="project",
    )(at, *parts, weight)


def local(
    queries, resp_kv, prefix_pool, out_weight, pre_len, prompt_blocks, prompt_owner, resp_seg
):
    wide, groups = lax.axis_size("wide"), lax.axis_size("tp") * lax.axis_size("sub")
    cores = 2 // lax.axis_size("sub")
    heads = resp_kv.shape[1] // PAIR
    me = lax.axis_index("wide").astype(jnp.int32)
    group = lax.axis_index("tp") * lax.axis_size("sub") + lax.axis_index("sub")
    where = jnp.stack([me, (1 - group).astype(jnp.int32)])
    ctrl = jnp.concatenate([pre_len, prompt_blocks, prompt_owner, resp_seg, where])
    columns = out_weight.shape[1]
    share = columns // groups
    if wide == 8 and cores == 2 and groups == 2:
        table = make_plan(wide, cores, True, ctrl)

        parts, theirs = line_attend(
            wide, cores, CAPS, ctrl, table, queries, resp_kv, prefix_pool, out_weight
        )
        axis = "tp" if lax.axis_size("tp") == 2 else "sub"
        arrived = [lax.ppermute(terms, axis, [(0, 1), (1, 0)]) for terms in theirs]
        mine = project(parts, out_weight, after(group, arrived[0]) * share, share)
        arrived = jnp.concatenate(arrived, axis=0)
        return (mine.astype(jnp.float32) + arrived.astype(jnp.float32)).astype(jnp.bfloat16)
    table = make_plan(wide, cores, False, ctrl)
    buffers = [lax.all_gather(prefix_pool, "wide", axis=0, tiled=True)]
    blocks = list(range(RB_DEV))
    parts = [
        attend([g], 0, blocks, False, CAPS, table, queries, resp_kv, buffers)[0] for g in range(heads)
    ]
    terms = project(parts, out_weight, jnp.int32(0), columns)
    return lax.psum_scatter(terms, ("tp", "sub"), scatter_dimension=1, tiled=True)


def solution(mesh):
    return jax.shard_map(
        local,
        mesh=mesh,
        in_specs=(
            P(("parts", "wide"), ("tp", "sub")),
            P(("parts", "wide"), ("tp", "sub")),
            P(("parts", "wide"), ("tp", "sub")),
            P(("tp", "sub"), None),
            P("parts"),
            P("parts"),
            P("parts"),
            P(("parts", "wide")),
        ),
        out_specs=P(("parts", "wide"), ("tp", "sub")),
        check_vma=False,
    )
```

```python
import math

import jax
import jax.numpy as jnp
from jax import lax
from jax.experimental import pallas as pl
from jax.experimental.pallas import tpu as pltpu
from jax.sharding import PartitionSpec as P

HD = 128
BLOCK = 128
RB_DEV = 2
PROMPTS = 4
PMAX = 16
GROUP = 8
PAIR = 2 * HD
WIDTH = GROUP * HD
ROWS = 512
SPAN = 4
NEG_LARGE = -1e30
SCALE = math.log2(math.e) / math.sqrt(HD)
VMEM_BYTES = 48 * 1024 * 1024

LEN_AT, BLOCKS_AT, OWNER_AT, SEG_AT, ME_AT, OTHER_AT = 0, 4, 8, 12, 14, 15


def params():
    return pltpu.CompilerParams(vmem_limit_bytes=VMEM_BYTES)


def as_int(flag):
    return jnp.where(flag, 1, 0)


class Layout:
    def __init__(self, ctrl, wide, cores):
        self.ctrl, self.wide, self.cores = ctrl, wide, cores
        self.stride = (PMAX + wide - 1) // wide
        self.me = ctrl[ME_AT]
        self.z, self.core = self.div(self.me, cores), self.mod(self.me, cores)
        ends, total = [], 0
        for p in range(PROMPTS):
            total = total + ctrl[BLOCKS_AT + p] + (RB_DEV - 1)
            ends.append(total)
        self.ends = ends

    def mod(self, value, size):
        return value & (size - 1) if size & (size - 1) == 0 else lax.rem(value, size)

    def div(self, value, size):
        if size & (size - 1) == 0:
            return lax.shift_right_logical(value, size.bit_length() - 1)
        return lax.div(value, size)

    def prompt_of(self, block):
        return sum(as_int(block >= end) for end in self.ends[:-1])

    def first_of(self, chip):
        return self.prompt_of(chip * self.cores * RB_DEV)

    def last_of(self, chip):
        return self.prompt_of((chip + 1) * self.cores * RB_DEV - 1)

    def length(self, p):
        return self.ctrl[LEN_AT + p]

    def held_by(self, p, j):
        return self.mod(self.ctrl[OWNER_AT + p] + j, self.wide)

    def held(self, p, who):
        first = self.mod(who - self.ctrl[OWNER_AT + p] + self.wide, self.wide)
        return sum(as_int(first + k * self.wide < self.length(p)) for k in range(self.stride))

    def listed(self, which, rank, room):
        return jnp.where(
            rank < room, which * CODE + rank, (EXTRA + which - 1) * CODE + rank - room
        )

    def in_plane(self, p, j, sums):
        who = self.held_by(p, j)
        chip = self.div(who, self.cores)
        gap = chip - self.z
        k = self.div(j, self.wide)
        at = who * SUMS
        down = sums[at + PROMPTS] - sums[at + p + 1] + k
        up = sums[at + p] + k
        near_down = down - jnp.where(
            chip == 0, sums[at + PROMPTS] - sums[at + self.last_of(1) + 1], 0
        )
        near_up = up - jnp.where(chip == 3, sums[at + self.first_of(2)], 0)
        far = jnp.where(gap < 0, down, up)
        two = (gap == 2) | (gap == -2)
        direct = two & ((self.z == 1) | (self.z == 2))
        code = jnp.where(two, 5 * CODE, 4 * CODE) + far
        code = jnp.where(direct, self.listed(3, far, CAPS.far), code)
        code = jnp.where(gap == 1, self.listed(2, near_up, CAPS.near), code)
        code = jnp.where(gap == -1, self.listed(1, near_down, CAPS.near), code)
        return jnp.where(gap == 0, p * self.stride + k, code)


CODE = 256
SHARED = 6
EXTRA = 7
SUMS = 8
SLOT_AT, SHARE_AT, SHARES_AT, LENGTH_AT, BASE_AT, LOW_AT, THEIRS_AT, OVER_AT, TABLE = (
    0, 32, 50, 52, 54, 56, 58, 59, 64
)


class Caps:
    def __init__(self, near, far, relay):
        self.near, self.far, self.relay = near, far, relay


CAPS = Caps(5, 5, 4)


def needs(lay, sums, cores):
    first, last = [lay.first_of(c) for c in range(4)], [lay.last_of(c) for c in range(4)]
    near, far = jnp.int32(0), jnp.int32(0)
    for core in range(cores):

        def held(chip, low, high, core=core):
            at = (chip * cores + core) * SUMS
            return sums[at + high + 1] - sums[at + low]

        top = PROMPTS - 1
        edge = [held(1, 0, last[0]), held(2, first[3], top)]
        for amount in edge + [
            held(0, first[1], last[1]),
            held(1, first[2], top),
            held(2, 0, last[1]),
            held(3, first[2], last[2]),
        ]:
            near = jnp.maximum(near, amount)
        for amount in (held(0, first[2], top), held(3, 0, last[1])):
            far = jnp.maximum(far, amount)
    return near, far


def plan_kernel(wide, cores, line, ctrl, table, sums):
    lay = Layout(ctrl, wide, cores)
    half = PMAX // cores
    table[THEIRS_AT] = ctrl[OTHER_AT]
    table[OVER_AT] = 0
    if line:

        def tally(who, carry):
            total = jnp.int32(0)
            for p in range(PROMPTS):
                sums[who * SUMS + p] = total
                total = total + lay.held(p, who)
            sums[who * SUMS + PROMPTS] = total
            return carry

        lax.fori_loop(0, wide, tally, 0)
        near, far = needs(lay, sums, cores)
        over = (near > CAPS.near) | (far > CAPS.far)
        table[OVER_AT] = as_int(over)

    def prompts_of(device):
        return [lay.prompt_of(device * RB_DEV + b) for b in range(RB_DEV)]

    mine = prompts_of(lay.me)
    same = mine[0] == mine[1]
    joined = same & (ctrl[SEG_AT] == ctrl[SEG_AT + 1])
    for slot in range(RB_DEV):
        p = mine[slot]
        count = lay.length(p)
        table[LENGTH_AT + slot] = count
        if slot == 1:
            count = jnp.where(same, 0, count)
        table[BASE_AT + slot] = jnp.where(same, 0, PMAX) if slot else 0
        table[LOW_AT + slot] = jnp.where(joined, 0, BLOCK) if slot else 0

        def place(j, carry, slot=slot, p=p):
            who = lay.held_by(p, j)
            code = (who * PROMPTS + p) * lay.stride + lay.div(j, wide)
            if line:
                shared = slot * half + lay.div(j, cores)
                passed = jnp.where(
                    lay.mod(who, cores) == lay.core,
                    lay.in_plane(p, j, sums),
                    SHARED * CODE + shared,
                )
                code = passed
            table[SLOT_AT + slot * PMAX + j] = code
            return carry

        lax.fori_loop(0, count, place, 0)
    if not line:
        return
    theirs = prompts_of(lay.z * cores + (cores - 1 - lay.core))
    for slot in range(RB_DEV):
        p = theirs[slot]
        shift = lay.mod(lay.core - ctrl[OWNER_AT + p] + wide, cores)
        count = lay.div(lay.length(p) - shift + cores - 1, cores)
        if slot == 1:
            count = jnp.where(theirs[1] == theirs[0], 0, count)
        table[SHARES_AT + slot] = count

        def share(i, carry, slot=slot, p=p, shift=shift):
            table[SHARE_AT + slot * half + i] = lay.in_plane(p, i * cores + shift, sums)
            return carry

        lax.fori_loop(0, count, share, 0)


def make_plan(wide, cores, line, ctrl):
    return pl.pallas_call(
        lambda *refs: plan_kernel(wide, cores, line, *refs),
        out_shape=jax.ShapeDtypeStruct((TABLE,), jnp.int32),
        in_specs=[pl.BlockSpec(memory_space=pltpu.SMEM)],
        out_specs=pl.BlockSpec(memory_space=pltpu.SMEM),
        scratch_shapes=[pltpu.SMEM((wide * SUMS,), jnp.int32)],
        compiler_params=params(),
        name="plan",
    )(ctrl)


def spot(ref, page):
    return ref.at[pl.ds(pl.multiple_of(page * BLOCK, BLOCK), BLOCK), :]


def page_at(buffer, page, column):
    rows = pl.ds(pl.multiple_of(page * BLOCK, BLOCK), BLOCK)
    return buffer.at[rows, pl.ds(column if buffer.shape[1] > PAIR else 0, PAIR)]


def start_page(buffers, code, column, target, sem):
    which = lax.shift_right_logical(code, CODE.bit_length() - 1)
    page = code & (CODE - 1)
    for i, buffer, offset in buffers:

        @pl.when(which == i)
        def _(buffer=buffer, offset=offset):
            source = page_at(buffer, page + offset, column)
            pltpu.make_async_copy(source, target, sem).start()


def wait_page(target, sem):
    pltpu.make_async_copy(target, target, sem).wait()


def send_kernel(wide, cores, groups, caps, skip, ctrl, pool, *refs):
    outs, sems = refs[:-1], refs[-1]
    rooms = (caps.near, caps.near, caps.far)
    lay = Layout(ctrl, wide, cores)
    z, last = lay.z, wide // cores - 1
    held = [lay.held(p, lay.me) for p in range(PROMPTS)]

    def above(p, top):
        return sum([jnp.where(o <= top, held[o], 0) for o in range(p + 1, PROMPTS)], jnp.int32(0))

    def below(p, low):
        return sum([jnp.where(o >= low, held[o], 0) for o in range(p)], jnp.int32(0))

    near_top = jnp.where(z == 0, lay.last_of(1), PROMPTS - 1)
    near_low = jnp.where(z == last, lay.first_of(2), 0)
    first_up, last_down = lay.first_of(z + 1), lay.last_of(z - 1)
    first_two, last_one = lay.first_of(2), lay.last_of(1)
    plans = []
    for p in range(PROMPTS):
        right = (z < last) & (p >= first_up) & (p <= near_top)
        left = (z > 0) & (p >= near_low) & (p <= last_down)
        far_up = (z == 0) & (p >= first_two)
        far_down = (z == last) & (p <= last_one)
        ranks = (above(p, near_top), below(p, near_low), above(p, PROMPTS - 1), below(p, 0))
        for k in range(lay.stride):
            for lane, wanted, rank in zip((0, 1, 2, 2), (right, left, far_up, far_down), ranks):
                at = rank + k - skip[lane]
                fits = (k < held[p]) & (at >= 0) & (at < rooms[lane])
                plans.append((wanted & fits, p * lay.stride + k, lane, at))

    def copies(plan):
        _, page, lane, rank = plan
        if groups is None:
            return [
                pltpu.make_async_copy(
                    spot(pool, page), spot(outs[lane], rank), sems.at[lane, page, 0]
                )
            ]
        return [
            pltpu.make_async_copy(
                page_at(pool, page, g * PAIR),
                spot(outs[n * 3 + lane], h * rooms[lane] + rank),
                sems.at[lane, page, n * len(groups[0]) + h],
            )
            for n, group in enumerate(groups)
            for h, g in enumerate(group)
        ]

    for plan in plans:

        @pl.when(plan[0])
        def _(plan=plan):
            for copy in copies(plan):
                copy.start()

    for plan in plans:

        @pl.when(plan[0])
        def _(plan=plan):
            for copy in copies(plan):
                copy.wait()


def relay_kernel(cores, caps, h, ctrl, far, left, right, out, sems):
    rows = caps.relay * BLOCK

    def copy(source, room, section):
        target = out.at[pl.ds(section * rows, rows), :]
        return pltpu.make_async_copy(
            source.at[pl.ds(h * room * BLOCK, rows), :], target, sems.at[section]
        )

    inner = ctrl[ME_AT] == 2 * cores
    for core in range(1, cores):
        inner = inner | (ctrl[ME_AT] == 2 * cores + core)
    copy(far, caps.far, 0).start()
    pl.when(inner)(lambda: copy(left, caps.near, 1).start())
    pl.when(jnp.logical_not(inner))(lambda: copy(right, caps.near, 1).start())
    copy(far, caps.far, 0).wait()
    copy(left, caps.near, 1).wait()


def numbered(refs, caps, h):
    if len(refs) == 1:
        return [(0, refs[0], 0)]
    offsets = (0, h * caps.near, h * caps.near, h * caps.far, 0)
    found = list(zip(range(5), refs[:5], offsets)) + [(5, refs[4], caps.relay)]
    if len(refs) == 9:
        found.append((SHARED, refs[5], 0))
    return found + [(EXTRA + i, ref, 0) for i, ref in enumerate(refs[-3:])]


def share_kernel(cores, caps, h, g, table, *refs):
    out, sems = refs[-2:]
    half = PMAX // cores
    buffers = numbered(refs[:-2], caps, h)
    for slot in range(RB_DEV):

        def begin(i, carry, slot=slot):
            at = slot * half + i
            start_page(buffers, table[SHARE_AT + at], g * PAIR, spot(out, at), sems.at[at])
            return carry

        lax.fori_loop(0, table[SHARES_AT + slot], begin, 0)
    for slot in range(RB_DEV):

        def finish(i, carry, slot=slot):
            at = slot * half + i
            wait_page(spot(out, at), sems.at[at])
            return carry

        lax.fori_loop(0, table[SHARES_AT + slot], finish, 0)


def attend_kernel(group, first, blocks, caps, carried, project, table, queries, own, *refs):
    refs = list(refs)
    weight = refs.pop(0) if project else None
    summed = refs.pop(0) if carried else None
    sems, stacked = refs.pop(), refs.pop()
    slab = refs.pop() if project else None
    store = refs.pop()
    terms = refs.pop() if project else None
    out = refs.pop()
    heads, room = len(group), len(blocks) * PMAX

    def region(i):
        if i == 0:
            return 0, table[LENGTH_AT + blocks[0]]
        base = table[BASE_AT + blocks[i]]
        return base, jnp.where(base == 0, 0, table[LENGTH_AT + blocks[i]])

    for h, g in enumerate(group):
        buffers = numbered(refs, caps, first + h)
        for i, b in enumerate(blocks):
            base, count = region(i)
            codes = SLOT_AT + table[BASE_AT + b]

            def begin(j, carry, h=h, g=g, buffers=buffers, base=base, codes=codes):
                at = h * room + base + j
                target, sem = spot(store, at), sems.at[at]
                start_page(buffers, table[codes + j], g * PAIR, target, sem)
                return carry

            lax.fori_loop(0, count, begin, 0)
            length = table[LENGTH_AT + b]

            def clear(j, carry, h=h, base=base):
                rows = pl.ds(pl.multiple_of((h * room + base + j) * BLOCK, BLOCK), BLOCK)
                store[rows, :] = jnp.zeros((BLOCK, PAIR), jnp.bfloat16)
                return carry

            lax.fori_loop(length, (length + SPAN - 1) & -SPAN, clear, 0)
    if project:
        share = slab.shape[1]
        theirs = pl.multiple_of(table[THEIRS_AT] * share, share)
        fetch = pltpu.make_async_copy(
            weight.at[pl.ds(group[0] * WIDTH, heads * WIDTH), pl.ds(theirs, share)],
            slab,
            sems.at[heads * room],
        )
        fetch.start()

    def one_block(h, i, b, base, count):
        tokens = pl.ds(pl.multiple_of(i * BLOCK, BLOCK), BLOCK)

        def columns(width, extra=0):
            return pl.ds(pl.multiple_of(h * width + extra, HD), min(width, HD))

        for e in range(GROUP):
            stacked[e * BLOCK : (e + 1) * BLOCK, :] = queries[tokens, columns(WIDTH, e * HD)]
        base = h * room + base

        def finish(j, carry):
            wait_page(spot(store, base + j), sems.at[base + j])
            return carry

        lax.fori_loop(0, count, finish, 0)
        length = table[LENGTH_AT + b]
        span = RB_DEV * BLOCK
        row = lax.broadcasted_iota(jnp.int32, (ROWS, span), 0) & (BLOCK - 1)
        key = lax.broadcasted_iota(jnp.int32, (ROWS, span), 1)
        own_mask = (key <= row + b * BLOCK) & (key >= table[LOW_AT + b])

        def run(spans):
            wide_key = lax.broadcasted_iota(jnp.int32, (ROWS, SPAN * BLOCK), 1)
            last_mask = wide_key < (length - (spans - 1) * SPAN) * BLOCK
            pieces = [(own[:, columns(PAIR)], own[:, columns(PAIR, HD)])]
            for t in range(spans):
                at = pl.multiple_of((base + t * SPAN) * BLOCK, BLOCK)
                piece = store[pl.ds(at, SPAN * BLOCK), :]
                pieces.append((piece[:, :HD], piece[:, HD:]))

            def score(r, t):
                scores = lax.dot_general(
                    stacked[r * ROWS : (r + 1) * ROWS, :],
                    pieces[t][0],
                    (((1,), (1,)), ((), ())),
                    preferred_element_type=jnp.float32,
                )
                if t == 0:
                    return jnp.where(own_mask, scores, NEG_LARGE)
                if t == spans:
                    return jnp.where(last_mask, scores, NEG_LARGE)
                return scores

            def highest(scores, sofar):
                for n in range(0, scores.shape[1], HD):
                    part = scores[:, n : n + HD]
                    sofar = part if sofar is None else jnp.maximum(sofar, part)
                return sofar

            def blend(scores, top, t):
                spread = jnp.concatenate([top] * (scores.shape[1] // HD), axis=1)
                weights = jnp.exp2((scores - spread) * SCALE).astype(jnp.bfloat16)
                values = pieces[t][1]
                values = jnp.concatenate([values, jnp.ones_like(values)], axis=1)
                return jnp.dot(weights, values, preferred_element_type=jnp.float32)

            chunks, ahead, peak = GROUP * BLOCK // ROWS, [], None
            for t in range(spans + 1):
                ahead.append(score(0, t))
                peak = highest(ahead[-1], peak)
            for r in range(chunks):
                now, ahead = ahead, []
                top = jnp.broadcast_to(jnp.max(peak, axis=1, keepdims=True), (ROWS, HD))
                total, peak = None, None
                for t in range(spans + 1):
                    if r + 1 < chunks:
                        ahead.append(score(r + 1, t))
                        peak = highest(ahead[-1], peak)
                    blended = blend(now[t], top, t)
                    total = blended if total is None else total + blended
                mean = (total[:, :HD] / total[:, HD:]).astype(jnp.bfloat16)
                for e in range(ROWS // BLOCK):
                    at = columns(WIDTH, (r * (ROWS // BLOCK) + e) * HD)
                    out[tokens, at] = mean[e * BLOCK : (e + 1) * BLOCK, :]

        spans = lax.shift_right_logical(length + SPAN - 1, SPAN.bit_length() - 1)
        for n in range(1, PMAX // SPAN + 1):
            pl.when(spans == n)(lambda n=n: run(n))

    def step(n, carry):
        if len(blocks) == 1:
            one_block(n, 0, blocks[0], *region(0))
            return carry
        h, i = lax.shift_right_logical(n, 1), n & 1
        base = jnp.where(i == 0, 0, region(1)[0])
        one_block(h, i, i, base, jnp.where(i == 0, region(0)[1], region(1)[1]))
        return carry

    lax.fori_loop(0, heads * len(blocks), step, 0)
    if project:
        fetch.wait()
        attended = out[...]
        width = math.gcd(share, 512)
        for n in range(0, share, width):
            term = jnp.dot(attended, slab[:, n : n + width], preferred_element_type=jnp.float32)
            if carried:
                term = term + summed[:, n : n + width]
            terms[:, n : n + width] = term.astype(terms.dtype)


def attend(
    group, first, blocks, last, caps, table, queries, resp_kv, buffers, weight=None, share=0, summed=None
):
    tokens, heads = len(blocks) * BLOCK, len(group)
    at = blocks[0] // len(blocks)
    project, carried = weight is not None, summed is not None
    any_spec = pl.BlockSpec(memory_space=pl.ANY)
    whole = pl.BlockSpec((tokens, share), lambda i, c: (0, 0))
    out_shape = [jax.ShapeDtypeStruct((tokens, heads * WIDTH), jnp.bfloat16)]
    out_specs = [pl.BlockSpec((tokens, heads * WIDTH), lambda i, c: (0, 0))]
    operands, in_specs = [], []
    scratch = [pltpu.VMEM((heads * len(blocks) * PMAX * BLOCK, PAIR), jnp.bfloat16)]
    if project:
        operands, in_specs = [weight], [any_spec]
        kept = jnp.bfloat16 if last else jnp.float32
        out_shape.append(jax.ShapeDtypeStruct((tokens, share), kept))
        out_specs.append(whole)
        scratch.append(pltpu.VMEM((heads * WIDTH, share), jnp.bfloat16))
    if carried:
        operands = operands + [summed]
        in_specs = in_specs + [pl.BlockSpec((tokens, share), lambda i, c: (at, 0))]
    column = group[0] // heads
    return pl.pallas_call(
        lambda *refs: attend_kernel(group, first, blocks, caps, carried, project, *refs),
        out_shape=out_shape,
        grid_spec=pltpu.PrefetchScalarGridSpec(
            num_scalar_prefetch=1,
            grid=(1,),
            in_specs=[
                pl.BlockSpec((tokens, heads * WIDTH), lambda i, c: (at, column)),
                pl.BlockSpec((RB_DEV * BLOCK, heads * PAIR), lambda i, c: (0, column)),
            ]
            + in_specs
            + [any_spec] * len(buffers),
            out_specs=out_specs,
            scratch_shapes=scratch
            + [
                pltpu.VMEM((GROUP * BLOCK, HD), jnp.bfloat16),
                pltpu.SemaphoreType.DMA((heads * len(blocks) * PMAX + 1,)),
            ],
        ),
        compiler_params=params(),
        cost_estimate=pl.CostEstimate(
            flops=2 * 2 * tokens * heads * WIDTH * 18 * BLOCK * 2,
            bytes_accessed=heads * (4 * tokens * WIDTH + PMAX * BLOCK * PAIR * 2 + share * WIDTH * 2),
            transcendentals=tokens * heads * GROUP * 18 * BLOCK,
        ),
        name="attend_heads_" + "_".join(map(str, group)) + "_blocks_" + "_".join(map(str, blocks)),
    )(table, queries, resp_kv, *operands, *buffers)


def pages_shape(count):
    return jax.ShapeDtypeStruct((count * BLOCK, PAIR), jnp.bfloat16)


def pack_send(wide, cores, groups, caps, skip, ctrl, pool):
    any_spec = pl.BlockSpec(memory_space=pl.ANY)
    pages = PROMPTS * ((PMAX + wide - 1) // wide)
    rooms = (caps.near, caps.near, caps.far)
    if groups is None:
        shapes = [jax.ShapeDtypeStruct((n * BLOCK, pool.shape[1]), jnp.bfloat16) for n in rooms]
    else:
        shapes = [pages_shape(n * len(group)) for group in groups for n in rooms]
    heads = 1 if groups is None else sum(map(len, groups))
    out = pl.pallas_call(
        lambda *refs: send_kernel(wide, cores, groups, caps, skip, *refs),
        out_shape=shapes,
        grid_spec=pltpu.PrefetchScalarGridSpec(
            num_scalar_prefetch=1,
            grid=(1,),
            in_specs=[pl.BlockSpec(pool.shape, lambda i, c: (0, 0))],
            out_specs=[any_spec] * len(shapes),
            scratch_shapes=[pltpu.SemaphoreType.DMA((3, pages, heads))],
        ),
        compiler_params=params(),
        cost_estimate=pl.CostEstimate(
            flops=0, bytes_accessed=2 * 12 * BLOCK * PAIR * 2 * heads, transcendentals=0
        ),
        name="pack_extra" if groups is None else f"pack_send_{groups[0][0]}",
    )(ctrl, pool)
    return [out[n : n + 3] for n in range(0, len(out), 3)]


def pack_share(cores, caps, h, g, table, buffers):
    any_spec = pl.BlockSpec(memory_space=pl.ANY)
    return pl.pallas_call(
        lambda *refs: share_kernel(cores, caps, h, g, *refs),
        out_shape=pages_shape(PMAX),
        grid_spec=pltpu.PrefetchScalarGridSpec(
            num_scalar_prefetch=1,
            grid=(1,),
            in_specs=[any_spec] * len(buffers),
            out_specs=any_spec,
            scratch_shapes=[pltpu.SemaphoreType.DMA((PMAX,))],
        ),
        compiler_params=params(),
        cost_estimate=pl.CostEstimate(
            flops=0, bytes_accessed=2 * 8 * BLOCK * PAIR * 2, transcendentals=0
        ),
        name=f"pack_share_{g}",
    )(table, *buffers)


def pack_relay(cores, caps, h, g, ctrl, far, left, right):
    any_spec = pl.BlockSpec(memory_space=pl.ANY)
    return pl.pallas_call(
        lambda *refs: relay_kernel(cores, caps, h, *refs),
        out_shape=pages_shape(2 * caps.relay),
        grid_spec=pltpu.PrefetchScalarGridSpec(
            num_scalar_prefetch=1,
            grid=(1,),
            in_specs=[any_spec] * 3,
            out_specs=any_spec,
            scratch_shapes=[pltpu.SemaphoreType.DMA((2,))],
        ),
        compiler_params=params(),
        cost_estimate=pl.CostEstimate(
            flops=0, bytes_accessed=4 * caps.relay * BLOCK * PAIR * 2, transcendentals=0
        ),
        name=f"pack_relay_{g}",
    )(ctrl, far, left, right)


def after(value, *earlier):
    return lax.optimization_barrier((value, *earlier))[0]


def line_attend(wide, cores, caps, ctrl, table, queries, resp_kv, pool, weight):
    heads = resp_kv.shape[1] // PAIR
    share = weight.shape[1] // 2

    def hop(x, moves):
        pairs = [(a * cores + c, b * cores + c) for a, b in moves for c in range(cores)]
        return lax.ppermute(x, "wide", pairs)

    swap = [(d, d // cores * cores + (cores - 1 - d % cores)) for d in range(wide)]
    groups = [[g] for g in range(heads)]

    def spread(right, left, far):
        return (
            hop(right, [(0, 1), (1, 2), (2, 3)]),
            hop(left, [(3, 2), (2, 1), (1, 0)]),
            hop(far, [(0, 2), (3, 1)]),
        )

    past = Caps(1, 1, 0)

    def past_the_end(ctrl, pool):
        skip = (caps.near, caps.near, caps.far)
        return spread(*pack_send(wide, cores, None, past, skip, ctrl, pool)[0])

    def nothing(ctrl, pool):
        return (jnp.zeros((past.near * BLOCK, pool.shape[1]), pool.dtype),) * 3

    extra = list(lax.cond(table[OVER_AT] == 1, past_the_end, nothing, ctrl, pool))

    def exchange(h, g, held, plan):
        shared = pack_share(cores, caps, h, g, plan, held + extra)
        return held + [lax.ppermute(shared, "wide", swap)] + extra

    both = list(range(RB_DEV))
    units = [(n, h, g) for n, group in enumerate(groups) for h, g in enumerate(group)]
    spreads, parts, summed, held = {}, [], None, {}

    def relay(u, plan):
        n, h, g = units[u]
        if n not in spreads:
            sends = pack_send(wide, cores, [groups[n]], caps, (0, 0, 0), ctrl, pool)
            spreads[n] = spread(*sends[0])
        left, right, far = spreads[n]
        onward = pack_relay(cores, caps, h, g, plan, far, left, right)
        held[u] = [pool, left, right, far, hop(onward, [(2, 3), (1, 0)])]
        return onward

    relay(0, after(ctrl, extra[0]))
    for u, (n, h, g) in enumerate(units[:-1]):
        onward = relay(u + 1, after(ctrl, parts[-1]) if parts else ctrl)
        buffers = exchange(h, g, held[u], after(table, onward))
        attended, summed = attend(
            [g], h, both, False, caps, table, queries, resp_kv, buffers, weight, share, summed
        )
        parts.append(attended)
    _, h, g = units[-1]
    plan = after(table, parts[-1]) if parts else table
    buffers = exchange(h, g, held[len(units) - 1], plan)
    ends, theirs, plan = [], [], table
    for b in both:
        attended, terms = attend(
            [g], h, [b], True, caps, plan, queries, resp_kv, buffers, weight, share, summed
        )
        ends.append(attended)
        theirs.append(terms)
        plan = after(table, attended)
    return parts + [jnp.concatenate(ends, axis=0)], theirs


def project_kernel(at, *refs):
    parts, weight, out = refs[:-2], refs[-2], refs[-1]
    total, row = None, 0
    for part in parts:
        end = row + part.shape[1]
        term = jnp.dot(part[...], weight[row:end, :], preferred_element_type=jnp.float32)
        total, row = term if total is None else total + term, end
    out[...] = total.astype(jnp.bfloat16)


def project(parts, weight, first_column, columns):
    tokens = parts[0].shape[0]
    tile = math.gcd(columns, 512)
    assert weight.shape[1] % tile == 0
    at = jnp.reshape(first_column // tile, (1,)).astype(jnp.int32)
    return pl.pallas_call(
        project_kernel,
        out_shape=jax.ShapeDtypeStruct((tokens, columns), jnp.bfloat16),
        grid_spec=pltpu.PrefetchScalarGridSpec(
            num_scalar_prefetch=1,
            grid=(columns // tile,),
            in_specs=[pl.BlockSpec(part.shape, lambda i, at: (0, 0)) for part in parts]
            + [pl.BlockSpec((weight.shape[0], tile), lambda i, at: (0, at[0] + i))],
            out_specs=pl.BlockSpec((tokens, tile), lambda i, at: (0, i)),
        ),
        compiler_params=params(),
        cost_estimate=pl.CostEstimate(
            flops=2 * tokens * columns * weight.shape[0],
            bytes_accessed=2 * columns * weight.shape[0],
            transcendentals=0,
        ),
        name="project",
    )(at, *parts, weight)


def local(
    queries, resp_kv, prefix_pool, out_weight, pre_len, prompt_blocks, prompt_owner, resp_seg
):
    wide, groups = lax.axis_size("wide"), lax.axis_size("tp") * lax.axis_size("sub")
    cores = 2 // lax.axis_size("sub")
    heads = resp_kv.shape[1] // PAIR
    me = lax.axis_index("wide").astype(jnp.int32)
    group = lax.axis_index("tp") * lax.axis_size("sub") + lax.axis_index("sub")
    where = jnp.stack([me, (1 - group).astype(jnp.int32)])
    ctrl = jnp.concatenate([pre_len, prompt_blocks, prompt_owner, resp_seg, where])
    columns = out_weight.shape[1]
    share = columns // groups
    if wide == 8 and cores == 2 and groups == 2:
        table = make_plan(wide, cores, True, ctrl)

        parts, theirs = line_attend(
            wide, cores, CAPS, ctrl, table, queries, resp_kv, prefix_pool, out_weight
        )
        axis = "tp" if lax.axis_size("tp") == 2 else "sub"
        arrived = [lax.ppermute(terms, axis, [(0, 1), (1, 0)]) for terms in theirs]
        half = share // 2
        mine = [
            project(parts, out_weight, group * share, half),
            project(parts, out_weight, after(group, arrived[0]) * share + half, half),
        ]
        mine = jnp.concatenate(mine, axis=1)
        arrived = jnp.concatenate(arrived, axis=0)
        return (mine.astype(jnp.float32) + arrived.astype(jnp.float32)).astype(jnp.bfloat16)
    table = make_plan(wide, cores, False, ctrl)
    buffers = [lax.all_gather(prefix_pool, "wide", axis=0, tiled=True)]
    blocks = list(range(RB_DEV))
    parts = [
        attend([g], 0, blocks, False, CAPS, table, queries, resp_kv, buffers)[0] for g in range(heads)
    ]
    terms = project(parts, out_weight, jnp.int32(0), columns)
    return lax.psum_scatter(terms, ("tp", "sub"), scatter_dimension=1, tiled=True)


def solution(mesh):
    return jax.shard_map(
        local,
        mesh=mesh,
        in_specs=(
            P(("parts", "wide"), ("tp", "sub")),
            P(("parts", "wide"), ("tp", "sub")),
            P(("parts", "wide"), ("tp", "sub")),
            P(("tp", "sub"), None),
            P("parts"),
            P("parts"),
            P("parts"),
            P(("parts", "wide")),
        ),
        out_specs=P(("parts", "wide"), ("tp", "sub")),
        check_vma=False,
    )
```

```python
import math

import jax
import jax.numpy as jnp
from jax import lax
from jax.experimental import pallas as pl
from jax.experimental.pallas import tpu as pltpu
from jax.sharding import PartitionSpec as P

HD = 128
BLOCK = 128
RB_DEV = 2
PROMPTS = 4
PMAX = 16
GROUP = 8
PAIR = 2 * HD
WIDTH = GROUP * HD
ROWS = 512
SPAN = 4
NEG_LARGE = -1e30
SCALE = math.log2(math.e) / math.sqrt(HD)
VMEM_BYTES = 48 * 1024 * 1024

LEN_AT, BLOCKS_AT, OWNER_AT, SEG_AT, ME_AT, OTHER_AT = 0, 4, 8, 12, 14, 15


def params():
    return pltpu.CompilerParams(vmem_limit_bytes=VMEM_BYTES)


def as_int(flag):
    return jnp.where(flag, 1, 0)


class Layout:
    def __init__(self, ctrl, wide, cores):
        self.ctrl, self.wide, self.cores = ctrl, wide, cores
        self.stride = (PMAX + wide - 1) // wide
        self.me = ctrl[ME_AT]
        self.z, self.core = self.div(self.me, cores), self.mod(self.me, cores)
        ends, total = [], 0
        for p in range(PROMPTS):
            total = total + ctrl[BLOCKS_AT + p] + (RB_DEV - 1)
            ends.append(total)
        self.ends = ends

    def mod(self, value, size):
        return value & (size - 1) if size & (size - 1) == 0 else lax.rem(value, size)

    def div(self, value, size):
        if size & (size - 1) == 0:
            return lax.shift_right_logical(value, size.bit_length() - 1)
        return lax.div(value, size)

    def prompt_of(self, block):
        return sum(as_int(block >= end) for end in self.ends[:-1])

    def first_of(self, chip):
        return self.prompt_of(chip * self.cores * RB_DEV)

    def last_of(self, chip):
        return self.prompt_of((chip + 1) * self.cores * RB_DEV - 1)

    def length(self, p):
        return self.ctrl[LEN_AT + p]

    def held_by(self, p, j):
        return self.mod(self.ctrl[OWNER_AT + p] + j, self.wide)

    def held(self, p, who):
        first = self.mod(who - self.ctrl[OWNER_AT + p] + self.wide, self.wide)
        return sum(as_int(first + k * self.wide < self.length(p)) for k in range(self.stride))

    def listed(self, which, rank, room):
        return jnp.where(
            rank < room, which * CODE + rank, (EXTRA + which - 1) * CODE + rank - room
        )

    def in_plane(self, p, j, sums):
        who = self.held_by(p, j)
        chip = self.div(who, self.cores)
        gap = chip - self.z
        k = self.div(j, self.wide)
        at = who * SUMS
        down = sums[at + PROMPTS] - sums[at + p + 1] + k
        up = sums[at + p] + k
        near_down = down - jnp.where(
            chip == 0, sums[at + PROMPTS] - sums[at + self.last_of(1) + 1], 0
        )
        near_up = up - jnp.where(chip == 3, sums[at + self.first_of(2)], 0)
        far = jnp.where(gap < 0, down, up)
        two = (gap == 2) | (gap == -2)
        direct = two & ((self.z == 1) | (self.z == 2))
        code = jnp.where(two, 5 * CODE, 4 * CODE) + far
        code = jnp.where(direct, self.listed(3, far, CAPS.far), code)
        code = jnp.where(gap == 1, self.listed(2, near_up, CAPS.near), code)
        code = jnp.where(gap == -1, self.listed(1, near_down, CAPS.near), code)
        return jnp.where(gap == 0, p * self.stride + k, code)


CODE = 256
PARTNER = 1
HERE = 8
SHARED = 6
EXTRA = 7
SUMS = 8
SLOT_AT, NEAR_AT, SHARE_AT, SHARES_AT, FROM_AT, LENGTH_AT, BASE_AT, LOW_AT, THEIRS_AT, OVER_AT, TABLE = (
    0, 32, 48, 64, 66, 68, 70, 72, 74, 75, 96
)


class Caps:
    def __init__(self, near, far, relay):
        self.near, self.far, self.relay = near, far, relay


CAPS = Caps(5, 5, 4)


def needs(lay, sums, cores):
    first, last = [lay.first_of(c) for c in range(4)], [lay.last_of(c) for c in range(4)]
    near, far = jnp.int32(0), jnp.int32(0)
    for core in range(cores):

        def held(chip, low, high, core=core):
            at = (chip * cores + core) * SUMS
            return sums[at + high + 1] - sums[at + low]

        top = PROMPTS - 1
        edge = [held(1, 0, last[0]), held(2, first[3], top)]
        for amount in edge + [
            held(0, first[1], last[1]),
            held(1, first[2], top),
            held(2, 0, last[1]),
            held(3, first[2], last[2]),
        ]:
            near = jnp.maximum(near, amount)
        for amount in (held(0, first[2], top), held(3, 0, last[1])):
            far = jnp.maximum(far, amount)
    return near, far


def plan_kernel(wide, cores, line, ctrl, table, sums):
    lay = Layout(ctrl, wide, cores)
    half = PMAX // cores
    table[THEIRS_AT] = ctrl[OTHER_AT]
    table[OVER_AT] = 0
    if line:

        def tally(who, carry):
            total = jnp.int32(0)
            for p in range(PROMPTS):
                sums[who * SUMS + p] = total
                total = total + lay.held(p, who)
            sums[who * SUMS + PROMPTS] = total
            return carry

        lax.fori_loop(0, wide, tally, 0)
        near, far = needs(lay, sums, cores)
        over = (near > CAPS.near) | (far > CAPS.far)
        table[OVER_AT] = as_int(over)

    def prompts_of(device):
        return [lay.prompt_of(device * RB_DEV + b) for b in range(RB_DEV)]

    mine = prompts_of(lay.me)
    same = mine[0] == mine[1]
    joined = same & (ctrl[SEG_AT] == ctrl[SEG_AT + 1])
    for slot in range(RB_DEV):
        p = mine[slot]
        length = lay.length(p)
        table[BASE_AT + slot] = jnp.where(same, 0, 1) if slot else 0
        table[LOW_AT + slot] = jnp.where(joined, 0, BLOCK) if slot else 0

        def place(j, counts, slot=slot, p=p):
            here, away = counts
            who = lay.held_by(p, j)
            k = lay.div(j, wide)
            if not line:
                table[SLOT_AT + slot * PMAX + away] = (who * PROMPTS + p) * lay.stride + k
                return here, away + 1
            is_mine = lay.mod(who, cores) == lay.core
            is_here = lay.div(who, cores) == lay.z

            @pl.when(is_here)
            def _():
                at = NEAR_AT + slot * HERE + here
                table[at] = jnp.where(is_mine, 0, PARTNER * CODE) + p * lay.stride + k

            @pl.when(jnp.logical_not(is_here))
            def _():
                passed = SHARED * CODE + slot * half + lay.div(j, cores)
                table[SLOT_AT + slot * PMAX + away] = jnp.where(
                    is_mine, lay.in_plane(p, j, sums), passed
                )

            return here + as_int(is_here), away + as_int(jnp.logical_not(is_here))

        here, away = lax.fori_loop(0, length, place, (jnp.int32(0), jnp.int32(0)))
        table[FROM_AT + slot] = here
        table[LENGTH_AT + slot] = away
    if not line:
        return
    theirs = prompts_of(lay.z * cores + (cores - 1 - lay.core))
    for slot in range(RB_DEV):
        p = theirs[slot]
        shift = lay.mod(lay.core - ctrl[OWNER_AT + p] + wide, cores)
        count = lay.div(lay.length(p) - shift + cores - 1, cores)
        if slot == 1:
            count = jnp.where(theirs[1] == theirs[0], 0, count)
        table[SHARES_AT + slot] = count

        def share(i, carry, slot=slot, p=p, shift=shift):
            table[SHARE_AT + slot * half + i] = lay.in_plane(p, i * cores + shift, sums)
            return carry

        lax.fori_loop(0, count, share, 0)


def make_plan(wide, cores, line, ctrl):
    return pl.pallas_call(
        lambda *refs: plan_kernel(wide, cores, line, *refs),
        out_shape=jax.ShapeDtypeStruct((TABLE,), jnp.int32),
        in_specs=[pl.BlockSpec(memory_space=pltpu.SMEM)],
        out_specs=pl.BlockSpec(memory_space=pltpu.SMEM),
        scratch_shapes=[pltpu.SMEM((wide * SUMS,), jnp.int32)],
        compiler_params=params(),
        name="plan",
    )(ctrl)


def spot(ref, page):
    return ref.at[pl.ds(pl.multiple_of(page * BLOCK, BLOCK), BLOCK), :]


def page_at(buffer, page, column):
    rows = pl.ds(pl.multiple_of(page * BLOCK, BLOCK), BLOCK)
    return buffer.at[rows, pl.ds(column if buffer.shape[1] > PAIR else 0, PAIR)]


def start_page(buffers, code, column, target, sem):
    which = lax.shift_right_logical(code, CODE.bit_length() - 1)
    page = code & (CODE - 1)
    for i, buffer, offset in buffers:

        @pl.when(which == i)
        def _(buffer=buffer, offset=offset):
            source = page_at(buffer, page + offset, column)
            pltpu.make_async_copy(source, target, sem).start()


def wait_page(target, sem):
    pltpu.make_async_copy(target, target, sem).wait()


def send_kernel(wide, cores, groups, caps, skip, ctrl, pool, *refs):
    outs, sems = refs[:-1], refs[-1]
    rooms = (caps.near, caps.near, caps.far)
    lay = Layout(ctrl, wide, cores)
    z, last = lay.z, wide // cores - 1
    held = [lay.held(p, lay.me) for p in range(PROMPTS)]

    def above(p, top):
        return sum([jnp.where(o <= top, held[o], 0) for o in range(p + 1, PROMPTS)], jnp.int32(0))

    def below(p, low):
        return sum([jnp.where(o >= low, held[o], 0) for o in range(p)], jnp.int32(0))

    near_top = jnp.where(z == 0, lay.last_of(1), PROMPTS - 1)
    near_low = jnp.where(z == last, lay.first_of(2), 0)
    first_up, last_down = lay.first_of(z + 1), lay.last_of(z - 1)
    first_two, last_one = lay.first_of(2), lay.last_of(1)
    plans = []
    for p in range(PROMPTS):
        right = (z < last) & (p >= first_up) & (p <= near_top)
        left = (z > 0) & (p >= near_low) & (p <= last_down)
        far_up = (z == 0) & (p >= first_two)
        far_down = (z == last) & (p <= last_one)
        ranks = (above(p, near_top), below(p, near_low), above(p, PROMPTS - 1), below(p, 0))
        for k in range(lay.stride):
            for lane, wanted, rank in zip((0, 1, 2, 2), (right, left, far_up, far_down), ranks):
                at = rank + k - skip[lane]
                fits = (k < held[p]) & (at >= 0) & (at < rooms[lane])
                plans.append((wanted & fits, p * lay.stride + k, lane, at))

    def copies(plan):
        _, page, lane, rank = plan
        if groups is None:
            return [
                pltpu.make_async_copy(
                    spot(pool, page), spot(outs[lane], rank), sems.at[lane, page, 0]
                )
            ]
        return [
            pltpu.make_async_copy(
                page_at(pool, page, g * PAIR),
                spot(outs[n * 3 + lane], h * rooms[lane] + rank),
                sems.at[lane, page, n * len(groups[0]) + h],
            )
            for n, group in enumerate(groups)
            for h, g in enumerate(group)
        ]

    for plan in plans:

        @pl.when(plan[0])
        def _(plan=plan):
            for copy in copies(plan):
                copy.start()

    for plan in plans:

        @pl.when(plan[0])
        def _(plan=plan):
            for copy in copies(plan):
                copy.wait()


def relay_kernel(cores, caps, h, ctrl, far, left, right, out, sems):
    rows = caps.relay * BLOCK

    def copy(source, room, section):
        target = out.at[pl.ds(section * rows, rows), :]
        return pltpu.make_async_copy(
            source.at[pl.ds(h * room * BLOCK, rows), :], target, sems.at[section]
        )

    inner = ctrl[ME_AT] == 2 * cores
    for core in range(1, cores):
        inner = inner | (ctrl[ME_AT] == 2 * cores + core)
    copy(far, caps.far, 0).start()
    pl.when(inner)(lambda: copy(left, caps.near, 1).start())
    pl.when(jnp.logical_not(inner))(lambda: copy(right, caps.near, 1).start())
    copy(far, caps.far, 0).wait()
    copy(left, caps.near, 1).wait()


def numbered(refs, caps, h):
    if len(refs) == 1:
        return [(0, refs[0], 0)]
    offsets = (0, h * caps.near, h * caps.near, h * caps.far, 0)
    found = list(zip(range(5), refs[:5], offsets)) + [(5, refs[4], caps.relay)]
    if len(refs) == 9:
        found.append((SHARED, refs[5], 0))
    return found + [(EXTRA + i, ref, 0) for i, ref in enumerate(refs[-3:])]


def share_kernel(cores, caps, h, g, table, *refs):
    out, sems = refs[-2:]
    half = PMAX // cores
    buffers = numbered(refs[:-2], caps, h)
    for slot in range(RB_DEV):

        def begin(i, carry, slot=slot):
            at = slot * half + i
            start_page(buffers, table[SHARE_AT + at], g * PAIR, spot(out, at), sems.at[at])
            return carry

        lax.fori_loop(0, table[SHARES_AT + slot], begin, 0)
    for slot in range(RB_DEV):

        def finish(i, carry, slot=slot):
            at = slot * half + i
            wait_page(spot(out, at), sems.at[at])
            return carry

        lax.fori_loop(0, table[SHARES_AT + slot], finish, 0)


def attend_kernel(mode, heads, first, h_in, blocks, caps, project, carried, table, *refs):
    refs = list(refs)
    queries = refs.pop(0)
    own = refs.pop(0) if mode != "finish" else None
    state_in = refs.pop(0) if mode == "finish" else None
    weight = refs.pop(0) if project else None
    summed = refs.pop(0) if carried else None
    sems, stacked = refs.pop(), refs.pop()
    slab = refs.pop() if project else None
    store = refs.pop()
    terms = refs.pop() if project else None
    out = refs.pop()
    head = first + pl.program_id(0) if heads > 1 else first
    if mode == "start":
        buffers = [(i, ref, 0) for i, ref in enumerate(refs)]
        codes_at, each, counts_at, room = NEAR_AT, HERE, FROM_AT, HERE
    else:
        buffers = numbered(refs, caps, h_in)
        codes_at, each, counts_at, room = SLOT_AT, PMAX, LENGTH_AT, PMAX

    def region(i):
        count = table[counts_at + blocks[i]]
        if i == 0:
            return 0, count
        apart = table[BASE_AT + blocks[i]]
        return apart * room, jnp.where(apart == 0, 0, count)

    for i, b in enumerate(blocks):
        base, count = region(i)
        codes = codes_at + table[BASE_AT + b] * each

        def begin(j, carry, base=base, codes=codes):
            target, sem = spot(store, base + j), sems.at[base + j]
            start_page(buffers, table[codes + j], head * PAIR, target, sem)
            return carry

        lax.fori_loop(0, count, begin, 0)
        held = table[counts_at + b]

        def clear(j, carry, base=base):
            store[pl.ds(pl.multiple_of((base + j) * BLOCK, BLOCK), BLOCK), :] = jnp.zeros(
                (BLOCK, PAIR), jnp.bfloat16
            )
            return carry

        lax.fori_loop(held, (held + SPAN - 1) & -SPAN, clear, 0)
    if project:
        share = slab.shape[1]
        theirs = pl.multiple_of(table[THEIRS_AT] * share, share)
        fetch = pltpu.make_async_copy(
            weight.at[pl.ds(head * WIDTH, WIDTH), pl.ds(theirs, share)],
            slab,
            sems.at[len(blocks) * room],
        )
        fetch.start()

    def one_block(i, b, base, count):
        tokens = pl.ds(pl.multiple_of(i * BLOCK, BLOCK), BLOCK)
        for e in range(GROUP):
            stacked[e * BLOCK : (e + 1) * BLOCK, :] = queries[tokens, e * HD : (e + 1) * HD]

        def finish(j, carry):
            wait_page(spot(store, base + j), sems.at[base + j])
            return carry

        lax.fori_loop(0, count, finish, 0)
        held = table[counts_at + b]
        if own is not None:
            span = RB_DEV * BLOCK
            row = lax.broadcasted_iota(jnp.int32, (ROWS, span), 0) & (BLOCK - 1)
            key = lax.broadcasted_iota(jnp.int32, (ROWS, span), 1)
            own_mask = (key <= row + b * BLOCK) & (key >= table[LOW_AT + b])

        def run(spans):
            pieces = []
            for t in range(spans):
                at = pl.multiple_of((base + t * SPAN) * BLOCK, BLOCK)
                piece = store[pl.ds(at, SPAN * BLOCK), :]
                mask = None
                if t == spans - 1:
                    wide_key = lax.broadcasted_iota(jnp.int32, (ROWS, SPAN * BLOCK), 1)
                    mask = wide_key < (held - t * SPAN) * BLOCK
                pieces.append((piece[:, :HD], piece[:, HD:], mask))
            if own is not None:
                pieces.append((own[:, :HD], own[:, HD:], own_mask))

            def score(r, t):
                keys, _, mask = pieces[t]
                scores = lax.dot_general(
                    stacked[r * ROWS : (r + 1) * ROWS, :],
                    keys,
                    (((1,), (1,)), ((), ())),
                    preferred_element_type=jnp.float32,
                )
                return scores if mask is None else jnp.where(mask, scores, NEG_LARGE)

            def highest(scores, sofar):
                for n in range(0, scores.shape[1], HD):
                    part = scores[:, n : n + HD]
                    sofar = part if sofar is None else jnp.maximum(sofar, part)
                return sofar

            def blend(scores, top, t):
                spread = jnp.concatenate([top] * (scores.shape[1] // HD), axis=1)
                weights = jnp.exp2((scores - spread) * SCALE).astype(jnp.bfloat16)
                values = pieces[t][1]
                values = jnp.concatenate([values, jnp.ones_like(values)], axis=1)
                return jnp.dot(weights, values, preferred_element_type=jnp.float32)

            def known(r):
                return pl.ds(pl.multiple_of(i * GROUP * BLOCK + r * ROWS, ROWS), ROWS)

            chunks, ahead = GROUP * BLOCK // ROWS, []
            peak = None if state_in is None else state_in[known(0), 2 * HD :]
            for t in range(len(pieces)):
                ahead.append(score(0, t))
                peak = highest(ahead[-1], peak)
            for r in range(chunks):
                now, ahead = ahead, []
                top = jnp.broadcast_to(jnp.max(peak, axis=1, keepdims=True), (ROWS, HD))
                total, peak = None, None
                if state_in is not None:
                    fade = jnp.exp2((state_in[known(r), 2 * HD :] - top) * SCALE)
                    total = state_in[known(r), : 2 * HD] * jnp.concatenate([fade, fade], axis=1)
                    if r + 1 < chunks:
                        peak = state_in[known(r + 1), 2 * HD :]
                for t in range(len(pieces)):
                    if r + 1 < chunks:
                        ahead.append(score(r + 1, t))
                        peak = highest(ahead[-1], peak)
                    blended = blend(now[t], top, t)
                    total = blended if total is None else total + blended
                if mode == "start":
                    out[known(r), : 2 * HD] = total
                    out[known(r), 2 * HD :] = top
                    continue
                mean = (total[:, :HD] / total[:, HD:]).astype(jnp.bfloat16)
                for e in range(ROWS // BLOCK):
                    column = (r * (ROWS // BLOCK) + e) * HD
                    out[tokens, column : column + HD] = mean[e * BLOCK : (e + 1) * BLOCK, :]

        spans = lax.shift_right_logical(held + SPAN - 1, SPAN.bit_length() - 1)
        for n in range(1 if mode == "whole" else 0, (SPAN if mode == "start" else PMAX) // SPAN + 1):
            pl.when(spans == n)(lambda n=n: run(n))

    if len(blocks) == 1:
        one_block(0, blocks[0], *region(0))
    else:

        def step(i, carry):
            base, count = [jnp.where(i == 0, *pair) for pair in zip(region(0), region(1))]
            one_block(i, i, base, count)
            return carry

        lax.fori_loop(0, len(blocks), step, 0)
    if project:
        fetch.wait()
        attended = out[...]
        width = math.gcd(share, 512)
        for n in range(0, share, width):
            term = jnp.dot(attended, slab[:, n : n + width], preferred_element_type=jnp.float32)
            if carried:
                term = term + summed[:, n : n + width]
            terms[:, n : n + width] = term.astype(terms.dtype)


STATE = 3 * HD


def attend(
    mode, heads, first, h, blocks, caps, table, queries, own, buffers,
    weight=None, share=0, summed=None, last=False,
):
    tokens = len(blocks) * BLOCK
    rows = tokens * GROUP
    at = blocks[0] // len(blocks)
    project, carried = weight is not None, summed is not None
    any_spec = pl.BlockSpec(memory_space=pl.ANY)
    room = HERE if mode == "start" else PMAX
    operands = [queries, own]
    in_specs = [pl.BlockSpec((tokens, WIDTH), lambda i, c: (at, first + i))]
    if mode == "finish":
        in_specs.append(pl.BlockSpec((None, rows, STATE), lambda i, c: (h[1], at, 0)))
    else:
        in_specs.append(pl.BlockSpec((RB_DEV * BLOCK, PAIR), lambda i, c: (0, first + i)))
    if mode == "start":
        out_shape = [jax.ShapeDtypeStruct((heads, rows, STATE), jnp.float32)]
        out_specs = [pl.BlockSpec((None, rows, STATE), lambda i, c: (i, 0, 0))]
    else:
        out_shape = [jax.ShapeDtypeStruct((tokens, WIDTH), jnp.bfloat16)]
        out_specs = [pl.BlockSpec((tokens, WIDTH), lambda i, c: (0, 0))]
    scratch = [pltpu.VMEM((len(blocks) * room * BLOCK, PAIR), jnp.bfloat16)]
    if project:
        operands.append(weight)
        in_specs.append(any_spec)
        kept = jnp.bfloat16 if last else jnp.float32
        out_shape.append(jax.ShapeDtypeStruct((tokens, share), kept))
        out_specs.append(pl.BlockSpec((tokens, share), lambda i, c: (0, 0)))
        scratch.append(pltpu.VMEM((WIDTH, share), jnp.bfloat16))
    if carried:
        row = at if summed.shape[0] > tokens else 0
        operands.append(summed)
        in_specs.append(pl.BlockSpec((tokens, share), lambda i, c: (row, 0)))
    keys = {"whole": 18, "start": 6, "finish": 12}[mode] * BLOCK
    out = pl.pallas_call(
        lambda *refs: attend_kernel(
            mode, heads, first, h[0], blocks, caps, project, carried, *refs
        ),
        out_shape=out_shape,
        grid_spec=pltpu.PrefetchScalarGridSpec(
            num_scalar_prefetch=1,
            grid=(heads,),
            in_specs=in_specs + [any_spec] * len(buffers),
            out_specs=out_specs,
            scratch_shapes=scratch
            + [
                pltpu.VMEM((GROUP * BLOCK, HD), jnp.bfloat16),
                pltpu.SemaphoreType.DMA((len(blocks) * room + 1,)),
            ],
        ),
        compiler_params=params(),
        cost_estimate=pl.CostEstimate(
            flops=2 * 2 * tokens * heads * WIDTH * keys * 2,
            bytes_accessed=heads * (4 * tokens * WIDTH + keys * PAIR * 2 + share * WIDTH * 2),
            transcendentals=heads * rows * keys,
        ),
        name=f"{mode}_{first}_" + "_".join(map(str, blocks)),
    )(table, *operands, *buffers)
    return out if project else out[0]


def pages_shape(count):
    return jax.ShapeDtypeStruct((count * BLOCK, PAIR), jnp.bfloat16)


def pack_send(wide, cores, groups, caps, skip, ctrl, pool):
    any_spec = pl.BlockSpec(memory_space=pl.ANY)
    pages = PROMPTS * ((PMAX + wide - 1) // wide)
    rooms = (caps.near, caps.near, caps.far)
    if groups is None:
        shapes = [jax.ShapeDtypeStruct((n * BLOCK, pool.shape[1]), jnp.bfloat16) for n in rooms]
    else:
        shapes = [pages_shape(n * len(group)) for group in groups for n in rooms]
    heads = 1 if groups is None else sum(map(len, groups))
    out = pl.pallas_call(
        lambda *refs: send_kernel(wide, cores, groups, caps, skip, *refs),
        out_shape=shapes,
        grid_spec=pltpu.PrefetchScalarGridSpec(
            num_scalar_prefetch=1,
            grid=(1,),
            in_specs=[pl.BlockSpec(pool.shape, lambda i, c: (0, 0))],
            out_specs=[any_spec] * len(shapes),
            scratch_shapes=[pltpu.SemaphoreType.DMA((3, pages, heads))],
        ),
        compiler_params=params(),
        cost_estimate=pl.CostEstimate(
            flops=0, bytes_accessed=2 * 12 * BLOCK * PAIR * 2 * heads, transcendentals=0
        ),
        name="pack_extra" if groups is None else f"pack_send_{groups[0][0]}",
    )(ctrl, pool)
    return [out[n : n + 3] for n in range(0, len(out), 3)]


def pack_share(cores, caps, h, g, table, buffers):
    any_spec = pl.BlockSpec(memory_space=pl.ANY)
    return pl.pallas_call(
        lambda *refs: share_kernel(cores, caps, h, g, *refs),
        out_shape=pages_shape(PMAX),
        grid_spec=pltpu.PrefetchScalarGridSpec(
            num_scalar_prefetch=1,
            grid=(1,),
            in_specs=[any_spec] * len(buffers),
            out_specs=any_spec,
            scratch_shapes=[pltpu.SemaphoreType.DMA((PMAX,))],
        ),
        compiler_params=params(),
        cost_estimate=pl.CostEstimate(
            flops=0, bytes_accessed=2 * 8 * BLOCK * PAIR * 2, transcendentals=0
        ),
        name=f"pack_share_{g}",
    )(table, *buffers)


def pack_relay(cores, caps, h, g, ctrl, far, left, right):
    any_spec = pl.BlockSpec(memory_space=pl.ANY)
    return pl.pallas_call(
        lambda *refs: relay_kernel(cores, caps, h, *refs),
        out_shape=pages_shape(2 * caps.relay),
        grid_spec=pltpu.PrefetchScalarGridSpec(
            num_scalar_prefetch=1,
            grid=(1,),
            in_specs=[any_spec] * 3,
            out_specs=any_spec,
            scratch_shapes=[pltpu.SemaphoreType.DMA((2,))],
        ),
        compiler_params=params(),
        cost_estimate=pl.CostEstimate(
            flops=0, bytes_accessed=4 * caps.relay * BLOCK * PAIR * 2, transcendentals=0
        ),
        name=f"pack_relay_{g}",
    )(ctrl, far, left, right)


def after(value, *earlier):
    return lax.optimization_barrier((value, *earlier))[0]


def line_attend(wide, cores, caps, ctrl, table, queries, resp_kv, pool, weight):
    heads = resp_kv.shape[1] // PAIR
    share = weight.shape[1] // 2

    def hop(x, moves):
        pairs = [(a * cores + c, b * cores + c) for a, b in moves for c in range(cores)]
        return lax.ppermute(x, "wide", pairs)

    swap = [(d, d // cores * cores + (cores - 1 - d % cores)) for d in range(wide)]
    groups = [[g] for g in range(heads)]

    def spread(right, left, far):
        return (
            hop(right, [(0, 1), (1, 2), (2, 3)]),
            hop(left, [(3, 2), (2, 1), (1, 0)]),
            hop(far, [(0, 2), (3, 1)]),
        )

    past = Caps(1, 1, 0)

    def past_the_end(ctrl, pool):
        skip = (caps.near, caps.near, caps.far)
        return spread(*pack_send(wide, cores, None, past, skip, ctrl, pool)[0])

    def nothing(ctrl, pool):
        return (jnp.zeros((past.near * BLOCK, pool.shape[1]), pool.dtype),) * 3

    extra = list(lax.cond(table[OVER_AT] == 1, past_the_end, nothing, ctrl, pool))

    def exchange(h, g, held, plan):
        shared = pack_share(cores, caps, h, g, plan, held + extra)
        return held + [lax.ppermute(shared, "wide", swap)] + extra

    partner = lax.ppermute(pool, "wide", swap)
    both = list(range(RB_DEV))
    spreads, held, states = {}, {}, {}

    def relay(g, plan):
        sends = pack_send(wide, cores, [groups[g]], caps, (0, 0, 0), ctrl, pool)
        left, right, far = spread(*sends[0])
        onward = pack_relay(cores, caps, 0, g, plan, far, left, right)
        held[g] = [pool, left, right, far, hop(onward, [(2, 3), (1, 0)])]
        return onward

    def begin(first, amount):
        state = attend(
            "start", amount, first, (0, 0), both, caps, table, queries, resp_kv, [pool, partner]
        )
        for n in range(amount):
            states[first + n] = (state, n)
        return state

    def finish(g, blocks, plan, buffers, summed):
        state, n = states[g]
        return attend(
            "finish", 1, g, (0, n), blocks, caps, plan, queries, state, buffers,
            weight, share, summed, g == heads - 1,
        )

    parts, summed, plan = [], None, table
    split = max(heads - 2, 0)
    waits = after(ctrl, extra[0], begin(0, heads - heads // 2))
    relay(0, waits)
    waits = after(ctrl, begin(heads - heads // 2, heads // 2)) if heads > 1 else ctrl
    for g in range(split):
        onward = relay(g + 1, waits)
        buffers = exchange(0, g, held[g], after(table, onward))
        attended, summed = finish(g, both, table, buffers, summed)
        parts.append(attended)
        waits = after(ctrl, attended)
    ends, theirs, exchanged = {}, [], {}
    for b in both:
        total = summed
        for g in range(split, heads):
            if b == 0:
                if g + 1 < heads:
                    plan = after(table, relay(g + 1, waits))
                exchanged[g] = exchange(0, g, held[g], plan)
                plan = table
            elif g == split:
                plan = after(table, ends[0, heads - 1])
            ends[b, g], total = finish(g, [b], plan, exchanged[g], total)
            plan = after(table, ends[b, g])
        theirs.append(total)
    for g in range(split, heads):
        parts.append(jnp.concatenate([ends[b, g] for b in both], axis=0))
    return parts, theirs


def project_kernel(at, *refs):
    parts, weight, out = refs[:-2], refs[-2], refs[-1]
    total, row = None, 0
    for part in parts:
        end = row + part.shape[1]
        term = jnp.dot(part[...], weight[row:end, :], preferred_element_type=jnp.float32)
        total, row = term if total is None else total + term, end
    out[...] = total.astype(jnp.bfloat16)


def project(parts, weight, first_column, columns):
    tokens = parts[0].shape[0]
    tile = math.gcd(columns, 512)
    assert weight.shape[1] % tile == 0
    at = jnp.reshape(first_column // tile, (1,)).astype(jnp.int32)
    return pl.pallas_call(
        project_kernel,
        out_shape=jax.ShapeDtypeStruct((tokens, columns), jnp.bfloat16),
        grid_spec=pltpu.PrefetchScalarGridSpec(
            num_scalar_prefetch=1,
            grid=(columns // tile,),
            in_specs=[pl.BlockSpec(part.shape, lambda i, at: (0, 0)) for part in parts]
            + [pl.BlockSpec((weight.shape[0], tile), lambda i, at: (0, at[0] + i))],
            out_specs=pl.BlockSpec((tokens, tile), lambda i, at: (0, i)),
        ),
        compiler_params=params(),
        cost_estimate=pl.CostEstimate(
            flops=2 * tokens * columns * weight.shape[0],
            bytes_accessed=2 * columns * weight.shape[0],
            transcendentals=0,
        ),
        name="project",
    )(at, *parts, weight)


def local(
    queries, resp_kv, prefix_pool, out_weight, pre_len, prompt_blocks, prompt_owner, resp_seg
):
    wide, groups = lax.axis_size("wide"), lax.axis_size("tp") * lax.axis_size("sub")
    cores = 2 // lax.axis_size("sub")
    heads = resp_kv.shape[1] // PAIR
    me = lax.axis_index("wide").astype(jnp.int32)
    group = lax.axis_index("tp") * lax.axis_size("sub") + lax.axis_index("sub")
    where = jnp.stack([me, (1 - group).astype(jnp.int32)])
    ctrl = jnp.concatenate([pre_len, prompt_blocks, prompt_owner, resp_seg, where])
    columns = out_weight.shape[1]
    share = columns // groups
    if wide == 8 and cores == 2 and groups == 2:
        table = make_plan(wide, cores, True, ctrl)

        parts, theirs = line_attend(
            wide, cores, CAPS, ctrl, table, queries, resp_kv, prefix_pool, out_weight
        )
        axis = "tp" if lax.axis_size("tp") == 2 else "sub"
        arrived = [lax.ppermute(terms, axis, [(0, 1), (1, 0)]) for terms in theirs]
        half = share // 2
        mine = [
            project(parts, out_weight, group * share, half),
            project(parts, out_weight, after(group, arrived[0]) * share + half, half),
        ]
        mine = jnp.concatenate(mine, axis=1)
        arrived = jnp.concatenate(arrived, axis=0)
        return (mine.astype(jnp.float32) + arrived.astype(jnp.float32)).astype(jnp.bfloat16)
    table = make_plan(wide, cores, False, ctrl)
    buffers = [lax.all_gather(prefix_pool, "wide", axis=0, tiled=True)]
    blocks = list(range(RB_DEV))
    parts = [
        attend("whole", 1, g, (0, 0), blocks, CAPS, table, queries, resp_kv, buffers)
        for g in range(heads)
    ]
    terms = project(parts, out_weight, jnp.int32(0), columns)
    return lax.psum_scatter(terms, ("tp", "sub"), scatter_dimension=1, tiled=True)


def solution(mesh):
    return jax.shard_map(
        local,
        mesh=mesh,
        in_specs=(
            P(("parts", "wide"), ("tp", "sub")),
            P(("parts", "wide"), ("tp", "sub")),
            P(("parts", "wide"), ("tp", "sub")),
            P(("tp", "sub"), None),
            P("parts"),
            P("parts"),
            P("parts"),
            P(("parts", "wide")),
        ),
        out_specs=P(("parts", "wide"), ("tp", "sub")),
        check_vma=False,
    )
```

```python
import math

import jax
import jax.numpy as jnp
from jax import lax
from jax.experimental import pallas as pl
from jax.experimental.pallas import tpu as pltpu
from jax.sharding import PartitionSpec as P

HD = 128
BLOCK = 128
RB_DEV = 2
PROMPTS = 4
PMAX = 16
GROUP = 8
PAIR = 2 * HD
WIDTH = GROUP * HD
ROWS = 512
SPAN = 4
NEG_LARGE = -1e30
SCALE = math.log2(math.e) / math.sqrt(HD)
VMEM_BYTES = 48 * 1024 * 1024

LEN_AT, BLOCKS_AT, OWNER_AT, SEG_AT, ME_AT, OTHER_AT = 0, 4, 8, 12, 14, 15


def params():
    return pltpu.CompilerParams(vmem_limit_bytes=VMEM_BYTES)


def as_int(flag):
    return jnp.where(flag, 1, 0)


class Layout:
    def __init__(self, ctrl, wide, cores):
        self.ctrl, self.wide, self.cores = ctrl, wide, cores
        self.stride = (PMAX + wide - 1) // wide
        self.me = ctrl[ME_AT]
        self.z, self.core = self.div(self.me, cores), self.mod(self.me, cores)
        ends, total = [], 0
        for p in range(PROMPTS):
            total = total + ctrl[BLOCKS_AT + p] + (RB_DEV - 1)
            ends.append(total)
        self.ends = ends

    def mod(self, value, size):
        return value & (size - 1) if size & (size - 1) == 0 else lax.rem(value, size)

    def div(self, value, size):
        if size & (size - 1) == 0:
            return lax.shift_right_logical(value, size.bit_length() - 1)
        return lax.div(value, size)

    def prompt_of(self, block):
        return sum(as_int(block >= end) for end in self.ends[:-1])

    def first_of(self, chip):
        return self.prompt_of(chip * self.cores * RB_DEV)

    def last_of(self, chip):
        return self.prompt_of((chip + 1) * self.cores * RB_DEV - 1)

    def length(self, p):
        return self.ctrl[LEN_AT + p]

    def held_by(self, p, j):
        return self.mod(self.ctrl[OWNER_AT + p] + j, self.wide)

    def held(self, p, who):
        first = self.mod(who - self.ctrl[OWNER_AT + p] + self.wide, self.wide)
        return sum(as_int(first + k * self.wide < self.length(p)) for k in range(self.stride))

    def listed(self, which, rank, room):
        return jnp.where(
            rank < room, which * CODE + rank, (EXTRA + which - 1) * CODE + rank - room
        )

    def in_plane(self, p, j, sums):
        who = self.held_by(p, j)
        chip = self.div(who, self.cores)
        gap = chip - self.z
        k = self.div(j, self.wide)
        at = who * SUMS
        down = sums[at + PROMPTS] - sums[at + p + 1] + k
        up = sums[at + p] + k
        near_down = down - jnp.where(
            chip == 0, sums[at + PROMPTS] - sums[at + self.last_of(1) + 1], 0
        )
        near_up = up - jnp.where(chip == 3, sums[at + self.first_of(2)], 0)
        far = jnp.where(gap < 0, down, up)
        two = (gap == 2) | (gap == -2)
        direct = two & ((self.z == 1) | (self.z == 2))
        code = jnp.where(two, 5 * CODE, 4 * CODE) + far
        code = jnp.where(direct, self.listed(3, far, CAPS.far), code)
        code = jnp.where(gap == 1, self.listed(2, near_up, CAPS.near), code)
        code = jnp.where(gap == -1, self.listed(1, near_down, CAPS.near), code)
        return jnp.where(gap == 0, p * self.stride + k, code)


CODE = 256
SHARED = 6
EXTRA = 7
SUMS = 8
SLOT_AT, SHARE_AT, SHARES_AT, LENGTH_AT, BASE_AT, LOW_AT, THEIRS_AT, OVER_AT, TABLE = (
    0, 32, 50, 52, 54, 56, 58, 59, 64
)


class Caps:
    def __init__(self, near, far, relay):
        self.near, self.far, self.relay = near, far, relay


CAPS = Caps(5, 5, 4)


def needs(lay, sums, cores):
    first, last = [lay.first_of(c) for c in range(4)], [lay.last_of(c) for c in range(4)]
    near, far = jnp.int32(0), jnp.int32(0)
    for core in range(cores):

        def held(chip, low, high, core=core):
            at = (chip * cores + core) * SUMS
            return sums[at + high + 1] - sums[at + low]

        top = PROMPTS - 1
        edge = [held(1, 0, last[0]), held(2, first[3], top)]
        for amount in edge + [
            held(0, first[1], last[1]),
            held(1, first[2], top),
            held(2, 0, last[1]),
            held(3, first[2], last[2]),
        ]:
            near = jnp.maximum(near, amount)
        for amount in (held(0, first[2], top), held(3, 0, last[1])):
            far = jnp.maximum(far, amount)
    return near, far


def plan_kernel(wide, cores, line, ctrl, table, sums):
    lay = Layout(ctrl, wide, cores)
    half = PMAX // cores
    table[THEIRS_AT] = ctrl[OTHER_AT]
    table[OVER_AT] = 0
    if line:

        def tally(who, carry):
            total = jnp.int32(0)
            for p in range(PROMPTS):
                sums[who * SUMS + p] = total
                total = total + lay.held(p, who)
            sums[who * SUMS + PROMPTS] = total
            return carry

        lax.fori_loop(0, wide, tally, 0)
        near, far = needs(lay, sums, cores)
        over = (near > CAPS.near) | (far > CAPS.far)
        table[OVER_AT] = as_int(over)

    def prompts_of(device):
        return [lay.prompt_of(device * RB_DEV + b) for b in range(RB_DEV)]

    mine = prompts_of(lay.me)
    same = mine[0] == mine[1]
    joined = same & (ctrl[SEG_AT] == ctrl[SEG_AT + 1])
    for slot in range(RB_DEV):
        p = mine[slot]
        count = lay.length(p)
        table[LENGTH_AT + slot] = count
        if slot == 1:
            count = jnp.where(same, 0, count)
        table[BASE_AT + slot] = jnp.where(same, 0, PMAX) if slot else 0
        table[LOW_AT + slot] = jnp.where(joined, 0, BLOCK) if slot else 0

        def place(j, carry, slot=slot, p=p):
            who = lay.held_by(p, j)
            code = (who * PROMPTS + p) * lay.stride + lay.div(j, wide)
            if line:
                shared = slot * half + lay.div(j, cores)
                passed = jnp.where(
                    lay.mod(who, cores) == lay.core,
                    lay.in_plane(p, j, sums),
                    SHARED * CODE + shared,
                )
                code = passed
            table[SLOT_AT + slot * PMAX + j] = code
            return carry

        lax.fori_loop(0, count, place, 0)
    if not line:
        return
    theirs = prompts_of(lay.z * cores + (cores - 1 - lay.core))
    for slot in range(RB_DEV):
        p = theirs[slot]
        shift = lay.mod(lay.core - ctrl[OWNER_AT + p] + wide, cores)
        count = lay.div(lay.length(p) - shift + cores - 1, cores)
        if slot == 1:
            count = jnp.where(theirs[1] == theirs[0], 0, count)
        table[SHARES_AT + slot] = count

        def share(i, carry, slot=slot, p=p, shift=shift):
            table[SHARE_AT + slot * half + i] = lay.in_plane(p, i * cores + shift, sums)
            return carry

        lax.fori_loop(0, count, share, 0)


def make_plan(wide, cores, line, ctrl):
    return pl.pallas_call(
        lambda *refs: plan_kernel(wide, cores, line, *refs),
        out_shape=jax.ShapeDtypeStruct((TABLE,), jnp.int32),
        in_specs=[pl.BlockSpec(memory_space=pltpu.SMEM)],
        out_specs=pl.BlockSpec(memory_space=pltpu.SMEM),
        scratch_shapes=[pltpu.SMEM((wide * SUMS,), jnp.int32)],
        compiler_params=params(),
        name="plan",
    )(ctrl)


def spot(ref, page):
    return ref.at[pl.ds(pl.multiple_of(page * BLOCK, BLOCK), BLOCK), :]


def page_at(buffer, page, column):
    rows = pl.ds(pl.multiple_of(page * BLOCK, BLOCK), BLOCK)
    return buffer.at[rows, pl.ds(column if buffer.shape[1] > PAIR else 0, PAIR)]


def start_page(buffers, code, column, target, sem):
    which = lax.shift_right_logical(code, CODE.bit_length() - 1)
    page = code & (CODE - 1)
    for i, buffer, offset in buffers:

        @pl.when(which == i)
        def _(buffer=buffer, offset=offset):
            source = page_at(buffer, page + offset, column)
            pltpu.make_async_copy(source, target, sem).start()


def wait_page(target, sem):
    pltpu.make_async_copy(target, target, sem).wait()


def send_kernel(wide, cores, groups, caps, skip, planned, ctrl, pool, *refs):
    if planned:
        *outs, table, sems, sums = refs
    else:
        *outs, sems = refs
    rooms = (caps.near, caps.near, caps.far)
    lay = Layout(ctrl, wide, cores)
    z, last = lay.z, wide // cores - 1
    held = [lay.held(p, lay.me) for p in range(PROMPTS)]

    def above(p, top):
        return sum([jnp.where(o <= top, held[o], 0) for o in range(p + 1, PROMPTS)], jnp.int32(0))

    def below(p, low):
        return sum([jnp.where(o >= low, held[o], 0) for o in range(p)], jnp.int32(0))

    near_top = jnp.where(z == 0, lay.last_of(1), PROMPTS - 1)
    near_low = jnp.where(z == last, lay.first_of(2), 0)
    first_up, last_down = lay.first_of(z + 1), lay.last_of(z - 1)
    first_two, last_one = lay.first_of(2), lay.last_of(1)
    plans = []
    for p in range(PROMPTS):
        right = (z < last) & (p >= first_up) & (p <= near_top)
        left = (z > 0) & (p >= near_low) & (p <= last_down)
        far_up = (z == 0) & (p >= first_two)
        far_down = (z == last) & (p <= last_one)
        ranks = (above(p, near_top), below(p, near_low), above(p, PROMPTS - 1), below(p, 0))
        for k in range(lay.stride):
            for lane, wanted, rank in zip((0, 1, 2, 2), (right, left, far_up, far_down), ranks):
                at = rank + k - skip[lane]
                fits = (k < held[p]) & (at >= 0) & (at < rooms[lane])
                plans.append((wanted & fits, p * lay.stride + k, lane, at))

    def copies(plan):
        _, page, lane, rank = plan
        if groups is None:
            return [
                pltpu.make_async_copy(
                    spot(pool, page), spot(outs[lane], rank), sems.at[lane, page, 0]
                )
            ]
        return [
            pltpu.make_async_copy(
                page_at(pool, page, g * PAIR),
                spot(outs[n * 3 + lane], h * rooms[lane] + rank),
                sems.at[lane, page, n * len(groups[0]) + h],
            )
            for n, group in enumerate(groups)
            for h, g in enumerate(group)
        ]

    for plan in plans:

        @pl.when(plan[0])
        def _(plan=plan):
            for copy in copies(plan):
                copy.start()

    if planned:
        plan_kernel(wide, cores, True, ctrl, table, sums)
    for plan in plans:

        @pl.when(plan[0])
        def _(plan=plan):
            for copy in copies(plan):
                copy.wait()


def relay_kernel(cores, caps, h, ctrl, far, left, right, out, sems):
    rows = caps.relay * BLOCK

    def copy(source, room, section):
        target = out.at[pl.ds(section * rows, rows), :]
        return pltpu.make_async_copy(
            source.at[pl.ds(h * room * BLOCK, rows), :], target, sems.at[section]
        )

    inner = ctrl[ME_AT] == 2 * cores
    for core in range(1, cores):
        inner = inner | (ctrl[ME_AT] == 2 * cores + core)
    copy(far, caps.far, 0).start()
    pl.when(inner)(lambda: copy(left, caps.near, 1).start())
    pl.when(jnp.logical_not(inner))(lambda: copy(right, caps.near, 1).start())
    copy(far, caps.far, 0).wait()
    copy(left, caps.near, 1).wait()


def numbered(refs, caps, h):
    if len(refs) == 1:
        return [(0, refs[0], 0)]
    offsets = (0, h * caps.near, h * caps.near, h * caps.far, 0)
    found = list(zip(range(5), refs[:5], offsets)) + [(5, refs[4], caps.relay)]
    if len(refs) == 7:
        found.append((SHARED, refs[5], 0))
    return found + [(EXTRA + i, refs[-1], i) for i in range(3)]


def share_kernel(cores, caps, h, g, table, *refs):
    out, sems = refs[-2:]
    half = PMAX // cores
    buffers = numbered(refs[:-2], caps, h)
    for slot in range(RB_DEV):

        def begin(i, carry, slot=slot):
            at = slot * half + i
            start_page(buffers, table[SHARE_AT + at], g * PAIR, spot(out, at), sems.at[at])
            return carry

        lax.fori_loop(0, table[SHARES_AT + slot], begin, 0)
    for slot in range(RB_DEV):

        def finish(i, carry, slot=slot):
            at = slot * half + i
            wait_page(spot(out, at), sems.at[at])
            return carry

        lax.fori_loop(0, table[SHARES_AT + slot], finish, 0)


def attend_kernel(group, first, blocks, caps, carried, project, table, queries, own, *refs):
    refs = list(refs)
    weight = refs.pop(0) if project else None
    summed = refs.pop(0) if carried else None
    sems, stacked = refs.pop(), refs.pop()
    slab = refs.pop() if project else None
    store = refs.pop()
    terms = refs.pop() if project else None
    out = refs.pop()
    heads, room = len(group), len(blocks) * PMAX

    def region(i):
        if i == 0:
            return 0, table[LENGTH_AT + blocks[0]]
        base = table[BASE_AT + blocks[i]]
        return base, jnp.where(base == 0, 0, table[LENGTH_AT + blocks[i]])

    for h, g in enumerate(group):
        buffers = numbered(refs, caps, first + h)
        for i, b in enumerate(blocks):
            base, count = region(i)
            codes = SLOT_AT + table[BASE_AT + b]

            def begin(j, carry, h=h, g=g, buffers=buffers, base=base, codes=codes):
                at = h * room + base + j
                target, sem = spot(store, at), sems.at[at]
                start_page(buffers, table[codes + j], g * PAIR, target, sem)
                return carry

            lax.fori_loop(0, count, begin, 0)
            length = table[LENGTH_AT + b]

            def clear(j, carry, h=h, base=base):
                rows = pl.ds(pl.multiple_of((h * room + base + j) * BLOCK, BLOCK), BLOCK)
                store[rows, :] = jnp.zeros((BLOCK, PAIR), jnp.bfloat16)
                return carry

            lax.fori_loop(length, (length + SPAN - 1) & -SPAN, clear, 0)
    if project:
        share = slab.shape[1]
        theirs = pl.multiple_of(table[THEIRS_AT] * share, share)
        fetch = pltpu.make_async_copy(
            weight.at[pl.ds(group[0] * WIDTH, heads * WIDTH), pl.ds(theirs, share)],
            slab,
            sems.at[heads * room],
        )
        fetch.start()

    def one_block(h, i, b, base, count):
        tokens = pl.ds(pl.multiple_of(i * BLOCK, BLOCK), BLOCK)

        def columns(width, extra=0):
            return pl.ds(pl.multiple_of(h * width + extra, HD), min(width, HD))

        for e in range(GROUP):
            stacked[e * BLOCK : (e + 1) * BLOCK, :] = queries[tokens, columns(WIDTH, e * HD)]
        base = h * room + base

        def finish(j, carry):
            wait_page(spot(store, base + j), sems.at[base + j])
            return carry

        lax.fori_loop(0, count, finish, 0)
        length = table[LENGTH_AT + b]
        span = RB_DEV * BLOCK
        row = lax.broadcasted_iota(jnp.int32, (ROWS, span), 0) & (BLOCK - 1)
        key = lax.broadcasted_iota(jnp.int32, (ROWS, span), 1)
        own_mask = (key <= row + b * BLOCK) & (key >= table[LOW_AT + b])

        def run(spans):
            wide_key = lax.broadcasted_iota(jnp.int32, (ROWS, SPAN * BLOCK), 1)
            last_mask = wide_key < (length - (spans - 1) * SPAN) * BLOCK
            pieces = [(own[:, columns(PAIR)], own[:, columns(PAIR, HD)])]
            for t in range(spans):
                at = pl.multiple_of((base + t * SPAN) * BLOCK, BLOCK)
                piece = store[pl.ds(at, SPAN * BLOCK), :]
                pieces.append((piece[:, :HD], piece[:, HD:]))

            def score(r, t):
                scores = lax.dot_general(
                    stacked[r * ROWS : (r + 1) * ROWS, :],
                    pieces[t][0],
                    (((1,), (1,)), ((), ())),
                    preferred_element_type=jnp.float32,
                )
                if t == 0:
                    return jnp.where(own_mask, scores, NEG_LARGE)
                if t == spans:
                    return jnp.where(last_mask, scores, NEG_LARGE)
                return scores

            def highest(scores, sofar):
                for n in range(0, scores.shape[1], HD):
                    part = scores[:, n : n + HD]
                    sofar = part if sofar is None else jnp.maximum(sofar, part)
                return sofar

            def blend(scores, top, t):
                spread = jnp.concatenate([top] * (scores.shape[1] // HD), axis=1)
                weights = jnp.exp2((scores - spread) * SCALE).astype(jnp.bfloat16)
                values = pieces[t][1]
                values = jnp.concatenate([values, jnp.ones_like(values)], axis=1)
                return jnp.dot(weights, values, preferred_element_type=jnp.float32)

            chunks, ahead, peak = GROUP * BLOCK // ROWS, [], None
            for t in range(spans + 1):
                ahead.append(score(0, t))
                peak = highest(ahead[-1], peak)
            for r in range(chunks):
                now, ahead = ahead, []
                top = jnp.broadcast_to(jnp.max(peak, axis=1, keepdims=True), (ROWS, HD))
                total, peak = None, None
                for t in range(spans + 1):
                    if r + 1 < chunks:
                        ahead.append(score(r + 1, t))
                        peak = highest(ahead[-1], peak)
                    blended = blend(now[t], top, t)
                    total = blended if total is None else total + blended
                mean = (total[:, :HD] / total[:, HD:]).astype(jnp.bfloat16)
                for e in range(ROWS // BLOCK):
                    at = columns(WIDTH, (r * (ROWS // BLOCK) + e) * HD)
                    out[tokens, at] = mean[e * BLOCK : (e + 1) * BLOCK, :]

        spans = lax.shift_right_logical(length + SPAN - 1, SPAN.bit_length() - 1)
        for n in range(1, PMAX // SPAN + 1):
            pl.when(spans == n)(lambda n=n: run(n))

    def step(n, carry):
        if len(blocks) == 1:
            one_block(n, 0, blocks[0], *region(0))
            return carry
        h, i = lax.shift_right_logical(n, 1), n & 1
        base = jnp.where(i == 0, 0, region(1)[0])
        one_block(h, i, i, base, jnp.where(i == 0, region(0)[1], region(1)[1]))
        return carry

    lax.fori_loop(0, heads * len(blocks), step, 0)
    if project:
        fetch.wait()
        attended = out[...]
        width = math.gcd(share, 512)
        for n in range(0, share, width):
            term = jnp.dot(attended, slab[:, n : n + width], preferred_element_type=jnp.float32)
            if carried:
                term = term + summed[:, n : n + width]
            terms[:, n : n + width] = term.astype(terms.dtype)


def attend(
    group, first, blocks, last, caps, table, queries, resp_kv, buffers, weight=None, share=0, summed=None
):
    tokens, heads = len(blocks) * BLOCK, len(group)
    at = blocks[0] // len(blocks)
    project, carried = weight is not None, summed is not None
    any_spec = pl.BlockSpec(memory_space=pl.ANY)
    whole = pl.BlockSpec((tokens, share), lambda i, c: (0, 0))
    out_shape = [jax.ShapeDtypeStruct((tokens, heads * WIDTH), jnp.bfloat16)]
    out_specs = [pl.BlockSpec((tokens, heads * WIDTH), lambda i, c: (0, 0))]
    operands, in_specs = [], []
    scratch = [pltpu.VMEM((heads * len(blocks) * PMAX * BLOCK, PAIR), jnp.bfloat16)]
    if project:
        operands, in_specs = [weight], [any_spec]
        kept = jnp.bfloat16 if last else jnp.float32
        out_shape.append(jax.ShapeDtypeStruct((tokens, share), kept))
        out_specs.append(whole)
        scratch.append(pltpu.VMEM((heads * WIDTH, share), jnp.bfloat16))
    if carried:
        operands = operands + [summed]
        in_specs = in_specs + [pl.BlockSpec((tokens, share), lambda i, c: (at, 0))]
    column = group[0] // heads
    return pl.pallas_call(
        lambda *refs: attend_kernel(group, first, blocks, caps, carried, project, *refs),
        out_shape=out_shape,
        grid_spec=pltpu.PrefetchScalarGridSpec(
            num_scalar_prefetch=1,
            grid=(1,),
            in_specs=[
                pl.BlockSpec((tokens, heads * WIDTH), lambda i, c: (at, column)),
                pl.BlockSpec((RB_DEV * BLOCK, heads * PAIR), lambda i, c: (0, column)),
            ]
            + in_specs
            + [any_spec] * len(buffers),
            out_specs=out_specs,
            scratch_shapes=scratch
            + [
                pltpu.VMEM((GROUP * BLOCK, HD), jnp.bfloat16),
                pltpu.SemaphoreType.DMA((heads * len(blocks) * PMAX + 1,)),
            ],
        ),
        compiler_params=params(),
        cost_estimate=pl.CostEstimate(
            flops=2 * 2 * tokens * heads * WIDTH * 18 * BLOCK * 2,
            bytes_accessed=heads * (4 * tokens * WIDTH + PMAX * BLOCK * PAIR * 2 + share * WIDTH * 2),
            transcendentals=tokens * heads * GROUP * 18 * BLOCK,
        ),
        name="attend_heads_" + "_".join(map(str, group)) + "_blocks_" + "_".join(map(str, blocks)),
    )(table, queries, resp_kv, *operands, *buffers)


def pages_shape(count):
    return jax.ShapeDtypeStruct((count * BLOCK, PAIR), jnp.bfloat16)


def pack_send(wide, cores, groups, caps, skip, ctrl, pool, planned=False):
    any_spec = pl.BlockSpec(memory_space=pl.ANY)
    pages = PROMPTS * ((PMAX + wide - 1) // wide)
    rooms = (caps.near, caps.near, caps.far)
    if groups is None:
        shapes = [jax.ShapeDtypeStruct((n * BLOCK, pool.shape[1]), jnp.bfloat16) for n in rooms]
    else:
        shapes = [pages_shape(n * len(group)) for group in groups for n in rooms]
    heads = 1 if groups is None else sum(map(len, groups))
    out_specs = [any_spec] * len(shapes)
    scratch = [pltpu.SemaphoreType.DMA((3, pages, heads))]
    if planned:
        shapes = shapes + [jax.ShapeDtypeStruct((TABLE,), jnp.int32)]
        out_specs = out_specs + [pl.BlockSpec(memory_space=pltpu.SMEM)]
        scratch.append(pltpu.SMEM((wide * SUMS,), jnp.int32))
    return pl.pallas_call(
        lambda *refs: send_kernel(wide, cores, groups, caps, skip, planned, *refs),
        out_shape=shapes,
        grid_spec=pltpu.PrefetchScalarGridSpec(
            num_scalar_prefetch=1,
            grid=(1,),
            in_specs=[pl.BlockSpec(pool.shape, lambda i, c: (0, 0))],
            out_specs=out_specs,
            scratch_shapes=scratch,
        ),
        compiler_params=params(),
        cost_estimate=pl.CostEstimate(
            flops=0, bytes_accessed=2 * 12 * BLOCK * PAIR * 2 * heads, transcendentals=0
        ),
        name="pack_extra" if groups is None else f"pack_send_{groups[0][0]}",
    )(ctrl, pool)


def pack_share(cores, caps, h, g, table, buffers):
    any_spec = pl.BlockSpec(memory_space=pl.ANY)
    return pl.pallas_call(
        lambda *refs: share_kernel(cores, caps, h, g, *refs),
        out_shape=pages_shape(PMAX),
        grid_spec=pltpu.PrefetchScalarGridSpec(
            num_scalar_prefetch=1,
            grid=(1,),
            in_specs=[any_spec] * len(buffers),
            out_specs=any_spec,
            scratch_shapes=[pltpu.SemaphoreType.DMA((PMAX,))],
        ),
        compiler_params=params(),
        cost_estimate=pl.CostEstimate(
            flops=0, bytes_accessed=2 * 8 * BLOCK * PAIR * 2, transcendentals=0
        ),
        name=f"pack_share_{g}",
    )(table, *buffers)


def pack_relay(cores, caps, h, g, ctrl, far, left, right):
    any_spec = pl.BlockSpec(memory_space=pl.ANY)
    return pl.pallas_call(
        lambda *refs: relay_kernel(cores, caps, h, *refs),
        out_shape=pages_shape(2 * caps.relay),
        grid_spec=pltpu.PrefetchScalarGridSpec(
            num_scalar_prefetch=1,
            grid=(1,),
            in_specs=[any_spec] * 3,
            out_specs=any_spec,
            scratch_shapes=[pltpu.SemaphoreType.DMA((2,))],
        ),
        compiler_params=params(),
        cost_estimate=pl.CostEstimate(
            flops=0, bytes_accessed=4 * caps.relay * BLOCK * PAIR * 2, transcendentals=0
        ),
        name=f"pack_relay_{g}",
    )(ctrl, far, left, right)


def after(value, *earlier):
    return lax.optimization_barrier((value, *earlier))[0]


def line_attend(wide, cores, caps, ctrl, queries, resp_kv, pool, weight):
    heads = resp_kv.shape[1] // PAIR
    share = weight.shape[1] // 2

    def hop(x, moves):
        pairs = [(a * cores + c, b * cores + c) for a, b in moves for c in range(cores)]
        return lax.ppermute(x, "wide", pairs)

    swap = [(d, d // cores * cores + (cores - 1 - d % cores)) for d in range(wide)]

    def spread(right, left, far):
        return (
            hop(right, [(0, 1), (1, 2), (2, 3)]),
            hop(left, [(3, 2), (2, 1), (1, 0)]),
            hop(far, [(0, 2), (3, 1)]),
        )

    past = Caps(1, 1, 0)

    def past_the_end(ctrl, pool):
        skip = (caps.near, caps.near, caps.far)
        lists = pack_send(wide, cores, None, past, skip, ctrl, pool)
        return jnp.concatenate(spread(*lists), axis=0)

    def nothing(ctrl, pool):
        return jnp.zeros((3 * past.near * BLOCK, pool.shape[1]), pool.dtype)

    both = list(range(RB_DEV))
    *lists, table = pack_send(wide, cores, [[0]], caps, (0, 0, 0), ctrl, pool, True)
    sends, spreads, held, parts = {0: lists}, {}, {}, []

    def relay(g, plan):
        spreads[g] = spread(*sends[g])
        if g + 1 < heads:
            sends[g + 1] = pack_send(wide, cores, [[g + 1]], caps, (0, 0, 0), ctrl, pool)
            plan = after(plan, sends[g + 1][0])
        left, right, far = spreads[g]
        onward = pack_relay(cores, caps, 0, g, plan, far, left, right)
        held[g] = [pool, left, right, far, hop(onward, [(2, 3), (1, 0)])]
        return onward

    onward = relay(0, ctrl)
    over = after(table, onward)[OVER_AT] == 1
    extra = lax.cond(over, past_the_end, nothing, ctrl, pool)

    def exchange(g, plan):
        shared = pack_share(cores, caps, 0, g, plan, held[g] + [extra])
        return held[g] + [lax.ppermute(shared, "wide", swap), extra]

    for g in range(heads - 1):
        onward = relay(g + 1, after(ctrl, parts[-1]) if parts else ctrl)
        buffers = exchange(g, after(table, onward))
        parts += attend([g], 0, both, False, caps, table, queries, resp_kv, buffers)
    last, summed = heads - 1, None
    buffers = exchange(last, after(table, parts[-1]) if parts else table)
    if parts:
        theirs = table[THEIRS_AT] * share
        summed = project(parts, weight, theirs, share, jnp.float32)
    ends, terms, plan = [], [], table
    for b in both:
        attended, term = attend(
            [last], 0, [b], True, caps, plan, queries, resp_kv, buffers, weight, share, summed
        )
        ends.append(attended)
        terms.append(term)
        plan = after(table, attended)
    return parts + [jnp.concatenate(ends, axis=0)], terms


def project_kernel(at, *refs):
    parts, weight, out = refs[:-2], refs[-2], refs[-1]
    total, row = None, 0
    for part in parts:
        end = row + part.shape[1]
        term = jnp.dot(part[...], weight[row:end, :], preferred_element_type=jnp.float32)
        total, row = term if total is None else total + term, end
    out[...] = total.astype(out.dtype)


def project(parts, weight, first_column, columns, kept=jnp.bfloat16):
    tokens = parts[0].shape[0]
    rows = sum(part.shape[1] for part in parts)
    tile = math.gcd(columns, 512)
    assert weight.shape[1] % tile == 0
    at = jnp.reshape(first_column // tile, (1,)).astype(jnp.int32)
    return pl.pallas_call(
        project_kernel,
        out_shape=jax.ShapeDtypeStruct((tokens, columns), kept),
        grid_spec=pltpu.PrefetchScalarGridSpec(
            num_scalar_prefetch=1,
            grid=(columns // tile,),
            in_specs=[pl.BlockSpec(part.shape, lambda i, at: (0, 0)) for part in parts]
            + [pl.BlockSpec((rows, tile), lambda i, at: (0, at[0] + i))],
            out_specs=pl.BlockSpec((tokens, tile), lambda i, at: (0, i)),
        ),
        compiler_params=params(),
        cost_estimate=pl.CostEstimate(
            flops=4 * tokens * columns * rows,
            bytes_accessed=2 * columns * rows,
            transcendentals=0,
        ),
        name="project",
    )(at, *parts, weight)


def local(
    queries, resp_kv, prefix_pool, out_weight, pre_len, prompt_blocks, prompt_owner, resp_seg
):
    wide, groups = lax.axis_size("wide"), lax.axis_size("tp") * lax.axis_size("sub")
    cores = 2 // lax.axis_size("sub")
    heads = resp_kv.shape[1] // PAIR
    me = lax.axis_index("wide").astype(jnp.int32)
    group = lax.axis_index("tp") * lax.axis_size("sub") + lax.axis_index("sub")
    where = jnp.stack([me, (1 - group).astype(jnp.int32)])
    ctrl = jnp.concatenate([pre_len, prompt_blocks, prompt_owner, resp_seg, where])
    columns = out_weight.shape[1]
    share = columns // groups
    if wide == 8 and cores == 2 and groups == 2:
        parts, theirs = line_attend(
            wide, cores, CAPS, ctrl, queries, resp_kv, prefix_pool, out_weight
        )
        axis = "tp" if lax.axis_size("tp") == 2 else "sub"
        arrived = [lax.ppermute(terms, axis, [(0, 1), (1, 0)]) for terms in theirs]
        half = share // 2
        mine = [
            project(parts, out_weight, group * share, half),
            project(parts, out_weight, after(group, arrived[0]) * share + half, half),
        ]
        mine = jnp.concatenate(mine, axis=1)
        arrived = jnp.concatenate(arrived, axis=0)
        return (mine.astype(jnp.float32) + arrived.astype(jnp.float32)).astype(jnp.bfloat16)
    table = make_plan(wide, cores, False, ctrl)
    buffers = [lax.all_gather(prefix_pool, "wide", axis=0, tiled=True)]
    blocks = list(range(RB_DEV))
    parts = [
        attend([g], 0, blocks, False, CAPS, table, queries, resp_kv, buffers)[0] for g in range(heads)
    ]
    terms = project(parts, out_weight, jnp.int32(0), columns)
    return lax.psum_scatter(terms, ("tp", "sub"), scatter_dimension=1, tiled=True)


def solution(mesh):
    return jax.shard_map(
        local,
        mesh=mesh,
        in_specs=(
            P(("parts", "wide"), ("tp", "sub")),
            P(("parts", "wide"), ("tp", "sub")),
            P(("parts", "wide"), ("tp", "sub")),
            P(("tp", "sub"), None),
            P("parts"),
            P("parts"),
            P("parts"),
            P(("parts", "wide")),
        ),
        out_specs=P(("parts", "wide"), ("tp", "sub")),
        check_vma=False,
    )
```

```python
import math

import jax
import jax.numpy as jnp
from jax import lax
from jax.experimental import pallas as pl
from jax.experimental.pallas import tpu as pltpu
from jax.sharding import PartitionSpec as P

HD = 128
BLOCK = 128
RB_DEV = 2
PROMPTS = 4
PMAX = 16
GROUP = 8
PAIR = 2 * HD
WIDTH = GROUP * HD
ROWS = 512
SPAN = 4
NEG_LARGE = -1e30
SCALE = math.log2(math.e) / math.sqrt(HD)
VMEM_BYTES = 48 * 1024 * 1024
SMALL = pl.CostEstimate(flops=1 << 20, bytes_accessed=1 << 14, transcendentals=0)

LEN_AT, BLOCKS_AT, OWNER_AT, SEG_AT, ME_AT, OTHER_AT = 0, 4, 8, 12, 14, 15


def params():
    return pltpu.CompilerParams(vmem_limit_bytes=VMEM_BYTES)


def as_int(flag):
    return jnp.where(flag, 1, 0)


class Layout:
    def __init__(self, ctrl, wide, cores):
        self.ctrl, self.wide, self.cores = ctrl, wide, cores
        self.stride = (PMAX + wide - 1) // wide
        self.me = ctrl[ME_AT]
        self.z, self.core = self.div(self.me, cores), self.mod(self.me, cores)
        ends, total = [], 0
        for p in range(PROMPTS):
            total = total + ctrl[BLOCKS_AT + p] + (RB_DEV - 1)
            ends.append(total)
        self.ends = ends

    def mod(self, value, size):
        return value & (size - 1) if size & (size - 1) == 0 else lax.rem(value, size)

    def div(self, value, size):
        if size & (size - 1) == 0:
            return lax.shift_right_logical(value, size.bit_length() - 1)
        return lax.div(value, size)

    def prompt_of(self, block):
        return sum(as_int(block >= end) for end in self.ends[:-1])

    def first_of(self, chip):
        return self.prompt_of(chip * self.cores * RB_DEV)

    def last_of(self, chip):
        return self.prompt_of((chip + 1) * self.cores * RB_DEV - 1)

    def length(self, p):
        return self.ctrl[LEN_AT + p]

    def held_by(self, p, j):
        return self.mod(self.ctrl[OWNER_AT + p] + j, self.wide)

    def held(self, p, who):
        first = self.mod(who - self.ctrl[OWNER_AT + p] + self.wide, self.wide)
        return sum(as_int(first + k * self.wide < self.length(p)) for k in range(self.stride))

    def listed(self, which, rank, room):
        return jnp.where(
            rank < room, which * CODE + rank, (EXTRA + which - 1) * CODE + rank - room
        )

    def in_plane(self, p, j, sums):
        who = self.held_by(p, j)
        chip = self.div(who, self.cores)
        gap = chip - self.z
        k = self.div(j, self.wide)
        at = who * SUMS
        down = sums[at + PROMPTS] - sums[at + p + 1] + k
        up = sums[at + p] + k
        near_down = down - jnp.where(
            chip == 0, sums[at + PROMPTS] - sums[at + self.last_of(1) + 1], 0
        )
        near_up = up - jnp.where(chip == 3, sums[at + self.first_of(2)], 0)
        far = jnp.where(gap < 0, down, up)
        two = (gap == 2) | (gap == -2)
        direct = two & ((self.z == 1) | (self.z == 2))
        code = jnp.where(two, 5 * CODE, 4 * CODE) + far
        code = jnp.where(direct, self.listed(3, far, CAPS.far), code)
        code = jnp.where(gap == 1, self.listed(2, near_up, CAPS.near), code)
        code = jnp.where(gap == -1, self.listed(1, near_down, CAPS.near), code)
        return jnp.where(gap == 0, p * self.stride + k, code)


CODE = 256
SHARED = 6
EXTRA = 7
SUMS = 8
SLOT_AT, SHARE_AT, SHARES_AT, LENGTH_AT, BASE_AT, LOW_AT, THEIRS_AT, OVER_AT, TABLE = (
    0, 32, 50, 52, 54, 56, 58, 59, 64
)


class Caps:
    def __init__(self, near, far, relay):
        self.near, self.far, self.relay = near, far, relay


CAPS = Caps(5, 5, 4)


def needs(lay, sums, cores):
    first, last = [lay.first_of(c) for c in range(4)], [lay.last_of(c) for c in range(4)]
    near, far = jnp.int32(0), jnp.int32(0)
    for core in range(cores):

        def held(chip, low, high, core=core):
            at = (chip * cores + core) * SUMS
            return sums[at + high + 1] - sums[at + low]

        top = PROMPTS - 1
        edge = [held(1, 0, last[0]), held(2, first[3], top)]
        for amount in edge + [
            held(0, first[1], last[1]),
            held(1, first[2], top),
            held(2, 0, last[1]),
            held(3, first[2], last[2]),
        ]:
            near = jnp.maximum(near, amount)
        for amount in (held(0, first[2], top), held(3, 0, last[1])):
            far = jnp.maximum(far, amount)
    return near, far


def plan_kernel(wide, cores, line, ctrl, table, sums):
    lay = Layout(ctrl, wide, cores)
    half = PMAX // cores
    table[THEIRS_AT] = ctrl[OTHER_AT]
    table[OVER_AT] = 0
    if line:

        def tally(who, carry):
            total = jnp.int32(0)
            for p in range(PROMPTS):
                sums[who * SUMS + p] = total
                total = total + lay.held(p, who)
            sums[who * SUMS + PROMPTS] = total
            return carry

        lax.fori_loop(0, wide, tally, 0)
        near, far = needs(lay, sums, cores)
        over = (near > CAPS.near) | (far > CAPS.far)
        table[OVER_AT] = as_int(over)

    def prompts_of(device):
        return [lay.prompt_of(device * RB_DEV + b) for b in range(RB_DEV)]

    mine = prompts_of(lay.me)
    same = mine[0] == mine[1]
    joined = same & (ctrl[SEG_AT] == ctrl[SEG_AT + 1])
    for slot in range(RB_DEV):
        p = mine[slot]
        count = lay.length(p)
        table[LENGTH_AT + slot] = count
        if slot == 1:
            count = jnp.where(same, 0, count)
        table[BASE_AT + slot] = jnp.where(same, 0, PMAX) if slot else 0
        table[LOW_AT + slot] = jnp.where(joined, 0, BLOCK) if slot else 0

        def place(j, carry, slot=slot, p=p):
            who = lay.held_by(p, j)
            code = (who * PROMPTS + p) * lay.stride + lay.div(j, wide)
            if line:
                shared = slot * half + lay.div(j, cores)
                passed = jnp.where(
                    lay.mod(who, cores) == lay.core,
                    lay.in_plane(p, j, sums),
                    SHARED * CODE + shared,
                )
                code = passed
            table[SLOT_AT + slot * PMAX + j] = code
            return carry

        lax.fori_loop(0, count, place, 0)
    if not line:
        return
    theirs = prompts_of(lay.z * cores + (cores - 1 - lay.core))
    for slot in range(RB_DEV):
        p = theirs[slot]
        shift = lay.mod(lay.core - ctrl[OWNER_AT + p] + wide, cores)
        count = lay.div(lay.length(p) - shift + cores - 1, cores)
        if slot == 1:
            count = jnp.where(theirs[1] == theirs[0], 0, count)
        table[SHARES_AT + slot] = count

        def share(i, carry, slot=slot, p=p, shift=shift):
            table[SHARE_AT + slot * half + i] = lay.in_plane(p, i * cores + shift, sums)
            return carry

        lax.fori_loop(0, count, share, 0)


def make_plan(wide, cores, line, ctrl):
    return pl.pallas_call(
        lambda *refs: plan_kernel(wide, cores, line, *refs),
        out_shape=jax.ShapeDtypeStruct((TABLE,), jnp.int32),
        in_specs=[pl.BlockSpec(memory_space=pltpu.SMEM)],
        out_specs=pl.BlockSpec(memory_space=pltpu.SMEM),
        scratch_shapes=[pltpu.SMEM((wide * SUMS,), jnp.int32)],
        compiler_params=params(),
        name="plan",
    )(ctrl)


def spot(ref, page):
    return ref.at[pl.ds(pl.multiple_of(page * BLOCK, BLOCK), BLOCK), :]


def page_at(buffer, page, column):
    rows = pl.ds(pl.multiple_of(page * BLOCK, BLOCK), BLOCK)
    return buffer.at[rows, pl.ds(column if buffer.shape[1] > PAIR else 0, PAIR)]


def start_page(buffers, code, column, target, sem):
    which = lax.shift_right_logical(code, CODE.bit_length() - 1)
    page = code & (CODE - 1)
    for i, buffer, offset in buffers:

        @pl.when(which == i)
        def _(buffer=buffer, offset=offset):
            source = page_at(buffer, page + offset, column)
            pltpu.make_async_copy(source, target, sem).start()


def wait_page(target, sem):
    pltpu.make_async_copy(target, target, sem).wait()


def send_kernel(wide, cores, groups, caps, skip, planned, ctrl, pool, *refs):
    if planned:
        *outs, table, sems, sums = refs
    else:
        *outs, sems = refs
    rooms = (caps.near, caps.near, caps.far)
    lay = Layout(ctrl, wide, cores)
    z, last = lay.z, wide // cores - 1
    held = [lay.held(p, lay.me) for p in range(PROMPTS)]

    def above(p, top):
        return sum([jnp.where(o <= top, held[o], 0) for o in range(p + 1, PROMPTS)], jnp.int32(0))

    def below(p, low):
        return sum([jnp.where(o >= low, held[o], 0) for o in range(p)], jnp.int32(0))

    near_top = jnp.where(z == 0, lay.last_of(1), PROMPTS - 1)
    near_low = jnp.where(z == last, lay.first_of(2), 0)
    first_up, last_down = lay.first_of(z + 1), lay.last_of(z - 1)
    first_two, last_one = lay.first_of(2), lay.last_of(1)
    plans = []
    for p in range(PROMPTS):
        right = (z < last) & (p >= first_up) & (p <= near_top)
        left = (z > 0) & (p >= near_low) & (p <= last_down)
        far_up = (z == 0) & (p >= first_two)
        far_down = (z == last) & (p <= last_one)
        ranks = (above(p, near_top), below(p, near_low), above(p, PROMPTS - 1), below(p, 0))
        for k in range(lay.stride):
            for lane, wanted, rank in zip((0, 1, 2, 2), (right, left, far_up, far_down), ranks):
                at = rank + k - skip[lane]
                fits = (k < held[p]) & (at >= 0) & (at < rooms[lane])
                plans.append((wanted & fits, p * lay.stride + k, lane, at))

    def copies(plan):
        _, page, lane, rank = plan
        if groups is None:
            return [
                pltpu.make_async_copy(
                    spot(pool, page), spot(outs[lane], rank), sems.at[lane, page, 0]
                )
            ]
        return [
            pltpu.make_async_copy(
                page_at(pool, page, g * PAIR),
                spot(outs[n * 3 + lane], h * rooms[lane] + rank),
                sems.at[lane, page, n * len(groups[0]) + h],
            )
            for n, group in enumerate(groups)
            for h, g in enumerate(group)
        ]

    for plan in plans:

        @pl.when(plan[0])
        def _(plan=plan):
            for copy in copies(plan):
                copy.start()

    if planned:
        plan_kernel(wide, cores, True, ctrl, table, sums)
    for plan in plans:

        @pl.when(plan[0])
        def _(plan=plan):
            for copy in copies(plan):
                copy.wait()


def relay_kernel(cores, caps, h, ctrl, far, left, right, out, sems):
    rows = caps.relay * BLOCK

    def copy(source, room, section):
        target = out.at[pl.ds(section * rows, rows), :]
        return pltpu.make_async_copy(
            source.at[pl.ds(h * room * BLOCK, rows), :], target, sems.at[section]
        )

    inner = ctrl[ME_AT] == 2 * cores
    for core in range(1, cores):
        inner = inner | (ctrl[ME_AT] == 2 * cores + core)
    copy(far, caps.far, 0).start()
    pl.when(inner)(lambda: copy(left, caps.near, 1).start())
    pl.when(jnp.logical_not(inner))(lambda: copy(right, caps.near, 1).start())
    copy(far, caps.far, 0).wait()
    copy(left, caps.near, 1).wait()


def numbered(refs, caps, h):
    if len(refs) == 1:
        return [(0, refs[0], 0)]
    offsets = (0, h * caps.near, h * caps.near, h * caps.far, 0)
    found = list(zip(range(5), refs[:5], offsets)) + [(5, refs[4], caps.relay)]
    if len(refs) == 7:
        found.append((SHARED, refs[5], 0))
    return found + [(EXTRA + i, refs[-1], i) for i in range(3)]


def share_kernel(cores, caps, h, g, table, *refs):
    out, sems = refs[-2:]
    half = PMAX // cores
    buffers = numbered(refs[:-2], caps, h)
    for slot in range(RB_DEV):

        def begin(i, carry, slot=slot):
            at = slot * half + i
            start_page(buffers, table[SHARE_AT + at], g * PAIR, spot(out, at), sems.at[at])
            return carry

        lax.fori_loop(0, table[SHARES_AT + slot], begin, 0)
    for slot in range(RB_DEV):

        def finish(i, carry, slot=slot):
            at = slot * half + i
            wait_page(spot(out, at), sems.at[at])
            return carry

        lax.fori_loop(0, table[SHARES_AT + slot], finish, 0)


def attend_kernel(group, first, blocks, caps, carried, project, table, queries, own, *refs):
    refs = list(refs)
    weight = refs.pop(0) if project else None
    summed = refs.pop(0) if carried else None
    sems, stacked = refs.pop(), refs.pop()
    slab = refs.pop() if project else None
    store = refs.pop()
    terms = refs.pop() if project else None
    out = refs.pop()
    heads, room = len(group), len(blocks) * PMAX

    def region(i):
        if i == 0:
            return 0, table[LENGTH_AT + blocks[0]]
        base = table[BASE_AT + blocks[i]]
        return base, jnp.where(base == 0, 0, table[LENGTH_AT + blocks[i]])

    for h, g in enumerate(group):
        buffers = numbered(refs, caps, first + h)
        for i, b in enumerate(blocks):
            base, count = region(i)
            codes = SLOT_AT + table[BASE_AT + b]

            def begin(j, carry, h=h, g=g, buffers=buffers, base=base, codes=codes):
                at = h * room + base + j
                target, sem = spot(store, at), sems.at[at]
                start_page(buffers, table[codes + j], g * PAIR, target, sem)
                return carry

            lax.fori_loop(0, count, begin, 0)
            length = table[LENGTH_AT + b]

            def clear(j, carry, h=h, base=base):
                rows = pl.ds(pl.multiple_of((h * room + base + j) * BLOCK, BLOCK), BLOCK)
                store[rows, :] = jnp.zeros((BLOCK, PAIR), jnp.bfloat16)
                return carry

            lax.fori_loop(length, (length + SPAN - 1) & -SPAN, clear, 0)
    if project:
        share = slab.shape[1]
        theirs = pl.multiple_of(table[THEIRS_AT] * share, share)
        fetch = pltpu.make_async_copy(
            weight.at[pl.ds(group[0] * WIDTH, heads * WIDTH), pl.ds(theirs, share)],
            slab,
            sems.at[heads * room],
        )
        fetch.start()

    def one_block(h, i, b, base, count):
        tokens = pl.ds(pl.multiple_of(i * BLOCK, BLOCK), BLOCK)

        def columns(width, extra=0):
            return pl.ds(pl.multiple_of(h * width + extra, HD), min(width, HD))

        for e in range(GROUP):
            stacked[e * BLOCK : (e + 1) * BLOCK, :] = queries[tokens, columns(WIDTH, e * HD)]
        base = h * room + base

        def finish(j, carry):
            wait_page(spot(store, base + j), sems.at[base + j])
            return carry

        lax.fori_loop(0, count, finish, 0)
        length = table[LENGTH_AT + b]
        span = RB_DEV * BLOCK
        row = lax.broadcasted_iota(jnp.int32, (ROWS, span), 0) & (BLOCK - 1)
        key = lax.broadcasted_iota(jnp.int32, (ROWS, span), 1)
        own_mask = (key <= row + b * BLOCK) & (key >= table[LOW_AT + b])

        def run(spans):
            wide_key = lax.broadcasted_iota(jnp.int32, (ROWS, SPAN * BLOCK), 1)
            last_mask = wide_key < (length - (spans - 1) * SPAN) * BLOCK
            pieces = [(own[:, columns(PAIR)], own[:, columns(PAIR, HD)])]
            for t in range(spans):
                at = pl.multiple_of((base + t * SPAN) * BLOCK, BLOCK)
                piece = store[pl.ds(at, SPAN * BLOCK), :]
                pieces.append((piece[:, :HD], piece[:, HD:]))

            def score(r, t):
                scores = lax.dot_general(
                    stacked[r * ROWS : (r + 1) * ROWS, :],
                    pieces[t][0],
                    (((1,), (1,)), ((), ())),
                    preferred_element_type=jnp.float32,
                )
                if t == 0:
                    return jnp.where(own_mask, scores, NEG_LARGE)
                if t == spans:
                    return jnp.where(last_mask, scores, NEG_LARGE)
                return scores

            def highest(scores, sofar):
                for n in range(0, scores.shape[1], HD):
                    part = scores[:, n : n + HD]
                    sofar = part if sofar is None else jnp.maximum(sofar, part)
                return sofar

            def blend(scores, top, t):
                spread = jnp.concatenate([top] * (scores.shape[1] // HD), axis=1)
                weights = jnp.exp2((scores - spread) * SCALE).astype(jnp.bfloat16)
                values = pieces[t][1]
                values = jnp.concatenate([values, jnp.ones_like(values)], axis=1)
                return jnp.dot(weights, values, preferred_element_type=jnp.float32)

            chunks, ahead, peak = GROUP * BLOCK // ROWS, [], None
            for t in range(spans + 1):
                ahead.append(score(0, t))
                peak = highest(ahead[-1], peak)
            for r in range(chunks):
                now, ahead = ahead, []
                top = jnp.broadcast_to(jnp.max(peak, axis=1, keepdims=True), (ROWS, HD))
                total, peak = None, None
                for t in range(spans + 1):
                    if r + 1 < chunks:
                        ahead.append(score(r + 1, t))
                        peak = highest(ahead[-1], peak)
                    blended = blend(now[t], top, t)
                    total = blended if total is None else total + blended
                mean = (total[:, :HD] / total[:, HD:]).astype(jnp.bfloat16)
                for e in range(ROWS // BLOCK):
                    at = columns(WIDTH, (r * (ROWS // BLOCK) + e) * HD)
                    out[tokens, at] = mean[e * BLOCK : (e + 1) * BLOCK, :]

        spans = lax.shift_right_logical(length + SPAN - 1, SPAN.bit_length() - 1)
        for n in range(1, PMAX // SPAN + 1):
            pl.when(spans == n)(lambda n=n: run(n))

    def step(n, carry):
        if len(blocks) == 1:
            one_block(n, 0, blocks[0], *region(0))
            return carry
        h, i = lax.shift_right_logical(n, 1), n & 1
        base = jnp.where(i == 0, 0, region(1)[0])
        one_block(h, i, i, base, jnp.where(i == 0, region(0)[1], region(1)[1]))
        return carry

    lax.fori_loop(0, heads * len(blocks), step, 0)
    if project:
        fetch.wait()
        attended = out[...]
        width = math.gcd(share, 512)
        for n in range(0, share, width):
            term = jnp.dot(attended, slab[:, n : n + width], preferred_element_type=jnp.float32)
            if carried:
                term = term + summed[:, n : n + width]
            terms[:, n : n + width] = term.astype(terms.dtype)


def attend(
    group, first, blocks, last, caps, table, queries, resp_kv, buffers, weight=None, share=0, summed=None
):
    tokens, heads = len(blocks) * BLOCK, len(group)
    at = blocks[0] // len(blocks)
    project, carried = weight is not None, summed is not None
    any_spec = pl.BlockSpec(memory_space=pl.ANY)
    whole = pl.BlockSpec((tokens, share), lambda i, c: (0, 0))
    out_shape = [jax.ShapeDtypeStruct((tokens, heads * WIDTH), jnp.bfloat16)]
    out_specs = [pl.BlockSpec((tokens, heads * WIDTH), lambda i, c: (0, 0))]
    operands, in_specs = [], []
    scratch = [pltpu.VMEM((heads * len(blocks) * PMAX * BLOCK, PAIR), jnp.bfloat16)]
    if project:
        operands, in_specs = [weight], [any_spec]
        kept = jnp.bfloat16 if last else jnp.float32
        out_shape.append(jax.ShapeDtypeStruct((tokens, share), kept))
        out_specs.append(whole)
        scratch.append(pltpu.VMEM((heads * WIDTH, share), jnp.bfloat16))
    if carried:
        operands = operands + [summed]
        in_specs = in_specs + [pl.BlockSpec((tokens, share), lambda i, c: (at, 0))]
    column = group[0] // heads
    return pl.pallas_call(
        lambda *refs: attend_kernel(group, first, blocks, caps, carried, project, *refs),
        out_shape=out_shape,
        grid_spec=pltpu.PrefetchScalarGridSpec(
            num_scalar_prefetch=1,
            grid=(1,),
            in_specs=[
                pl.BlockSpec((tokens, heads * WIDTH), lambda i, c: (at, column)),
                pl.BlockSpec((RB_DEV * BLOCK, heads * PAIR), lambda i, c: (0, column)),
            ]
            + in_specs
            + [any_spec] * len(buffers),
            out_specs=out_specs,
            scratch_shapes=scratch
            + [
                pltpu.VMEM((GROUP * BLOCK, HD), jnp.bfloat16),
                pltpu.SemaphoreType.DMA((heads * len(blocks) * PMAX + 1,)),
            ],
        ),
        compiler_params=params(),
        cost_estimate=SMALL,
        name="attend_heads_" + "_".join(map(str, group)) + "_blocks_" + "_".join(map(str, blocks)),
    )(table, queries, resp_kv, *operands, *buffers)


def pages_shape(count):
    return jax.ShapeDtypeStruct((count * BLOCK, PAIR), jnp.bfloat16)


def pack_send(wide, cores, groups, caps, skip, ctrl, pool, planned=False):
    any_spec = pl.BlockSpec(memory_space=pl.ANY)
    pages = PROMPTS * ((PMAX + wide - 1) // wide)
    rooms = (caps.near, caps.near, caps.far)
    if groups is None:
        shapes = [jax.ShapeDtypeStruct((n * BLOCK, pool.shape[1]), jnp.bfloat16) for n in rooms]
    else:
        shapes = [pages_shape(n * len(group)) for group in groups for n in rooms]
    heads = 1 if groups is None else sum(map(len, groups))
    out_specs = [any_spec] * len(shapes)
    scratch = [pltpu.SemaphoreType.DMA((3, pages, heads))]
    if planned:
        shapes = shapes + [jax.ShapeDtypeStruct((TABLE,), jnp.int32)]
        out_specs = out_specs + [pl.BlockSpec(memory_space=pltpu.SMEM)]
        scratch.append(pltpu.SMEM((wide * SUMS,), jnp.int32))
    return pl.pallas_call(
        lambda *refs: send_kernel(wide, cores, groups, caps, skip, planned, *refs),
        out_shape=shapes,
        grid_spec=pltpu.PrefetchScalarGridSpec(
            num_scalar_prefetch=1,
            grid=(1,),
            in_specs=[pl.BlockSpec(pool.shape, lambda i, c: (0, 0))],
            out_specs=out_specs,
            scratch_shapes=scratch,
        ),
        compiler_params=params(),
        cost_estimate=SMALL,
        name="pack_extra" if groups is None else f"pack_send_{groups[0][0]}",
    )(ctrl, pool)


def pack_share(cores, caps, h, g, table, buffers):
    any_spec = pl.BlockSpec(memory_space=pl.ANY)
    return pl.pallas_call(
        lambda *refs: share_kernel(cores, caps, h, g, *refs),
        out_shape=pages_shape(PMAX),
        grid_spec=pltpu.PrefetchScalarGridSpec(
            num_scalar_prefetch=1,
            grid=(1,),
            in_specs=[any_spec] * len(buffers),
            out_specs=any_spec,
            scratch_shapes=[pltpu.SemaphoreType.DMA((PMAX,))],
        ),
        compiler_params=params(),
        cost_estimate=SMALL,
        name=f"pack_share_{g}",
    )(table, *buffers)


def pack_relay(cores, caps, h, g, ctrl, far, left, right):
    any_spec = pl.BlockSpec(memory_space=pl.ANY)
    return pl.pallas_call(
        lambda *refs: relay_kernel(cores, caps, h, *refs),
        out_shape=pages_shape(2 * caps.relay),
        grid_spec=pltpu.PrefetchScalarGridSpec(
            num_scalar_prefetch=1,
            grid=(1,),
            in_specs=[any_spec] * 3,
            out_specs=any_spec,
            scratch_shapes=[pltpu.SemaphoreType.DMA((2,))],
        ),
        compiler_params=params(),
        cost_estimate=SMALL,
        name=f"pack_relay_{g}",
    )(ctrl, far, left, right)


def after(value, *earlier):
    return lax.optimization_barrier((value, *earlier))[0]


def line_attend(wide, cores, caps, ctrl, queries, resp_kv, pool, weight):
    heads = resp_kv.shape[1] // PAIR
    share = weight.shape[1] // 2

    def hop(x, moves):
        pairs = [(a * cores + c, b * cores + c) for a, b in moves for c in range(cores)]
        return lax.ppermute(x, "wide", pairs)

    swap = [(d, d // cores * cores + (cores - 1 - d % cores)) for d in range(wide)]

    def spread(right, left, far):
        return (
            hop(right, [(0, 1), (1, 2), (2, 3)]),
            hop(left, [(3, 2), (2, 1), (1, 0)]),
            hop(far, [(0, 2), (3, 1)]),
        )

    past = Caps(1, 1, 0)

    def past_the_end(ctrl, pool):
        skip = (caps.near, caps.near, caps.far)
        lists = pack_send(wide, cores, None, past, skip, ctrl, pool)
        return jnp.concatenate(spread(*lists), axis=0)

    def nothing(ctrl, pool):
        return jnp.zeros((3 * past.near * BLOCK, pool.shape[1]), pool.dtype)

    both, last = list(range(RB_DEV)), heads - 1
    half = heads // 2
    groups = [[g] for g in range(half)] + [list(range(half, heads))]
    *lists, table = pack_send(wide, cores, groups[:1], caps, (0, 0, 0), ctrl, pool, True)
    sends, spreads, held, parts = {0: lists}, {}, {}, []

    def relay(g, plan):
        n = min(g, half)
        if n not in spreads:
            spreads[n] = spread(*sends[n])
            if n + 1 < len(groups):
                sends[n + 1] = pack_send(wide, cores, [groups[n + 1]], caps, (0, 0, 0), ctrl, pool)
                plan = after(plan, sends[n + 1][0])
        left, right, far = spreads[n]
        onward = pack_relay(cores, caps, g - n, g, plan, far, left, right)
        held[g] = g - n, [pool, left, right, far, hop(onward, [(2, 3), (1, 0)])]
        return onward

    onward = relay(0, ctrl)
    over = after(table, onward)[OVER_AT] == 1
    extra = lax.cond(over, past_the_end, nothing, ctrl, pool)

    def exchange(g, plan):
        h, buffers = held[g]
        shared = pack_share(cores, caps, h, g, plan, buffers + [extra])
        return h, buffers + [lax.ppermute(shared, "wide", swap), extra]

    theirs, summed, waits = table[THEIRS_AT] * share, None, ctrl
    for g in range(last):
        onward = relay(g + 1, waits)
        h, buffers = exchange(g, after(table, onward))
        parts += attend([g], h, both, False, caps, table, queries, resp_kv, buffers)
        waits = after(ctrl, parts[-1])
        if g == 0:
            summed = project(parts, weight, 0, theirs, share, jnp.float32)
            waits = after(ctrl, summed)
    h, buffers = exchange(last, after(table, parts[-1]) if parts else table)
    if last > 1:
        summed = project(parts[1:], weight, 1, theirs, share, jnp.float32, summed)
    ends, terms, plan = [], [], table
    for b in both:
        end, term = attend(
            [last], h, [b], True, caps, plan, queries, resp_kv, buffers, weight, share, summed
        )
        ends.append(end)
        terms.append(term)
        plan = after(table, end)
    return parts + [jnp.concatenate(ends, axis=0)], terms


def project_kernel(carried, at, *refs):
    parts, weight, out = refs[: -2 - carried], refs[-2 - carried], refs[-1]
    total, row = refs[-2][...] if carried else None, 0
    for part in parts:
        end = row + part.shape[1]
        term = jnp.dot(part[...], weight[row:end, :], preferred_element_type=jnp.float32)
        total, row = term if total is None else total + term, end
    out[...] = total.astype(out.dtype)


def project(parts, weight, first, first_column, columns, kept=jnp.bfloat16, summed=None):
    tokens, rows = parts[0].shape[0], sum(part.shape[1] for part in parts)
    tile = math.gcd(columns, 512)
    assert weight.shape[1] % tile == 0
    at = jnp.reshape(first_column // tile, (1,)).astype(jnp.int32)
    skip = first * WIDTH
    if skip % rows:
        weight_spec = pl.BlockSpec(
            (pl.Element(rows), pl.Element(tile)), lambda i, at: (skip, (at[0] + i) * tile)
        )
    else:
        weight_spec = pl.BlockSpec((rows, tile), lambda i, at: (skip // rows, at[0] + i))
    operands, in_specs = [*parts, weight], [
        pl.BlockSpec(part.shape, lambda i, at: (0, 0)) for part in parts
    ] + [weight_spec]
    if summed is not None:
        operands.append(summed)
        in_specs.append(pl.BlockSpec((tokens, tile), lambda i, at: (0, i)))
    return pl.pallas_call(
        lambda *refs: project_kernel(summed is not None, *refs),
        out_shape=jax.ShapeDtypeStruct((tokens, columns), kept),
        grid_spec=pltpu.PrefetchScalarGridSpec(
            num_scalar_prefetch=1,
            grid=(columns // tile,),
            in_specs=in_specs,
            out_specs=pl.BlockSpec((tokens, tile), lambda i, at: (0, i)),
        ),
        compiler_params=params(),
        cost_estimate=SMALL,
        name="project",
    )(at, *operands)


def local(
    queries, resp_kv, prefix_pool, out_weight, pre_len, prompt_blocks, prompt_owner, resp_seg
):
    wide, groups = lax.axis_size("wide"), lax.axis_size("tp") * lax.axis_size("sub")
    cores = 2 // lax.axis_size("sub")
    heads = resp_kv.shape[1] // PAIR
    me = lax.axis_index("wide").astype(jnp.int32)
    group = lax.axis_index("tp") * lax.axis_size("sub") + lax.axis_index("sub")
    where = jnp.stack([me, (1 - group).astype(jnp.int32)])
    ctrl = jnp.concatenate([pre_len, prompt_blocks, prompt_owner, resp_seg, where])
    columns = out_weight.shape[1]
    share = columns // groups
    if wide == 8 and cores == 2 and groups == 2:
        parts, theirs = line_attend(
            wide, cores, CAPS, ctrl, queries, resp_kv, prefix_pool, out_weight
        )
        axis = "tp" if lax.axis_size("tp") == 2 else "sub"
        arrived = [lax.ppermute(terms, axis, [(0, 1), (1, 0)]) for terms in theirs]
        half = share // 2
        mine = [
            project(parts, out_weight, 0, group * share, half),
            project(parts, out_weight, 0, after(group, arrived[0]) * share + half, half),
        ]
        mine = jnp.concatenate(mine, axis=1)
        arrived = jnp.concatenate(arrived, axis=0)
        return (mine.astype(jnp.float32) + arrived.astype(jnp.float32)).astype(jnp.bfloat16)
    table = make_plan(wide, cores, False, ctrl)
    buffers = [lax.all_gather(prefix_pool, "wide", axis=0, tiled=True)]
    blocks = list(range(RB_DEV))
    parts = [
        attend([g], 0, blocks, False, CAPS, table, queries, resp_kv, buffers)[0] for g in range(heads)
    ]
    terms = project(parts, out_weight, 0, jnp.int32(0), columns)
    return lax.psum_scatter(terms, ("tp", "sub"), scatter_dimension=1, tiled=True)


def solution(mesh):
    return jax.shard_map(
        local,
        mesh=mesh,
        in_specs=(
            P(("parts", "wide"), ("tp", "sub")),
            P(("parts", "wide"), ("tp", "sub")),
            P(("parts", "wide"), ("tp", "sub")),
            P(("tp", "sub"), None),
            P("parts"),
            P("parts"),
            P("parts"),
            P(("parts", "wide")),
        ),
        out_specs=P(("parts", "wide"), ("tp", "sub")),
        check_vma=False,
    )
```

```python
import math

import jax
import jax.numpy as jnp
from jax import lax
from jax.experimental import pallas as pl
from jax.experimental.pallas import tpu as pltpu
from jax.sharding import PartitionSpec as P

HD = 128
BLOCK = 128
RB_DEV = 2
PROMPTS = 4
PMAX = 16
GROUP = 8
PAIR = 2 * HD
WIDTH = GROUP * HD
ROWS = 512
SPAN = 4
NEG_LARGE = -1e30
SCALE = math.log2(math.e) / math.sqrt(HD)
MIB = 1024 * 1024
ATTEND_MIB, PROJECT_MIB = 24, 18
SMALL = pl.CostEstimate(flops=1 << 20, bytes_accessed=1 << 14, transcendentals=0)

LEN_AT, BLOCKS_AT, OWNER_AT, SEG_AT, ME_AT, OTHER_AT = 0, 4, 8, 12, 14, 15


def params(mib):
    return pltpu.CompilerParams(vmem_limit_bytes=mib * MIB)


def as_int(flag):
    return jnp.where(flag, 1, 0)


class Layout:
    def __init__(self, ctrl, wide, cores):
        self.ctrl, self.wide, self.cores = ctrl, wide, cores
        self.stride = (PMAX + wide - 1) // wide
        self.me = ctrl[ME_AT]
        self.z, self.core = self.div(self.me, cores), self.mod(self.me, cores)
        ends, total = [], 0
        for p in range(PROMPTS):
            total = total + ctrl[BLOCKS_AT + p] + (RB_DEV - 1)
            ends.append(total)
        self.ends = ends

    def mod(self, value, size):
        return value & (size - 1) if size & (size - 1) == 0 else lax.rem(value, size)

    def div(self, value, size):
        if size & (size - 1) == 0:
            return lax.shift_right_logical(value, size.bit_length() - 1)
        return lax.div(value, size)

    def prompt_of(self, block):
        return sum(as_int(block >= end) for end in self.ends[:-1])

    def first_of(self, chip):
        return self.prompt_of(chip * self.cores * RB_DEV)

    def last_of(self, chip):
        return self.prompt_of((chip + 1) * self.cores * RB_DEV - 1)

    def length(self, p):
        return self.ctrl[LEN_AT + p]

    def held_by(self, p, j):
        return self.mod(self.ctrl[OWNER_AT + p] + j, self.wide)

    def held(self, p, who):
        first = self.mod(who - self.ctrl[OWNER_AT + p] + self.wide, self.wide)
        return sum(as_int(first + k * self.wide < self.length(p)) for k in range(self.stride))

    def listed(self, which, rank, room):
        return jnp.where(
            rank < room, which * CODE + rank, (EXTRA + which - 1) * CODE + rank - room
        )

    def in_plane(self, p, j, sums):
        who = self.held_by(p, j)
        chip = self.div(who, self.cores)
        gap = chip - self.z
        k = self.div(j, self.wide)
        at = who * SUMS
        down = sums[at + PROMPTS] - sums[at + p + 1] + k
        up = sums[at + p] + k
        near_down = down - jnp.where(
            chip == 0, sums[at + PROMPTS] - sums[at + self.last_of(1) + 1], 0
        )
        near_up = up - jnp.where(chip == 3, sums[at + self.first_of(2)], 0)
        far = jnp.where(gap < 0, down, up)
        two = (gap == 2) | (gap == -2)
        direct = two & ((self.z == 1) | (self.z == 2))
        code = jnp.where(two, 5 * CODE, 4 * CODE) + far
        code = jnp.where(direct, self.listed(3, far, CAPS.far), code)
        code = jnp.where(gap == 1, self.listed(2, near_up, CAPS.near), code)
        code = jnp.where(gap == -1, self.listed(1, near_down, CAPS.near), code)
        return jnp.where(gap == 0, p * self.stride + k, code)


CODE = 256
SHARED = 6
EXTRA = 7
SUMS = 8
SLOT_AT, SHARE_AT, SHARES_AT, LENGTH_AT, BASE_AT, LOW_AT, THEIRS_AT, OVER_AT, TABLE = (
    0, 32, 50, 52, 54, 56, 58, 59, 64
)


class Caps:
    def __init__(self, near, far, relay):
        self.near, self.far, self.relay = near, far, relay


CAPS = Caps(5, 5, 4)


def needs(lay, sums, cores):
    first, last = [lay.first_of(c) for c in range(4)], [lay.last_of(c) for c in range(4)]
    near, far = jnp.int32(0), jnp.int32(0)
    for core in range(cores):

        def held(chip, low, high, core=core):
            at = (chip * cores + core) * SUMS
            return sums[at + high + 1] - sums[at + low]

        top = PROMPTS - 1
        edge = [held(1, 0, last[0]), held(2, first[3], top)]
        for amount in edge + [
            held(0, first[1], last[1]),
            held(1, first[2], top),
            held(2, 0, last[1]),
            held(3, first[2], last[2]),
        ]:
            near = jnp.maximum(near, amount)
        for amount in (held(0, first[2], top), held(3, 0, last[1])):
            far = jnp.maximum(far, amount)
    return near, far


def plan_kernel(wide, cores, line, ctrl, table, sums):
    lay = Layout(ctrl, wide, cores)
    half = PMAX // cores
    table[THEIRS_AT] = ctrl[OTHER_AT]
    table[OVER_AT] = 0
    if line:

        def tally(who, carry):
            total = jnp.int32(0)
            for p in range(PROMPTS):
                sums[who * SUMS + p] = total
                total = total + lay.held(p, who)
            sums[who * SUMS + PROMPTS] = total
            return carry

        lax.fori_loop(0, wide, tally, 0)
        near, far = needs(lay, sums, cores)
        over = (near > CAPS.near) | (far > CAPS.far)
        table[OVER_AT] = as_int(over)

    def prompts_of(device):
        return [lay.prompt_of(device * RB_DEV + b) for b in range(RB_DEV)]

    mine = prompts_of(lay.me)
    same = mine[0] == mine[1]
    joined = same & (ctrl[SEG_AT] == ctrl[SEG_AT + 1])
    for slot in range(RB_DEV):
        p = mine[slot]
        count = lay.length(p)
        table[LENGTH_AT + slot] = count
        if slot == 1:
            count = jnp.where(same, 0, count)
        table[BASE_AT + slot] = jnp.where(same, 0, PMAX) if slot else 0
        table[LOW_AT + slot] = jnp.where(joined, 0, BLOCK) if slot else 0

        def place(j, carry, slot=slot, p=p):
            who = lay.held_by(p, j)
            code = (who * PROMPTS + p) * lay.stride + lay.div(j, wide)
            if line:
                shared = slot * half + lay.div(j, cores)
                passed = jnp.where(
                    lay.mod(who, cores) == lay.core,
                    lay.in_plane(p, j, sums),
                    SHARED * CODE + shared,
                )
                code = passed
            table[SLOT_AT + slot * PMAX + j] = code
            return carry

        lax.fori_loop(0, count, place, 0)
    if not line:
        return
    theirs = prompts_of(lay.z * cores + (cores - 1 - lay.core))
    for slot in range(RB_DEV):
        p = theirs[slot]
        shift = lay.mod(lay.core - ctrl[OWNER_AT + p] + wide, cores)
        count = lay.div(lay.length(p) - shift + cores - 1, cores)
        if slot == 1:
            count = jnp.where(theirs[1] == theirs[0], 0, count)
        table[SHARES_AT + slot] = count

        def share(i, carry, slot=slot, p=p, shift=shift):
            table[SHARE_AT + slot * half + i] = lay.in_plane(p, i * cores + shift, sums)
            return carry

        lax.fori_loop(0, count, share, 0)


def make_plan(wide, cores, line, ctrl):
    return pl.pallas_call(
        lambda *refs: plan_kernel(wide, cores, line, *refs),
        out_shape=jax.ShapeDtypeStruct((TABLE,), jnp.int32),
        in_specs=[pl.BlockSpec(memory_space=pltpu.SMEM)],
        out_specs=pl.BlockSpec(memory_space=pltpu.SMEM),
        scratch_shapes=[pltpu.SMEM((wide * SUMS,), jnp.int32)],
        compiler_params=params(6),
        name="plan",
    )(ctrl)


def spot(ref, page):
    return ref.at[pl.ds(pl.multiple_of(page * BLOCK, BLOCK), BLOCK), :]


def page_at(buffer, page, column):
    rows = pl.ds(pl.multiple_of(page * BLOCK, BLOCK), BLOCK)
    return buffer.at[rows, pl.ds(column if buffer.shape[1] > PAIR else 0, PAIR)]


def start_page(buffers, code, column, target, sem):
    which = lax.shift_right_logical(code, CODE.bit_length() - 1)
    page = code & (CODE - 1)
    for i, buffer, offset in buffers:

        @pl.when(which == i)
        def _(buffer=buffer, offset=offset):
            source = page_at(buffer, page + offset, column)
            pltpu.make_async_copy(source, target, sem).start()


def wait_page(target, sem):
    pltpu.make_async_copy(target, target, sem).wait()


def send_kernel(wide, cores, groups, caps, skip, planned, ctrl, pool, *refs):
    if planned:
        *outs, table, sems, sums = refs
    else:
        *outs, sems = refs
    rooms = (caps.near, caps.near, caps.far)
    lay = Layout(ctrl, wide, cores)
    z, last = lay.z, wide // cores - 1
    held = [lay.held(p, lay.me) for p in range(PROMPTS)]

    def above(p, top):
        return sum([jnp.where(o <= top, held[o], 0) for o in range(p + 1, PROMPTS)], jnp.int32(0))

    def below(p, low):
        return sum([jnp.where(o >= low, held[o], 0) for o in range(p)], jnp.int32(0))

    near_top = jnp.where(z == 0, lay.last_of(1), PROMPTS - 1)
    near_low = jnp.where(z == last, lay.first_of(2), 0)
    first_up, last_down = lay.first_of(z + 1), lay.last_of(z - 1)
    first_two, last_one = lay.first_of(2), lay.last_of(1)
    plans = []
    for p in range(PROMPTS):
        right = (z < last) & (p >= first_up) & (p <= near_top)
        left = (z > 0) & (p >= near_low) & (p <= last_down)
        far_up = (z == 0) & (p >= first_two)
        far_down = (z == last) & (p <= last_one)
        ranks = (above(p, near_top), below(p, near_low), above(p, PROMPTS - 1), below(p, 0))
        for k in range(lay.stride):
            for lane, wanted, rank in zip((0, 1, 2, 2), (right, left, far_up, far_down), ranks):
                at = rank + k - skip[lane]
                fits = (k < held[p]) & (at >= 0) & (at < rooms[lane])
                plans.append((wanted & fits, p * lay.stride + k, lane, at))

    def copies(plan):
        _, page, lane, rank = plan
        if groups is None:
            return [
                pltpu.make_async_copy(
                    spot(pool, page), spot(outs[lane], rank), sems.at[lane, page, 0]
                )
            ]
        return [
            pltpu.make_async_copy(
                page_at(pool, page, g * PAIR),
                spot(outs[n * 3 + lane], h * rooms[lane] + rank),
                sems.at[lane, page, n * len(groups[0]) + h],
            )
            for n, group in enumerate(groups)
            for h, g in enumerate(group)
        ]

    for plan in plans:

        @pl.when(plan[0])
        def _(plan=plan):
            for copy in copies(plan):
                copy.start()

    if planned:
        plan_kernel(wide, cores, True, ctrl, table, sums)
    for plan in plans:

        @pl.when(plan[0])
        def _(plan=plan):
            for copy in copies(plan):
                copy.wait()


def relay_kernel(cores, caps, h, ctrl, far, left, right, out, sems):
    rows = caps.relay * BLOCK

    def copy(source, room, section):
        target = out.at[pl.ds(section * rows, rows), :]
        return pltpu.make_async_copy(
            source.at[pl.ds(h * room * BLOCK, rows), :], target, sems.at[section]
        )

    inner = ctrl[ME_AT] == 2 * cores
    for core in range(1, cores):
        inner = inner | (ctrl[ME_AT] == 2 * cores + core)
    copy(far, caps.far, 0).start()
    pl.when(inner)(lambda: copy(left, caps.near, 1).start())
    pl.when(jnp.logical_not(inner))(lambda: copy(right, caps.near, 1).start())
    copy(far, caps.far, 0).wait()
    copy(left, caps.near, 1).wait()


def numbered(refs, caps, h):
    if len(refs) == 1:
        return [(0, refs[0], 0)]
    offsets = (0, h * caps.near, h * caps.near, h * caps.far, 0)
    found = list(zip(range(5), refs[:5], offsets)) + [(5, refs[4], caps.relay)]
    if len(refs) == 7:
        found.append((SHARED, refs[5], 0))
    return found + [(EXTRA + i, refs[-1], i) for i in range(3)]


def share_kernel(cores, caps, h, g, table, *refs):
    out, sems = refs[-2:]
    half = PMAX // cores
    buffers = numbered(refs[:-2], caps, h)
    for slot in range(RB_DEV):

        def begin(i, carry, slot=slot):
            at = slot * half + i
            start_page(buffers, table[SHARE_AT + at], g * PAIR, spot(out, at), sems.at[at])
            return carry

        lax.fori_loop(0, table[SHARES_AT + slot], begin, 0)
    for slot in range(RB_DEV):

        def finish(i, carry, slot=slot):
            at = slot * half + i
            wait_page(spot(out, at), sems.at[at])
            return carry

        lax.fori_loop(0, table[SHARES_AT + slot], finish, 0)


def attend_kernel(group, first, blocks, caps, carried, project, table, queries, own, *refs):
    refs = list(refs)
    weight = refs.pop(0) if project else None
    summed = refs.pop(0) if carried else None
    sems, stacked = refs.pop(), refs.pop()
    slab = refs.pop() if project else None
    store = refs.pop()
    terms = refs.pop() if project else None
    out = refs.pop()
    heads, room = len(group), len(blocks) * PMAX

    def region(i):
        if i == 0:
            return 0, table[LENGTH_AT + blocks[0]]
        base = table[BASE_AT + blocks[i]]
        return base, jnp.where(base == 0, 0, table[LENGTH_AT + blocks[i]])

    for h, g in enumerate(group):
        buffers = numbered(refs, caps, first + h)
        for i, b in enumerate(blocks):
            base, count = region(i)
            codes = SLOT_AT + table[BASE_AT + b]

            def begin(j, carry, h=h, g=g, buffers=buffers, base=base, codes=codes):
                at = h * room + base + j
                target, sem = spot(store, at), sems.at[at]
                start_page(buffers, table[codes + j], g * PAIR, target, sem)
                return carry

            lax.fori_loop(0, count, begin, 0)
            length = table[LENGTH_AT + b]

            def clear(j, carry, h=h, base=base):
                rows = pl.ds(pl.multiple_of((h * room + base + j) * BLOCK, BLOCK), BLOCK)
                store[rows, :] = jnp.zeros((BLOCK, PAIR), jnp.bfloat16)
                return carry

            lax.fori_loop(length, (length + SPAN - 1) & -SPAN, clear, 0)
    if project:
        share = slab.shape[1]
        theirs = pl.multiple_of(table[THEIRS_AT] * share, share)
        fetch = pltpu.make_async_copy(
            weight.at[pl.ds(group[0] * WIDTH, heads * WIDTH), pl.ds(theirs, share)],
            slab,
            sems.at[heads * room],
        )
        fetch.start()

    def one_block(h, i, b, base, count):
        tokens = pl.ds(pl.multiple_of(i * BLOCK, BLOCK), BLOCK)

        def columns(width, extra=0):
            return pl.ds(pl.multiple_of(h * width + extra, HD), min(width, HD))

        for e in range(GROUP):
            stacked[e * BLOCK : (e + 1) * BLOCK, :] = queries[tokens, columns(WIDTH, e * HD)]
        base = h * room + base

        def finish(j, carry):
            wait_page(spot(store, base + j), sems.at[base + j])
            return carry

        lax.fori_loop(0, count, finish, 0)
        length = table[LENGTH_AT + b]
        span = RB_DEV * BLOCK
        row = lax.broadcasted_iota(jnp.int32, (ROWS, span), 0) & (BLOCK - 1)
        key = lax.broadcasted_iota(jnp.int32, (ROWS, span), 1)
        own_mask = (key <= row + b * BLOCK) & (key >= table[LOW_AT + b])

        def run(spans):
            wide_key = lax.broadcasted_iota(jnp.int32, (ROWS, SPAN * BLOCK), 1)
            last_mask = wide_key < (length - (spans - 1) * SPAN) * BLOCK
            pieces = [(own[:, columns(PAIR)], own[:, columns(PAIR, HD)])]
            for t in range(spans):
                at = pl.multiple_of((base + t * SPAN) * BLOCK, BLOCK)
                piece = store[pl.ds(at, SPAN * BLOCK), :]
                pieces.append((piece[:, :HD], piece[:, HD:]))

            def score(r, t):
                scores = lax.dot_general(
                    stacked[r * ROWS : (r + 1) * ROWS, :],
                    pieces[t][0],
                    (((1,), (1,)), ((), ())),
                    preferred_element_type=jnp.float32,
                )
                if t == 0:
                    return jnp.where(own_mask, scores, NEG_LARGE)
                if t == spans:
                    return jnp.where(last_mask, scores, NEG_LARGE)
                return scores

            def highest(scores, sofar):
                for n in range(0, scores.shape[1], HD):
                    part = scores[:, n : n + HD]
                    sofar = part if sofar is None else jnp.maximum(sofar, part)
                return sofar

            def blend(scores, top, t):
                spread = jnp.concatenate([top] * (scores.shape[1] // HD), axis=1)
                weights = jnp.exp2((scores - spread) * SCALE).astype(jnp.bfloat16)
                values = pieces[t][1]
                values = jnp.concatenate([values, jnp.ones_like(values)], axis=1)
                return jnp.dot(weights, values, preferred_element_type=jnp.float32)

            chunks, ahead, peak = GROUP * BLOCK // ROWS, [], None
            for t in range(spans + 1):
                ahead.append(score(0, t))
                peak = highest(ahead[-1], peak)
            for r in range(chunks):
                now, ahead = ahead, []
                top = jnp.broadcast_to(jnp.max(peak, axis=1, keepdims=True), (ROWS, HD))
                total, peak = None, None
                for t in range(spans + 1):
                    if r + 1 < chunks:
                        ahead.append(score(r + 1, t))
                        peak = highest(ahead[-1], peak)
                    blended = blend(now[t], top, t)
                    total = blended if total is None else total + blended
                mean = (total[:, :HD] / total[:, HD:]).astype(jnp.bfloat16)
                for e in range(ROWS // BLOCK):
                    at = columns(WIDTH, (r * (ROWS // BLOCK) + e) * HD)
                    out[tokens, at] = mean[e * BLOCK : (e + 1) * BLOCK, :]

        spans = lax.shift_right_logical(length + SPAN - 1, SPAN.bit_length() - 1)
        for n in range(1, PMAX // SPAN + 1):
            pl.when(spans == n)(lambda n=n: run(n))

    def step(n, carry):
        if len(blocks) == 1:
            one_block(n, 0, blocks[0], *region(0))
            return carry
        h, i = lax.shift_right_logical(n, 1), n & 1
        base = jnp.where(i == 0, 0, region(1)[0])
        one_block(h, i, i, base, jnp.where(i == 0, region(0)[1], region(1)[1]))
        return carry

    lax.fori_loop(0, heads * len(blocks), step, 0)
    if project:
        fetch.wait()
        attended = out[...]
        width = math.gcd(share, 512)
        for n in range(0, share, width):
            term = jnp.dot(attended, slab[:, n : n + width], preferred_element_type=jnp.float32)
            if carried:
                term = term + summed[:, n : n + width]
            terms[:, n : n + width] = term.astype(terms.dtype)


def attend(
    group, first, blocks, last, caps, table, queries, resp_kv, buffers, weight=None, share=0, summed=None
):
    tokens, heads = len(blocks) * BLOCK, len(group)
    at = blocks[0] // len(blocks)
    project, carried = weight is not None, summed is not None
    any_spec = pl.BlockSpec(memory_space=pl.ANY)
    whole = pl.BlockSpec((tokens, share), lambda i, c: (0, 0))
    out_shape = [jax.ShapeDtypeStruct((tokens, heads * WIDTH), jnp.bfloat16)]
    out_specs = [pl.BlockSpec((tokens, heads * WIDTH), lambda i, c: (0, 0))]
    operands, in_specs = [], []
    scratch = [pltpu.VMEM((heads * len(blocks) * PMAX * BLOCK, PAIR), jnp.bfloat16)]
    if project:
        operands, in_specs = [weight], [any_spec]
        kept = jnp.bfloat16 if last else jnp.float32
        out_shape.append(jax.ShapeDtypeStruct((tokens, share), kept))
        out_specs.append(whole)
        scratch.append(pltpu.VMEM((heads * WIDTH, share), jnp.bfloat16))
    if carried:
        operands = operands + [summed]
        in_specs = in_specs + [pl.BlockSpec((tokens, share), lambda i, c: (at, 0))]
    column = group[0] // heads
    return pl.pallas_call(
        lambda *refs: attend_kernel(group, first, blocks, caps, carried, project, *refs),
        out_shape=out_shape,
        grid_spec=pltpu.PrefetchScalarGridSpec(
            num_scalar_prefetch=1,
            grid=(1,),
            in_specs=[
                pl.BlockSpec((tokens, heads * WIDTH), lambda i, c: (at, column)),
                pl.BlockSpec((RB_DEV * BLOCK, heads * PAIR), lambda i, c: (0, column)),
            ]
            + in_specs
            + [any_spec] * len(buffers),
            out_specs=out_specs,
            scratch_shapes=scratch
            + [
                pltpu.VMEM((GROUP * BLOCK, HD), jnp.bfloat16),
                pltpu.SemaphoreType.DMA((heads * len(blocks) * PMAX + 1,)),
            ],
        ),
        compiler_params=params(ATTEND_MIB),
        cost_estimate=SMALL,
        name="attend_heads_" + "_".join(map(str, group)) + "_blocks_" + "_".join(map(str, blocks)),
    )(table, queries, resp_kv, *operands, *buffers)


def pages_shape(count):
    return jax.ShapeDtypeStruct((count * BLOCK, PAIR), jnp.bfloat16)


def pack_send(wide, cores, groups, caps, skip, ctrl, pool, planned=False):
    any_spec = pl.BlockSpec(memory_space=pl.ANY)
    pages = PROMPTS * ((PMAX + wide - 1) // wide)
    rooms = (caps.near, caps.near, caps.far)
    if groups is None:
        shapes = [jax.ShapeDtypeStruct((n * BLOCK, pool.shape[1]), jnp.bfloat16) for n in rooms]
    else:
        shapes = [pages_shape(n * len(group)) for group in groups for n in rooms]
    heads = 1 if groups is None else sum(map(len, groups))
    out_specs = [any_spec] * len(shapes)
    scratch = [pltpu.SemaphoreType.DMA((3, pages, heads))]
    if planned:
        shapes = shapes + [jax.ShapeDtypeStruct((TABLE,), jnp.int32)]
        out_specs = out_specs + [pl.BlockSpec(memory_space=pltpu.SMEM)]
        scratch.append(pltpu.SMEM((wide * SUMS,), jnp.int32))
    return pl.pallas_call(
        lambda *refs: send_kernel(wide, cores, groups, caps, skip, planned, *refs),
        out_shape=shapes,
        grid_spec=pltpu.PrefetchScalarGridSpec(
            num_scalar_prefetch=1,
            grid=(1,),
            in_specs=[pl.BlockSpec(pool.shape, lambda i, c: (0, 0))],
            out_specs=out_specs,
            scratch_shapes=scratch,
        ),
        compiler_params=params(8),
        cost_estimate=SMALL,
        name="pack_extra" if groups is None else f"pack_send_{groups[0][0]}",
    )(ctrl, pool)


def pack_share(cores, caps, h, g, table, buffers):
    any_spec = pl.BlockSpec(memory_space=pl.ANY)
    return pl.pallas_call(
        lambda *refs: share_kernel(cores, caps, h, g, *refs),
        out_shape=pages_shape(PMAX),
        grid_spec=pltpu.PrefetchScalarGridSpec(
            num_scalar_prefetch=1,
            grid=(1,),
            in_specs=[any_spec] * len(buffers),
            out_specs=any_spec,
            scratch_shapes=[pltpu.SemaphoreType.DMA((PMAX,))],
        ),
        compiler_params=params(6),
        cost_estimate=SMALL,
        name=f"pack_share_{g}",
    )(table, *buffers)


def pack_relay(cores, caps, h, g, ctrl, far, left, right):
    any_spec = pl.BlockSpec(memory_space=pl.ANY)
    return pl.pallas_call(
        lambda *refs: relay_kernel(cores, caps, h, *refs),
        out_shape=pages_shape(2 * caps.relay),
        grid_spec=pltpu.PrefetchScalarGridSpec(
            num_scalar_prefetch=1,
            grid=(1,),
            in_specs=[any_spec] * 3,
            out_specs=any_spec,
            scratch_shapes=[pltpu.SemaphoreType.DMA((2,))],
        ),
        compiler_params=params(6),
        cost_estimate=SMALL,
        name=f"pack_relay_{g}",
    )(ctrl, far, left, right)


def after(value, *earlier):
    return lax.optimization_barrier((value, *earlier))[0]


def line_attend(wide, cores, caps, ctrl, queries, resp_kv, pool, weight):
    heads = resp_kv.shape[1] // PAIR
    share = weight.shape[1] // 2

    def hop(x, moves):
        pairs = [(a * cores + c, b * cores + c) for a, b in moves for c in range(cores)]
        return lax.ppermute(x, "wide", pairs)

    swap = [(d, d // cores * cores + (cores - 1 - d % cores)) for d in range(wide)]

    def spread(right, left, far):
        return (
            hop(right, [(0, 1), (1, 2), (2, 3)]),
            hop(left, [(3, 2), (2, 1), (1, 0)]),
            hop(far, [(0, 2), (3, 1)]),
        )

    past = Caps(1, 1, 0)

    def past_the_end(ctrl, pool):
        skip = (caps.near, caps.near, caps.far)
        lists = pack_send(wide, cores, None, past, skip, ctrl, pool)
        return jnp.concatenate(spread(*lists), axis=0)

    def nothing(ctrl, pool):
        return jnp.zeros((3 * past.near * BLOCK, pool.shape[1]), pool.dtype)

    both, last = list(range(RB_DEV)), heads - 1
    half = heads // 2
    groups = [[g] for g in range(half)] + [list(range(half, heads))]
    *lists, table = pack_send(wide, cores, groups[:1], caps, (0, 0, 0), ctrl, pool, True)
    sends, spreads, held, parts = {0: lists}, {}, {}, []

    def relay(g, plan):
        n = min(g, half)
        if n not in spreads:
            spreads[n] = spread(*sends[n])
            if n + 1 < len(groups):
                sends[n + 1] = pack_send(wide, cores, [groups[n + 1]], caps, (0, 0, 0), ctrl, pool)
                plan = after(plan, sends[n + 1][0])
        left, right, far = spreads[n]
        onward = pack_relay(cores, caps, g - n, g, plan, far, left, right)
        held[g] = g - n, [pool, left, right, far, hop(onward, [(2, 3), (1, 0)])]
        return onward

    onward = relay(0, ctrl)
    over = after(table, onward)[OVER_AT] == 1
    extra = lax.cond(over, past_the_end, nothing, ctrl, pool)

    def exchange(g, plan):
        h, buffers = held[g]
        shared = pack_share(cores, caps, h, g, plan, buffers + [extra])
        return h, buffers + [lax.ppermute(shared, "wide", swap), extra]

    theirs, summed, waits = table[THEIRS_AT] * share, None, ctrl
    for g in range(last):
        onward = relay(g + 1, waits)
        h, buffers = exchange(g, after(table, onward))
        parts += attend([g], h, both, False, caps, table, queries, resp_kv, buffers)
        waits = after(ctrl, parts[-1])
        if g == 0:
            summed = project(parts, weight, 0, theirs, share, jnp.float32)
            waits = after(ctrl, summed)
    h, buffers = exchange(last, after(table, parts[-1]) if parts else table)
    if last > 1:
        summed = project(parts[1:], weight, 1, theirs, share, jnp.float32, summed)
    ends, terms, plan = [], [], table
    for b in both:
        end, term = attend(
            [last], h, [b], True, caps, plan, queries, resp_kv, buffers, weight, share, summed
        )
        ends.append(end)
        terms.append(term)
        plan = after(table, end)
    return parts + [jnp.concatenate(ends, axis=0)], terms


def project_kernel(carried, at, *refs):
    parts, weight, out = refs[: -2 - carried], refs[-2 - carried], refs[-1]
    total, row = refs[-2][...] if carried else None, 0
    for part in parts:
        end = row + part.shape[1]
        term = jnp.dot(part[...], weight[row:end, :], preferred_element_type=jnp.float32)
        total, row = term if total is None else total + term, end
    out[...] = total.astype(out.dtype)


def project(parts, weight, first, first_column, columns, kept=jnp.bfloat16, summed=None):
    tokens, rows = parts[0].shape[0], sum(part.shape[1] for part in parts)
    tile = math.gcd(columns, 512)
    assert weight.shape[1] % tile == 0
    at = jnp.reshape(first_column // tile, (1,)).astype(jnp.int32)
    skip = first * WIDTH
    if skip % rows:
        weight_spec = pl.BlockSpec(
            (pl.Element(rows), pl.Element(tile)), lambda i, at: (skip, (at[0] + i) * tile)
        )
    else:
        weight_spec = pl.BlockSpec((rows, tile), lambda i, at: (skip // rows, at[0] + i))
    operands, in_specs = [*parts, weight], [
        pl.BlockSpec(part.shape, lambda i, at: (0, 0)) for part in parts
    ] + [weight_spec]
    if summed is not None:
        operands.append(summed)
        in_specs.append(pl.BlockSpec((tokens, tile), lambda i, at: (0, i)))
    return pl.pallas_call(
        lambda *refs: project_kernel(summed is not None, *refs),
        out_shape=jax.ShapeDtypeStruct((tokens, columns), kept),
        grid_spec=pltpu.PrefetchScalarGridSpec(
            num_scalar_prefetch=1,
            grid=(columns // tile,),
            in_specs=in_specs,
            out_specs=pl.BlockSpec((tokens, tile), lambda i, at: (0, i)),
        ),
        compiler_params=params(PROJECT_MIB),
        cost_estimate=SMALL,
        name="project",
    )(at, *operands)


def local(
    queries, resp_kv, prefix_pool, out_weight, pre_len, prompt_blocks, prompt_owner, resp_seg
):
    wide, groups = lax.axis_size("wide"), lax.axis_size("tp") * lax.axis_size("sub")
    cores = 2 // lax.axis_size("sub")
    heads = resp_kv.shape[1] // PAIR
    me = lax.axis_index("wide").astype(jnp.int32)
    group = lax.axis_index("tp") * lax.axis_size("sub") + lax.axis_index("sub")
    where = jnp.stack([me, (1 - group).astype(jnp.int32)])
    ctrl = jnp.concatenate([pre_len, prompt_blocks, prompt_owner, resp_seg, where])
    columns = out_weight.shape[1]
    share = columns // groups
    if wide == 8 and cores == 2 and groups == 2:
        parts, theirs = line_attend(
            wide, cores, CAPS, ctrl, queries, resp_kv, prefix_pool, out_weight
        )
        axis = "tp" if lax.axis_size("tp") == 2 else "sub"
        arrived = [lax.ppermute(terms, axis, [(0, 1), (1, 0)]) for terms in theirs]
        half = share // 2
        mine = [
            project(parts, out_weight, 0, group * share, half),
            project(parts, out_weight, 0, after(group, arrived[0]) * share + half, half),
        ]
        mine = jnp.concatenate(mine, axis=1)
        arrived = jnp.concatenate(arrived, axis=0)
        return (mine.astype(jnp.float32) + arrived.astype(jnp.float32)).astype(jnp.bfloat16)
    table = make_plan(wide, cores, False, ctrl)
    buffers = [lax.all_gather(prefix_pool, "wide", axis=0, tiled=True)]
    blocks = list(range(RB_DEV))
    parts = [
        attend([g], 0, blocks, False, CAPS, table, queries, resp_kv, buffers)[0] for g in range(heads)
    ]
    terms = project(parts, out_weight, 0, jnp.int32(0), columns)
    return lax.psum_scatter(terms, ("tp", "sub"), scatter_dimension=1, tiled=True)


def solution(mesh):
    return jax.shard_map(
        local,
        mesh=mesh,
        in_specs=(
            P(("parts", "wide"), ("tp", "sub")),
            P(("parts", "wide"), ("tp", "sub")),
            P(("parts", "wide"), ("tp", "sub")),
            P(("tp", "sub"), None),
            P("parts"),
            P("parts"),
            P("parts"),
            P(("parts", "wide")),
        ),
        out_specs=P(("parts", "wide"), ("tp", "sub")),
        check_vma=False,
    )
```

```python
import math

import jax
import jax.numpy as jnp
from jax import lax
from jax.experimental import pallas as pl
from jax.experimental.pallas import tpu as pltpu
from jax.sharding import PartitionSpec as P

HD = 128
BLOCK = 128
RB_DEV = 2
PROMPTS = 4
PMAX = 16
GROUP = 8
PAIR = 2 * HD
WIDTH = GROUP * HD
ROWS = 512
SPAN = 4
NEG_LARGE = -1e30
SCALE = math.log2(math.e) / math.sqrt(HD)
MIB = 1024 * 1024
ATTEND_MIB, PROJECT_MIB = 28, 18
SMALL = pl.CostEstimate(flops=1 << 20, bytes_accessed=1 << 14, transcendentals=0)

LEN_AT, BLOCKS_AT, OWNER_AT, SEG_AT, ME_AT, OTHER_AT = 0, 4, 8, 12, 14, 15


def params(mib):
    return pltpu.CompilerParams(vmem_limit_bytes=mib * MIB)


def as_int(flag):
    return jnp.where(flag, 1, 0)


class Layout:
    def __init__(self, ctrl, wide, cores):
        self.ctrl, self.wide, self.cores = ctrl, wide, cores
        self.stride = (PMAX + wide - 1) // wide
        self.me = ctrl[ME_AT]
        self.z, self.core = self.div(self.me, cores), self.mod(self.me, cores)
        ends, total = [], 0
        for p in range(PROMPTS):
            total = total + ctrl[BLOCKS_AT + p] + (RB_DEV - 1)
            ends.append(total)
        self.ends = ends

    def mod(self, value, size):
        return value & (size - 1) if size & (size - 1) == 0 else lax.rem(value, size)

    def div(self, value, size):
        if size & (size - 1) == 0:
            return lax.shift_right_logical(value, size.bit_length() - 1)
        return lax.div(value, size)

    def prompt_of(self, block):
        return sum(as_int(block >= end) for end in self.ends[:-1])

    def first_of(self, chip):
        return self.prompt_of(chip * self.cores * RB_DEV)

    def last_of(self, chip):
        return self.prompt_of((chip + 1) * self.cores * RB_DEV - 1)

    def length(self, p):
        return self.ctrl[LEN_AT + p]

    def held_by(self, p, j):
        return self.mod(self.ctrl[OWNER_AT + p] + j, self.wide)

    def held(self, p, who):
        first = self.mod(who - self.ctrl[OWNER_AT + p] + self.wide, self.wide)
        return sum(as_int(first + k * self.wide < self.length(p)) for k in range(self.stride))

    def listed(self, which, rank, room):
        return jnp.where(
            rank < room, which * CODE + rank, (EXTRA + which - 1) * CODE + rank - room
        )

    def in_plane(self, p, j, sums):
        who = self.held_by(p, j)
        chip = self.div(who, self.cores)
        gap = chip - self.z
        k = self.div(j, self.wide)
        at = who * SUMS
        down = sums[at + PROMPTS] - sums[at + p + 1] + k
        up = sums[at + p] + k
        near_down = down - jnp.where(
            chip == 0, sums[at + PROMPTS] - sums[at + self.last_of(1) + 1], 0
        )
        near_up = up - jnp.where(chip == 3, sums[at + self.first_of(2)], 0)
        far = jnp.where(gap < 0, down, up)
        two = (gap == 2) | (gap == -2)
        direct = two & ((self.z == 1) | (self.z == 2))
        code = jnp.where(two, 5 * CODE, 4 * CODE) + far
        code = jnp.where(direct, self.listed(3, far, CAPS.far), code)
        code = jnp.where(gap == 1, self.listed(2, near_up, CAPS.near), code)
        code = jnp.where(gap == -1, self.listed(1, near_down, CAPS.near), code)
        return jnp.where(gap == 0, p * self.stride + k, code)


CODE = 256
SHARED = 6
EXTRA = 7
SUMS = 8
SLOT_AT, SHARE_AT, SHARES_AT, LENGTH_AT, BASE_AT, LOW_AT, THEIRS_AT, OVER_AT, TABLE = (
    0, 32, 50, 52, 54, 56, 58, 59, 64
)


class Caps:
    def __init__(self, near, far, relay):
        self.near, self.far, self.relay = near, far, relay


CAPS = Caps(5, 5, 4)


def needs(lay, sums, cores):
    first, last = [lay.first_of(c) for c in range(4)], [lay.last_of(c) for c in range(4)]
    near, far = jnp.int32(0), jnp.int32(0)
    for core in range(cores):

        def held(chip, low, high, core=core):
            at = (chip * cores + core) * SUMS
            return sums[at + high + 1] - sums[at + low]

        top = PROMPTS - 1
        edge = [held(1, 0, last[0]), held(2, first[3], top)]
        for amount in edge + [
            held(0, first[1], last[1]),
            held(1, first[2], top),
            held(2, 0, last[1]),
            held(3, first[2], last[2]),
        ]:
            near = jnp.maximum(near, amount)
        for amount in (held(0, first[2], top), held(3, 0, last[1])):
            far = jnp.maximum(far, amount)
    return near, far


def plan_kernel(wide, cores, line, ctrl, table, sums):
    lay = Layout(ctrl, wide, cores)
    half = PMAX // cores
    table[THEIRS_AT] = ctrl[OTHER_AT]
    table[OVER_AT] = 0
    if line:

        def tally(who, carry):
            total = jnp.int32(0)
            for p in range(PROMPTS):
                sums[who * SUMS + p] = total
                total = total + lay.held(p, who)
            sums[who * SUMS + PROMPTS] = total
            return carry

        lax.fori_loop(0, wide, tally, 0)
        near, far = needs(lay, sums, cores)
        over = (near > CAPS.near) | (far > CAPS.far)
        table[OVER_AT] = as_int(over)

    def prompts_of(device):
        return [lay.prompt_of(device * RB_DEV + b) for b in range(RB_DEV)]

    mine = prompts_of(lay.me)
    same = mine[0] == mine[1]
    joined = same & (ctrl[SEG_AT] == ctrl[SEG_AT + 1])
    for slot in range(RB_DEV):
        p = mine[slot]
        count = lay.length(p)
        table[LENGTH_AT + slot] = count
        if slot == 1:
            count = jnp.where(same, 0, count)
        table[BASE_AT + slot] = jnp.where(same, 0, PMAX) if slot else 0
        table[LOW_AT + slot] = jnp.where(joined, 0, BLOCK) if slot else 0

        def place(j, carry, slot=slot, p=p):
            who = lay.held_by(p, j)
            code = (who * PROMPTS + p) * lay.stride + lay.div(j, wide)
            if line:
                shared = slot * half + lay.div(j, cores)
                passed = jnp.where(
                    lay.mod(who, cores) == lay.core,
                    lay.in_plane(p, j, sums),
                    SHARED * CODE + shared,
                )
                code = passed
            table[SLOT_AT + slot * PMAX + j] = code
            return carry

        lax.fori_loop(0, count, place, 0)
    if not line:
        return
    theirs = prompts_of(lay.z * cores + (cores - 1 - lay.core))
    for slot in range(RB_DEV):
        p = theirs[slot]
        shift = lay.mod(lay.core - ctrl[OWNER_AT + p] + wide, cores)
        count = lay.div(lay.length(p) - shift + cores - 1, cores)
        if slot == 1:
            count = jnp.where(theirs[1] == theirs[0], 0, count)
        table[SHARES_AT + slot] = count

        def share(i, carry, slot=slot, p=p, shift=shift):
            table[SHARE_AT + slot * half + i] = lay.in_plane(p, i * cores + shift, sums)
            return carry

        lax.fori_loop(0, count, share, 0)


def make_plan(wide, cores, line, ctrl):
    return pl.pallas_call(
        lambda *refs: plan_kernel(wide, cores, line, *refs),
        out_shape=jax.ShapeDtypeStruct((TABLE,), jnp.int32),
        in_specs=[pl.BlockSpec(memory_space=pltpu.SMEM)],
        out_specs=pl.BlockSpec(memory_space=pltpu.SMEM),
        scratch_shapes=[pltpu.SMEM((wide * SUMS,), jnp.int32)],
        compiler_params=params(6),
        name="plan",
    )(ctrl)


def spot(ref, page):
    return ref.at[pl.ds(pl.multiple_of(page * BLOCK, BLOCK), BLOCK), :]


def page_at(buffer, page, column):
    rows = pl.ds(pl.multiple_of(page * BLOCK, BLOCK), BLOCK)
    return buffer.at[rows, pl.ds(column if buffer.shape[1] > PAIR else 0, PAIR)]


def start_page(buffers, code, column, target, sem):
    which = lax.shift_right_logical(code, CODE.bit_length() - 1)
    page = code & (CODE - 1)
    for i, buffer, offset in buffers:

        @pl.when(which == i)
        def _(buffer=buffer, offset=offset):
            source = page_at(buffer, page + offset, column)
            pltpu.make_async_copy(source, target, sem).start()


def wait_page(target, sem):
    pltpu.make_async_copy(target, target, sem).wait()


def send_kernel(wide, cores, groups, caps, skip, planned, ctrl, pool, *refs):
    if planned:
        *outs, table, sems, sums = refs
    else:
        *outs, sems = refs
    rooms = (caps.near, caps.near, caps.far)
    lay = Layout(ctrl, wide, cores)
    z, last = lay.z, wide // cores - 1
    held = [lay.held(p, lay.me) for p in range(PROMPTS)]

    def above(p, top):
        return sum([jnp.where(o <= top, held[o], 0) for o in range(p + 1, PROMPTS)], jnp.int32(0))

    def below(p, low):
        return sum([jnp.where(o >= low, held[o], 0) for o in range(p)], jnp.int32(0))

    near_top = jnp.where(z == 0, lay.last_of(1), PROMPTS - 1)
    near_low = jnp.where(z == last, lay.first_of(2), 0)
    first_up, last_down = lay.first_of(z + 1), lay.last_of(z - 1)
    first_two, last_one = lay.first_of(2), lay.last_of(1)
    plans = []
    for p in range(PROMPTS):
        right = (z < last) & (p >= first_up) & (p <= near_top)
        left = (z > 0) & (p >= near_low) & (p <= last_down)
        far_up = (z == 0) & (p >= first_two)
        far_down = (z == last) & (p <= last_one)
        ranks = (above(p, near_top), below(p, near_low), above(p, PROMPTS - 1), below(p, 0))
        for k in range(lay.stride):
            for lane, wanted, rank in zip((0, 1, 2, 2), (right, left, far_up, far_down), ranks):
                at = rank + k - skip[lane]
                fits = (k < held[p]) & (at >= 0) & (at < rooms[lane])
                plans.append((wanted & fits, p * lay.stride + k, lane, at))

    def copies(plan):
        _, page, lane, rank = plan
        if groups is None:
            return [
                pltpu.make_async_copy(
                    spot(pool, page), spot(outs[lane], rank), sems.at[lane, page, 0]
                )
            ]
        return [
            pltpu.make_async_copy(
                page_at(pool, page, g * PAIR),
                spot(outs[n * 3 + lane], h * rooms[lane] + rank),
                sems.at[lane, page, n * len(groups[0]) + h],
            )
            for n, group in enumerate(groups)
            for h, g in enumerate(group)
        ]

    for plan in plans:

        @pl.when(plan[0])
        def _(plan=plan):
            for copy in copies(plan):
                copy.start()

    if planned:
        plan_kernel(wide, cores, True, ctrl, table, sums)
    for plan in plans:

        @pl.when(plan[0])
        def _(plan=plan):
            for copy in copies(plan):
                copy.wait()


def relay_kernel(cores, caps, h, ctrl, far, left, right, out, sems):
    rows = caps.relay * BLOCK

    def copy(source, room, section):
        target = out.at[pl.ds(section * rows, rows), :]
        return pltpu.make_async_copy(
            source.at[pl.ds(h * room * BLOCK, rows), :], target, sems.at[section]
        )

    inner = ctrl[ME_AT] == 2 * cores
    for core in range(1, cores):
        inner = inner | (ctrl[ME_AT] == 2 * cores + core)
    copy(far, caps.far, 0).start()
    pl.when(inner)(lambda: copy(left, caps.near, 1).start())
    pl.when(jnp.logical_not(inner))(lambda: copy(right, caps.near, 1).start())
    copy(far, caps.far, 0).wait()
    copy(left, caps.near, 1).wait()


def numbered(refs, caps, h):
    if len(refs) == 1:
        return [(0, refs[0], 0)]
    offsets = (0, h * caps.near, h * caps.near, h * caps.far, 0)
    found = list(zip(range(5), refs[:5], offsets)) + [(5, refs[4], caps.relay)]
    if len(refs) == 7:
        found.append((SHARED, refs[5], 0))
    return found + [(EXTRA + i, refs[-1], i) for i in range(3)]


def share_kernel(cores, caps, h, g, table, *refs):
    out, sems = refs[-2:]
    half = PMAX // cores
    buffers = numbered(refs[:-2], caps, h)
    for slot in range(RB_DEV):

        def begin(i, carry, slot=slot):
            at = slot * half + i
            start_page(buffers, table[SHARE_AT + at], g * PAIR, spot(out, at), sems.at[at])
            return carry

        lax.fori_loop(0, table[SHARES_AT + slot], begin, 0)
    for slot in range(RB_DEV):

        def finish(i, carry, slot=slot):
            at = slot * half + i
            wait_page(spot(out, at), sems.at[at])
            return carry

        lax.fori_loop(0, table[SHARES_AT + slot], finish, 0)


def attend_kernel(group, first, blocks, caps, carried, project, table, queries, own, *refs):
    refs = list(refs)
    weight = refs.pop(0) if project else None
    summed = refs.pop(0) if carried else None
    sems, stacked = refs.pop(), refs.pop()
    slab = refs.pop() if project else None
    store = refs.pop()
    terms = refs.pop() if project else None
    out = refs.pop()
    heads, room = len(group), len(blocks) * PMAX

    def region(i):
        if i == 0:
            return 0, table[LENGTH_AT + blocks[0]]
        base = table[BASE_AT + blocks[i]]
        return base, jnp.where(base == 0, 0, table[LENGTH_AT + blocks[i]])

    for h, g in enumerate(group):
        buffers = numbered(refs, caps, first + h)
        for i, b in enumerate(blocks):
            base, count = region(i)
            codes = SLOT_AT + table[BASE_AT + b]

            def begin(j, carry, h=h, g=g, buffers=buffers, base=base, codes=codes):
                at = h * room + base + j
                target, sem = spot(store, at), sems.at[at]
                start_page(buffers, table[codes + j], g * PAIR, target, sem)
                return carry

            lax.fori_loop(0, count, begin, 0)
            length = table[LENGTH_AT + b]

            def clear(j, carry, h=h, base=base):
                rows = pl.ds(pl.multiple_of((h * room + base + j) * BLOCK, BLOCK), BLOCK)
                store[rows, :] = jnp.zeros((BLOCK, PAIR), jnp.bfloat16)
                return carry

            lax.fori_loop(length, (length + SPAN - 1) & -SPAN, clear, 0)
    if project:
        share = slab.shape[1]
        theirs = pl.multiple_of(table[THEIRS_AT] * share, share)
        fetch = pltpu.make_async_copy(
            weight.at[pl.ds(group[0] * WIDTH, heads * WIDTH), pl.ds(theirs, share)],
            slab,
            sems.at[heads * room],
        )
        fetch.start()

    def one_block(h, i, b, base, count):
        tokens = pl.ds(pl.multiple_of(i * BLOCK, BLOCK), BLOCK)

        def columns(width, extra=0):
            return pl.ds(pl.multiple_of(h * width + extra, HD), min(width, HD))

        for e in range(GROUP):
            stacked[e * BLOCK : (e + 1) * BLOCK, :] = queries[tokens, columns(WIDTH, e * HD)]
        base = h * room + base

        def finish(j, carry):
            wait_page(spot(store, base + j), sems.at[base + j])
            return carry

        lax.fori_loop(0, count, finish, 0)
        length = table[LENGTH_AT + b]
        span = RB_DEV * BLOCK
        row = lax.broadcasted_iota(jnp.int32, (ROWS, span), 0) & (BLOCK - 1)
        key = lax.broadcasted_iota(jnp.int32, (ROWS, span), 1)
        own_mask = (key <= row + b * BLOCK) & (key >= table[LOW_AT + b])

        def run(spans):
            wide_key = lax.broadcasted_iota(jnp.int32, (ROWS, SPAN * BLOCK), 1)
            last_mask = wide_key < (length - (spans - 1) * SPAN) * BLOCK
            pieces = [(own[:, columns(PAIR)], own[:, columns(PAIR, HD)])]
            for t in range(spans):
                at = pl.multiple_of((base + t * SPAN) * BLOCK, BLOCK)
                piece = store[pl.ds(at, SPAN * BLOCK), :]
                pieces.append((piece[:, :HD], piece[:, HD:]))

            def score(r, t):
                scores = lax.dot_general(
                    stacked[r * ROWS : (r + 1) * ROWS, :],
                    pieces[t][0],
                    (((1,), (1,)), ((), ())),
                    preferred_element_type=jnp.float32,
                )
                if t == 0:
                    return jnp.where(own_mask, scores, NEG_LARGE)
                if t == spans:
                    return jnp.where(last_mask, scores, NEG_LARGE)
                return scores

            def highest(scores, sofar):
                for n in range(0, scores.shape[1], HD):
                    part = scores[:, n : n + HD]
                    sofar = part if sofar is None else jnp.maximum(sofar, part)
                return sofar

            def blend(scores, top, t):
                spread = jnp.concatenate([top] * (scores.shape[1] // HD), axis=1)
                weights = jnp.exp2((scores - spread) * SCALE).astype(jnp.bfloat16)
                values = pieces[t][1]
                values = jnp.concatenate([values, jnp.ones_like(values)], axis=1)
                return jnp.dot(weights, values, preferred_element_type=jnp.float32)

            chunks, ahead, peak = GROUP * BLOCK // ROWS, [], None
            for t in range(spans + 1):
                ahead.append(score(0, t))
                peak = highest(ahead[-1], peak)
            for r in range(chunks):
                now, ahead = ahead, []
                top = jnp.broadcast_to(jnp.max(peak, axis=1, keepdims=True), (ROWS, HD))
                total, peak = None, None
                for t in range(spans + 1):
                    if r + 1 < chunks:
                        ahead.append(score(r + 1, t))
                        peak = highest(ahead[-1], peak)
                    blended = blend(now[t], top, t)
                    total = blended if total is None else total + blended
                mean = (total[:, :HD] / total[:, HD:]).astype(jnp.bfloat16)
                for e in range(ROWS // BLOCK):
                    at = columns(WIDTH, (r * (ROWS // BLOCK) + e) * HD)
                    out[tokens, at] = mean[e * BLOCK : (e + 1) * BLOCK, :]

        spans = lax.shift_right_logical(length + SPAN - 1, SPAN.bit_length() - 1)
        for n in range(1, PMAX // SPAN + 1):
            pl.when(spans == n)(lambda n=n: run(n))

    def step(n, carry):
        if len(blocks) == 1:
            one_block(n, 0, blocks[0], *region(0))
            return carry
        h, i = lax.shift_right_logical(n, 1), n & 1
        base = jnp.where(i == 0, 0, region(1)[0])
        one_block(h, i, i, base, jnp.where(i == 0, region(0)[1], region(1)[1]))
        return carry

    lax.fori_loop(0, heads * len(blocks), step, 0)
    if project:
        fetch.wait()
        attended = out[...]
        width = math.gcd(share, 512)
        for n in range(0, share, width):
            term = jnp.dot(attended, slab[:, n : n + width], preferred_element_type=jnp.float32)
            if carried:
                term = term + summed[:, n : n + width]
            terms[:, n : n + width] = term.astype(terms.dtype)


def attend(
    group, first, blocks, last, caps, table, queries, resp_kv, buffers, weight=None, share=0, summed=None
):
    tokens, heads = len(blocks) * BLOCK, len(group)
    at = blocks[0] // len(blocks)
    project, carried = weight is not None, summed is not None
    any_spec = pl.BlockSpec(memory_space=pl.ANY)
    whole = pl.BlockSpec((tokens, share), lambda i, c: (0, 0))
    out_shape = [jax.ShapeDtypeStruct((tokens, heads * WIDTH), jnp.bfloat16)]
    out_specs = [pl.BlockSpec((tokens, heads * WIDTH), lambda i, c: (0, 0))]
    operands, in_specs = [], []
    scratch = [pltpu.VMEM((heads * len(blocks) * PMAX * BLOCK, PAIR), jnp.bfloat16)]
    if project:
        operands, in_specs = [weight], [any_spec]
        kept = jnp.bfloat16 if last else jnp.float32
        out_shape.append(jax.ShapeDtypeStruct((tokens, share), kept))
        out_specs.append(whole)
        scratch.append(pltpu.VMEM((heads * WIDTH, share), jnp.bfloat16))
    if carried:
        operands = operands + [summed]
        in_specs = in_specs + [pl.BlockSpec((tokens, share), lambda i, c: (at, 0))]
    column = group[0] // heads
    return pl.pallas_call(
        lambda *refs: attend_kernel(group, first, blocks, caps, carried, project, *refs),
        out_shape=out_shape,
        grid_spec=pltpu.PrefetchScalarGridSpec(
            num_scalar_prefetch=1,
            grid=(1,),
            in_specs=[
                pl.BlockSpec((tokens, heads * WIDTH), lambda i, c: (at, column)),
                pl.BlockSpec((RB_DEV * BLOCK, heads * PAIR), lambda i, c: (0, column)),
            ]
            + in_specs
            + [any_spec] * len(buffers),
            out_specs=out_specs,
            scratch_shapes=scratch
            + [
                pltpu.VMEM((GROUP * BLOCK, HD), jnp.bfloat16),
                pltpu.SemaphoreType.DMA((heads * len(blocks) * PMAX + 1,)),
            ],
        ),
        compiler_params=params(ATTEND_MIB),
        cost_estimate=SMALL,
        name="attend_heads_" + "_".join(map(str, group)) + "_blocks_" + "_".join(map(str, blocks)),
    )(table, queries, resp_kv, *operands, *buffers)


def pages_shape(count):
    return jax.ShapeDtypeStruct((count * BLOCK, PAIR), jnp.bfloat16)


def pack_send(wide, cores, groups, caps, skip, ctrl, pool, planned=False):
    any_spec = pl.BlockSpec(memory_space=pl.ANY)
    pages = PROMPTS * ((PMAX + wide - 1) // wide)
    rooms = (caps.near, caps.near, caps.far)
    if groups is None:
        shapes = [jax.ShapeDtypeStruct((n * BLOCK, pool.shape[1]), jnp.bfloat16) for n in rooms]
    else:
        shapes = [pages_shape(n * len(group)) for group in groups for n in rooms]
    heads = 1 if groups is None else sum(map(len, groups))
    out_specs = [any_spec] * len(shapes)
    scratch = [pltpu.SemaphoreType.DMA((3, pages, heads))]
    if planned:
        shapes = shapes + [jax.ShapeDtypeStruct((TABLE,), jnp.int32)]
        out_specs = out_specs + [pl.BlockSpec(memory_space=pltpu.SMEM)]
        scratch.append(pltpu.SMEM((wide * SUMS,), jnp.int32))
    return pl.pallas_call(
        lambda *refs: send_kernel(wide, cores, groups, caps, skip, planned, *refs),
        out_shape=shapes,
        grid_spec=pltpu.PrefetchScalarGridSpec(
            num_scalar_prefetch=1,
            grid=(1,),
            in_specs=[pl.BlockSpec(pool.shape, lambda i, c: (0, 0))],
            out_specs=out_specs,
            scratch_shapes=scratch,
        ),
        compiler_params=params(8),
        cost_estimate=SMALL,
        name="pack_extra" if groups is None else f"pack_send_{groups[0][0]}",
    )(ctrl, pool)


def pack_share(cores, caps, h, g, table, buffers):
    any_spec = pl.BlockSpec(memory_space=pl.ANY)
    return pl.pallas_call(
        lambda *refs: share_kernel(cores, caps, h, g, *refs),
        out_shape=pages_shape(PMAX),
        grid_spec=pltpu.PrefetchScalarGridSpec(
            num_scalar_prefetch=1,
            grid=(1,),
            in_specs=[any_spec] * len(buffers),
            out_specs=pl.BlockSpec((PMAX * BLOCK, PAIR), lambda i, c: (0, 0)),
            scratch_shapes=[pltpu.SemaphoreType.DMA((PMAX,))],
        ),
        compiler_params=params(6),
        cost_estimate=SMALL,
        name=f"pack_share_{g}",
    )(table, *buffers)


def pack_relay(cores, caps, h, g, ctrl, far, left, right):
    any_spec = pl.BlockSpec(memory_space=pl.ANY)
    return pl.pallas_call(
        lambda *refs: relay_kernel(cores, caps, h, *refs),
        out_shape=pages_shape(2 * caps.relay),
        grid_spec=pltpu.PrefetchScalarGridSpec(
            num_scalar_prefetch=1,
            grid=(1,),
            in_specs=[any_spec] * 3,
            out_specs=pl.BlockSpec((2 * caps.relay * BLOCK, PAIR), lambda i, c: (0, 0)),
            scratch_shapes=[pltpu.SemaphoreType.DMA((2,))],
        ),
        compiler_params=params(6),
        cost_estimate=SMALL,
        name=f"pack_relay_{g}",
    )(ctrl, far, left, right)


def after(value, *earlier):
    return lax.optimization_barrier((value, *earlier))[0]


def line_attend(wide, cores, caps, ctrl, queries, resp_kv, pool, weight):
    heads = resp_kv.shape[1] // PAIR
    share = weight.shape[1] // 2

    def hop(x, moves):
        pairs = [(a * cores + c, b * cores + c) for a, b in moves for c in range(cores)]
        return lax.ppermute(x, "wide", pairs)

    swap = [(d, d // cores * cores + (cores - 1 - d % cores)) for d in range(wide)]

    def spread(right, left, far):
        return (
            hop(right, [(0, 1), (1, 2), (2, 3)]),
            hop(left, [(3, 2), (2, 1), (1, 0)]),
            hop(far, [(0, 2), (3, 1)]),
        )

    past = Caps(1, 1, 0)

    def past_the_end(ctrl, pool):
        skip = (caps.near, caps.near, caps.far)
        lists = pack_send(wide, cores, None, past, skip, ctrl, pool)
        return jnp.concatenate(spread(*lists), axis=0)

    def nothing(ctrl, pool):
        return jnp.zeros((3 * past.near * BLOCK, pool.shape[1]), pool.dtype)

    both, last = list(range(RB_DEV)), heads - 1
    *lists, table = pack_send(wide, cores, [[0]], caps, (0, 0, 0), ctrl, pool, True)
    sends, held, parts = {0: lists}, {}, []

    def relay(g, plan):
        left, right, far = spread(*sends[g])
        if g + 1 < heads:
            sends[g + 1] = pack_send(wide, cores, [[g + 1]], caps, (0, 0, 0), ctrl, pool)
            plan = after(plan, sends[g + 1][0])
        onward = pack_relay(cores, caps, 0, g, plan, far, left, right)
        held[g] = [pool, left, right, far, hop(onward, [(2, 3), (1, 0)])]
        return onward

    onward = relay(0, ctrl)
    over = after(table, onward)[OVER_AT] == 1
    extra = lax.cond(over, past_the_end, nothing, ctrl, pool)

    def exchange(g, plan):
        shared = pack_share(cores, caps, 0, g, plan, held[g] + [extra])
        return held[g] + [lax.ppermute(shared, "wide", swap), extra]

    summed = None
    for g in range(last):
        onward = relay(g + 1, after(ctrl, parts[-1]) if parts else ctrl)
        buffers = exchange(g, after(table, onward))
        attended, summed = attend(
            [g], 0, both, False, caps, table, queries, resp_kv, buffers, weight, share, summed
        )
        parts.append(attended)
    buffers = exchange(last, after(table, parts[-1]) if parts else table)
    ends, terms, plan = [], [], table
    for b in both:
        end, term = attend(
            [last], 0, [b], True, caps, plan, queries, resp_kv, buffers, weight, share, summed
        )
        ends.append(end)
        terms.append(term)
        plan = after(table, end)
    return parts + [jnp.concatenate(ends, axis=0)], terms


def project_kernel(carried, at, *refs):
    parts, weight, out = refs[: -2 - carried], refs[-2 - carried], refs[-1]
    total, row = refs[-2][...] if carried else None, 0
    for part in parts:
        end = row + part.shape[1]
        term = jnp.dot(part[...], weight[row:end, :], preferred_element_type=jnp.float32)
        total, row = term if total is None else total + term, end
    out[...] = total.astype(out.dtype)


def project(parts, weight, first, first_column, columns, kept=jnp.bfloat16, summed=None):
    tokens, rows = parts[0].shape[0], sum(part.shape[1] for part in parts)
    tile = math.gcd(columns, 512)
    assert weight.shape[1] % tile == 0
    at = jnp.reshape(first_column // tile, (1,)).astype(jnp.int32)
    skip = first * WIDTH
    if skip % rows:
        weight_spec = pl.BlockSpec(
            (pl.Element(rows), pl.Element(tile)), lambda i, at: (skip, (at[0] + i) * tile)
        )
    else:
        weight_spec = pl.BlockSpec((rows, tile), lambda i, at: (skip // rows, at[0] + i))
    operands, in_specs = [*parts, weight], [
        pl.BlockSpec(part.shape, lambda i, at: (0, 0)) for part in parts
    ] + [weight_spec]
    if summed is not None:
        operands.append(summed)
        in_specs.append(pl.BlockSpec((tokens, tile), lambda i, at: (0, i)))
    return pl.pallas_call(
        lambda *refs: project_kernel(summed is not None, *refs),
        out_shape=jax.ShapeDtypeStruct((tokens, columns), kept),
        grid_spec=pltpu.PrefetchScalarGridSpec(
            num_scalar_prefetch=1,
            grid=(columns // tile,),
            in_specs=in_specs,
            out_specs=pl.BlockSpec((tokens, tile), lambda i, at: (0, i)),
        ),
        compiler_params=params(PROJECT_MIB),
        cost_estimate=SMALL,
        name="project",
    )(at, *operands)


def local(
    queries, resp_kv, prefix_pool, out_weight, pre_len, prompt_blocks, prompt_owner, resp_seg
):
    wide, groups = lax.axis_size("wide"), lax.axis_size("tp") * lax.axis_size("sub")
    cores = 2 // lax.axis_size("sub")
    heads = resp_kv.shape[1] // PAIR
    me = lax.axis_index("wide").astype(jnp.int32)
    group = lax.axis_index("tp") * lax.axis_size("sub") + lax.axis_index("sub")
    where = jnp.stack([me, (1 - group).astype(jnp.int32)])
    ctrl = jnp.concatenate([pre_len, prompt_blocks, prompt_owner, resp_seg, where])
    columns = out_weight.shape[1]
    share = columns // groups
    if wide == 8 and cores == 2 and groups == 2:
        parts, theirs = line_attend(
            wide, cores, CAPS, ctrl, queries, resp_kv, prefix_pool, out_weight
        )
        axis = "tp" if lax.axis_size("tp") == 2 else "sub"
        arrived = [lax.ppermute(terms, axis, [(0, 1), (1, 0)]) for terms in theirs]
        half = share // 2
        mine = [
            project(parts, out_weight, 0, group * share, half),
            project(parts, out_weight, 0, after(group, arrived[0]) * share + half, half),
        ]
        mine = jnp.concatenate(mine, axis=1)
        arrived = jnp.concatenate(arrived, axis=0)
        return (mine.astype(jnp.float32) + arrived.astype(jnp.float32)).astype(jnp.bfloat16)
    table = make_plan(wide, cores, False, ctrl)
    buffers = [lax.all_gather(prefix_pool, "wide", axis=0, tiled=True)]
    blocks = list(range(RB_DEV))
    parts = [
        attend([g], 0, blocks, False, CAPS, table, queries, resp_kv, buffers)[0] for g in range(heads)
    ]
    terms = project(parts, out_weight, 0, jnp.int32(0), columns)
    return lax.psum_scatter(terms, ("tp", "sub"), scatter_dimension=1, tiled=True)


def solution(mesh):
    return jax.shard_map(
        local,
        mesh=mesh,
        in_specs=(
            P(("parts", "wide"), ("tp", "sub")),
            P(("parts", "wide"), ("tp", "sub")),
            P(("parts", "wide"), ("tp", "sub")),
            P(("tp", "sub"), None),
            P("parts"),
            P("parts"),
            P("parts"),
            P(("parts", "wide")),
        ),
        out_specs=P(("parts", "wide"), ("tp", "sub")),
        check_vma=False,
    )
```

```python
import math

import jax
import jax.numpy as jnp
from jax import lax
from jax.experimental import pallas as pl
from jax.experimental.pallas import tpu as pltpu
from jax.sharding import PartitionSpec as P

HD = 128
BLOCK = 128
RB_DEV = 2
PROMPTS = 4
PMAX = 16
GROUP = 8
PAIR = 2 * HD
WIDTH = GROUP * HD
ROWS = 512
SPAN = 4
NEG_LARGE = -1e30
SCALE = math.log2(math.e) / math.sqrt(HD)
MIB = 1024 * 1024
ATTEND_MIB, PROJECT_MIB = 28, 18
SMALL = pl.CostEstimate(flops=1 << 20, bytes_accessed=1 << 14, transcendentals=0)

LEN_AT, BLOCKS_AT, OWNER_AT, SEG_AT, ME_AT, OTHER_AT = 0, 4, 8, 12, 14, 15


def params(mib):
    return pltpu.CompilerParams(vmem_limit_bytes=mib * MIB)


def as_int(flag):
    return jnp.where(flag, 1, 0)


class Layout:
    def __init__(self, ctrl, wide, cores):
        self.ctrl, self.wide, self.cores = ctrl, wide, cores
        self.stride = (PMAX + wide - 1) // wide
        self.me = ctrl[ME_AT]
        self.z, self.core = self.div(self.me, cores), self.mod(self.me, cores)
        ends, total = [], 0
        for p in range(PROMPTS):
            total = total + ctrl[BLOCKS_AT + p] + (RB_DEV - 1)
            ends.append(total)
        self.ends = ends

    def mod(self, value, size):
        return value & (size - 1) if size & (size - 1) == 0 else lax.rem(value, size)

    def div(self, value, size):
        if size & (size - 1) == 0:
            return lax.shift_right_logical(value, size.bit_length() - 1)
        return lax.div(value, size)

    def prompt_of(self, block):
        return sum(as_int(block >= end) for end in self.ends[:-1])

    def first_of(self, chip):
        return self.prompt_of(chip * self.cores * RB_DEV)

    def last_of(self, chip):
        return self.prompt_of((chip + 1) * self.cores * RB_DEV - 1)

    def length(self, p):
        return self.ctrl[LEN_AT + p]

    def held_by(self, p, j):
        return self.mod(self.ctrl[OWNER_AT + p] + j, self.wide)

    def held(self, p, who):
        first = self.mod(who - self.ctrl[OWNER_AT + p] + self.wide, self.wide)
        return sum(as_int(first + k * self.wide < self.length(p)) for k in range(self.stride))

    def listed(self, which, rank, room):
        return jnp.where(
            rank < room, which * CODE + rank, (EXTRA + which - 1) * CODE + rank - room
        )

    def in_plane(self, p, j, sums):
        who = self.held_by(p, j)
        chip = self.div(who, self.cores)
        gap = chip - self.z
        k = self.div(j, self.wide)
        at = who * SUMS
        down = sums[at + PROMPTS] - sums[at + p + 1] + k
        up = sums[at + p] + k
        near_down = down - jnp.where(
            chip == 0, sums[at + PROMPTS] - sums[at + self.last_of(1) + 1], 0
        )
        near_up = up - jnp.where(chip == 3, sums[at + self.first_of(2)], 0)
        far = jnp.where(gap < 0, down, up)
        two = (gap == 2) | (gap == -2)
        direct = two & ((self.z == 1) | (self.z == 2))
        code = jnp.where(two, 5 * CODE, 4 * CODE) + far
        code = jnp.where(direct, self.listed(3, far, CAPS.far), code)
        code = jnp.where(gap == 1, self.listed(2, near_up, CAPS.near), code)
        code = jnp.where(gap == -1, self.listed(1, near_down, CAPS.near), code)
        return jnp.where(gap == 0, p * self.stride + k, code)


CODE = 256
SHARED = 6
EXTRA = 7
SUMS = 8
SLOT_AT, SHARE_AT, SHARES_AT, LENGTH_AT, BASE_AT, LOW_AT, THEIRS_AT, OVER_AT, TABLE = (
    0, 32, 50, 52, 54, 56, 58, 59, 64
)


class Caps:
    def __init__(self, near, far, relay):
        self.near, self.far, self.relay = near, far, relay


CAPS = Caps(5, 5, 4)


def needs(lay, sums, cores):
    first, last = [lay.first_of(c) for c in range(4)], [lay.last_of(c) for c in range(4)]
    near, far = jnp.int32(0), jnp.int32(0)
    for core in range(cores):

        def held(chip, low, high, core=core):
            at = (chip * cores + core) * SUMS
            return sums[at + high + 1] - sums[at + low]

        top = PROMPTS - 1
        edge = [held(1, 0, last[0]), held(2, first[3], top)]
        for amount in edge + [
            held(0, first[1], last[1]),
            held(1, first[2], top),
            held(2, 0, last[1]),
            held(3, first[2], last[2]),
        ]:
            near = jnp.maximum(near, amount)
        for amount in (held(0, first[2], top), held(3, 0, last[1])):
            far = jnp.maximum(far, amount)
    return near, far


def plan_kernel(wide, cores, line, ctrl, table, sums):
    lay = Layout(ctrl, wide, cores)
    half = PMAX // cores
    table[THEIRS_AT] = ctrl[OTHER_AT]
    table[OVER_AT] = 0
    if line:

        def tally(who, carry):
            total = jnp.int32(0)
            for p in range(PROMPTS):
                sums[who * SUMS + p] = total
                total = total + lay.held(p, who)
            sums[who * SUMS + PROMPTS] = total
            return carry

        lax.fori_loop(0, wide, tally, 0)
        near, far = needs(lay, sums, cores)
        over = (near > CAPS.near) | (far > CAPS.far)
        table[OVER_AT] = as_int(over)

    def prompts_of(device):
        return [lay.prompt_of(device * RB_DEV + b) for b in range(RB_DEV)]

    mine = prompts_of(lay.me)
    same = mine[0] == mine[1]
    joined = same & (ctrl[SEG_AT] == ctrl[SEG_AT + 1])
    for slot in range(RB_DEV):
        p = mine[slot]
        count = lay.length(p)
        table[LENGTH_AT + slot] = count
        if slot == 1:
            count = jnp.where(same, 0, count)
        table[BASE_AT + slot] = jnp.where(same, 0, PMAX) if slot else 0
        table[LOW_AT + slot] = jnp.where(joined, 0, BLOCK) if slot else 0

        def place(j, carry, slot=slot, p=p):
            who = lay.held_by(p, j)
            code = (who * PROMPTS + p) * lay.stride + lay.div(j, wide)
            if line:
                shared = slot * half + lay.div(j, cores)
                passed = jnp.where(
                    lay.mod(who, cores) == lay.core,
                    lay.in_plane(p, j, sums),
                    SHARED * CODE + shared,
                )
                code = passed
            table[SLOT_AT + slot * PMAX + j] = code
            return carry

        lax.fori_loop(0, count, place, 0)
    if not line:
        return
    theirs = prompts_of(lay.z * cores + (cores - 1 - lay.core))
    for slot in range(RB_DEV):
        p = theirs[slot]
        shift = lay.mod(lay.core - ctrl[OWNER_AT + p] + wide, cores)
        count = lay.div(lay.length(p) - shift + cores - 1, cores)
        if slot == 1:
            count = jnp.where(theirs[1] == theirs[0], 0, count)
        table[SHARES_AT + slot] = count

        def share(i, carry, slot=slot, p=p, shift=shift):
            table[SHARE_AT + slot * half + i] = lay.in_plane(p, i * cores + shift, sums)
            return carry

        lax.fori_loop(0, count, share, 0)


def make_plan(wide, cores, line, ctrl):
    return pl.pallas_call(
        lambda *refs: plan_kernel(wide, cores, line, *refs),
        out_shape=jax.ShapeDtypeStruct((TABLE,), jnp.int32),
        in_specs=[pl.BlockSpec(memory_space=pltpu.SMEM)],
        out_specs=pl.BlockSpec(memory_space=pltpu.SMEM),
        scratch_shapes=[pltpu.SMEM((wide * SUMS,), jnp.int32)],
        compiler_params=params(6),
        name="plan",
    )(ctrl)


def spot(ref, page):
    return ref.at[pl.ds(pl.multiple_of(page * BLOCK, BLOCK), BLOCK), :]


def page_at(buffer, page, column):
    rows = pl.ds(pl.multiple_of(page * BLOCK, BLOCK), BLOCK)
    return buffer.at[rows, pl.ds(column if buffer.shape[1] > PAIR else 0, PAIR)]


def start_page(buffers, code, column, target, sem):
    which = lax.shift_right_logical(code, CODE.bit_length() - 1)
    page = code & (CODE - 1)
    for i, buffer, offset in buffers:

        @pl.when(which == i)
        def _(buffer=buffer, offset=offset):
            source = page_at(buffer, page + offset, column)
            pltpu.make_async_copy(source, target, sem).start()


def wait_page(target, sem):
    pltpu.make_async_copy(target, target, sem).wait()


def send_kernel(wide, cores, groups, caps, skip, planned, ctrl, pool, *refs):
    if planned:
        *outs, table, sems, sums = refs
    else:
        *outs, sems = refs
    rooms = (caps.near, caps.near, caps.far)
    lay = Layout(ctrl, wide, cores)
    z, last = lay.z, wide // cores - 1
    held = [lay.held(p, lay.me) for p in range(PROMPTS)]

    def above(p, top):
        return sum([jnp.where(o <= top, held[o], 0) for o in range(p + 1, PROMPTS)], jnp.int32(0))

    def below(p, low):
        return sum([jnp.where(o >= low, held[o], 0) for o in range(p)], jnp.int32(0))

    near_top = jnp.where(z == 0, lay.last_of(1), PROMPTS - 1)
    near_low = jnp.where(z == last, lay.first_of(2), 0)
    first_up, last_down = lay.first_of(z + 1), lay.last_of(z - 1)
    first_two, last_one = lay.first_of(2), lay.last_of(1)
    plans = []
    for p in range(PROMPTS):
        right = (z < last) & (p >= first_up) & (p <= near_top)
        left = (z > 0) & (p >= near_low) & (p <= last_down)
        far_up = (z == 0) & (p >= first_two)
        far_down = (z == last) & (p <= last_one)
        ranks = (above(p, near_top), below(p, near_low), above(p, PROMPTS - 1), below(p, 0))
        for k in range(lay.stride):
            for lane, wanted, rank in zip((0, 1, 2, 2), (right, left, far_up, far_down), ranks):
                at = rank + k - skip[lane]
                fits = (k < held[p]) & (at >= 0) & (at < rooms[lane])
                plans.append((wanted & fits, p * lay.stride + k, lane, at))

    def copies(plan):
        _, page, lane, rank = plan
        if groups is None:
            return [
                pltpu.make_async_copy(
                    spot(pool, page), spot(outs[lane], rank), sems.at[lane, page, 0]
                )
            ]
        return [
            pltpu.make_async_copy(
                page_at(pool, page, g * PAIR),
                spot(outs[n * 3 + lane], h * rooms[lane] + rank),
                sems.at[lane, page, n * len(groups[0]) + h],
            )
            for n, group in enumerate(groups)
            for h, g in enumerate(group)
        ]

    for plan in plans:

        @pl.when(plan[0])
        def _(plan=plan):
            for copy in copies(plan):
                copy.start()

    if planned:
        plan_kernel(wide, cores, True, ctrl, table, sums)
    for plan in plans:

        @pl.when(plan[0])
        def _(plan=plan):
            for copy in copies(plan):
                copy.wait()


def relay_kernel(cores, caps, ctrl, far, left, right, *refs):
    following, out, sems = refs[:-2], refs[-2], refs[-1]
    rows = caps.relay * BLOCK

    def copy(source, section):
        target = out.at[pl.ds(section * rows, rows), :]
        return pltpu.make_async_copy(source.at[pl.ds(0, rows), :], target, sems.at[section])

    at_left = at_right = False
    for core in range(cores):
        at_left = at_left | (ctrl[ME_AT] == cores + core)
        at_right = at_right | (ctrl[ME_AT] == 2 * cores + core)
    inner = at_left | at_right
    pl.when(inner)(lambda: copy(far, 0).start())
    pl.when(at_right)(lambda: copy(left, 1).start())
    pl.when(at_left)(lambda: copy(right, 1).start())

    @pl.when(inner)
    def _():
        copy(far, 0).wait()
        copy(far, 1).wait()

    for source in following:

        @pl.when(jnp.logical_not(inner))
        def _(source=source):
            target = out.at[pl.ds(0, caps.far * BLOCK), :]
            move = pltpu.make_async_copy(source, target, sems.at[2])
            move.start()
            move.wait()


def numbered(refs, caps, h):
    if len(refs) == 1:
        return [(0, refs[0], 0)]
    offsets = (0, h * caps.near, h * caps.near, h * caps.far, 0)
    found = list(zip(range(5), refs[:5], offsets)) + [(5, refs[4], caps.relay)]
    if len(refs) == 7:
        found.append((SHARED, refs[5], 0))
    return found + [(EXTRA + i, refs[-1], i) for i in range(3)]


def share_kernel(cores, caps, h, g, table, *refs):
    out, sems = refs[-2:]
    half = PMAX // cores
    buffers = numbered(refs[:-2], caps, h)
    for slot in range(RB_DEV):

        def begin(i, carry, slot=slot):
            at = slot * half + i
            start_page(buffers, table[SHARE_AT + at], g * PAIR, spot(out, at), sems.at[at])
            return carry

        lax.fori_loop(0, table[SHARES_AT + slot], begin, 0)
    for slot in range(RB_DEV):

        def finish(i, carry, slot=slot):
            at = slot * half + i
            wait_page(spot(out, at), sems.at[at])
            return carry

        lax.fori_loop(0, table[SHARES_AT + slot], finish, 0)


def attend_kernel(group, first, blocks, caps, carried, project, table, queries, own, *refs):
    refs = list(refs)
    weight = refs.pop(0) if project else None
    summed = refs.pop(0) if carried else None
    sems, stacked = refs.pop(), refs.pop()
    slab = refs.pop() if project else None
    store = refs.pop()
    terms = refs.pop() if project else None
    out = refs.pop()
    heads, room = len(group), len(blocks) * PMAX

    def region(i):
        if i == 0:
            return 0, table[LENGTH_AT + blocks[0]]
        base = table[BASE_AT + blocks[i]]
        return base, jnp.where(base == 0, 0, table[LENGTH_AT + blocks[i]])

    for h, g in enumerate(group):
        buffers = numbered(refs, caps, first + h)
        for i, b in enumerate(blocks):
            base, count = region(i)
            codes = SLOT_AT + table[BASE_AT + b]

            def begin(j, carry, h=h, g=g, buffers=buffers, base=base, codes=codes):
                at = h * room + base + j
                target, sem = spot(store, at), sems.at[at]
                start_page(buffers, table[codes + j], g * PAIR, target, sem)
                return carry

            lax.fori_loop(0, count, begin, 0)
            length = table[LENGTH_AT + b]

            def clear(j, carry, h=h, base=base):
                rows = pl.ds(pl.multiple_of((h * room + base + j) * BLOCK, BLOCK), BLOCK)
                store[rows, :] = jnp.zeros((BLOCK, PAIR), jnp.bfloat16)
                return carry

            lax.fori_loop(length, (length + SPAN - 1) & -SPAN, clear, 0)
    if project:
        share = slab.shape[1]
        theirs = pl.multiple_of(table[THEIRS_AT] * share, share)
        fetch = pltpu.make_async_copy(
            weight.at[pl.ds(group[0] * WIDTH, heads * WIDTH), pl.ds(theirs, share)],
            slab,
            sems.at[heads * room],
        )
        fetch.start()

    def one_block(h, i, b, base, count):
        tokens = pl.ds(pl.multiple_of(i * BLOCK, BLOCK), BLOCK)

        def columns(width, extra=0):
            return pl.ds(pl.multiple_of(h * width + extra, HD), min(width, HD))

        for e in range(GROUP):
            stacked[e * BLOCK : (e + 1) * BLOCK, :] = queries[tokens, columns(WIDTH, e * HD)]
        base = h * room + base

        def finish(j, carry):
            wait_page(spot(store, base + j), sems.at[base + j])
            return carry

        lax.fori_loop(0, count, finish, 0)
        length = table[LENGTH_AT + b]
        span = RB_DEV * BLOCK
        row = lax.broadcasted_iota(jnp.int32, (ROWS, span), 0) & (BLOCK - 1)
        key = lax.broadcasted_iota(jnp.int32, (ROWS, span), 1)
        own_mask = (key <= row + b * BLOCK) & (key >= table[LOW_AT + b])

        def run(spans):
            wide_key = lax.broadcasted_iota(jnp.int32, (ROWS, SPAN * BLOCK), 1)
            last_mask = wide_key < (length - (spans - 1) * SPAN) * BLOCK
            pieces = [(own[:, columns(PAIR)], own[:, columns(PAIR, HD)])]
            for t in range(spans):
                at = pl.multiple_of((base + t * SPAN) * BLOCK, BLOCK)
                piece = store[pl.ds(at, SPAN * BLOCK), :]
                pieces.append((piece[:, :HD], piece[:, HD:]))

            def score(r, t):
                scores = lax.dot_general(
                    stacked[r * ROWS : (r + 1) * ROWS, :],
                    pieces[t][0],
                    (((1,), (1,)), ((), ())),
                    preferred_element_type=jnp.float32,
                )
                if t == 0:
                    return jnp.where(own_mask, scores, NEG_LARGE)
                if t == spans:
                    return jnp.where(last_mask, scores, NEG_LARGE)
                return scores

            def highest(scores, sofar):
                for n in range(0, scores.shape[1], HD):
                    part = scores[:, n : n + HD]
                    sofar = part if sofar is None else jnp.maximum(sofar, part)
                return sofar

            def blend(scores, top, t):
                spread = jnp.concatenate([top] * (scores.shape[1] // HD), axis=1)
                weights = jnp.exp2((scores - spread) * SCALE).astype(jnp.bfloat16)
                values = pieces[t][1]
                values = jnp.concatenate([values, jnp.ones_like(values)], axis=1)
                return jnp.dot(weights, values, preferred_element_type=jnp.float32)

            chunks, ahead, peak = GROUP * BLOCK // ROWS, [], None
            for t in range(spans + 1):
                ahead.append(score(0, t))
                peak = highest(ahead[-1], peak)
            for r in range(chunks):
                now, ahead = ahead, []
                top = jnp.broadcast_to(jnp.max(peak, axis=1, keepdims=True), (ROWS, HD))
                total, peak = None, None
                for t in range(spans + 1):
                    if r + 1 < chunks:
                        ahead.append(score(r + 1, t))
                        peak = highest(ahead[-1], peak)
                    blended = blend(now[t], top, t)
                    total = blended if total is None else total + blended
                mean = (total[:, :HD] / total[:, HD:]).astype(jnp.bfloat16)
                for e in range(ROWS // BLOCK):
                    at = columns(WIDTH, (r * (ROWS // BLOCK) + e) * HD)
                    out[tokens, at] = mean[e * BLOCK : (e + 1) * BLOCK, :]

        spans = lax.shift_right_logical(length + SPAN - 1, SPAN.bit_length() - 1)
        for n in range(1, PMAX // SPAN + 1):
            pl.when(spans == n)(lambda n=n: run(n))

    def step(n, carry):
        if len(blocks) == 1:
            one_block(n, 0, blocks[0], *region(0))
            return carry
        h, i = lax.shift_right_logical(n, 1), n & 1
        base = jnp.where(i == 0, 0, region(1)[0])
        one_block(h, i, i, base, jnp.where(i == 0, region(0)[1], region(1)[1]))
        return carry

    lax.fori_loop(0, heads * len(blocks), step, 0)
    if project:
        fetch.wait()
        attended = out[...]
        width = math.gcd(share, 512)
        for n in range(0, share, width):
            term = jnp.dot(attended, slab[:, n : n + width], preferred_element_type=jnp.float32)
            if carried:
                term = term + summed[:, n : n + width]
            terms[:, n : n + width] = term.astype(terms.dtype)


def attend(
    group, first, blocks, last, caps, table, queries, resp_kv, buffers, weight=None, share=0, summed=None
):
    tokens, heads = len(blocks) * BLOCK, len(group)
    at = blocks[0] // len(blocks)
    project, carried = weight is not None, summed is not None
    any_spec = pl.BlockSpec(memory_space=pl.ANY)
    whole = pl.BlockSpec((tokens, share), lambda i, c: (0, 0))
    out_shape = [jax.ShapeDtypeStruct((tokens, heads * WIDTH), jnp.bfloat16)]
    out_specs = [pl.BlockSpec((tokens, heads * WIDTH), lambda i, c: (0, 0))]
    operands, in_specs = [], []
    scratch = [pltpu.VMEM((heads * len(blocks) * PMAX * BLOCK, PAIR), jnp.bfloat16)]
    if project:
        operands, in_specs = [weight], [any_spec]
        kept = jnp.bfloat16 if last else jnp.float32
        out_shape.append(jax.ShapeDtypeStruct((tokens, share), kept))
        out_specs.append(whole)
        scratch.append(pltpu.VMEM((heads * WIDTH, share), jnp.bfloat16))
    if carried:
        operands = operands + [summed]
        in_specs = in_specs + [pl.BlockSpec((tokens, share), lambda i, c: (at, 0))]
    column = group[0] // heads
    return pl.pallas_call(
        lambda *refs: attend_kernel(group, first, blocks, caps, carried, project, *refs),
        out_shape=out_shape,
        grid_spec=pltpu.PrefetchScalarGridSpec(
            num_scalar_prefetch=1,
            grid=(1,),
            in_specs=[
                pl.BlockSpec((tokens, heads * WIDTH), lambda i, c: (at, column)),
                pl.BlockSpec((RB_DEV * BLOCK, heads * PAIR), lambda i, c: (0, column)),
            ]
            + in_specs
            + [any_spec] * len(buffers),
            out_specs=out_specs,
            scratch_shapes=scratch
            + [
                pltpu.VMEM((GROUP * BLOCK, HD), jnp.bfloat16),
                pltpu.SemaphoreType.DMA((heads * len(blocks) * PMAX + 1,)),
            ],
        ),
        compiler_params=params(ATTEND_MIB),
        cost_estimate=SMALL,
        name="attend_heads_" + "_".join(map(str, group)) + "_blocks_" + "_".join(map(str, blocks)),
    )(table, queries, resp_kv, *operands, *buffers)


def pages_shape(count):
    return jax.ShapeDtypeStruct((count * BLOCK, PAIR), jnp.bfloat16)


def pack_send(wide, cores, groups, caps, skip, ctrl, pool, planned=False):
    any_spec = pl.BlockSpec(memory_space=pl.ANY)
    pages = PROMPTS * ((PMAX + wide - 1) // wide)
    rooms = (caps.near, caps.near, caps.far)
    if groups is None:
        shapes = [jax.ShapeDtypeStruct((n * BLOCK, pool.shape[1]), jnp.bfloat16) for n in rooms]
    else:
        shapes = [pages_shape(n * len(group)) for group in groups for n in rooms]
    heads = 1 if groups is None else sum(map(len, groups))
    out_specs = [any_spec] * len(shapes)
    scratch = [pltpu.SemaphoreType.DMA((3, pages, heads))]
    if planned:
        shapes = shapes + [jax.ShapeDtypeStruct((TABLE,), jnp.int32)]
        out_specs = out_specs + [pl.BlockSpec(memory_space=pltpu.SMEM)]
        scratch.append(pltpu.SMEM((wide * SUMS,), jnp.int32))
    return pl.pallas_call(
        lambda *refs: send_kernel(wide, cores, groups, caps, skip, planned, *refs),
        out_shape=shapes,
        grid_spec=pltpu.PrefetchScalarGridSpec(
            num_scalar_prefetch=1,
            grid=(1,),
            in_specs=[pl.BlockSpec(pool.shape, lambda i, c: (0, 0))],
            out_specs=out_specs,
            scratch_shapes=scratch,
        ),
        compiler_params=params(8),
        cost_estimate=SMALL,
        name="pack_extra" if groups is None else f"pack_send_{groups[0][0]}",
    )(ctrl, pool)


def pack_share(cores, caps, h, g, table, buffers):
    any_spec = pl.BlockSpec(memory_space=pl.ANY)
    return pl.pallas_call(
        lambda *refs: share_kernel(cores, caps, h, g, *refs),
        out_shape=pages_shape(PMAX),
        grid_spec=pltpu.PrefetchScalarGridSpec(
            num_scalar_prefetch=1,
            grid=(1,),
            in_specs=[any_spec] * len(buffers),
            out_specs=pl.BlockSpec((PMAX * BLOCK, PAIR), lambda i, c: (0, 0)),
            scratch_shapes=[pltpu.SemaphoreType.DMA((PMAX,))],
        ),
        compiler_params=params(6),
        cost_estimate=SMALL,
        name=f"pack_share_{g}",
    )(table, *buffers)


def pack_relay(cores, caps, g, ctrl, *lists):
    any_spec = pl.BlockSpec(memory_space=pl.ANY)
    pages = max(2 * caps.relay, caps.far)
    return pl.pallas_call(
        lambda *refs: relay_kernel(cores, caps, *refs),
        out_shape=pages_shape(pages),
        grid_spec=pltpu.PrefetchScalarGridSpec(
            num_scalar_prefetch=1,
            grid=(1,),
            in_specs=[any_spec] * len(lists),
            out_specs=pl.BlockSpec((pages * BLOCK, PAIR), lambda i, c: (0, 0)),
            scratch_shapes=[pltpu.SemaphoreType.DMA((3,))],
        ),
        compiler_params=params(6),
        cost_estimate=SMALL,
        name=f"pack_relay_{g}",
    )(ctrl, *lists)


def after(value, *earlier):
    return lax.optimization_barrier((value, *earlier))[0]


def line_attend(wide, cores, caps, ctrl, queries, resp_kv, pool, weight):
    heads = resp_kv.shape[1] // PAIR
    share = weight.shape[1] // 2

    def hop(x, moves):
        pairs = [(a * cores + c, b * cores + c) for a, b in moves for c in range(cores)]
        return lax.ppermute(x, "wide", pairs)

    swap = [(d, d // cores * cores + (cores - 1 - d % cores)) for d in range(wide)]

    def sideways(right, left):
        return hop(right, [(0, 1), (1, 2), (2, 3)]), hop(left, [(3, 2), (2, 1), (1, 0)])

    past = Caps(1, 1, 0)

    def past_the_end(ctrl, pool):
        skip = (caps.near, caps.near, caps.far)
        right, left, far = pack_send(wide, cores, None, past, skip, ctrl, pool)
        found = *sideways(right, left), hop(far, [(0, 2), (3, 1)])
        return jnp.concatenate(found, axis=0)

    def nothing(ctrl, pool):
        return jnp.zeros((3 * past.near * BLOCK, pool.shape[1]), pool.dtype)

    both, last = list(range(RB_DEV)), heads - 1
    *lists, table = pack_send(wide, cores, [[0]], caps, (0, 0, 0), ctrl, pool, True)
    sends, far, held, parts = {0: lists}, {}, {}, []

    def relay(g, plan):
        following = []
        left, right = sideways(*sends[g][:2])
        if g == 0:
            far[0] = hop(sends[0][2], [(0, 2), (3, 1)])
        if g + 1 < heads:
            sends[g + 1] = pack_send(wide, cores, [[g + 1]], caps, (0, 0, 0), ctrl, pool)
            following = sends[g + 1][2:]
        onward = pack_relay(cores, caps, g, plan, far[g], left, right, *following)
        far[g + 1] = hop(onward, [(2, 3), (1, 0), (0, 2), (3, 1)])
        held[g] = [pool, left, right, far[g], far[g + 1]]
        return onward

    onward = relay(0, ctrl)
    over = after(table, onward)[OVER_AT] == 1
    extra = lax.cond(over, past_the_end, nothing, ctrl, pool)

    def exchange(g, plan):
        shared = pack_share(cores, caps, 0, g, plan, held[g] + [extra])
        return held[g] + [lax.ppermute(shared, "wide", swap), extra]

    summed = None
    for g in range(last):
        onward = relay(g + 1, after(ctrl, parts[-1]) if parts else ctrl)
        buffers = exchange(g, after(table, onward))
        attended, summed = attend(
            [g], 0, both, False, caps, table, queries, resp_kv, buffers, weight, share, summed
        )
        parts.append(attended)
    buffers = exchange(last, after(table, parts[-1]) if parts else table)
    ends, terms, plan = [], [], table
    for b in both:
        end, term = attend(
            [last], 0, [b], True, caps, plan, queries, resp_kv, buffers, weight, share, summed
        )
        ends.append(end)
        terms.append(term)
        plan = after(table, end)
    return parts + [jnp.concatenate(ends, axis=0)], terms


def project_kernel(carried, at, *refs):
    parts, weight, out = refs[: -2 - carried], refs[-2 - carried], refs[-1]
    total, row = refs[-2][...] if carried else None, 0
    for part in parts:
        end = row + part.shape[1]
        term = jnp.dot(part[...], weight[row:end, :], preferred_element_type=jnp.float32)
        total, row = term if total is None else total + term, end
    out[...] = total.astype(out.dtype)


def project(parts, weight, first, first_column, columns, kept=jnp.bfloat16, summed=None):
    tokens, rows = parts[0].shape[0], sum(part.shape[1] for part in parts)
    tile = math.gcd(columns, 512)
    assert weight.shape[1] % tile == 0
    at = jnp.reshape(first_column // tile, (1,)).astype(jnp.int32)
    skip = first * WIDTH
    if skip % rows:
        weight_spec = pl.BlockSpec(
            (pl.Element(rows), pl.Element(tile)), lambda i, at: (skip, (at[0] + i) * tile)
        )
    else:
        weight_spec = pl.BlockSpec((rows, tile), lambda i, at: (skip // rows, at[0] + i))
    operands, in_specs = [*parts, weight], [
        pl.BlockSpec(part.shape, lambda i, at: (0, 0)) for part in parts
    ] + [weight_spec]
    if summed is not None:
        operands.append(summed)
        in_specs.append(pl.BlockSpec((tokens, tile), lambda i, at: (0, i)))
    return pl.pallas_call(
        lambda *refs: project_kernel(summed is not None, *refs),
        out_shape=jax.ShapeDtypeStruct((tokens, columns), kept),
        grid_spec=pltpu.PrefetchScalarGridSpec(
            num_scalar_prefetch=1,
            grid=(columns // tile,),
            in_specs=in_specs,
            out_specs=pl.BlockSpec((tokens, tile), lambda i, at: (0, i)),
        ),
        compiler_params=params(PROJECT_MIB),
        cost_estimate=SMALL,
        name="project",
    )(at, *operands)


def local(
    queries, resp_kv, prefix_pool, out_weight, pre_len, prompt_blocks, prompt_owner, resp_seg
):
    wide, groups = lax.axis_size("wide"), lax.axis_size("tp") * lax.axis_size("sub")
    cores = 2 // lax.axis_size("sub")
    heads = resp_kv.shape[1] // PAIR
    me = lax.axis_index("wide").astype(jnp.int32)
    group = lax.axis_index("tp") * lax.axis_size("sub") + lax.axis_index("sub")
    where = jnp.stack([me, (1 - group).astype(jnp.int32)])
    ctrl = jnp.concatenate([pre_len, prompt_blocks, prompt_owner, resp_seg, where])
    columns = out_weight.shape[1]
    share = columns // groups
    if wide == 8 and cores == 2 and groups == 2:
        parts, theirs = line_attend(
            wide, cores, CAPS, ctrl, queries, resp_kv, prefix_pool, out_weight
        )
        axis = "tp" if lax.axis_size("tp") == 2 else "sub"
        arrived = [lax.ppermute(terms, axis, [(0, 1), (1, 0)]) for terms in theirs]
        half = share // 2
        mine = [
            project(parts, out_weight, 0, group * share, half),
            project(parts, out_weight, 0, after(group, arrived[0]) * share + half, half),
        ]
        mine = jnp.concatenate(mine, axis=1)
        arrived = jnp.concatenate(arrived, axis=0)
        return (mine.astype(jnp.float32) + arrived.astype(jnp.float32)).astype(jnp.bfloat16)
    table = make_plan(wide, cores, False, ctrl)
    buffers = [lax.all_gather(prefix_pool, "wide", axis=0, tiled=True)]
    blocks = list(range(RB_DEV))
    parts = [
        attend([g], 0, blocks, False, CAPS, table, queries, resp_kv, buffers)[0] for g in range(heads)
    ]
    terms = project(parts, out_weight, 0, jnp.int32(0), columns)
    return lax.psum_scatter(terms, ("tp", "sub"), scatter_dimension=1, tiled=True)


def solution(mesh):
    return jax.shard_map(
        local,
        mesh=mesh,
        in_specs=(
            P(("parts", "wide"), ("tp", "sub")),
            P(("parts", "wide"), ("tp", "sub")),
            P(("parts", "wide"), ("tp", "sub")),
            P(("tp", "sub"), None),
            P("parts"),
            P("parts"),
            P("parts"),
            P(("parts", "wide")),
        ),
        out_specs=P(("parts", "wide"), ("tp", "sub")),
        check_vma=False,
    )
```

```python
import math

import jax
import jax.numpy as jnp
from jax import lax
from jax.experimental import pallas as pl
from jax.experimental.pallas import tpu as pltpu
from jax.sharding import PartitionSpec as P

HD = 128
BLOCK = 128
RB_DEV = 2
PROMPTS = 4
PMAX = 16
GROUP = 8
PAIR = 2 * HD
WIDTH = GROUP * HD
ROWS = 512
SPAN = 4
NEG_LARGE = -1e30
SCALE = math.log2(math.e) / math.sqrt(HD)
MIB = 1024 * 1024
ATTEND_MIB, PROJECT_MIB = 28, 18
SMALL = pl.CostEstimate(flops=1 << 20, bytes_accessed=1 << 14, transcendentals=0)

LEN_AT, BLOCKS_AT, OWNER_AT, SEG_AT, ME_AT, OTHER_AT = 0, 4, 8, 12, 14, 15


def params(mib):
    return pltpu.CompilerParams(vmem_limit_bytes=mib * MIB)


def as_int(flag):
    return jnp.where(flag, 1, 0)


class Layout:
    def __init__(self, ctrl, wide, cores):
        self.ctrl, self.wide, self.cores = ctrl, wide, cores
        self.stride = (PMAX + wide - 1) // wide
        self.me = ctrl[ME_AT]
        self.z, self.core = self.div(self.me, cores), self.mod(self.me, cores)
        ends, total = [], 0
        for p in range(PROMPTS):
            total = total + ctrl[BLOCKS_AT + p] + (RB_DEV - 1)
            ends.append(total)
        self.ends = ends

    def mod(self, value, size):
        return value & (size - 1) if size & (size - 1) == 0 else lax.rem(value, size)

    def div(self, value, size):
        if size & (size - 1) == 0:
            return lax.shift_right_logical(value, size.bit_length() - 1)
        return lax.div(value, size)

    def prompt_of(self, block):
        return sum(as_int(block >= end) for end in self.ends[:-1])

    def first_of(self, chip):
        return self.prompt_of(chip * self.cores * RB_DEV)

    def last_of(self, chip):
        return self.prompt_of((chip + 1) * self.cores * RB_DEV - 1)

    def length(self, p):
        return self.ctrl[LEN_AT + p]

    def held_by(self, p, j):
        return self.mod(self.ctrl[OWNER_AT + p] + j, self.wide)

    def held(self, p, who):
        first = self.mod(who - self.ctrl[OWNER_AT + p] + self.wide, self.wide)
        return sum(as_int(first + k * self.wide < self.length(p)) for k in range(self.stride))

    def listed(self, which, rank, room):
        return jnp.where(
            rank < room, which * CODE + rank, (EXTRA + which - 1) * CODE + rank - room
        )

    def in_plane(self, p, j, sums):
        who = self.held_by(p, j)
        chip = self.div(who, self.cores)
        gap = chip - self.z
        k = self.div(j, self.wide)
        at = who * SUMS
        down = sums[at + PROMPTS] - sums[at + p + 1] + k
        up = sums[at + p] + k
        near_down = down - jnp.where(
            chip == 0, sums[at + PROMPTS] - sums[at + self.last_of(1) + 1], 0
        )
        near_up = up - jnp.where(chip == 3, sums[at + self.first_of(2)], 0)
        far = jnp.where(gap < 0, down, up)
        two = (gap == 2) | (gap == -2)
        direct = two & ((self.z == 1) | (self.z == 2))
        code = jnp.where(two, 5 * CODE, 4 * CODE) + far
        code = jnp.where(direct, self.listed(3, far, CAPS.far), code)
        code = jnp.where(gap == 1, self.listed(2, near_up, CAPS.near), code)
        code = jnp.where(gap == -1, self.listed(1, near_down, CAPS.near), code)
        return jnp.where(gap == 0, p * self.stride + k, code)


CODE = 256
SHARED = 6
EXTRA = 7
SUMS = 8
SLOT_AT, SHARE_AT, SHARES_AT, LENGTH_AT, BASE_AT, LOW_AT, THEIRS_AT, OVER_AT, TABLE = (
    0, 32, 50, 52, 54, 56, 58, 59, 64
)


class Caps:
    def __init__(self, near, far, relay):
        self.near, self.far, self.relay = near, far, relay


CAPS = Caps(5, 5, 4)


def needs(lay, sums, cores):
    first, last = [lay.first_of(c) for c in range(4)], [lay.last_of(c) for c in range(4)]
    near, far = jnp.int32(0), jnp.int32(0)
    for core in range(cores):

        def held(chip, low, high, core=core):
            at = (chip * cores + core) * SUMS
            return sums[at + high + 1] - sums[at + low]

        top = PROMPTS - 1
        edge = [held(1, 0, last[0]), held(2, first[3], top)]
        for amount in edge + [
            held(0, first[1], last[1]),
            held(1, first[2], top),
            held(2, 0, last[1]),
            held(3, first[2], last[2]),
        ]:
            near = jnp.maximum(near, amount)
        for amount in (held(0, first[2], top), held(3, 0, last[1])):
            far = jnp.maximum(far, amount)
    return near, far


def plan_kernel(wide, cores, line, ctrl, table, sums):
    lay = Layout(ctrl, wide, cores)
    half = PMAX // cores
    table[THEIRS_AT] = ctrl[OTHER_AT]
    table[OVER_AT] = 0
    if line:

        def tally(who, carry):
            total = jnp.int32(0)
            for p in range(PROMPTS):
                sums[who * SUMS + p] = total
                total = total + lay.held(p, who)
            sums[who * SUMS + PROMPTS] = total
            return carry

        lax.fori_loop(0, wide, tally, 0)
        near, far = needs(lay, sums, cores)
        over = (near > CAPS.near) | (far > CAPS.far)
        table[OVER_AT] = as_int(over)

    def prompts_of(device):
        return [lay.prompt_of(device * RB_DEV + b) for b in range(RB_DEV)]

    mine = prompts_of(lay.me)
    same = mine[0] == mine[1]
    joined = same & (ctrl[SEG_AT] == ctrl[SEG_AT + 1])
    for slot in range(RB_DEV):
        p = mine[slot]
        count = lay.length(p)
        table[LENGTH_AT + slot] = count
        if slot == 1:
            count = jnp.where(same, 0, count)
        table[BASE_AT + slot] = jnp.where(same, 0, PMAX) if slot else 0
        table[LOW_AT + slot] = jnp.where(joined, 0, BLOCK) if slot else 0

        def place(j, carry, slot=slot, p=p):
            who = lay.held_by(p, j)
            code = (who * PROMPTS + p) * lay.stride + lay.div(j, wide)
            if line:
                shared = slot * half + lay.div(j, cores)
                passed = jnp.where(
                    lay.mod(who, cores) == lay.core,
                    lay.in_plane(p, j, sums),
                    SHARED * CODE + shared,
                )
                code = passed
            table[SLOT_AT + slot * PMAX + j] = code
            return carry

        lax.fori_loop(0, count, place, 0)
    if not line:
        return
    theirs = prompts_of(lay.z * cores + (cores - 1 - lay.core))
    for slot in range(RB_DEV):
        p = theirs[slot]
        shift = lay.mod(lay.core - ctrl[OWNER_AT + p] + wide, cores)
        count = lay.div(lay.length(p) - shift + cores - 1, cores)
        if slot == 1:
            count = jnp.where(theirs[1] == theirs[0], 0, count)
        table[SHARES_AT + slot] = count

        def share(i, carry, slot=slot, p=p, shift=shift):
            table[SHARE_AT + slot * half + i] = lay.in_plane(p, i * cores + shift, sums)
            return carry

        lax.fori_loop(0, count, share, 0)


def make_plan(wide, cores, line, ctrl):
    return pl.pallas_call(
        lambda *refs: plan_kernel(wide, cores, line, *refs),
        out_shape=jax.ShapeDtypeStruct((TABLE,), jnp.int32),
        in_specs=[pl.BlockSpec(memory_space=pltpu.SMEM)],
        out_specs=pl.BlockSpec(memory_space=pltpu.SMEM),
        scratch_shapes=[pltpu.SMEM((wide * SUMS,), jnp.int32)],
        compiler_params=params(6),
        name="plan",
    )(ctrl)


def spot(ref, page):
    return ref.at[pl.ds(pl.multiple_of(page * BLOCK, BLOCK), BLOCK), :]


def page_at(buffer, page, column):
    rows = pl.ds(pl.multiple_of(page * BLOCK, BLOCK), BLOCK)
    return buffer.at[rows, pl.ds(column if buffer.shape[1] > PAIR else 0, PAIR)]


def start_page(buffers, code, column, target, sem):
    which = lax.shift_right_logical(code, CODE.bit_length() - 1)
    page = code & (CODE - 1)
    for i, buffer, offset in buffers:

        @pl.when(which == i)
        def _(buffer=buffer, offset=offset):
            source = page_at(buffer, page + offset, column)
            pltpu.make_async_copy(source, target, sem).start()


def wait_page(target, sem):
    pltpu.make_async_copy(target, target, sem).wait()


def send_kernel(wide, cores, groups, caps, skip, planned, ctrl, pool, *refs):
    if planned:
        *outs, table, sems, sums = refs
    else:
        *outs, sems = refs
    rooms = (caps.near, caps.near, caps.far)
    lay = Layout(ctrl, wide, cores)
    z, last = lay.z, wide // cores - 1
    held = [lay.held(p, lay.me) for p in range(PROMPTS)]

    def above(p, top):
        return sum([jnp.where(o <= top, held[o], 0) for o in range(p + 1, PROMPTS)], jnp.int32(0))

    def below(p, low):
        return sum([jnp.where(o >= low, held[o], 0) for o in range(p)], jnp.int32(0))

    near_top = jnp.where(z == 0, lay.last_of(1), PROMPTS - 1)
    near_low = jnp.where(z == last, lay.first_of(2), 0)
    first_up, last_down = lay.first_of(z + 1), lay.last_of(z - 1)
    first_two, last_one = lay.first_of(2), lay.last_of(1)
    plans = []
    for p in range(PROMPTS):
        right = (z < last) & (p >= first_up) & (p <= near_top)
        left = (z > 0) & (p >= near_low) & (p <= last_down)
        far_up = (z == 0) & (p >= first_two)
        far_down = (z == last) & (p <= last_one)
        ranks = (above(p, near_top), below(p, near_low), above(p, PROMPTS - 1), below(p, 0))
        for k in range(lay.stride):
            for lane, wanted, rank in zip((0, 1, 2, 2), (right, left, far_up, far_down), ranks):
                at = rank + k - skip[lane]
                fits = (k < held[p]) & (at >= 0) & (at < rooms[lane])
                plans.append((wanted & fits, p * lay.stride + k, lane, at))

    def copies(plan):
        _, page, lane, rank = plan
        if groups is None:
            return [
                pltpu.make_async_copy(
                    spot(pool, page), spot(outs[lane], rank), sems.at[lane, page, 0]
                )
            ]
        return [
            pltpu.make_async_copy(
                page_at(pool, page, g * PAIR),
                spot(outs[n * 3 + lane], h * rooms[lane] + rank),
                sems.at[lane, page, n * len(groups[0]) + h],
            )
            for n, group in enumerate(groups)
            for h, g in enumerate(group)
        ]

    for plan in plans:

        @pl.when(plan[0])
        def _(plan=plan):
            for copy in copies(plan):
                copy.start()

    if planned:
        plan_kernel(wide, cores, True, ctrl, table, sums)
    for plan in plans:

        @pl.when(plan[0])
        def _(plan=plan):
            for copy in copies(plan):
                copy.wait()


def relay_kernel(cores, caps, ctrl, far, left, right, *refs):
    following, out, sems = refs[:-2], refs[-2], refs[-1]
    rows = caps.relay * BLOCK

    def copy(source, section):
        target = out.at[pl.ds(section * rows, rows), :]
        return pltpu.make_async_copy(source.at[pl.ds(0, rows), :], target, sems.at[section])

    at_left = at_right = False
    for core in range(cores):
        at_left = at_left | (ctrl[ME_AT] == cores + core)
        at_right = at_right | (ctrl[ME_AT] == 2 * cores + core)
    inner = at_left | at_right
    pl.when(inner)(lambda: copy(far, 0).start())
    pl.when(at_right)(lambda: copy(left, 1).start())
    pl.when(at_left)(lambda: copy(right, 1).start())

    @pl.when(inner)
    def _():
        copy(far, 0).wait()
        copy(far, 1).wait()

    for source in following:

        @pl.when(jnp.logical_not(inner))
        def _(source=source):
            target = out.at[pl.ds(0, caps.far * BLOCK), :]
            move = pltpu.make_async_copy(source, target, sems.at[2])
            move.start()
            move.wait()


def numbered(refs, caps, h):
    if len(refs) == 1:
        return [(0, refs[0], 0)]
    offsets = (0, h * caps.near, h * caps.near, h * caps.far, 0)
    found = list(zip(range(5), refs[:5], offsets)) + [(5, refs[4], caps.relay)]
    if len(refs) == 7:
        found.append((SHARED, refs[5], 0))
    return found + [(EXTRA + i, refs[-1], i) for i in range(3)]


def share_kernel(cores, caps, h, g, table, *refs):
    out, sems = refs[-2:]
    half = PMAX // cores
    buffers = numbered(refs[:-2], caps, h)
    for slot in range(RB_DEV):

        def begin(i, carry, slot=slot):
            at = slot * half + i
            start_page(buffers, table[SHARE_AT + at], g * PAIR, spot(out, at), sems.at[at])
            return carry

        lax.fori_loop(0, table[SHARES_AT + slot], begin, 0)
    for slot in range(RB_DEV):

        def finish(i, carry, slot=slot):
            at = slot * half + i
            wait_page(spot(out, at), sems.at[at])
            return carry

        lax.fori_loop(0, table[SHARES_AT + slot], finish, 0)


def attend_kernel(group, first, blocks, caps, carried, project, table, queries, own, *refs):
    refs = list(refs)
    weight = refs.pop(0) if project else None
    summed = refs.pop(0) if carried else None
    sems, stacked = refs.pop(), refs.pop()
    slab = refs.pop() if project else None
    store = refs.pop()
    terms = refs.pop() if project else None
    out = refs.pop()
    heads, room = len(group), len(blocks) * PMAX

    def region(i):
        if i == 0:
            return 0, table[LENGTH_AT + blocks[0]]
        base = table[BASE_AT + blocks[i]]
        return base, jnp.where(base == 0, 0, table[LENGTH_AT + blocks[i]])

    for h, g in enumerate(group):
        buffers = numbered(refs, caps, first + h)
        for i, b in enumerate(blocks):
            base, count = region(i)
            codes = SLOT_AT + table[BASE_AT + b]

            def begin(j, carry, h=h, g=g, buffers=buffers, base=base, codes=codes):
                at = h * room + base + j
                target, sem = spot(store, at), sems.at[at]
                start_page(buffers, table[codes + j], g * PAIR, target, sem)
                return carry

            lax.fori_loop(0, count, begin, 0)
            length = table[LENGTH_AT + b]

            def clear(j, carry, h=h, base=base):
                rows = pl.ds(pl.multiple_of((h * room + base + j) * BLOCK, BLOCK), BLOCK)
                store[rows, :] = jnp.zeros((BLOCK, PAIR), jnp.bfloat16)
                return carry

            lax.fori_loop(length, (length + SPAN - 1) & -SPAN, clear, 0)
    if project:
        share = slab.shape[1]
        theirs = pl.multiple_of(table[THEIRS_AT] * share, share)
        fetch = pltpu.make_async_copy(
            weight.at[pl.ds(group[0] * WIDTH, heads * WIDTH), pl.ds(theirs, share)],
            slab,
            sems.at[heads * room],
        )
        fetch.start()

    def one_block(h, i, b, base, count):
        tokens = pl.ds(pl.multiple_of(i * BLOCK, BLOCK), BLOCK)

        def columns(width, extra=0):
            return pl.ds(pl.multiple_of(h * width + extra, HD), min(width, HD))

        for e in range(GROUP):
            stacked[e * BLOCK : (e + 1) * BLOCK, :] = queries[tokens, columns(WIDTH, e * HD)]
        base = h * room + base

        def finish(j, carry):
            wait_page(spot(store, base + j), sems.at[base + j])
            return carry

        lax.fori_loop(0, count, finish, 0)
        length = table[LENGTH_AT + b]
        span = RB_DEV * BLOCK
        row = lax.broadcasted_iota(jnp.int32, (ROWS, span), 0) & (BLOCK - 1)
        key = lax.broadcasted_iota(jnp.int32, (ROWS, span), 1)
        own_mask = (key <= row + b * BLOCK) & (key >= table[LOW_AT + b])

        def run(spans):
            wide_key = lax.broadcasted_iota(jnp.int32, (ROWS, SPAN * BLOCK), 1)
            last_mask = wide_key < (length - (spans - 1) * SPAN) * BLOCK
            pieces = [(own[:, columns(PAIR)], own[:, columns(PAIR, HD)])]
            for t in range(spans):
                at = pl.multiple_of((base + t * SPAN) * BLOCK, BLOCK)
                piece = store[pl.ds(at, SPAN * BLOCK), :]
                pieces.append((piece[:, :HD], piece[:, HD:]))

            def score(r, t):
                scores = lax.dot_general(
                    stacked[r * ROWS : (r + 1) * ROWS, :],
                    pieces[t][0],
                    (((1,), (1,)), ((), ())),
                    preferred_element_type=jnp.float32,
                )
                if t == 0:
                    return jnp.where(own_mask, scores, NEG_LARGE)
                if t == spans:
                    return jnp.where(last_mask, scores, NEG_LARGE)
                return scores

            def highest(scores, sofar):
                for n in range(0, scores.shape[1], HD):
                    part = scores[:, n : n + HD]
                    sofar = part if sofar is None else jnp.maximum(sofar, part)
                return sofar

            def blend(scores, top, t):
                spread = jnp.concatenate([top] * (scores.shape[1] // HD), axis=1)
                weights = jnp.exp2((scores - spread) * SCALE).astype(jnp.bfloat16)
                values = pieces[t][1]
                values = jnp.concatenate([values, jnp.ones_like(values)], axis=1)
                return jnp.dot(weights, values, preferred_element_type=jnp.float32)

            chunks, ahead, peak = GROUP * BLOCK // ROWS, [], None
            for t in range(spans + 1):
                ahead.append(score(0, t))
                peak = highest(ahead[-1], peak)
            for r in range(chunks):
                now, ahead = ahead, []
                top = jnp.broadcast_to(jnp.max(peak, axis=1, keepdims=True), (ROWS, HD))
                total, peak = None, None
                for t in range(spans + 1):
                    if r + 1 < chunks:
                        ahead.append(score(r + 1, t))
                        peak = highest(ahead[-1], peak)
                    blended = blend(now[t], top, t)
                    total = blended if total is None else total + blended
                mean = (total[:, :HD] / total[:, HD:]).astype(jnp.bfloat16)
                for e in range(ROWS // BLOCK):
                    at = columns(WIDTH, (r * (ROWS // BLOCK) + e) * HD)
                    out[tokens, at] = mean[e * BLOCK : (e + 1) * BLOCK, :]

        spans = lax.shift_right_logical(length + SPAN - 1, SPAN.bit_length() - 1)
        for n in range(1, PMAX // SPAN + 1):
            pl.when(spans == n)(lambda n=n: run(n))

    def step(n, carry):
        if len(blocks) == 1:
            one_block(n, 0, blocks[0], *region(0))
            return carry
        h, i = lax.shift_right_logical(n, 1), n & 1
        base = jnp.where(i == 0, 0, region(1)[0])
        one_block(h, i, i, base, jnp.where(i == 0, region(0)[1], region(1)[1]))
        return carry

    lax.fori_loop(0, heads * len(blocks), step, 0)
    if project:
        fetch.wait()
        attended = out[...]
        width = math.gcd(share, 512)
        for n in range(0, share, width):
            term = jnp.dot(attended, slab[:, n : n + width], preferred_element_type=jnp.float32)
            if carried:
                term = term + summed[:, n : n + width]
            terms[:, n : n + width] = term.astype(terms.dtype)


def attend(
    group, first, blocks, last, caps, table, queries, resp_kv, buffers, weight=None, share=0, summed=None
):
    tokens, heads = len(blocks) * BLOCK, len(group)
    at = blocks[0] // len(blocks)
    project, carried = weight is not None, summed is not None
    any_spec = pl.BlockSpec(memory_space=pl.ANY)
    whole = pl.BlockSpec((tokens, share), lambda i, c: (0, 0))
    out_shape = [jax.ShapeDtypeStruct((tokens, heads * WIDTH), jnp.bfloat16)]
    out_specs = [pl.BlockSpec((tokens, heads * WIDTH), lambda i, c: (0, 0))]
    operands, in_specs = [], []
    scratch = [pltpu.VMEM((heads * len(blocks) * PMAX * BLOCK, PAIR), jnp.bfloat16)]
    if project:
        operands, in_specs = [weight], [any_spec]
        kept = jnp.bfloat16 if last else jnp.float32
        out_shape.append(jax.ShapeDtypeStruct((tokens, share), kept))
        out_specs.append(whole)
        scratch.append(pltpu.VMEM((heads * WIDTH, share), jnp.bfloat16))
    if carried:
        operands = operands + [summed]
        in_specs = in_specs + [pl.BlockSpec((tokens, share), lambda i, c: (at, 0))]
    column = group[0] // heads
    return pl.pallas_call(
        lambda *refs: attend_kernel(group, first, blocks, caps, carried, project, *refs),
        out_shape=out_shape,
        grid_spec=pltpu.PrefetchScalarGridSpec(
            num_scalar_prefetch=1,
            grid=(1,),
            in_specs=[
                pl.BlockSpec((tokens, heads * WIDTH), lambda i, c: (at, column)),
                pl.BlockSpec((RB_DEV * BLOCK, heads * PAIR), lambda i, c: (0, column)),
            ]
            + in_specs
            + [any_spec] * len(buffers),
            out_specs=out_specs,
            scratch_shapes=scratch
            + [
                pltpu.VMEM((GROUP * BLOCK, HD), jnp.bfloat16),
                pltpu.SemaphoreType.DMA((heads * len(blocks) * PMAX + 1,)),
            ],
        ),
        compiler_params=params(ATTEND_MIB),
        cost_estimate=SMALL,
        name="attend_heads_" + "_".join(map(str, group)) + "_blocks_" + "_".join(map(str, blocks)),
    )(table, queries, resp_kv, *operands, *buffers)


def pages_shape(count):
    return jax.ShapeDtypeStruct((count * BLOCK, PAIR), jnp.bfloat16)


def pack_send(wide, cores, groups, caps, skip, ctrl, pool, planned=False):
    any_spec = pl.BlockSpec(memory_space=pl.ANY)
    pages = PROMPTS * ((PMAX + wide - 1) // wide)
    rooms = (caps.near, caps.near, caps.far)
    if groups is None:
        shapes = [jax.ShapeDtypeStruct((n * BLOCK, pool.shape[1]), jnp.bfloat16) for n in rooms]
    else:
        shapes = [pages_shape(n * len(group)) for group in groups for n in rooms]
    heads = 1 if groups is None else sum(map(len, groups))
    out_specs = [any_spec] * len(shapes)
    scratch = [pltpu.SemaphoreType.DMA((3, pages, heads))]
    if planned:
        shapes = shapes + [jax.ShapeDtypeStruct((TABLE,), jnp.int32)]
        out_specs = out_specs + [pl.BlockSpec(memory_space=pltpu.SMEM)]
        scratch.append(pltpu.SMEM((wide * SUMS,), jnp.int32))
    return pl.pallas_call(
        lambda *refs: send_kernel(wide, cores, groups, caps, skip, planned, *refs),
        out_shape=shapes,
        grid_spec=pltpu.PrefetchScalarGridSpec(
            num_scalar_prefetch=1,
            grid=(1,),
            in_specs=[pl.BlockSpec(pool.shape, lambda i, c: (0, 0))],
            out_specs=out_specs,
            scratch_shapes=scratch,
        ),
        compiler_params=params(8),
        cost_estimate=SMALL,
        name="pack_extra" if groups is None else f"pack_send_{groups[0][0]}",
    )(ctrl, pool)


def pack_share(cores, caps, h, g, table, buffers):
    any_spec = pl.BlockSpec(memory_space=pl.ANY)
    return pl.pallas_call(
        lambda *refs: share_kernel(cores, caps, h, g, *refs),
        out_shape=pages_shape(PMAX),
        grid_spec=pltpu.PrefetchScalarGridSpec(
            num_scalar_prefetch=1,
            grid=(1,),
            in_specs=[any_spec] * len(buffers),
            out_specs=pl.BlockSpec((PMAX * BLOCK, PAIR), lambda i, c: (0, 0)),
            scratch_shapes=[pltpu.SemaphoreType.DMA((PMAX,))],
        ),
        compiler_params=params(6),
        cost_estimate=SMALL,
        name=f"pack_share_{g}",
    )(table, *buffers)


def pack_relay(cores, caps, g, ctrl, *lists):
    any_spec = pl.BlockSpec(memory_space=pl.ANY)
    pages = max(2 * caps.relay, caps.far)
    return pl.pallas_call(
        lambda *refs: relay_kernel(cores, caps, *refs),
        out_shape=pages_shape(pages),
        grid_spec=pltpu.PrefetchScalarGridSpec(
            num_scalar_prefetch=1,
            grid=(1,),
            in_specs=[any_spec] * len(lists),
            out_specs=pl.BlockSpec((pages * BLOCK, PAIR), lambda i, c: (0, 0)),
            scratch_shapes=[pltpu.SemaphoreType.DMA((3,))],
        ),
        compiler_params=params(6),
        cost_estimate=SMALL,
        name=f"pack_relay_{g}",
    )(ctrl, *lists)


def after(value, *earlier):
    return lax.optimization_barrier((value, *earlier))[0]


def line_attend(wide, cores, caps, ctrl, queries, resp_kv, pool, weight):
    heads = resp_kv.shape[1] // PAIR
    share = weight.shape[1] // 2

    def hop(x, moves):
        pairs = [(a * cores + c, b * cores + c) for a, b in moves for c in range(cores)]
        return lax.ppermute(x, "wide", pairs)

    swap = [(d, d // cores * cores + (cores - 1 - d % cores)) for d in range(wide)]

    def sideways(right, left):
        return hop(right, [(0, 1), (1, 2), (2, 3)]), hop(left, [(3, 2), (2, 1), (1, 0)])

    past = Caps(1, 1, 0)

    def past_the_end(ctrl, pool):
        skip = (caps.near, caps.near, caps.far)
        right, left, far = pack_send(wide, cores, None, past, skip, ctrl, pool)
        found = *sideways(right, left), hop(far, [(0, 2), (3, 1)])
        return jnp.concatenate(found, axis=0)

    def nothing(ctrl, pool):
        return jnp.zeros((3 * past.near * BLOCK, pool.shape[1]), pool.dtype)

    both, last = list(range(RB_DEV)), heads - 1
    sends, far, onwards, held, parts = {}, {}, {}, {}, []
    for g in range(min(2, heads)):
        planned = g == min(1, heads - 1)
        sends[g] = pack_send(wide, cores, [[g]], caps, (0, 0, 0), ctrl, pool, planned)
    *sends[min(1, heads - 1)], table = sends[min(1, heads - 1)]
    over = table[OVER_AT] == 1
    extra = lax.cond(over, past_the_end, nothing, ctrl, pool)

    def relay(g, plan):
        following = []
        left, right = sideways(*sends[g][:2])
        if g == 0:
            far[0] = hop(sends[0][2], [(0, 2), (3, 1)])
        if g + 1 < heads:
            if g + 1 not in sends:
                sends[g + 1] = pack_send(wide, cores, [[g + 1]], caps, (0, 0, 0), ctrl, pool)
            following = sends[g + 1][2:]
        onward = pack_relay(cores, caps, g, plan, far[g], left, right, *following)
        onwards[g] = onward
        far[g + 1] = hop(onward, [(2, 3), (1, 0)] + ([(0, 2), (3, 1)] if following else []))
        held[g] = [pool, left, right, far[g], far[g + 1]]

    relay(0, after(ctrl, extra))

    def exchange(g, plan):
        shared = pack_share(cores, caps, 0, g, plan, held[g] + [extra])
        return held[g] + [lax.ppermute(shared, "wide", swap), extra]

    summed = None
    for g in range(last):
        relay(g + 1, after(ctrl, parts[-1]) if parts else ctrl)
        buffers = exchange(g, after(table, onwards[g + 1]))
        attended, summed = attend(
            [g], 0, both, False, caps, table, queries, resp_kv, buffers, weight, share, summed
        )
        parts.append(attended)
    buffers = exchange(last, after(table, parts[-1]) if parts else table)
    ends, terms, plan = [], [], table
    for b in both:
        end, term = attend(
            [last], 0, [b], True, caps, plan, queries, resp_kv, buffers, weight, share, summed
        )
        ends.append(end)
        terms.append(term)
        plan = after(table, end)
    return parts + [jnp.concatenate(ends, axis=0)], terms


def project_kernel(carried, at, *refs):
    parts, weight, out = refs[: -2 - carried], refs[-2 - carried], refs[-1]
    total, row = refs[-2][...] if carried else None, 0
    for part in parts:
        end = row + part.shape[1]
        term = jnp.dot(part[...], weight[row:end, :], preferred_element_type=jnp.float32)
        total, row = term if total is None else total + term, end
    out[...] = total.astype(out.dtype)


def project(parts, weight, first, first_column, columns, kept=jnp.bfloat16, summed=None):
    tokens, rows = parts[0].shape[0], sum(part.shape[1] for part in parts)
    tile = math.gcd(columns, 512)
    assert weight.shape[1] % tile == 0
    at = jnp.reshape(first_column // tile, (1,)).astype(jnp.int32)
    skip = first * WIDTH
    if skip % rows:
        weight_spec = pl.BlockSpec(
            (pl.Element(rows), pl.Element(tile)), lambda i, at: (skip, (at[0] + i) * tile)
        )
    else:
        weight_spec = pl.BlockSpec((rows, tile), lambda i, at: (skip // rows, at[0] + i))
    operands, in_specs = [*parts, weight], [
        pl.BlockSpec(part.shape, lambda i, at: (0, 0)) for part in parts
    ] + [weight_spec]
    if summed is not None:
        operands.append(summed)
        in_specs.append(pl.BlockSpec((tokens, tile), lambda i, at: (0, i)))
    return pl.pallas_call(
        lambda *refs: project_kernel(summed is not None, *refs),
        out_shape=jax.ShapeDtypeStruct((tokens, columns), kept),
        grid_spec=pltpu.PrefetchScalarGridSpec(
            num_scalar_prefetch=1,
            grid=(columns // tile,),
            in_specs=in_specs,
            out_specs=pl.BlockSpec((tokens, tile), lambda i, at: (0, i)),
        ),
        compiler_params=params(PROJECT_MIB),
        cost_estimate=SMALL,
        name="project",
    )(at, *operands)


def add_terms(total, arrived, block):
    rows, columns = arrived.shape
    tile = columns // 2
    spec = pl.BlockSpec((rows, tile), lambda i: (block, i))

    def kernel(own, other, out):
        out[...] = (own[...].astype(jnp.float32) + other[...].astype(jnp.float32)).astype(out.dtype)

    return pl.pallas_call(
        kernel,
        out_shape=jax.ShapeDtypeStruct(total.shape, total.dtype),
        grid=(columns // tile,),
        in_specs=[spec, pl.BlockSpec((rows, tile), lambda i: (0, i))],
        out_specs=spec,
        input_output_aliases={0: 0},
        compiler_params=params(8),
        cost_estimate=SMALL,
        name=f"add_terms_{block}",
    )(total, arrived)


def local(
    queries, resp_kv, prefix_pool, out_weight, pre_len, prompt_blocks, prompt_owner, resp_seg
):
    wide, groups = lax.axis_size("wide"), lax.axis_size("tp") * lax.axis_size("sub")
    cores = 2 // lax.axis_size("sub")
    heads = resp_kv.shape[1] // PAIR
    me = lax.axis_index("wide").astype(jnp.int32)
    group = lax.axis_index("tp") * lax.axis_size("sub") + lax.axis_index("sub")
    where = jnp.stack([me, (1 - group).astype(jnp.int32)])
    ctrl = jnp.concatenate([pre_len, prompt_blocks, prompt_owner, resp_seg, where])
    columns = out_weight.shape[1]
    share = columns // groups
    if wide == 8 and cores == 2 and groups == 2:
        parts, theirs = line_attend(
            wide, cores, CAPS, ctrl, queries, resp_kv, prefix_pool, out_weight
        )
        axis = "tp" if lax.axis_size("tp") == 2 else "sub"
        arrived = [lax.ppermute(terms, axis, [(0, 1), (1, 0)]) for terms in theirs]
        half = share // 2
        mine = [
            project(parts, out_weight, 0, group * share, half),
            project(parts, out_weight, 0, after(group, arrived[0]) * share + half, half),
        ]
        mine = jnp.concatenate(mine, axis=1)
        return add_terms(add_terms(mine, arrived[0], 0), arrived[1], 1)
    table = make_plan(wide, cores, False, ctrl)
    buffers = [lax.all_gather(prefix_pool, "wide", axis=0, tiled=True)]
    blocks = list(range(RB_DEV))
    parts = [
        attend([g], 0, blocks, False, CAPS, table, queries, resp_kv, buffers)[0] for g in range(heads)
    ]
    terms = project(parts, out_weight, 0, jnp.int32(0), columns)
    return lax.psum_scatter(terms, ("tp", "sub"), scatter_dimension=1, tiled=True)


def solution(mesh):
    return jax.shard_map(
        local,
        mesh=mesh,
        in_specs=(
            P(("parts", "wide"), ("tp", "sub")),
            P(("parts", "wide"), ("tp", "sub")),
            P(("parts", "wide"), ("tp", "sub")),
            P(("tp", "sub"), None),
            P("parts"),
            P("parts"),
            P("parts"),
            P(("parts", "wide")),
        ),
        out_specs=P(("parts", "wide"), ("tp", "sub")),
        check_vma=False,
    )
```

```python
import math

import jax
import jax.numpy as jnp
from jax import lax
from jax.experimental import pallas as pl
from jax.experimental.pallas import tpu as pltpu
from jax.sharding import PartitionSpec as P

HD = 128
BLOCK = 128
RB_DEV = 2
PROMPTS = 4
PMAX = 16
GROUP = 8
PAIR = 2 * HD
WIDTH = GROUP * HD
ROWS = 512
SPAN = 4
NEG_LARGE = -1e30
SCALE = math.log2(math.e) / math.sqrt(HD)
MIB = 1024 * 1024
ATTEND_MIB, PROJECT_MIB = 28, 18
SMALL = pl.CostEstimate(flops=1 << 20, bytes_accessed=1 << 14, transcendentals=0)

LEN_AT, BLOCKS_AT, OWNER_AT, SEG_AT, ME_AT, OTHER_AT = 0, 4, 8, 12, 14, 15


def params(mib):
    return pltpu.CompilerParams(vmem_limit_bytes=mib * MIB)


def as_int(flag):
    return jnp.where(flag, 1, 0)


class Layout:
    def __init__(self, ctrl, wide, cores):
        self.ctrl, self.wide, self.cores = ctrl, wide, cores
        self.stride = (PMAX + wide - 1) // wide
        self.me = ctrl[ME_AT]
        self.z, self.core = self.div(self.me, cores), self.mod(self.me, cores)
        ends, total = [], 0
        for p in range(PROMPTS):
            total = total + ctrl[BLOCKS_AT + p] + (RB_DEV - 1)
            ends.append(total)
        self.ends = ends

    def mod(self, value, size):
        return value & (size - 1) if size & (size - 1) == 0 else lax.rem(value, size)

    def div(self, value, size):
        if size & (size - 1) == 0:
            return lax.shift_right_logical(value, size.bit_length() - 1)
        return lax.div(value, size)

    def prompt_of(self, block):
        return sum(as_int(block >= end) for end in self.ends[:-1])

    def first_of(self, chip):
        return self.prompt_of(chip * self.cores * RB_DEV)

    def last_of(self, chip):
        return self.prompt_of((chip + 1) * self.cores * RB_DEV - 1)

    def length(self, p):
        return self.ctrl[LEN_AT + p]

    def held_by(self, p, j):
        return self.mod(self.ctrl[OWNER_AT + p] + j, self.wide)

    def held(self, p, who):
        first = self.mod(who - self.ctrl[OWNER_AT + p] + self.wide, self.wide)
        return sum(as_int(first + k * self.wide < self.length(p)) for k in range(self.stride))

    def listed(self, which, rank, room):
        return jnp.where(
            rank < room, which * CODE + rank, (EXTRA + which - 1) * CODE + rank - room
        )

    def in_plane(self, p, j, sums):
        who = self.held_by(p, j)
        chip = self.div(who, self.cores)
        gap = chip - self.z
        k = self.div(j, self.wide)
        at = who * SUMS
        down = sums[at + PROMPTS] - sums[at + p + 1] + k
        up = sums[at + p] + k
        near_down = down - jnp.where(
            chip == 0, sums[at + PROMPTS] - sums[at + self.last_of(1) + 1], 0
        )
        near_up = up - jnp.where(chip == 3, sums[at + self.first_of(2)], 0)
        far = jnp.where(gap < 0, down, up)
        two = (gap == 2) | (gap == -2)
        direct = two & ((self.z == 1) | (self.z == 2))
        code = jnp.where(two, 5 * CODE, 4 * CODE) + far
        code = jnp.where(direct, self.listed(3, far, CAPS.far), code)
        code = jnp.where(gap == 1, self.listed(2, near_up, CAPS.near), code)
        code = jnp.where(gap == -1, self.listed(1, near_down, CAPS.near), code)
        return jnp.where(gap == 0, p * self.stride + k, code)


CODE = 256
SHARED = 6
EXTRA = 7
SUMS = 8
SLOT_AT, SHARE_AT, SHARES_AT, LENGTH_AT, BASE_AT, LOW_AT, THEIRS_AT, OVER_AT, TABLE = (
    0, 32, 50, 52, 54, 56, 58, 59, 64
)


class Caps:
    def __init__(self, near, far, relay):
        self.near, self.far, self.relay = near, far, relay


CAPS = Caps(5, 5, 4)


def needs(lay, sums, cores):
    first, last = [lay.first_of(c) for c in range(4)], [lay.last_of(c) for c in range(4)]
    near, far = jnp.int32(0), jnp.int32(0)
    for core in range(cores):

        def held(chip, low, high, core=core):
            at = (chip * cores + core) * SUMS
            return sums[at + high + 1] - sums[at + low]

        top = PROMPTS - 1
        edge = [held(1, 0, last[0]), held(2, first[3], top)]
        for amount in edge + [
            held(0, first[1], last[1]),
            held(1, first[2], top),
            held(2, 0, last[1]),
            held(3, first[2], last[2]),
        ]:
            near = jnp.maximum(near, amount)
        for amount in (held(0, first[2], top), held(3, 0, last[1])):
            far = jnp.maximum(far, amount)
    return near, far


def plan_kernel(wide, cores, line, ctrl, table, sums):
    lay = Layout(ctrl, wide, cores)
    half = PMAX // cores
    table[THEIRS_AT] = ctrl[OTHER_AT]
    table[OVER_AT] = 0
    if line:

        def tally(who, carry):
            total = jnp.int32(0)
            for p in range(PROMPTS):
                sums[who * SUMS + p] = total
                total = total + lay.held(p, who)
            sums[who * SUMS + PROMPTS] = total
            return carry

        lax.fori_loop(0, wide, tally, 0)
        near, far = needs(lay, sums, cores)
        over = (near > CAPS.near) | (far > CAPS.far)
        table[OVER_AT] = as_int(over)

    def prompts_of(device):
        return [lay.prompt_of(device * RB_DEV + b) for b in range(RB_DEV)]

    mine = prompts_of(lay.me)
    same = mine[0] == mine[1]
    joined = same & (ctrl[SEG_AT] == ctrl[SEG_AT + 1])
    for slot in range(RB_DEV):
        p = mine[slot]
        count = lay.length(p)
        table[LENGTH_AT + slot] = count
        if slot == 1:
            count = jnp.where(same, 0, count)
        table[BASE_AT + slot] = jnp.where(same, 0, PMAX) if slot else 0
        table[LOW_AT + slot] = jnp.where(joined, 0, BLOCK) if slot else 0

        def place(j, carry, slot=slot, p=p):
            who = lay.held_by(p, j)
            code = (who * PROMPTS + p) * lay.stride + lay.div(j, wide)
            if line:
                shared = slot * half + lay.div(j, cores)
                passed = jnp.where(
                    lay.mod(who, cores) == lay.core,
                    lay.in_plane(p, j, sums),
                    SHARED * CODE + shared,
                )
                code = passed
            table[SLOT_AT + slot * PMAX + j] = code
            return carry

        lax.fori_loop(0, count, place, 0)
    if not line:
        return
    theirs = prompts_of(lay.z * cores + (cores - 1 - lay.core))
    for slot in range(RB_DEV):
        p = theirs[slot]
        shift = lay.mod(lay.core - ctrl[OWNER_AT + p] + wide, cores)
        count = lay.div(lay.length(p) - shift + cores - 1, cores)
        if slot == 1:
            count = jnp.where(theirs[1] == theirs[0], 0, count)
        table[SHARES_AT + slot] = count

        def share(i, carry, slot=slot, p=p, shift=shift):
            table[SHARE_AT + slot * half + i] = lay.in_plane(p, i * cores + shift, sums)
            return carry

        lax.fori_loop(0, count, share, 0)


def make_plan(wide, cores, line, ctrl):
    return pl.pallas_call(
        lambda *refs: plan_kernel(wide, cores, line, *refs),
        out_shape=jax.ShapeDtypeStruct((TABLE,), jnp.int32),
        in_specs=[pl.BlockSpec(memory_space=pltpu.SMEM)],
        out_specs=pl.BlockSpec(memory_space=pltpu.SMEM),
        scratch_shapes=[pltpu.SMEM((wide * SUMS,), jnp.int32)],
        compiler_params=params(6),
        name="plan",
    )(ctrl)


def spot(ref, page):
    return ref.at[pl.ds(pl.multiple_of(page * BLOCK, BLOCK), BLOCK), :]


def page_at(buffer, page, column):
    rows = pl.ds(pl.multiple_of(page * BLOCK, BLOCK), BLOCK)
    return buffer.at[rows, pl.ds(column if buffer.shape[1] > PAIR else 0, PAIR)]


def start_page(buffers, code, column, target, sem):
    which = lax.shift_right_logical(code, CODE.bit_length() - 1)
    page = code & (CODE - 1)
    for i, buffer, offset in buffers:

        @pl.when(which == i)
        def _(buffer=buffer, offset=offset):
            source = page_at(buffer, page + offset, column)
            pltpu.make_async_copy(source, target, sem).start()


def wait_page(target, sem):
    pltpu.make_async_copy(target, target, sem).wait()


def send_kernel(wide, cores, groups, caps, skip, planned, ctrl, pool, *refs):
    if planned:
        *outs, table, sems, sums = refs
    else:
        *outs, sems = refs
    rooms = (caps.near, caps.near, caps.far)
    lay = Layout(ctrl, wide, cores)
    z, last = lay.z, wide // cores - 1
    held = [lay.held(p, lay.me) for p in range(PROMPTS)]

    def above(p, top):
        return sum([jnp.where(o <= top, held[o], 0) for o in range(p + 1, PROMPTS)], jnp.int32(0))

    def below(p, low):
        return sum([jnp.where(o >= low, held[o], 0) for o in range(p)], jnp.int32(0))

    near_top = jnp.where(z == 0, lay.last_of(1), PROMPTS - 1)
    near_low = jnp.where(z == last, lay.first_of(2), 0)
    first_up, last_down = lay.first_of(z + 1), lay.last_of(z - 1)
    first_two, last_one = lay.first_of(2), lay.last_of(1)
    plans = []
    for p in range(PROMPTS):
        right = (z < last) & (p >= first_up) & (p <= near_top)
        left = (z > 0) & (p >= near_low) & (p <= last_down)
        far_up = (z == 0) & (p >= first_two)
        far_down = (z == last) & (p <= last_one)
        ranks = (above(p, near_top), below(p, near_low), above(p, PROMPTS - 1), below(p, 0))
        for k in range(lay.stride):
            for lane, wanted, rank in zip((0, 1, 2, 2), (right, left, far_up, far_down), ranks):
                at = rank + k - skip[lane]
                fits = (k < held[p]) & (at >= 0) & (at < rooms[lane])
                plans.append((wanted & fits, p * lay.stride + k, lane, at))

    def copies(plan):
        _, page, lane, rank = plan
        if groups is None:
            return [
                pltpu.make_async_copy(
                    spot(pool, page), spot(outs[lane], rank), sems.at[lane, page, 0]
                )
            ]
        return [
            pltpu.make_async_copy(
                page_at(pool, page, g * PAIR),
                spot(outs[n * 3 + lane], h * rooms[lane] + rank),
                sems.at[lane, page, n * len(groups[0]) + h],
            )
            for n, group in enumerate(groups)
            for h, g in enumerate(group)
        ]

    for plan in plans:

        @pl.when(plan[0])
        def _(plan=plan):
            for copy in copies(plan):
                copy.start()

    if planned:
        plan_kernel(wide, cores, True, ctrl, table, sums)
    for plan in plans:

        @pl.when(plan[0])
        def _(plan=plan):
            for copy in copies(plan):
                copy.wait()


def relay_kernel(cores, caps, ctrl, far, left, right, *refs):
    following, out, sems = refs[:-2], refs[-2], refs[-1]
    rows = caps.relay * BLOCK

    def copy(source, section):
        target = out.at[pl.ds(section * rows, rows), :]
        return pltpu.make_async_copy(source.at[pl.ds(0, rows), :], target, sems.at[section])

    at_left = at_right = False
    for core in range(cores):
        at_left = at_left | (ctrl[ME_AT] == cores + core)
        at_right = at_right | (ctrl[ME_AT] == 2 * cores + core)
    inner = at_left | at_right
    pl.when(inner)(lambda: copy(far, 0).start())
    pl.when(at_right)(lambda: copy(left, 1).start())
    pl.when(at_left)(lambda: copy(right, 1).start())

    @pl.when(inner)
    def _():
        copy(far, 0).wait()
        copy(far, 1).wait()

    for source in following:

        @pl.when(jnp.logical_not(inner))
        def _(source=source):
            target = out.at[pl.ds(0, caps.far * BLOCK), :]
            move = pltpu.make_async_copy(source, target, sems.at[2])
            move.start()
            move.wait()


def numbered(refs, caps, h):
    if len(refs) == 1:
        return [(0, refs[0], 0)]
    offsets = (0, h * caps.near, h * caps.near, h * caps.far, 0)
    found = list(zip(range(5), refs[:5], offsets)) + [(5, refs[4], caps.relay)]
    if len(refs) == 7:
        found.append((SHARED, refs[5], 0))
    return found + [(EXTRA + i, refs[-1], i) for i in range(3)]


def share_kernel(cores, caps, h, g, table, *refs):
    out, sems = refs[-2:]
    half = PMAX // cores
    buffers = numbered(refs[:-2], caps, h)
    for slot in range(RB_DEV):

        def begin(i, carry, slot=slot):
            at = slot * half + i
            start_page(buffers, table[SHARE_AT + at], g * PAIR, spot(out, at), sems.at[at])
            return carry

        lax.fori_loop(0, table[SHARES_AT + slot], begin, 0)
    for slot in range(RB_DEV):

        def finish(i, carry, slot=slot):
            at = slot * half + i
            wait_page(spot(out, at), sems.at[at])
            return carry

        lax.fori_loop(0, table[SHARES_AT + slot], finish, 0)


def attend_kernel(group, first, blocks, caps, carried, project, table, queries, own, *refs):
    refs = list(refs)
    weight = refs.pop(0) if project else None
    summed = refs.pop(0) if carried else None
    sems, stacked = refs.pop(), refs.pop()
    slab = refs.pop() if project else None
    store = refs.pop()
    terms = refs.pop() if project else None
    out = refs.pop()
    heads, room = len(group), len(blocks) * PMAX

    def region(i):
        if i == 0:
            return 0, table[LENGTH_AT + blocks[0]]
        base = table[BASE_AT + blocks[i]]
        return base, jnp.where(base == 0, 0, table[LENGTH_AT + blocks[i]])

    for h, g in enumerate(group):
        buffers = numbered(refs, caps, first + h)
        for i, b in enumerate(blocks):
            base, count = region(i)
            codes = SLOT_AT + table[BASE_AT + b]

            def begin(j, carry, h=h, g=g, buffers=buffers, base=base, codes=codes):
                at = h * room + base + j
                target, sem = spot(store, at), sems.at[at]
                start_page(buffers, table[codes + j], g * PAIR, target, sem)
                return carry

            lax.fori_loop(0, count, begin, 0)
            length = table[LENGTH_AT + b]

            def clear(j, carry, h=h, base=base):
                rows = pl.ds(pl.multiple_of((h * room + base + j) * BLOCK, BLOCK), BLOCK)
                store[rows, :] = jnp.zeros((BLOCK, PAIR), jnp.bfloat16)
                return carry

            lax.fori_loop(length, (length + SPAN - 1) & -SPAN, clear, 0)
    if project:
        share = slab.shape[1]
        theirs = pl.multiple_of(table[THEIRS_AT] * share, share)
        fetch = pltpu.make_async_copy(
            weight.at[pl.ds(group[0] * WIDTH, heads * WIDTH), pl.ds(theirs, share)],
            slab,
            sems.at[heads * room],
        )
        fetch.start()

    def one_block(h, i, b, base, count):
        tokens = pl.ds(pl.multiple_of(i * BLOCK, BLOCK), BLOCK)

        def columns(width, extra=0):
            return pl.ds(pl.multiple_of(h * width + extra, HD), min(width, HD))

        for e in range(GROUP):
            stacked[e * BLOCK : (e + 1) * BLOCK, :] = queries[tokens, columns(WIDTH, e * HD)]
        base = h * room + base

        def finish(j, carry):
            wait_page(spot(store, base + j), sems.at[base + j])
            return carry

        lax.fori_loop(0, count, finish, 0)
        length = table[LENGTH_AT + b]
        span = RB_DEV * BLOCK
        row = lax.broadcasted_iota(jnp.int32, (ROWS, span), 0) & (BLOCK - 1)
        key = lax.broadcasted_iota(jnp.int32, (ROWS, span), 1)
        own_mask = (key <= row + b * BLOCK) & (key >= table[LOW_AT + b])

        def run(spans):
            wide_key = lax.broadcasted_iota(jnp.int32, (ROWS, SPAN * BLOCK), 1)
            last_mask = wide_key < (length - (spans - 1) * SPAN) * BLOCK
            pieces = [(own[:, columns(PAIR)], own[:, columns(PAIR, HD)])]
            for t in range(spans):
                at = pl.multiple_of((base + t * SPAN) * BLOCK, BLOCK)
                piece = store[pl.ds(at, SPAN * BLOCK), :]
                pieces.append((piece[:, :HD], piece[:, HD:]))

            def score(r, t):
                scores = lax.dot_general(
                    stacked[r * ROWS : (r + 1) * ROWS, :],
                    pieces[t][0],
                    (((1,), (1,)), ((), ())),
                    preferred_element_type=jnp.float32,
                )
                if t == 0:
                    return jnp.where(own_mask, scores, NEG_LARGE)
                if t == spans:
                    return jnp.where(last_mask, scores, NEG_LARGE)
                return scores

            def highest(scores, sofar):
                for n in range(0, scores.shape[1], HD):
                    part = scores[:, n : n + HD]
                    sofar = part if sofar is None else jnp.maximum(sofar, part)
                return sofar

            def blend(scores, top, t):
                spread = jnp.concatenate([top] * (scores.shape[1] // HD), axis=1)
                weights = jnp.exp2((scores - spread) * SCALE).astype(jnp.bfloat16)
                values = pieces[t][1]
                values = jnp.concatenate([values, jnp.ones_like(values)], axis=1)
                return jnp.dot(weights, values, preferred_element_type=jnp.float32)

            chunks, ahead, peak = GROUP * BLOCK // ROWS, [], None
            for t in range(spans + 1):
                ahead.append(score(0, t))
                peak = highest(ahead[-1], peak)
            for r in range(chunks):
                now, ahead = ahead, []
                top = jnp.broadcast_to(jnp.max(peak, axis=1, keepdims=True), (ROWS, HD))
                total, peak = None, None
                for t in range(spans + 1):
                    if r + 1 < chunks:
                        ahead.append(score(r + 1, t))
                        peak = highest(ahead[-1], peak)
                    blended = blend(now[t], top, t)
                    total = blended if total is None else total + blended
                mean = (total[:, :HD] / total[:, HD:]).astype(jnp.bfloat16)
                for e in range(ROWS // BLOCK):
                    at = columns(WIDTH, (r * (ROWS // BLOCK) + e) * HD)
                    out[tokens, at] = mean[e * BLOCK : (e + 1) * BLOCK, :]

        spans = lax.shift_right_logical(length + SPAN - 1, SPAN.bit_length() - 1)
        for n in range(1, PMAX // SPAN + 1):
            pl.when(spans == n)(lambda n=n: run(n))

    def step(n, carry):
        if len(blocks) == 1:
            one_block(n, 0, blocks[0], *region(0))
            return carry
        h, i = lax.shift_right_logical(n, 1), n & 1
        base = jnp.where(i == 0, 0, region(1)[0])
        one_block(h, i, i, base, jnp.where(i == 0, region(0)[1], region(1)[1]))
        return carry

    lax.fori_loop(0, heads * len(blocks), step, 0)
    if project:
        fetch.wait()
        attended = out[...]
        width = math.gcd(share, 512)
        for n in range(0, share, width):
            term = jnp.dot(attended, slab[:, n : n + width], preferred_element_type=jnp.float32)
            if carried:
                term = term + summed[:, n : n + width]
            terms[:, n : n + width] = term.astype(terms.dtype)


def attend(
    group, first, blocks, last, caps, table, queries, resp_kv, buffers, weight=None, share=0, summed=None
):
    tokens, heads = len(blocks) * BLOCK, len(group)
    at = blocks[0] // len(blocks)
    project, carried = weight is not None, summed is not None
    any_spec = pl.BlockSpec(memory_space=pl.ANY)
    whole = pl.BlockSpec((tokens, share), lambda i, c: (0, 0))
    out_shape = [jax.ShapeDtypeStruct((tokens, heads * WIDTH), jnp.bfloat16)]
    out_specs = [pl.BlockSpec((tokens, heads * WIDTH), lambda i, c: (0, 0))]
    operands, in_specs = [], []
    scratch = [pltpu.VMEM((heads * len(blocks) * PMAX * BLOCK, PAIR), jnp.bfloat16)]
    if project:
        operands, in_specs = [weight], [any_spec]
        kept = jnp.bfloat16 if last else jnp.float32
        out_shape.append(jax.ShapeDtypeStruct((tokens, share), kept))
        out_specs.append(whole)
        scratch.append(pltpu.VMEM((heads * WIDTH, share), jnp.bfloat16))
    if carried:
        operands = operands + [summed]
        in_specs = in_specs + [pl.BlockSpec((tokens, share), lambda i, c: (at, 0))]
    column = group[0] // heads
    return pl.pallas_call(
        lambda *refs: attend_kernel(group, first, blocks, caps, carried, project, *refs),
        out_shape=out_shape,
        grid_spec=pltpu.PrefetchScalarGridSpec(
            num_scalar_prefetch=1,
            grid=(1,),
            in_specs=[
                pl.BlockSpec((tokens, heads * WIDTH), lambda i, c: (at, column)),
                pl.BlockSpec((RB_DEV * BLOCK, heads * PAIR), lambda i, c: (0, column)),
            ]
            + in_specs
            + [any_spec] * len(buffers),
            out_specs=out_specs,
            scratch_shapes=scratch
            + [
                pltpu.VMEM((GROUP * BLOCK, HD), jnp.bfloat16),
                pltpu.SemaphoreType.DMA((heads * len(blocks) * PMAX + 1,)),
            ],
        ),
        compiler_params=params(ATTEND_MIB),
        cost_estimate=SMALL,
        name="attend_heads_" + "_".join(map(str, group)) + "_blocks_" + "_".join(map(str, blocks)),
    )(table, queries, resp_kv, *operands, *buffers)


def pages_shape(count):
    return jax.ShapeDtypeStruct((count * BLOCK, PAIR), jnp.bfloat16)


def pack_send(wide, cores, groups, caps, skip, ctrl, pool, planned=False):
    any_spec = pl.BlockSpec(memory_space=pl.ANY)
    pages = PROMPTS * ((PMAX + wide - 1) // wide)
    rooms = (caps.near, caps.near, caps.far)
    if groups is None:
        shapes = [jax.ShapeDtypeStruct((n * BLOCK, pool.shape[1]), jnp.bfloat16) for n in rooms]
    else:
        shapes = [pages_shape(n * len(group)) for group in groups for n in rooms]
    heads = 1 if groups is None else sum(map(len, groups))
    out_specs = [any_spec] * len(shapes)
    scratch = [pltpu.SemaphoreType.DMA((3, pages, heads))]
    if planned:
        shapes = shapes + [jax.ShapeDtypeStruct((TABLE,), jnp.int32)]
        out_specs = out_specs + [pl.BlockSpec(memory_space=pltpu.SMEM)]
        scratch.append(pltpu.SMEM((wide * SUMS,), jnp.int32))
    return pl.pallas_call(
        lambda *refs: send_kernel(wide, cores, groups, caps, skip, planned, *refs),
        out_shape=shapes,
        grid_spec=pltpu.PrefetchScalarGridSpec(
            num_scalar_prefetch=1,
            grid=(1,),
            in_specs=[pl.BlockSpec(pool.shape, lambda i, c: (0, 0))],
            out_specs=out_specs,
            scratch_shapes=scratch,
        ),
        compiler_params=params(8),
        cost_estimate=SMALL,
        name="pack_extra" if groups is None else f"pack_send_{groups[0][0]}",
    )(ctrl, pool)


def pack_share(cores, caps, h, g, table, buffers):
    any_spec = pl.BlockSpec(memory_space=pl.ANY)
    return pl.pallas_call(
        lambda *refs: share_kernel(cores, caps, h, g, *refs),
        out_shape=pages_shape(PMAX),
        grid_spec=pltpu.PrefetchScalarGridSpec(
            num_scalar_prefetch=1,
            grid=(1,),
            in_specs=[any_spec] * len(buffers),
            out_specs=pl.BlockSpec((PMAX * BLOCK, PAIR), lambda i, c: (0, 0)),
            scratch_shapes=[pltpu.SemaphoreType.DMA((PMAX,))],
        ),
        compiler_params=params(6),
        cost_estimate=SMALL,
        name=f"pack_share_{g}",
    )(table, *buffers)


def pack_relay(cores, caps, g, ctrl, *lists):
    any_spec = pl.BlockSpec(memory_space=pl.ANY)
    pages = max(2 * caps.relay, caps.far)
    return pl.pallas_call(
        lambda *refs: relay_kernel(cores, caps, *refs),
        out_shape=pages_shape(pages),
        grid_spec=pltpu.PrefetchScalarGridSpec(
            num_scalar_prefetch=1,
            grid=(1,),
            in_specs=[any_spec] * len(lists),
            out_specs=pl.BlockSpec((pages * BLOCK, PAIR), lambda i, c: (0, 0)),
            scratch_shapes=[pltpu.SemaphoreType.DMA((3,))],
        ),
        compiler_params=params(6),
        cost_estimate=SMALL,
        name=f"pack_relay_{g}",
    )(ctrl, *lists)


def after(value, *earlier):
    return lax.optimization_barrier((value, *earlier))[0]


def line_attend(wide, cores, caps, ctrl, queries, resp_kv, pool, weight):
    heads = resp_kv.shape[1] // PAIR
    share = weight.shape[1] // 2

    def hop(x, moves):
        pairs = [(a * cores + c, b * cores + c) for a, b in moves for c in range(cores)]
        return lax.ppermute(x, "wide", pairs)

    swap = [(d, d // cores * cores + (cores - 1 - d % cores)) for d in range(wide)]

    def sideways(right, left):
        return hop(right, [(0, 1), (1, 2), (2, 3)]), hop(left, [(3, 2), (2, 1), (1, 0)])

    past = Caps(1, 1, 0)

    def past_the_end(ctrl, pool):
        skip = (caps.near, caps.near, caps.far)
        right, left, far = pack_send(wide, cores, None, past, skip, ctrl, pool)
        found = *sideways(right, left), hop(far, [(0, 2), (3, 1)])
        return jnp.concatenate(found, axis=0)

    def nothing(ctrl, pool):
        return jnp.zeros((3 * past.near * BLOCK, pool.shape[1]), pool.dtype)

    both, last = list(range(RB_DEV)), heads - 1
    sends, far, onwards, held, parts = {}, {}, {}, {}, []
    tables, extras = [], []

    def pack(g, plan):
        planned = g == min(1, last)
        lists = pack_send(wide, cores, [[g]], caps, (0, 0, 0), plan, pool, planned)
        sends[g] = lists[:3]
        tables.extend(lists[3:])

    pack(0, ctrl)

    def relay(g, plan):
        following = []
        left, right = sideways(*sends[g][:2])
        if g == 0:
            far[0] = hop(sends[0][2], [(0, 2), (3, 1)])
        if g + 1 < heads:
            pack(g + 1, ctrl if g else after(ctrl, left))
            following = sends[g + 1][2:]
        if not extras:
            over = tables[0][OVER_AT] == 1
            extras.append(lax.cond(over, past_the_end, nothing, ctrl, pool))
            plan = after(plan, extras[0])
        onward = pack_relay(cores, caps, g, plan, far[g], left, right, *following)
        onwards[g] = onward
        far[g + 1] = hop(onward, [(2, 3), (1, 0)] + ([(0, 2), (3, 1)] if following else []))
        held[g] = [pool, left, right, far[g], far[g + 1]]

    relay(0, ctrl)

    table, extra = tables[0], extras[0]

    def exchange(g, plan):
        shared = pack_share(cores, caps, 0, g, plan, held[g] + [extra])
        return held[g] + [lax.ppermute(shared, "wide", swap), extra]

    summed = None
    for g in range(last):
        relay(g + 1, after(ctrl, parts[-1]) if parts else ctrl)
        buffers = exchange(g, after(table, onwards[g + 1]))
        attended, summed = attend(
            [g], 0, both, False, caps, table, queries, resp_kv, buffers, weight, share, summed
        )
        parts.append(attended)
    buffers = exchange(last, after(table, parts[-1]) if parts else table)
    ends, terms, plan = [], [], table
    for b in both:
        end, term = attend(
            [last], 0, [b], True, caps, plan, queries, resp_kv, buffers, weight, share, summed
        )
        ends.append(end)
        terms.append(term)
        plan = after(table, end)
    return parts + [jnp.concatenate(ends, axis=0)], terms


def project_kernel(carried, at, *refs):
    parts, weight, out = refs[: -2 - carried], refs[-2 - carried], refs[-1]
    total, row = refs[-2][...] if carried else None, 0
    for part in parts:
        end = row + part.shape[1]
        term = jnp.dot(part[...], weight[row:end, :], preferred_element_type=jnp.float32)
        total, row = term if total is None else total + term, end
    out[...] = total.astype(out.dtype)


def project(parts, weight, first, first_column, columns, kept=jnp.bfloat16, summed=None):
    tokens, rows = parts[0].shape[0], sum(part.shape[1] for part in parts)
    tile = math.gcd(columns, 512)
    assert weight.shape[1] % tile == 0
    at = jnp.reshape(first_column // tile, (1,)).astype(jnp.int32)
    skip = first * WIDTH
    if skip % rows:
        weight_spec = pl.BlockSpec(
            (pl.Element(rows), pl.Element(tile)), lambda i, at: (skip, (at[0] + i) * tile)
        )
    else:
        weight_spec = pl.BlockSpec((rows, tile), lambda i, at: (skip // rows, at[0] + i))
    operands, in_specs = [*parts, weight], [
        pl.BlockSpec(part.shape, lambda i, at: (0, 0)) for part in parts
    ] + [weight_spec]
    if summed is not None:
        operands.append(summed)
        in_specs.append(pl.BlockSpec((tokens, tile), lambda i, at: (0, i)))
    return pl.pallas_call(
        lambda *refs: project_kernel(summed is not None, *refs),
        out_shape=jax.ShapeDtypeStruct((tokens, columns), kept),
        grid_spec=pltpu.PrefetchScalarGridSpec(
            num_scalar_prefetch=1,
            grid=(columns // tile,),
            in_specs=in_specs,
            out_specs=pl.BlockSpec((tokens, tile), lambda i, at: (0, i)),
        ),
        compiler_params=params(PROJECT_MIB),
        cost_estimate=SMALL,
        name="project",
    )(at, *operands)


def add_terms(total, arrived, block):
    rows, columns = arrived.shape
    tile = columns // 2
    spec = pl.BlockSpec((rows, tile), lambda i: (block, i))

    def kernel(own, other, out):
        out[...] = (own[...].astype(jnp.float32) + other[...].astype(jnp.float32)).astype(out.dtype)

    return pl.pallas_call(
        kernel,
        out_shape=jax.ShapeDtypeStruct(total.shape, total.dtype),
        grid=(columns // tile,),
        in_specs=[spec, pl.BlockSpec((rows, tile), lambda i: (0, i))],
        out_specs=spec,
        input_output_aliases={0: 0},
        compiler_params=params(8),
        cost_estimate=SMALL,
        name=f"add_terms_{block}",
    )(total, arrived)


def local(
    queries, resp_kv, prefix_pool, out_weight, pre_len, prompt_blocks, prompt_owner, resp_seg
):
    wide, groups = lax.axis_size("wide"), lax.axis_size("tp") * lax.axis_size("sub")
    cores = 2 // lax.axis_size("sub")
    heads = resp_kv.shape[1] // PAIR
    me = lax.axis_index("wide").astype(jnp.int32)
    group = lax.axis_index("tp") * lax.axis_size("sub") + lax.axis_index("sub")
    where = jnp.stack([me, (1 - group).astype(jnp.int32)])
    ctrl = jnp.concatenate([pre_len, prompt_blocks, prompt_owner, resp_seg, where])
    columns = out_weight.shape[1]
    share = columns // groups
    if wide == 8 and cores == 2 and groups == 2:
        parts, theirs = line_attend(
            wide, cores, CAPS, ctrl, queries, resp_kv, prefix_pool, out_weight
        )
        axis = "tp" if lax.axis_size("tp") == 2 else "sub"
        arrived = [lax.ppermute(terms, axis, [(0, 1), (1, 0)]) for terms in theirs]
        half = share // 2
        mine = [
            project(parts, out_weight, 0, group * share, half),
            project(parts, out_weight, 0, after(group, arrived[0]) * share + half, half),
        ]
        mine = jnp.concatenate(mine, axis=1)
        return add_terms(add_terms(mine, arrived[0], 0), arrived[1], 1)
    table = make_plan(wide, cores, False, ctrl)
    buffers = [lax.all_gather(prefix_pool, "wide", axis=0, tiled=True)]
    blocks = list(range(RB_DEV))
    parts = [
        attend([g], 0, blocks, False, CAPS, table, queries, resp_kv, buffers)[0] for g in range(heads)
    ]
    terms = project(parts, out_weight, 0, jnp.int32(0), columns)
    return lax.psum_scatter(terms, ("tp", "sub"), scatter_dimension=1, tiled=True)


def solution(mesh):
    return jax.shard_map(
        local,
        mesh=mesh,
        in_specs=(
            P(("parts", "wide"), ("tp", "sub")),
            P(("parts", "wide"), ("tp", "sub")),
            P(("parts", "wide"), ("tp", "sub")),
            P(("tp", "sub"), None),
            P("parts"),
            P("parts"),
            P("parts"),
            P(("parts", "wide")),
        ),
        out_specs=P(("parts", "wide"), ("tp", "sub")),
        check_vma=False,
    )
```

```python
import math

import jax
import jax.numpy as jnp
from jax import lax
from jax.experimental import pallas as pl
from jax.experimental.pallas import tpu as pltpu
from jax.sharding import PartitionSpec as P

HD = 128
BLOCK = 128
RB_DEV = 2
PROMPTS = 4
PMAX = 16
GROUP = 8
PAIR = 2 * HD
WIDTH = GROUP * HD
ROWS = 512
SPAN = 4
NEG_LARGE = -1e30
SCALE = math.log2(math.e) / math.sqrt(HD)
MIB = 1024 * 1024
ATTEND_MIB, PROJECT_MIB = 28, 18
SMALL = pl.CostEstimate(flops=1 << 20, bytes_accessed=1 << 14, transcendentals=0)

LEN_AT, BLOCKS_AT, OWNER_AT, SEG_AT, ME_AT, OTHER_AT = 0, 4, 8, 12, 14, 15


def params(mib):
    return pltpu.CompilerParams(vmem_limit_bytes=mib * MIB)


def as_int(flag):
    return jnp.where(flag, 1, 0)


class Layout:
    def __init__(self, ctrl, wide, cores):
        self.ctrl, self.wide, self.cores = ctrl, wide, cores
        self.stride = (PMAX + wide - 1) // wide
        self.me = ctrl[ME_AT]
        self.z, self.core = self.div(self.me, cores), self.mod(self.me, cores)
        ends, total = [], 0
        for p in range(PROMPTS):
            total = total + ctrl[BLOCKS_AT + p] + (RB_DEV - 1)
            ends.append(total)
        self.ends = ends

    def mod(self, value, size):
        return value & (size - 1) if size & (size - 1) == 0 else lax.rem(value, size)

    def div(self, value, size):
        if size & (size - 1) == 0:
            return lax.shift_right_logical(value, size.bit_length() - 1)
        return lax.div(value, size)

    def prompt_of(self, block):
        return sum(as_int(block >= end) for end in self.ends[:-1])

    def first_of(self, chip):
        return self.prompt_of(chip * self.cores * RB_DEV)

    def last_of(self, chip):
        return self.prompt_of((chip + 1) * self.cores * RB_DEV - 1)

    def length(self, p):
        return self.ctrl[LEN_AT + p]

    def held_by(self, p, j):
        return self.mod(self.ctrl[OWNER_AT + p] + j, self.wide)

    def held(self, p, who):
        first = self.mod(who - self.ctrl[OWNER_AT + p] + self.wide, self.wide)
        return sum(as_int(first + k * self.wide < self.length(p)) for k in range(self.stride))

    def listed(self, which, rank, room):
        return jnp.where(
            rank < room, which * CODE + rank, (EXTRA + which - 1) * CODE + rank - room
        )

    def in_plane(self, p, j, sums):
        who = self.held_by(p, j)
        chip = self.div(who, self.cores)
        gap = chip - self.z
        k = self.div(j, self.wide)
        at = who * SUMS
        down = sums[at + PROMPTS] - sums[at + p + 1] + k
        up = sums[at + p] + k
        near_down = down - jnp.where(
            chip == 0, sums[at + PROMPTS] - sums[at + self.last_of(1) + 1], 0
        )
        near_up = up - jnp.where(chip == 3, sums[at + self.first_of(2)], 0)
        far = jnp.where(gap < 0, down, up)
        two = (gap == 2) | (gap == -2)
        direct = two & ((self.z == 1) | (self.z == 2))
        code = jnp.where(two, 5 * CODE, 4 * CODE) + far
        code = jnp.where(direct, self.listed(3, far, CAPS.far), code)
        code = jnp.where(gap == 1, self.listed(2, near_up, CAPS.near), code)
        code = jnp.where(gap == -1, self.listed(1, near_down, CAPS.near), code)
        return jnp.where(gap == 0, p * self.stride + k, code)


CODE = 256
SHARED = 6
EXTRA = 7
SUMS = 8
SLOT_AT, SHARE_AT, SHARES_AT, LENGTH_AT, BASE_AT, LOW_AT, THEIRS_AT, OVER_AT, TABLE = (
    0, 32, 50, 52, 54, 56, 58, 59, 64
)


class Caps:
    def __init__(self, near, far, relay):
        self.near, self.far, self.relay = near, far, relay


CAPS = Caps(5, 5, 4)


def needs(lay, sums, cores):
    first, last = [lay.first_of(c) for c in range(4)], [lay.last_of(c) for c in range(4)]
    near, far = jnp.int32(0), jnp.int32(0)
    for core in range(cores):

        def held(chip, low, high, core=core):
            at = (chip * cores + core) * SUMS
            return sums[at + high + 1] - sums[at + low]

        top = PROMPTS - 1
        edge = [held(1, 0, last[0]), held(2, first[3], top)]
        for amount in edge + [
            held(0, first[1], last[1]),
            held(1, first[2], top),
            held(2, 0, last[1]),
            held(3, first[2], last[2]),
        ]:
            near = jnp.maximum(near, amount)
        for amount in (held(0, first[2], top), held(3, 0, last[1])):
            far = jnp.maximum(far, amount)
    return near, far


def plan_kernel(wide, cores, line, ctrl, table, sums):
    lay = Layout(ctrl, wide, cores)
    half = PMAX // cores
    table[THEIRS_AT] = ctrl[OTHER_AT]
    table[OVER_AT] = 0
    if line:

        def tally(who, carry):
            total = jnp.int32(0)
            for p in range(PROMPTS):
                sums[who * SUMS + p] = total
                total = total + lay.held(p, who)
            sums[who * SUMS + PROMPTS] = total
            return carry

        lax.fori_loop(0, wide, tally, 0)
        near, far = needs(lay, sums, cores)
        over = (near > CAPS.near) | (far > CAPS.far)
        table[OVER_AT] = as_int(over)

    def prompts_of(device):
        return [lay.prompt_of(device * RB_DEV + b) for b in range(RB_DEV)]

    mine = prompts_of(lay.me)
    same = mine[0] == mine[1]
    joined = same & (ctrl[SEG_AT] == ctrl[SEG_AT + 1])
    for slot in range(RB_DEV):
        p = mine[slot]
        count = lay.length(p)
        table[LENGTH_AT + slot] = count
        if slot == 1:
            count = jnp.where(same, 0, count)
        table[BASE_AT + slot] = jnp.where(same, 0, PMAX) if slot else 0
        table[LOW_AT + slot] = jnp.where(joined, 0, BLOCK) if slot else 0

        def place(j, carry, slot=slot, p=p):
            who = lay.held_by(p, j)
            code = (who * PROMPTS + p) * lay.stride + lay.div(j, wide)
            if line:
                shared = slot * half + lay.div(j, cores)
                passed = jnp.where(
                    lay.mod(who, cores) == lay.core,
                    lay.in_plane(p, j, sums),
                    SHARED * CODE + shared,
                )
                code = passed
            table[SLOT_AT + slot * PMAX + j] = code
            return carry

        lax.fori_loop(0, count, place, 0)
    if not line:
        return
    theirs = prompts_of(lay.z * cores + (cores - 1 - lay.core))
    for slot in range(RB_DEV):
        p = theirs[slot]
        shift = lay.mod(lay.core - ctrl[OWNER_AT + p] + wide, cores)
        count = lay.div(lay.length(p) - shift + cores - 1, cores)
        if slot == 1:
            count = jnp.where(theirs[1] == theirs[0], 0, count)
        table[SHARES_AT + slot] = count

        def share(i, carry, slot=slot, p=p, shift=shift):
            table[SHARE_AT + slot * half + i] = lay.in_plane(p, i * cores + shift, sums)
            return carry

        lax.fori_loop(0, count, share, 0)


def make_plan(wide, cores, line, ctrl):
    return pl.pallas_call(
        lambda *refs: plan_kernel(wide, cores, line, *refs),
        out_shape=jax.ShapeDtypeStruct((TABLE,), jnp.int32),
        in_specs=[pl.BlockSpec(memory_space=pltpu.SMEM)],
        out_specs=pl.BlockSpec(memory_space=pltpu.SMEM),
        scratch_shapes=[pltpu.SMEM((wide * SUMS,), jnp.int32)],
        compiler_params=params(6),
        name="plan",
    )(ctrl)


def spot(ref, page):
    return ref.at[pl.ds(pl.multiple_of(page * BLOCK, BLOCK), BLOCK), :]


def page_at(buffer, page, column):
    rows = pl.ds(pl.multiple_of(page * BLOCK, BLOCK), BLOCK)
    return buffer.at[rows, pl.ds(column if buffer.shape[1] > PAIR else 0, PAIR)]


def start_page(buffers, code, column, target, sem):
    which = lax.shift_right_logical(code, CODE.bit_length() - 1)
    page = code & (CODE - 1)
    for i, buffer, offset in buffers:

        @pl.when(which == i)
        def _(buffer=buffer, offset=offset):
            source = page_at(buffer, page + offset, column)
            pltpu.make_async_copy(source, target, sem).start()


def wait_page(target, sem):
    pltpu.make_async_copy(target, target, sem).wait()


def send_kernel(wide, cores, groups, caps, skip, planned, ctrl, pool, *refs):
    if planned:
        *outs, table, sems, sums = refs
    else:
        *outs, sems = refs
    rooms = (caps.near, caps.near, caps.far)
    lay = Layout(ctrl, wide, cores)
    z, last = lay.z, wide // cores - 1
    held = [lay.held(p, lay.me) for p in range(PROMPTS)]

    def above(p, top):
        return sum([jnp.where(o <= top, held[o], 0) for o in range(p + 1, PROMPTS)], jnp.int32(0))

    def below(p, low):
        return sum([jnp.where(o >= low, held[o], 0) for o in range(p)], jnp.int32(0))

    near_top = jnp.where(z == 0, lay.last_of(1), PROMPTS - 1)
    near_low = jnp.where(z == last, lay.first_of(2), 0)
    first_up, last_down = lay.first_of(z + 1), lay.last_of(z - 1)
    first_two, last_one = lay.first_of(2), lay.last_of(1)
    plans = []
    for p in range(PROMPTS):
        right = (z < last) & (p >= first_up) & (p <= near_top)
        left = (z > 0) & (p >= near_low) & (p <= last_down)
        far_up = (z == 0) & (p >= first_two)
        far_down = (z == last) & (p <= last_one)
        ranks = (above(p, near_top), below(p, near_low), above(p, PROMPTS - 1), below(p, 0))
        for k in range(lay.stride):
            for lane, wanted, rank in zip((0, 1, 2, 2), (right, left, far_up, far_down), ranks):
                at = rank + k - skip[lane]
                fits = (k < held[p]) & (at >= 0) & (at < rooms[lane])
                plans.append((wanted & fits, p * lay.stride + k, lane, at))

    def copies(plan):
        _, page, lane, rank = plan
        if groups is None:
            return [
                pltpu.make_async_copy(
                    spot(pool, page), spot(outs[lane], rank), sems.at[lane, page, 0]
                )
            ]
        return [
            pltpu.make_async_copy(
                page_at(pool, page, g * PAIR),
                spot(outs[n * 3 + lane], h * rooms[lane] + rank),
                sems.at[lane, page, n * len(groups[0]) + h],
            )
            for n, group in enumerate(groups)
            for h, g in enumerate(group)
        ]

    for plan in plans:

        @pl.when(plan[0])
        def _(plan=plan):
            for copy in copies(plan):
                copy.start()

    if planned:
        plan_kernel(wide, cores, True, ctrl, table, sums)
    for plan in plans:

        @pl.when(plan[0])
        def _(plan=plan):
            for copy in copies(plan):
                copy.wait()


def relay_kernel(cores, caps, ctrl, far, left, right, *refs):
    following, out, sems = refs[:-2], refs[-2], refs[-1]
    rows = caps.relay * BLOCK

    def copy(source, section):
        target = out.at[pl.ds(section * rows, rows), :]
        return pltpu.make_async_copy(source.at[pl.ds(0, rows), :], target, sems.at[section])

    at_left = at_right = False
    for core in range(cores):
        at_left = at_left | (ctrl[ME_AT] == cores + core)
        at_right = at_right | (ctrl[ME_AT] == 2 * cores + core)
    inner = at_left | at_right
    pl.when(inner)(lambda: copy(far, 0).start())
    pl.when(at_right)(lambda: copy(left, 1).start())
    pl.when(at_left)(lambda: copy(right, 1).start())

    @pl.when(inner)
    def _():
        copy(far, 0).wait()
        copy(far, 1).wait()

    for source in following:

        @pl.when(jnp.logical_not(inner))
        def _(source=source):
            target = out.at[pl.ds(0, caps.far * BLOCK), :]
            move = pltpu.make_async_copy(source, target, sems.at[2])
            move.start()
            move.wait()


def numbered(refs, caps, h):
    if len(refs) == 1:
        return [(0, refs[0], 0)]
    offsets = (0, h * caps.near, h * caps.near, h * caps.far, 0)
    found = list(zip(range(5), refs[:5], offsets)) + [(5, refs[4], caps.relay)]
    if len(refs) == 7:
        found.append((SHARED, refs[5], 0))
    return found + [(EXTRA + i, refs[-1], i) for i in range(3)]


def share_kernel(cores, caps, h, g, table, *refs):
    out, sems = refs[-2:]
    half = PMAX // cores
    buffers = numbered(refs[:-2], caps, h)
    for slot in range(RB_DEV):

        def begin(i, carry, slot=slot):
            at = slot * half + i
            start_page(buffers, table[SHARE_AT + at], g * PAIR, spot(out, at), sems.at[at])
            return carry

        lax.fori_loop(0, table[SHARES_AT + slot], begin, 0)
    for slot in range(RB_DEV):

        def finish(i, carry, slot=slot):
            at = slot * half + i
            wait_page(spot(out, at), sems.at[at])
            return carry

        lax.fori_loop(0, table[SHARES_AT + slot], finish, 0)


def attend_kernel(group, first, blocks, caps, carried, project, table, queries, own, *refs):
    refs = list(refs)
    weight = refs.pop(0) if project else None
    summed = refs.pop(0) if carried else None
    sems, stacked = refs.pop(), refs.pop()
    slab = refs.pop() if project else None
    store = refs.pop()
    terms = refs.pop() if project else None
    out = refs.pop()
    heads, room = len(group), len(blocks) * PMAX

    def region(i):
        if i == 0:
            return 0, table[LENGTH_AT + blocks[0]]
        base = table[BASE_AT + blocks[i]]
        return base, jnp.where(base == 0, 0, table[LENGTH_AT + blocks[i]])

    for h, g in enumerate(group):
        buffers = numbered(refs, caps, first + h)
        for i, b in enumerate(blocks):
            base, count = region(i)
            codes = SLOT_AT + table[BASE_AT + b]

            def begin(j, carry, h=h, g=g, buffers=buffers, base=base, codes=codes):
                at = h * room + base + j
                target, sem = spot(store, at), sems.at[at]
                start_page(buffers, table[codes + j], g * PAIR, target, sem)
                return carry

            lax.fori_loop(0, count, begin, 0)
            length = table[LENGTH_AT + b]

            def clear(j, carry, h=h, base=base):
                rows = pl.ds(pl.multiple_of((h * room + base + j) * BLOCK, BLOCK), BLOCK)
                store[rows, :] = jnp.zeros((BLOCK, PAIR), jnp.bfloat16)
                return carry

            lax.fori_loop(length, (length + SPAN - 1) & -SPAN, clear, 0)
    if project:
        share = slab.shape[1]
        theirs = pl.multiple_of(table[THEIRS_AT] * share, share)
        fetch = pltpu.make_async_copy(
            weight.at[pl.ds(group[0] * WIDTH, heads * WIDTH), pl.ds(theirs, share)],
            slab,
            sems.at[heads * room],
        )
        fetch.start()

    def one_block(h, i, b, base, count):
        tokens = pl.ds(pl.multiple_of(i * BLOCK, BLOCK), BLOCK)

        def columns(width, extra=0):
            return pl.ds(pl.multiple_of(h * width + extra, HD), min(width, HD))

        for e in range(GROUP):
            stacked[e * BLOCK : (e + 1) * BLOCK, :] = queries[tokens, columns(WIDTH, e * HD)]
        base = h * room + base

        def finish(j, carry):
            wait_page(spot(store, base + j), sems.at[base + j])
            return carry

        lax.fori_loop(0, count, finish, 0)
        length = table[LENGTH_AT + b]
        span = RB_DEV * BLOCK
        row = lax.broadcasted_iota(jnp.int32, (ROWS, span), 0) & (BLOCK - 1)
        key = lax.broadcasted_iota(jnp.int32, (ROWS, span), 1)
        own_mask = (key <= row + b * BLOCK) & (key >= table[LOW_AT + b])

        def run(spans):
            wide_key = lax.broadcasted_iota(jnp.int32, (ROWS, SPAN * BLOCK), 1)
            last_mask = wide_key < (length - (spans - 1) * SPAN) * BLOCK
            pieces = [(own[:, columns(PAIR)], own[:, columns(PAIR, HD)])]
            for t in range(spans):
                at = pl.multiple_of((base + t * SPAN) * BLOCK, BLOCK)
                piece = store[pl.ds(at, SPAN * BLOCK), :]
                pieces.append((piece[:, :HD], piece[:, HD:]))

            def score(r, t):
                scores = lax.dot_general(
                    stacked[r * ROWS : (r + 1) * ROWS, :],
                    pieces[t][0],
                    (((1,), (1,)), ((), ())),
                    preferred_element_type=jnp.float32,
                )
                if t == 0:
                    return jnp.where(own_mask, scores, NEG_LARGE)
                if t == spans:
                    return jnp.where(last_mask, scores, NEG_LARGE)
                return scores

            def highest(scores, sofar):
                for n in range(0, scores.shape[1], HD):
                    part = scores[:, n : n + HD]
                    sofar = part if sofar is None else jnp.maximum(sofar, part)
                return sofar

            def blend(scores, top, t):
                spread = jnp.concatenate([top] * (scores.shape[1] // HD), axis=1)
                weights = jnp.exp2((scores - spread) * SCALE).astype(jnp.bfloat16)
                values = pieces[t][1]
                values = jnp.concatenate([values, jnp.ones_like(values)], axis=1)
                return jnp.dot(weights, values, preferred_element_type=jnp.float32)

            chunks, ahead, peak = GROUP * BLOCK // ROWS, [], None
            for t in range(spans + 1):
                ahead.append(score(0, t))
                peak = highest(ahead[-1], peak)
            for r in range(chunks):
                now, ahead = ahead, []
                top = jnp.broadcast_to(jnp.max(peak, axis=1, keepdims=True), (ROWS, HD))
                total, peak = None, None
                for t in range(spans + 1):
                    if r + 1 < chunks:
                        ahead.append(score(r + 1, t))
                        peak = highest(ahead[-1], peak)
                    blended = blend(now[t], top, t)
                    total = blended if total is None else total + blended
                mean = (total[:, :HD] / total[:, HD:]).astype(jnp.bfloat16)
                for e in range(ROWS // BLOCK):
                    at = columns(WIDTH, (r * (ROWS // BLOCK) + e) * HD)
                    out[tokens, at] = mean[e * BLOCK : (e + 1) * BLOCK, :]

        spans = lax.shift_right_logical(length + SPAN - 1, SPAN.bit_length() - 1)
        for n in range(1, PMAX // SPAN + 1):
            pl.when(spans == n)(lambda n=n: run(n))

    def step(n, carry):
        if len(blocks) == 1:
            one_block(n, 0, blocks[0], *region(0))
            return carry
        h, i = lax.shift_right_logical(n, 1), n & 1
        base = jnp.where(i == 0, 0, region(1)[0])
        one_block(h, i, i, base, jnp.where(i == 0, region(0)[1], region(1)[1]))
        return carry

    lax.fori_loop(0, heads * len(blocks), step, 0)
    if project:
        fetch.wait()
        attended = out[...]
        width = math.gcd(share, 512)
        for n in range(0, share, width):
            term = jnp.dot(attended, slab[:, n : n + width], preferred_element_type=jnp.float32)
            if carried:
                term = term + summed[:, n : n + width]
            terms[:, n : n + width] = term.astype(terms.dtype)


def attend(
    group, first, blocks, last, caps, table, queries, resp_kv, buffers, weight=None, share=0, summed=None
):
    tokens, heads = len(blocks) * BLOCK, len(group)
    at = blocks[0] // len(blocks)
    project, carried = weight is not None, summed is not None
    any_spec = pl.BlockSpec(memory_space=pl.ANY)
    whole = pl.BlockSpec((tokens, share), lambda i, c: (0, 0))
    out_shape = [jax.ShapeDtypeStruct((tokens, heads * WIDTH), jnp.bfloat16)]
    out_specs = [pl.BlockSpec((tokens, heads * WIDTH), lambda i, c: (0, 0))]
    operands, in_specs = [], []
    scratch = [pltpu.VMEM((heads * len(blocks) * PMAX * BLOCK, PAIR), jnp.bfloat16)]
    if project:
        operands, in_specs = [weight], [any_spec]
        kept = jnp.bfloat16 if last else jnp.float32
        out_shape.append(jax.ShapeDtypeStruct((tokens, share), kept))
        out_specs.append(whole)
        scratch.append(pltpu.VMEM((heads * WIDTH, share), jnp.bfloat16))
    if carried:
        operands = operands + [summed]
        in_specs = in_specs + [pl.BlockSpec((tokens, share), lambda i, c: (at, 0))]
    column = group[0] // heads
    return pl.pallas_call(
        lambda *refs: attend_kernel(group, first, blocks, caps, carried, project, *refs),
        out_shape=out_shape,
        grid_spec=pltpu.PrefetchScalarGridSpec(
            num_scalar_prefetch=1,
            grid=(1,),
            in_specs=[
                pl.BlockSpec((tokens, heads * WIDTH), lambda i, c: (at, column)),
                pl.BlockSpec((RB_DEV * BLOCK, heads * PAIR), lambda i, c: (0, column)),
            ]
            + in_specs
            + [any_spec] * len(buffers),
            out_specs=out_specs,
            scratch_shapes=scratch
            + [
                pltpu.VMEM((GROUP * BLOCK, HD), jnp.bfloat16),
                pltpu.SemaphoreType.DMA((heads * len(blocks) * PMAX + 1,)),
            ],
        ),
        compiler_params=params(ATTEND_MIB),
        cost_estimate=SMALL,
        name="attend_heads_" + "_".join(map(str, group)) + "_blocks_" + "_".join(map(str, blocks)),
    )(table, queries, resp_kv, *operands, *buffers)


def pages_shape(count):
    return jax.ShapeDtypeStruct((count * BLOCK, PAIR), jnp.bfloat16)


def pack_send(wide, cores, groups, caps, skip, ctrl, pool, planned=False):
    any_spec = pl.BlockSpec(memory_space=pl.ANY)
    pages = PROMPTS * ((PMAX + wide - 1) // wide)
    rooms = (caps.near, caps.near, caps.far)
    if groups is None:
        shapes = [jax.ShapeDtypeStruct((n * BLOCK, pool.shape[1]), jnp.bfloat16) for n in rooms]
    else:
        shapes = [pages_shape(n * len(group)) for group in groups for n in rooms]
    heads = 1 if groups is None else sum(map(len, groups))
    columns, first = (PAIR, groups[0][0]) if heads == 1 and groups else (pool.shape[1], 0)
    out_specs = [any_spec] * len(shapes)
    scratch = [pltpu.SemaphoreType.DMA((3, pages, heads))]
    if planned:
        shapes = shapes + [jax.ShapeDtypeStruct((TABLE,), jnp.int32)]
        out_specs = out_specs + [pl.BlockSpec(memory_space=pltpu.SMEM)]
        scratch.append(pltpu.SMEM((wide * SUMS,), jnp.int32))
    return pl.pallas_call(
        lambda *refs: send_kernel(wide, cores, groups, caps, skip, planned, *refs),
        out_shape=shapes,
        grid_spec=pltpu.PrefetchScalarGridSpec(
            num_scalar_prefetch=1,
            grid=(1,),
            in_specs=[pl.BlockSpec((pool.shape[0], columns), lambda i, c: (0, first))],
            out_specs=out_specs,
            scratch_shapes=scratch,
        ),
        compiler_params=params(8),
        cost_estimate=SMALL,
        name="pack_extra" if groups is None else f"pack_send_{groups[0][0]}",
    )(ctrl, pool)


def pack_share(cores, caps, h, g, table, buffers):
    any_spec = pl.BlockSpec(memory_space=pl.ANY)
    return pl.pallas_call(
        lambda *refs: share_kernel(cores, caps, h, g, *refs),
        out_shape=pages_shape(PMAX),
        grid_spec=pltpu.PrefetchScalarGridSpec(
            num_scalar_prefetch=1,
            grid=(1,),
            in_specs=[any_spec] * len(buffers),
            out_specs=pl.BlockSpec((PMAX * BLOCK, PAIR), lambda i, c: (0, 0)),
            scratch_shapes=[pltpu.SemaphoreType.DMA((PMAX,))],
        ),
        compiler_params=params(6),
        cost_estimate=SMALL,
        name=f"pack_share_{g}",
    )(table, *buffers)


def pack_relay(cores, caps, g, ctrl, *lists):
    any_spec = pl.BlockSpec(memory_space=pl.ANY)
    pages = max(2 * caps.relay, caps.far)
    return pl.pallas_call(
        lambda *refs: relay_kernel(cores, caps, *refs),
        out_shape=pages_shape(pages),
        grid_spec=pltpu.PrefetchScalarGridSpec(
            num_scalar_prefetch=1,
            grid=(1,),
            in_specs=[any_spec] * len(lists),
            out_specs=pl.BlockSpec((pages * BLOCK, PAIR), lambda i, c: (0, 0)),
            scratch_shapes=[pltpu.SemaphoreType.DMA((3,))],
        ),
        compiler_params=params(6),
        cost_estimate=SMALL,
        name=f"pack_relay_{g}",
    )(ctrl, *lists)


def after(value, *earlier):
    return lax.optimization_barrier((value, *earlier))[0]


def line_attend(wide, cores, caps, ctrl, queries, resp_kv, pool, weight):
    heads = resp_kv.shape[1] // PAIR
    share = weight.shape[1] // 2

    def hop(x, moves):
        pairs = [(a * cores + c, b * cores + c) for a, b in moves for c in range(cores)]
        return lax.ppermute(x, "wide", pairs)

    swap = [(d, d // cores * cores + (cores - 1 - d % cores)) for d in range(wide)]

    def sideways(right, left):
        return hop(right, [(0, 1), (1, 2), (2, 3)]), hop(left, [(3, 2), (2, 1), (1, 0)])

    past = Caps(1, 1, 0)

    def past_the_end(ctrl, pool):
        skip = (caps.near, caps.near, caps.far)
        right, left, far = pack_send(wide, cores, None, past, skip, ctrl, pool)
        found = *sideways(right, left), hop(far, [(0, 2), (3, 1)])
        return jnp.concatenate(found, axis=0)

    def nothing(ctrl, pool):
        return jnp.zeros((3 * past.near * BLOCK, pool.shape[1]), pool.dtype)

    both, last = list(range(RB_DEV)), heads - 1
    sends, far, onwards, held, parts = {}, {}, {}, {}, []
    for g in range(min(2, heads)):
        planned = g == min(1, heads - 1)
        sends[g] = pack_send(wide, cores, [[g]], caps, (0, 0, 0), ctrl, pool, planned)
    *sends[min(1, heads - 1)], table = sends[min(1, heads - 1)]
    over = table[OVER_AT] == 1
    extra = lax.cond(over, past_the_end, nothing, ctrl, pool)

    def relay(g, plan):
        following = []
        left, right = sideways(*sends[g][:2])
        if g == 0:
            far[0] = hop(sends[0][2], [(0, 2), (3, 1)])
        if g + 1 < heads:
            if g + 1 not in sends:
                sends[g + 1] = pack_send(wide, cores, [[g + 1]], caps, (0, 0, 0), ctrl, pool)
            following = sends[g + 1][2:]
        onward = pack_relay(cores, caps, g, plan, far[g], left, right, *following)
        onwards[g] = onward
        far[g + 1] = hop(onward, [(2, 3), (1, 0)] + ([(0, 2), (3, 1)] if following else []))
        held[g] = [pool, left, right, far[g], far[g + 1]]

    relay(0, after(ctrl, extra))

    def exchange(g, plan):
        shared = pack_share(cores, caps, 0, g, plan, held[g] + [extra])
        return held[g] + [lax.ppermute(shared, "wide", swap), extra]

    summed = None
    for g in range(last):
        relay(g + 1, after(ctrl, parts[-1]) if parts else ctrl)
        buffers = exchange(g, after(table, onwards[g + 1]))
        attended, summed = attend(
            [g], 0, both, False, caps, table, queries, resp_kv, buffers, weight, share, summed
        )
        parts.append(attended)
    buffers = exchange(last, after(table, parts[-1]) if parts else table)
    ends, terms, plan = [], [], table
    for b in both:
        end, term = attend(
            [last], 0, [b], True, caps, plan, queries, resp_kv, buffers, weight, share, summed
        )
        ends.append(end)
        terms.append(term)
        plan = after(table, end)
    return parts + [jnp.concatenate(ends, axis=0)], terms


def project_kernel(carried, at, *refs):
    parts, weight, out = refs[: -2 - carried], refs[-2 - carried], refs[-1]
    total, row = refs[-2][...] if carried else None, 0
    for part in parts:
        end = row + part.shape[1]
        term = jnp.dot(part[...], weight[row:end, :], preferred_element_type=jnp.float32)
        total, row = term if total is None else total + term, end
    out[...] = total.astype(out.dtype)


def project(parts, weight, first, first_column, columns, kept=jnp.bfloat16, summed=None):
    tokens, rows = parts[0].shape[0], sum(part.shape[1] for part in parts)
    tile = math.gcd(columns, 512)
    assert weight.shape[1] % tile == 0
    at = jnp.reshape(first_column // tile, (1,)).astype(jnp.int32)
    skip = first * WIDTH
    if skip % rows:
        weight_spec = pl.BlockSpec(
            (pl.Element(rows), pl.Element(tile)), lambda i, at: (skip, (at[0] + i) * tile)
        )
    else:
        weight_spec = pl.BlockSpec((rows, tile), lambda i, at: (skip // rows, at[0] + i))
    operands, in_specs = [*parts, weight], [
        pl.BlockSpec(part.shape, lambda i, at: (0, 0)) for part in parts
    ] + [weight_spec]
    if summed is not None:
        operands.append(summed)
        in_specs.append(pl.BlockSpec((tokens, tile), lambda i, at: (0, i)))
    return pl.pallas_call(
        lambda *refs: project_kernel(summed is not None, *refs),
        out_shape=jax.ShapeDtypeStruct((tokens, columns), kept),
        grid_spec=pltpu.PrefetchScalarGridSpec(
            num_scalar_prefetch=1,
            grid=(columns // tile,),
            in_specs=in_specs,
            out_specs=pl.BlockSpec((tokens, tile), lambda i, at: (0, i)),
        ),
        compiler_params=params(PROJECT_MIB),
        cost_estimate=SMALL,
        name="project",
    )(at, *operands)


def add_terms(total, arrived, block):
    rows, columns = arrived.shape
    tile = columns // 2
    spec = pl.BlockSpec((rows, tile), lambda i: (block, i))

    def kernel(own, other, out):
        out[...] = (own[...].astype(jnp.float32) + other[...].astype(jnp.float32)).astype(out.dtype)

    return pl.pallas_call(
        kernel,
        out_shape=jax.ShapeDtypeStruct(total.shape, total.dtype),
        grid=(columns // tile,),
        in_specs=[spec, pl.BlockSpec((rows, tile), lambda i: (0, i))],
        out_specs=spec,
        input_output_aliases={0: 0},
        compiler_params=params(8),
        cost_estimate=SMALL,
        name=f"add_terms_{block}",
    )(total, arrived)


def local(
    queries, resp_kv, prefix_pool, out_weight, pre_len, prompt_blocks, prompt_owner, resp_seg
):
    wide, groups = lax.axis_size("wide"), lax.axis_size("tp") * lax.axis_size("sub")
    cores = 2 // lax.axis_size("sub")
    heads = resp_kv.shape[1] // PAIR
    me = lax.axis_index("wide").astype(jnp.int32)
    group = lax.axis_index("tp") * lax.axis_size("sub") + lax.axis_index("sub")
    where = jnp.stack([me, (1 - group).astype(jnp.int32)])
    ctrl = jnp.concatenate([pre_len, prompt_blocks, prompt_owner, resp_seg, where])
    columns = out_weight.shape[1]
    share = columns // groups
    if wide == 8 and cores == 2 and groups == 2:
        parts, theirs = line_attend(
            wide, cores, CAPS, ctrl, queries, resp_kv, prefix_pool, out_weight
        )
        axis = "tp" if lax.axis_size("tp") == 2 else "sub"
        arrived = [lax.ppermute(terms, axis, [(0, 1), (1, 0)]) for terms in theirs]
        half = share // 2
        mine = [
            project(parts, out_weight, 0, group * share, half),
            project(parts, out_weight, 0, after(group, arrived[0]) * share + half, half),
        ]
        mine = jnp.concatenate(mine, axis=1)
        return add_terms(add_terms(mine, arrived[0], 0), arrived[1], 1)
    table = make_plan(wide, cores, False, ctrl)
    buffers = [lax.all_gather(prefix_pool, "wide", axis=0, tiled=True)]
    blocks = list(range(RB_DEV))
    parts = [
        attend([g], 0, blocks, False, CAPS, table, queries, resp_kv, buffers)[0] for g in range(heads)
    ]
    terms = project(parts, out_weight, 0, jnp.int32(0), columns)
    return lax.psum_scatter(terms, ("tp", "sub"), scatter_dimension=1, tiled=True)


def solution(mesh):
    return jax.shard_map(
        local,
        mesh=mesh,
        in_specs=(
            P(("parts", "wide"), ("tp", "sub")),
            P(("parts", "wide"), ("tp", "sub")),
            P(("parts", "wide"), ("tp", "sub")),
            P(("tp", "sub"), None),
            P("parts"),
            P("parts"),
            P("parts"),
            P(("parts", "wide")),
        ),
        out_specs=P(("parts", "wide"), ("tp", "sub")),
        check_vma=False,
    )
```
